32 devices in a mesh: dp: 4 (over y, x), fsdp: 8 (over z, core).
Axes of the slice: x: 2, y: 2, z: 4, core: 2. Of those that a mesh axis runs over, the one named last changes fastest.
Arguments:
- latents: bfloat16 [64, 864, 768], P(('dp', 'fsdp')), may hold values from -6 to 6
- captions: bfloat16 [64, 256, 1024], P(('dp', 'fsdp')), may hold values from -6 to 6
- caption_lengths: int32 [64], P(('dp', 'fsdp')), may hold values from 5 to 256, as said below
- timesteps: int32 [64], P(('dp', 'fsdp')), may hold values from 0 to 999
- cotangent: bfloat16 [64, 864, 768], P(('dp', 'fsdp')), may hold values from -6 to 6
- master_weights: float32 [15151104], P(('dp', 'fsdp')), may hold values from -2 to 2
- first_moment: float32 [15151104], P(('dp', 'fsdp')), may hold values from -0.08563604577551912 to 0.08563604577551912
- second_moment: float32 [15151104], P(('dp', 'fsdp')), may hold values from 3.3000896e-05 to 0.00052867435
Outputs:
- output: bfloat16 [64, 864, 768], P(('dp', 'fsdp'))
- input_grad: bfloat16 [64, 864, 768], P(('dp', 'fsdp'))
- grad_norm: float32 [], replicated
- new_master: float32 [15151104], P(('dp', 'fsdp'))
- new_first: float32 [15151104], P(('dp', 'fsdp'))
- new_second: float32 [15151104], P(('dp', 'fsdp'))
The draws below stay inside these ranges and needn't reach their ends.
Inputs may be any that keep to these rules, and one draw needn't show every extreme that they name: `caption_lengths`: some clip has a caption of exactly 256 tokens and another one of exactly 5.
All inputs are finite; a program needn't handle non-finite values.
Results may differ from the reference program's by a relative error of at most 0.023.
Values may be sent and summed in bfloat16 or wider, within the bound.
A program may use at most 320 MiB of HBM per device.

```python
import math
import jax
import jax.numpy as jnp
from jax import lax

D = 768
HEADS = 12
HD = 64
FF = 3072
CTX = 1024
FRAMES = 864
CAP = 256
STEP = 5
CLIPS = 64
PARAMS = 15151104


CLIP_VALUE = 500.0


def region_sizes():
    return [9 * D * D, 9 * D, 3 * D * D, D * D, D, D * D, 2 * CTX * D, D * D, D, D * FF, FF, FF * D, D]


def region_scale(scales):
    position = jnp.arange(PARAMS)
    result = jnp.zeros((PARAMS,), jnp.float32)
    start = 0
    for extent, amount in zip(region_sizes(), scales):
        result = jnp.where((position >= start) & (position < start + extent), amount, result)
        start += extent
    return result


def draw_master_weights(key, part):
    key = jax.random.fold_in(key, 11)
    inverse_root = 1.0 / math.sqrt(D)
    scales = [inverse_root, 0.5, inverse_root, math.sqrt(FRAMES) * inverse_root / 4.0, 0.2, inverse_root, 1.0 / math.sqrt(CTX), math.sqrt(CAP) * inverse_root / 2.0, 0.2, inverse_root, 0.2, 1.0 / math.sqrt(FF), 0.2]
    base = jax.random.truncated_normal(key, -4.0, 4.0, (PARAMS,), jnp.float32)
    return base * region_scale(scales)


def draw_first_moment(key, part):
    key = jax.random.fold_in(key, 12)
    expected = 2.0 * CLIP_VALUE / math.sqrt(PARAMS)
    base = jax.random.truncated_normal(key, -3.0, 3.0, (PARAMS,), jnp.float32)
    return base * (expected / 9.0)


def draw_second_moment(key, part):
    key = jax.random.fold_in(key, 13)
    expected = 2.0 * CLIP_VALUE / math.sqrt(PARAMS)
    spread = jnp.exp(jax.random.uniform(key, (PARAMS,), jnp.float32, math.log(0.5), math.log(8.0)))
    return spread * (0.001001 * expected * expected)


def draw_caption_lengths(key, part):
    key = jax.random.fold_in(key, 21)
    subkeys = jax.random.split(key, 3)
    lengths = jax.random.randint(subkeys[0], (CLIPS,), 5, CAP + 1)
    longest = jax.random.randint(subkeys[1], (), 0, CLIPS)
    shortest = (longest + 1 + jax.random.randint(subkeys[2], (), 0, CLIPS - 1)) % CLIPS
    position = jnp.arange(CLIPS)
    lengths = jnp.where(position == longest, CAP, lengths)
    return jnp.where(position == shortest, 5, lengths).astype(jnp.int32)


def plant(drawn, stream_key, smallest, top_value):
    dims = drawn.shape
    spot = [jax.random.randint(jax.random.fold_in(stream_key, axis), (), 0, dims[axis]) for axis in range(len(dims))]
    drawn = drawn.at[tuple(spot)].set(smallest)
    longest = dims.index(max(dims))
    spot[longest] = (spot[longest] + 1) % dims[longest]
    return drawn.at[tuple(spot)].set(top_value)


def steps_of(rng, shape, shards, low, largest):
    def one(dim, parts):
        heights = jax.random.uniform(jax.random.fold_in(jax.random.fold_in(rng, 6), dim), (parts,), jnp.float32, low / len(shards), largest / len(shards))
        return jnp.repeat(jnp.exp(heights), shape[dim] // parts).reshape((-1,) + (1,) * (len(shape) - dim - 1))

    factor_of = one(*shards[0])
    for cut in shards[1:]:
        factor_of = factor_of * one(*cut)
    return factor_of


def normal_values(stream_key, dims, scale, bound, cuts=(), held_as=jnp.bfloat16):
    drawn = scale * jax.random.normal(stream_key, dims, jnp.float32)
    if cuts:
        drawn = drawn * steps_of(stream_key, dims, cuts, -0.22, 0.18)
    return jnp.clip(drawn, -bound, bound).astype(held_as)


def setup_inputs(seed: int = 0) -> dict:
    seeds = jax.random.split(jax.random.key(seed), 9)
    latents = normal_values(seeds[0], (CLIPS, FRAMES, D), 1.0, 6.0, ((0, 32),))
    captions = normal_values(seeds[1], (CLIPS, CAP, CTX), 1.0, 6.0, ((0, 32),))
    caption_lengths = draw_caption_lengths(jax.random.fold_in(seeds[8], 71), 0)
    timesteps = plant(jax.random.randint(seeds[3], (CLIPS,), 0, 1000), jax.random.fold_in(seeds[3], 1), 0, 999).astype(jnp.int32)
    cotangent = normal_values(seeds[4], (CLIPS, FRAMES, D), 1.0, 6.0, ((0, 32),))
    master_weights = draw_master_weights(jax.random.fold_in(seeds[8], 71), 0)
    first_moment = draw_first_moment(jax.random.fold_in(seeds[8], 71), 0)
    second_moment = draw_second_moment(jax.random.fold_in(seeds[8], 71), 0)
    return dict(latents=latents, captions=captions, caption_lengths=caption_lengths, timesteps=timesteps, cotangent=cotangent, master_weights=master_weights, first_moment=first_moment, second_moment=second_moment)


NORM_EPS = 1e-06
BETA_ONE = 0.9
BETA_TWO = 0.999
ADAM_EPS = 1e-08
RATE = 0.03
DECAY = 0.01
CLIP = 500.0

@jax.custom_vjp
def low(v):
    return lax.optimization_barrier(v.astype(jnp.bfloat16)).astype(jnp.float32)

@jax.custom_vjp
def low_back(v):
    return v

def low_keep(v):
    return (low(v), None)

def low_pass(kept, grad):
    return (grad,)

def back_keep(v):
    return (v, None)

def back_low(kept, grad):
    return (low(grad),)
low.defvjp(low_keep, low_pass)
low_back.defvjp(back_keep, back_low)

def layout_sizes():
    return [(D, 9 * D), (9 * D,), (D, 3 * D), (D, D), (D,), (D, D), (CTX, 2 * D), (D, D), (D,), (D, FF), (FF,), (FF, D), (D,)]

def unpack(flat_vector):
    pieces = []
    offset = 0
    for layout_shape in layout_sizes():
        number = math.prod(layout_shape)
        pieces.append(flat_vector[offset:offset + number].reshape(layout_shape))
        offset += number
    return pieces

def embed(steps_in):
    half_width = D // 2
    frequency = jnp.exp(-math.log(10000.0) * jnp.arange(half_width, dtype=jnp.float32) / half_width)
    angles = steps_in.astype(jnp.float32)[:, None] * frequency[None, :]
    return jnp.concatenate([jnp.cos(angles), jnp.sin(angles)], axis=1)

def hmul(left_side, right_side):
    return jnp.dot(left_side, right_side, precision=lax.Precision.HIGHEST)

def both(operand):
    return low_back(low(operand))

def normalize(hidden):
    centred = hidden - lax.optimization_barrier(jnp.mean(hidden, axis=-1, keepdims=True))
    return centred * lax.rsqrt(lax.optimization_barrier(jnp.mean(centred * centred, axis=-1, keepdims=True)) + NORM_EPS)

def attend(queries, keyset, valueset, usable):
    query_view = queries.reshape(queries.shape[0], HEADS, HD)
    key_view = keyset.reshape(keyset.shape[0], HEADS, HD)
    value_view = valueset.reshape(valueset.shape[0], HEADS, HD)
    scores = low_back(jnp.einsum('qhd,khd->hqk', query_view, key_view, precision=lax.Precision.HIGHEST)) * HD ** (-0.5)
    if usable is not None:
        scores = jnp.where(usable[None, None, :], scores, -1e+30)
    probability = low(jnp.exp(scores - jax.nn.logsumexp(scores, axis=-1, keepdims=True)))
    mixture = jnp.einsum('hqk,khd->qhd', probability, value_view, precision=lax.Precision.HIGHEST)
    return mixture.reshape(queries.shape[0], HEADS * HD)

def clip_forward(weights, latent, caption, length, mod_row):
    triple_weight, output_weight, output_bias, cross_query, cross_keyval, cross_output, cross_bias, up_weight, up_bias, down_weight, down_bias = weights
    mod_parts = [mod_row[block_index * D:(block_index + 1) * D] for block_index in range(9)]
    first_in = low(normalize(latent) * (1.0 + mod_parts[1]) + mod_parts[0])
    triple = both(hmul(first_in, triple_weight))
    attended = both(attend(triple[:, :D], triple[:, D:2 * D], triple[:, 2 * D:], None))
    branch_one = low_back(hmul(attended, output_weight) + output_bias)
    after_self = latent + mod_parts[2] * branch_one
    second_in = low(normalize(after_self) * (1.0 + mod_parts[4]) + mod_parts[3])
    cross_queries = both(hmul(second_in, cross_query))
    cross_pairs = both(hmul(caption, cross_keyval))
    usable = jnp.arange(CAP) < length
    crossed = both(attend(cross_queries, cross_pairs[:, :D], cross_pairs[:, D:], usable))
    branch_two = low_back(hmul(crossed, cross_output) + cross_bias)
    after_cross = after_self + mod_parts[5] * branch_two
    third_in = low(normalize(after_cross) * (1.0 + mod_parts[7]) + mod_parts[6])
    hidden = low_back(hmul(third_in, up_weight) + up_bias)
    activated = low(jax.nn.gelu(hidden, approximate=True))
    branch_three = low_back(hmul(activated, down_weight) + down_bias)
    return after_cross + mod_parts[8] * branch_three

def reference(latents, captions, caption_lengths, timesteps, cotangent, master_weights, first_moment, second_moment):
    caption_data = captions.astype(jnp.float32)

    def forward(inputs, flat_vector):
        weights = unpack(low(flat_vector))
        condition = low(jax.nn.silu(embed(timesteps)))
        modulation = low_back(hmul(condition, weights[0]) + weights[1])

        def one_clip(packed):
            latent, caption, length, mod_row = packed
            return clip_forward(weights[2:], latent, caption, length, mod_row)
        return lax.map(jax.checkpoint(one_clip), (inputs, caption_data, caption_lengths, modulation))
    output, pullback = jax.vjp(forward, latents.astype(jnp.float32), master_weights)
    grad_inputs, grad_flat = pullback(cotangent.astype(jnp.float32))
    grad_norm = jnp.sqrt(jnp.sum(grad_flat * grad_flat))
    clipped = grad_flat * (CLIP / jnp.maximum(grad_norm, CLIP))
    new_first = BETA_ONE * first_moment + (1.0 - BETA_ONE) * clipped
    new_second = BETA_TWO * second_moment + (1.0 - BETA_TWO) * clipped * clipped
    step_first = new_first / (1.0 - BETA_ONE ** STEP)
    step_second = new_second / (1.0 - BETA_TWO ** STEP)
    new_master = master_weights - RATE * (step_first / (jnp.sqrt(step_second) + ADAM_EPS) + DECAY * master_weights)
    return (output.astype(jnp.bfloat16), grad_inputs.astype(jnp.bfloat16), grad_norm, new_master, new_first, new_second)
```

```python
import functools
import math

import jax
import jax.numpy as jnp
from jax import lax
from jax.experimental import pallas as pl
from jax.experimental.pallas import tpu as pltpu
from jax.sharding import PartitionSpec as P

D = 768
HEADS = 12
HD = 64
FF = 3072
CTX = 1024
STEP = 5


NORM_EPS = 1e-06
BETA_ONE = 0.9
BETA_TWO = 0.999
ADAM_EPS = 1e-08
RATE = 0.03
DECAY = 0.01
CLIP = 500.0


def layout_sizes():
    return [
        (D, 9 * D),
        (9 * D,),
        (D, 3 * D),
        (D, D),
        (D,),
        (D, D),
        (CTX, 2 * D),
        (D, D),
        (D,),
        (D, FF),
        (FF,),
        (FF, D),
        (D,),
    ]


def unpack(flat_vector):
    pieces = []
    offset = 0
    for layout_shape in layout_sizes():
        number = math.prod(layout_shape)
        pieces.append(flat_vector[offset : offset + number].reshape(layout_shape))
        offset += number
    return pieces


def embed(steps_in):
    half_width = D // 2
    frequency = jnp.exp(-math.log(10000.0) * jnp.arange(half_width, dtype=jnp.float32) / half_width)
    angles = steps_in.astype(jnp.float32)[:, None] * frequency[None, :]
    return jnp.concatenate([jnp.cos(angles), jnp.sin(angles)], axis=1)


def normalize(hidden):
    centred = hidden - jnp.mean(hidden, axis=-1, keepdims=True)
    inverse = lax.rsqrt(jnp.mean(centred * centred, axis=-1, keepdims=True) + NORM_EPS)
    return (centred * inverse, inverse)


def norm_back(normed, inverse, grad_normed):
    return inverse * (
        grad_normed
        - jnp.mean(grad_normed, axis=-1, keepdims=True)
        - normed * jnp.mean(grad_normed * normed, axis=-1, keepdims=True)
    )


F32 = jnp.float32
BF = jnp.bfloat16
VMEM_LIMIT = 60 << 20


def nn(left_side, right_side):
    return lax.dot_general(
        left_side, right_side, (((1,), (0,)), ((), ())), preferred_element_type=F32
    )


def nt(left_side, right_side):
    return lax.dot_general(
        left_side, right_side, (((1,), (1,)), ((), ())), preferred_element_type=F32
    )


def tn(left_side, right_side):
    return lax.dot_general(
        left_side, right_side, (((0,), (0,)), ((), ())), preferred_element_type=F32
    )


def call(body, grid, in_specs, out_specs, out_shape, name, scratch=()):
    return pl.pallas_call(
        body,
        grid=grid,
        in_specs=in_specs,
        out_specs=out_specs,
        out_shape=out_shape,
        scratch_shapes=list(scratch),
        compiler_params=pltpu.CompilerParams(vmem_limit_bytes=VMEM_LIMIT),
        name=name,
    )


def struct(shape, dtype):
    return jax.ShapeDtypeStruct(shape, dtype)


def rows_spec(rows, width):
    return pl.BlockSpec((1, rows, width), lambda i, j: (i, j, 0))


def clip_spec(count, width):
    return pl.BlockSpec((1, count, width), lambda i, j: (i, 0, 0))


def whole_spec(shape):
    return pl.BlockSpec(shape, lambda *_: (0,) * len(shape))


def row_block(frames):
    for parts in (2, 3, 4, 6):
        if frames % (16 * parts) == 0:
            return frames // parts
    return frames


def add_to(ref, first, value):
    @pl.when(first)
    def _():
        ref[...] = value

    @pl.when(jnp.logical_not(first))
    def _():
        ref[...] += value


def column_sum(value):
    return jnp.sum(value, axis=0, keepdims=True)


def qkv_kernel(x_ref, mod_ref, w_ref, out_ref):
    normed, _ = normalize(x_ref[0].astype(F32))
    first_in = (normed * (1.0 + mod_ref[0, 1:2]) + mod_ref[0, 0:1]).astype(BF)
    out_ref[0] = nn(first_in, w_ref[...]).astype(BF)


def qkv_forward(latents, mod, weight):
    clips, frames, width = latents.shape
    rows = row_block(frames)
    wide = weight.shape[1]
    return call(
        qkv_kernel,
        (clips, frames // rows),
        [rows_spec(rows, width), clip_spec(9, width), whole_spec(weight.shape)],
        rows_spec(rows, wide),
        struct((clips, frames, wide), BF),
        "qkv_forward",
    )(latents, mod, weight)


def head_lanes():
    lane = lax.broadcasted_iota(jnp.int32, (1, 2 * HD), 1)
    return lane, lane < HD


def usable_bias(length, count):
    row = lax.broadcasted_iota(jnp.int32, (count, 2 * HD), 0)
    return jnp.where(row < length, 0.0, -1e30).astype(BF)


def attend_kernel(*refs, masked):
    if masked:
        len_ref, q_ref, k_ref, v_ref, o_ref, l_ref = refs
    else:
        q_ref, k_ref, v_ref, o_ref, l_ref = refs
    k, v = k_ref[0], v_ref[0]
    scaled = q_ref[0] * jnp.asarray(HD**-0.5, BF)
    lane, low = head_lanes()
    one = jnp.ones((), BF)
    zero = jnp.zeros((), BF)
    values = [jnp.where(low, v, one), jnp.where(low, one, v)]
    if masked:
        bias = usable_bias(len_ref[pl.program_id(0)], k.shape[0])
        tag = jnp.where(lane % HD == 0, one, zero)
        queries = [jnp.where(low, scaled, tag), jnp.where(low, tag, scaled)]
        keys = [jnp.where(low, k, bias), jnp.where(low, bias, k)]
    else:
        queries = [jnp.where(low, scaled, zero), jnp.where(low, zero, scaled)]
        keys = [k, k]
    tops, mixes = [], []
    for head in range(2):
        scores = nt(queries[head], keys[head])
        top = jnp.max(scores, axis=1, keepdims=True)
        mixes.append(nn(jnp.exp(scores - top).astype(BF), values[head]))
        tops.append(top)
    total = jnp.where(low, mixes[1], mixes[0])
    l_ref[0, 0] = jnp.where(low, tops[1], tops[0]) + jnp.log(total)
    o_ref[0] = (jnp.where(low, mixes[0], mixes[1]) / pltpu.roll(total, HD, 1)).astype(BF)


def pair_spec(rows, offset):
    return pl.BlockSpec((1, rows, 2 * HD), lambda i, j: (i, 0, j + offset))


def lse_spec(rows):
    return pl.BlockSpec((1, 1, rows, 2 * HD), lambda i, j: (i, j, 0, 0))


def attend_forward(queries, key_offset, pairs, value_offset, lengths, name):
    clips, frames = queries.shape[:2]
    slots = pairs.shape[1]
    groups = HEADS // 2
    masked = lengths is not None
    specs = [
        pair_spec(frames, 0),
        pair_spec(slots, key_offset),
        pair_spec(slots, value_offset),
    ]
    args = [queries, pairs, pairs]
    if masked:
        specs.insert(0, pl.BlockSpec(memory_space=pltpu.SMEM))
        args.insert(0, lengths)
    return call(
        functools.partial(attend_kernel, masked=masked),
        (clips, groups),
        specs,
        [pair_spec(frames, 0), lse_spec(frames)],
        [struct((clips, frames, D), BF), struct((clips, groups, frames, 2 * HD), F32)],
        name,
    )(*args)


def three_parts(value):
    high = value.astype(BF)
    rest = value - high.astype(F32)
    middle = rest.astype(BF)
    return high, middle, (rest - middle.astype(F32)).astype(BF)


def attend_back_kernel(*refs, masked):
    if masked:
        len_ref, q_ref, k_ref, v_ref, do_ref, o_ref, l_ref, dq_ref, dk_ref, dv_ref = refs
    else:
        q_ref, k_ref, v_ref, do_ref, o_ref, l_ref, dq_ref, dk_ref, dv_ref = refs
    k, v, grad = k_ref[0], v_ref[0], do_ref[0]
    scaled = q_ref[0] * jnp.asarray(HD**-0.5, BF)
    lane, low = head_lanes()
    spot = lane % HD
    one = jnp.ones((), BF)
    zero = jnp.zeros((), BF)
    product = grad.astype(F32) * o_ref[0].astype(F32)
    delta_low = jnp.sum(jnp.where(low, product, 0.0), axis=1, keepdims=True)
    delta_high = jnp.sum(jnp.where(low, 0.0, product), axis=1, keepdims=True)

    def negated(value, last):
        high, middle, rest = three_parts(-value)
        return jnp.where(
            spot == 0,
            high,
            jnp.where(spot == 1, middle, jnp.where(spot == 2, rest, last)),
        )

    tag = jnp.where(spot == 3, one, zero) if masked else zero
    lse_lanes = negated(l_ref[0, 0], tag)
    delta_lanes = negated(jnp.where(low, delta_high, delta_low), zero)
    ones = jnp.broadcast_to(jnp.where(spot < 3, one, zero), k.shape)
    key_lanes = ones
    if masked:
        bias = usable_bias(len_ref[pl.program_id(0)], k.shape[0])
        key_lanes = jnp.where(spot == 3, bias, ones)
    transposed = k.astype(F32).T.astype(BF)
    grad_queries, grad_keys, grad_values = [], [], []
    for head in range(2):

        def merge(own, other):
            return jnp.where(low, own, other) if head == 0 else jnp.where(low, other, own)

        probability = jnp.exp(nt(merge(k, key_lanes), merge(scaled, lse_lanes)))
        centred = nt(merge(v, ones), merge(grad, delta_lanes))
        grad_scores = (probability * centred).astype(BF)
        grad_values.append(nn(probability.astype(BF), grad))
        grad_keys.append(nn(grad_scores, scaled))
        grad_queries.append(nn(transposed[HD * head : HD * (head + 1)], grad_scores))
    dv_ref[0] = jnp.where(low, grad_values[0], grad_values[1]).astype(BF)
    dk_ref[0] = jnp.where(low, grad_keys[0], grad_keys[1]).astype(BF)
    dq_ref[0] = (jnp.concatenate(grad_queries, axis=0).T * HD**-0.5).astype(BF)


def attend_backward(queries, key_offset, pairs, value_offset, lengths, grad, mixed, lse, name):
    clips, frames = queries.shape[:2]
    slots = pairs.shape[1]
    groups = HEADS // 2
    masked = lengths is not None
    specs = [
        pair_spec(frames, 0),
        pair_spec(slots, key_offset),
        pair_spec(slots, value_offset),
        pair_spec(frames, 0),
        pair_spec(frames, 0),
        lse_spec(frames),
    ]
    args = [queries, pairs, pairs, grad, mixed, lse]
    if masked:
        specs.insert(0, pl.BlockSpec(memory_space=pltpu.SMEM))
        args.insert(0, lengths)
    return call(
        functools.partial(attend_back_kernel, masked=masked),
        (clips, groups),
        specs,
        [pair_spec(frames, 0), pair_spec(slots, 0), pair_spec(slots, 0)],
        [
            struct((clips, frames, D), BF),
            struct((clips, slots, D), BF),
            struct((clips, slots, D), BF),
        ],
        name,
    )(*args)


def after_self_kernel(o_ref, x_ref, mod_ref, wo_ref, bo_ref, wq_ref, z_ref, h_ref, q_ref):
    branch = nn(o_ref[0], wo_ref[...]) + bo_ref[...]
    hidden = x_ref[0].astype(F32) + mod_ref[0, 2:3] * branch
    normed, _ = normalize(hidden)
    second_in = (normed * (1.0 + mod_ref[0, 4:5]) + mod_ref[0, 3:4]).astype(BF)
    z_ref[0] = branch.astype(BF)
    h_ref[0] = hidden
    q_ref[0] = nn(second_in, wq_ref[...]).astype(BF)


def after_self(mixed, latents, mod, weight, bias, query_weight):
    clips, frames, width = latents.shape
    rows = row_block(frames)
    spec = rows_spec(rows, width)
    square = whole_spec((width, width))
    return call(
        after_self_kernel,
        (clips, frames // rows),
        [spec, spec, clip_spec(9, width), square, whole_spec((1, width)), square],
        [spec, spec, spec],
        [
            struct(latents.shape, BF),
            struct(latents.shape, F32),
            struct(latents.shape, BF),
        ],
        "after_self",
    )(mixed, latents, mod, weight, bias, query_weight)


def after_cross_kernel(o_ref, h_ref, mod_ref, wo_ref, bo_ref, z_ref, out_ref):
    branch = nn(o_ref[0], wo_ref[...]) + bo_ref[...]
    z_ref[0] = branch.astype(BF)
    out_ref[0] = h_ref[0] + mod_ref[0, 5:6] * branch


def after_cross(mixed, hidden, mod, weight, bias):
    clips, frames, width = hidden.shape
    rows = row_block(frames)
    spec = rows_spec(rows, width)
    return call(
        after_cross_kernel,
        (clips, frames // rows),
        [
            spec,
            spec,
            clip_spec(9, width),
            whole_spec((width, width)),
            whole_spec((1, width)),
        ],
        [spec, spec],
        [struct(hidden.shape, BF), struct(hidden.shape, F32)],
        "after_cross",
    )(mixed, hidden, mod, weight, bias)


GELU_ROOT = math.sqrt(2.0 / math.pi)


def feed_kernel(
    h_ref,
    dy_ref,
    mod_ref,
    up_ref,
    upb_ref,
    down_ref,
    downb_ref,
    out_ref,
    dh_ref,
    dup_ref,
    ddown_ref,
    dupb_ref,
    ddownb_ref,
    sums_ref,
    in_s,
    int_s,
    dz_s,
    dzt_s,
    z_s,
    *,
    clips,
    frames,
    rows,
):
    step = pl.program_id(0)
    last = pl.num_programs(0) - 1
    spans = [
        (clip, start, clip * frames + start)
        for clip in range(clips)
        for start in range(0, frames, rows)
    ]

    @pl.when(step == 0)
    def _():
        bias_sum = jnp.zeros((1, h_ref.shape[2]), F32)
        for clip, start, at in spans:
            normed, _ = normalize(h_ref[clip, start : start + rows])
            third_in = normed * (1.0 + mod_ref[clip, 7:8]) + mod_ref[clip, 6:7]
            dz = (mod_ref[clip, 8:9] * dy_ref[clip, start : start + rows].astype(F32)).astype(BF)
            in_s[at : at + rows] = third_in.astype(BF)
            dz_s[at : at + rows] = dz
            bias_sum += column_sum(dz.astype(F32))
        ddownb_ref[...] = bias_sum
        int_s[...] = in_s[...].T
        dzt_s[...] = dz_s[...].T

    up, down = up_ref[...], down_ref[...]
    grad_up = grad_down = grad_bias = None
    for clip, start, at in spans:
        here = pl.ds(at, rows)
        hidden = nn(in_s[here], up) + upb_ref[...]
        square = hidden * hidden
        tanh = jnp.tanh(GELU_ROOT * hidden * (1.0 + 0.044715 * square))
        half = 0.5 + 0.5 * tanh
        activated = (hidden * half).astype(BF)
        slope = half + hidden * half * (1.0 - tanh) * (
            GELU_ROOT * (1.0 + 3 * 0.044715 * square)
        )
        dz = dz_s[here]
        grad_hidden = (nt(dz, down) * slope).astype(BF)
        branch = nn(activated, down)
        grad_in = nt(grad_hidden, up)

        @pl.when(step == 0)
        def _(branch=branch, grad_in=grad_in, here=here, clip=clip, start=start):
            z_s[here] = branch
            dh_ref[clip, start : start + rows] = grad_in

        @pl.when(step > 0)
        def _(branch=branch, grad_in=grad_in, here=here, clip=clip, start=start):
            z_s[here] += branch
            dh_ref[clip, start : start + rows] += grad_in

        one_up = nn(int_s[:, at : at + rows], grad_hidden)
        one_down = nn(dzt_s[:, at : at + rows], activated)
        one_bias = column_sum(grad_hidden.astype(F32))
        grad_up = one_up if grad_up is None else grad_up + one_up
        grad_down = one_down if grad_down is None else grad_down + one_down
        grad_bias = one_bias if grad_bias is None else grad_bias + one_bias
    dup_ref[...] = grad_up.astype(BF)
    ddown_ref[...] = grad_down.T.astype(BF)
    dupb_ref[...] = grad_bias

    @pl.when(step == last)
    def _():
        for clip in range(clips):
            sums = None
            for start in range(0, frames, rows):
                at = clip * frames + start
                block = slice(start, start + rows)
                hidden = h_ref[clip, block]
                dy = dy_ref[clip, block].astype(F32)
                branch = z_s[at : at + rows] + downb_ref[...]
                out_ref[clip, block] = (hidden + mod_ref[clip, 8:9] * branch).astype(BF)
                normed, inverse = normalize(hidden)
                grad_in = dh_ref[clip, block]
                dh_ref[clip, block] = dy + norm_back(
                    normed, inverse, grad_in * (1.0 + mod_ref[clip, 7:8])
                )
                here = [
                    column_sum(grad_in),
                    column_sum(grad_in * normed),
                    column_sum(dy * branch),
                ]
                sums = here if sums is None else [a + b for a, b in zip(sums, here)]
            for index in range(3):
                sums_ref[clip, index : index + 1] = sums[index]


def feed(hidden, cotangent, mod, up, up_bias, down, down_bias, block=512):
    clips, frames, width = hidden.shape
    inner = up.shape[1]
    rows = row_block(frames)
    tokens = clips * frames

    def once(shape):
        return pl.BlockSpec(
            shape, lambda j: (0,) * len(shape), pipeline_mode=pl.Buffered(1)
        )

    def columns(count):
        return pl.BlockSpec((count, block), lambda j: (0, j))

    lines = pl.BlockSpec((block, width), lambda j: (j, 0))
    cube = once((clips, frames, width))
    return call(
        functools.partial(feed_kernel, clips=clips, frames=frames, rows=rows),
        (inner // block,),
        [
            cube,
            cube,
            once(mod.shape),
            columns(width),
            columns(1),
            lines,
            once((1, width)),
        ],
        [
            cube,
            cube,
            columns(width),
            lines,
            columns(1),
            once((1, width)),
            once((clips, 3, width)),
        ],
        [
            struct(hidden.shape, BF),
            struct(hidden.shape, F32),
            struct(up.shape, BF),
            struct(down.shape, BF),
            struct((1, inner), F32),
            struct((1, width), F32),
            struct((clips, 3, width), F32),
        ],
        "feed",
        [
            pltpu.VMEM((tokens, width), BF),
            pltpu.VMEM((width, tokens), BF),
            pltpu.VMEM((tokens, width), BF),
            pltpu.VMEM((width, tokens), BF),
            pltpu.VMEM((tokens, width), F32),
        ],
    )(hidden, cotangent, mod, up, up_bias, down, down_bias)


def ends():
    i, j = pl.program_id(0), pl.program_id(1)
    first = (i == 0) & (j == 0)
    last = (i == pl.num_programs(0) - 1) & (j == pl.num_programs(1) - 1)
    return j == 0, first, last


def before_cross_kernel(
    dh_ref, z_ref, o_ref, mod_ref, w_ref, do_ref, dw_ref, db_ref, sums_ref, dw_s
):
    new_clip, first, last = ends()
    dh = dh_ref[0]
    dz = (mod_ref[0, 5:6] * dh).astype(BF)
    add_to(sums_ref, new_clip, column_sum(dh * z_ref[0].astype(F32))[None])
    add_to(db_ref, first, column_sum(dz.astype(F32)))
    do_ref[0] = nt(dz, w_ref[...]).astype(BF)
    add_to(dw_s, first, tn(o_ref[0], dz))

    @pl.when(last)
    def _():
        dw_ref[...] = dw_s[...].astype(BF)


def before_cross(dh, branch, mixed, mod, weight):
    clips, frames, width = dh.shape
    rows = row_block(frames)
    spec = rows_spec(rows, width)
    square = whole_spec((width, width))
    return call(
        before_cross_kernel,
        (clips, frames // rows),
        [spec, spec, spec, clip_spec(9, width), square],
        [spec, square, whole_spec((1, width)), clip_spec(1, width)],
        [
            struct(dh.shape, BF),
            struct((width, width), BF),
            struct((1, width), F32),
            struct((clips, 1, width), F32),
        ],
        "before_cross",
        [pltpu.VMEM((width, width), F32)],
    )(dh, branch, mixed, mod, weight)


def before_self_kernel(
    dq_ref,
    h_ref,
    dh_ref,
    z_ref,
    o_ref,
    mod_ref,
    wq_ref,
    wo_ref,
    out_ref,
    do_ref,
    dwq_ref,
    dwo_ref,
    db_ref,
    sums_ref,
    dwq_s,
    dwo_s,
):
    new_clip, first, last = ends()
    normed, inverse = normalize(h_ref[0])
    second_in = (normed * (1.0 + mod_ref[0, 4:5]) + mod_ref[0, 3:4]).astype(BF)
    grad_query = dq_ref[0]
    add_to(dwq_s, first, tn(second_in, grad_query))
    grad_in = nt(grad_query, wq_ref[...])
    dh = dh_ref[0] + norm_back(normed, inverse, grad_in * (1.0 + mod_ref[0, 4:5]))
    out_ref[0] = dh
    dz = (mod_ref[0, 2:3] * dh).astype(BF)
    sums = jnp.concatenate(
        [
            column_sum(grad_in),
            column_sum(grad_in * normed),
            column_sum(dh * z_ref[0].astype(F32)),
        ],
        axis=0,
    )
    add_to(sums_ref, new_clip, sums[None])
    add_to(db_ref, first, column_sum(dz.astype(F32)))
    do_ref[0] = nt(dz, wo_ref[...]).astype(BF)
    add_to(dwo_s, first, tn(o_ref[0], dz))

    @pl.when(last)
    def _():
        dwq_ref[...] = dwq_s[...].astype(BF)
        dwo_ref[...] = dwo_s[...].astype(BF)


def before_self(grad_query, hidden, dh, branch, mixed, mod, query_weight, weight):
    clips, frames, width = dh.shape
    rows = row_block(frames)
    spec = rows_spec(rows, width)
    square = whole_spec((width, width))
    return call(
        before_self_kernel,
        (clips, frames // rows),
        [spec, spec, spec, spec, spec, clip_spec(9, width), square, square],
        [spec, spec, square, square, whole_spec((1, width)), clip_spec(3, width)],
        [
            struct(dh.shape, F32),
            struct(dh.shape, BF),
            struct((width, width), BF),
            struct((width, width), BF),
            struct((1, width), F32),
            struct((clips, 3, width), F32),
        ],
        "before_self",
        [pltpu.VMEM((width, width), F32), pltpu.VMEM((width, width), F32)],
    )(grad_query, hidden, dh, branch, mixed, mod, query_weight, weight)


def input_kernel(
    dq_ref, dk_ref, dv_ref, x_ref, dh_ref, mod_ref, w_ref, out_ref, dw_ref, sums_ref, dw_s
):
    new_clip, first, last = ends()
    width = x_ref.shape[2]
    normed, inverse = normalize(x_ref[0].astype(F32))
    first_in = (normed * (1.0 + mod_ref[0, 1:2]) + mod_ref[0, 0:1]).astype(BF)
    turned = first_in.T
    grad_in = None
    for index, ref in enumerate((dq_ref, dk_ref, dv_ref)):
        columns = slice(index * width, (index + 1) * width)
        grad = ref[0]
        part = nt(grad, w_ref[:, columns])
        grad_in = part if grad_in is None else grad_in + part
        add_to(dw_s.at[:, columns], first, nn(turned, grad))
    out_ref[0] = (
        dh_ref[0] + norm_back(normed, inverse, grad_in * (1.0 + mod_ref[0, 1:2]))
    ).astype(BF)
    sums = jnp.concatenate([column_sum(grad_in), column_sum(grad_in * normed)], axis=0)
    add_to(sums_ref, new_clip, sums[None])

    @pl.when(last)
    def _():
        dw_ref[...] = dw_s[...].astype(BF)


def input_back(grads, latents, dh, mod, weight):
    clips, frames, width = dh.shape
    rows = row_block(frames)
    spec = rows_spec(rows, width)
    return call(
        input_kernel,
        (clips, frames // rows),
        [spec] * 5 + [clip_spec(9, width), whole_spec(weight.shape)],
        [spec, whole_spec(weight.shape), clip_spec(2, width)],
        [
            struct(dh.shape, BF),
            struct(weight.shape, BF),
            struct((clips, 2, width), F32),
        ],
        "input_back",
        [pltpu.VMEM(weight.shape, F32)],
    )(*grads, latents, dh, mod, weight)


def block_pass(latents, captions, lengths, cotangent, mod, weights):
    (
        triple_weight,
        output_weight,
        output_bias,
        cross_query,
        cross_keyval,
        cross_output,
        cross_bias,
        up_weight,
        up_bias,
        down_weight,
        down_bias,
    ) = weights
    clips, frames, width = latents.shape
    slots = captions.shape[1]
    groups = HEADS // 2
    caption_flat = captions.reshape(clips * slots, captions.shape[2])
    triple = qkv_forward(latents, mod, triple_weight)
    mixed_one, lse_one = attend_forward(triple, groups, triple, 2 * groups, None, "self_forward")
    branch_one, hidden_one, cross_queries = after_self(
        mixed_one, latents, mod, output_weight, output_bias, cross_query
    )
    pairs = (
        jnp.dot(caption_flat, cross_keyval, preferred_element_type=F32)
        .astype(BF)
        .reshape(clips, slots, 2 * width)
    )
    mixed_two, lse_two = attend_forward(cross_queries, 0, pairs, groups, lengths, "cross_forward")
    branch_two, hidden_two = after_cross(mixed_two, hidden_one, mod, cross_output, cross_bias)
    output, dh_two, grad_up, grad_down, grad_up_bias, grad_down_bias, sums_three = feed(
        hidden_two, cotangent, mod, up_weight, up_bias, down_weight, down_bias
    )
    grad_mixed_two, grad_cross_output, grad_cross_bias, gate_two = before_cross(
        dh_two, branch_two, mixed_two, mod, cross_output
    )
    grad_cq, grad_ck, grad_cv = attend_backward(
        cross_queries, 0, pairs, groups, lengths, grad_mixed_two, mixed_two, lse_two, "cross_back"
    )
    grad_pairs = jnp.concatenate([grad_ck, grad_cv], axis=-1).reshape(clips * slots, 2 * width)
    grad_keyval = jnp.dot(caption_flat.T, grad_pairs, preferred_element_type=F32).astype(BF)
    dh_one, grad_mixed_one, grad_cross_query, grad_output, grad_output_bias, sums_two = before_self(
        grad_cq, hidden_one, dh_two, branch_one, mixed_one, mod, cross_query, output_weight
    )
    grads_one = attend_backward(
        triple,
        groups,
        triple,
        2 * groups,
        None,
        grad_mixed_one,
        mixed_one,
        lse_one,
        "self_back",
    )
    input_grad, grad_triple, sums_one = input_back(grads_one, latents, dh_one, mod, triple_weight)
    grad_mod = jnp.concatenate(
        [sums_one, sums_two[:, 2:], sums_two[:, :2], gate_two, sums_three], axis=1
    ).astype(BF)
    return (
        output,
        input_grad,
        grad_mod,
        [
            grad_triple,
            grad_output,
            grad_output_bias,
            grad_cross_query,
            grad_keyval,
            grad_cross_output,
            grad_cross_bias,
            grad_up,
            grad_up_bias,
            grad_down,
            grad_down_bias,
        ],
    )


def local(
    latents,
    captions,
    caption_lengths,
    timesteps,
    cotangent,
    master_weights,
    first_moment,
    second_moment,
):
    clip_count, frames, model_width = latents.shape
    share = master_weights.shape[0]
    outer_count = lax.axis_size("dp")
    inner_count = lax.axis_size("fsdp")
    gathered = lax.all_gather(
        master_weights.astype(BF).reshape(1, share), ("dp", "fsdp"), axis=0, tiled=True
    ).reshape(-1)
    weights = unpack(gathered)
    condition = jax.nn.silu(embed(timesteps)).astype(BF)
    modulation = jnp.dot(condition, weights[0], preferred_element_type=F32) + weights[1].astype(F32)
    mod = modulation.reshape(clip_count, 9, model_width)
    block_weights = [w.astype(F32).reshape(1, -1) if w.ndim == 1 else w for w in weights[2:]]
    output, input_grad, grad_mod, gradients = block_pass(
        latents, captions, caption_lengths, cotangent, mod, block_weights
    )
    grad_mod = grad_mod.reshape(clip_count, 9 * model_width)
    grad_ada = jnp.dot(condition.T, grad_mod, preferred_element_type=F32)
    grad_ada_bias = jnp.sum(grad_mod.astype(F32), axis=0)
    gradient_list = [grad_ada, grad_ada_bias] + gradients
    flat_grad = jnp.concatenate([piece.astype(F32).reshape(-1) for piece in gradient_list])
    owner_rows = flat_grad.reshape(outer_count * inner_count, share)
    grad_shard = lax.psum_scatter(
        owner_rows, ("dp", "fsdp"), scatter_dimension=0, tiled=True
    ).reshape(share)
    squares = lax.psum(jnp.sum(grad_shard * grad_shard), ("dp", "fsdp"))
    grad_norm = jnp.sqrt(squares)
    clipped = grad_shard * (CLIP / jnp.maximum(grad_norm, CLIP))
    new_first = BETA_ONE * first_moment + (1.0 - BETA_ONE) * clipped
    new_second = BETA_TWO * second_moment + (1.0 - BETA_TWO) * clipped * clipped
    step_first = new_first / (1.0 - BETA_ONE**STEP)
    step_second = new_second / (1.0 - BETA_TWO**STEP)
    new_master = master_weights - RATE * (
        step_first / (jnp.sqrt(step_second) + ADAM_EPS) + DECAY * master_weights
    )
    return (output, input_grad, grad_norm, new_master, new_first, new_second)


def solution(mesh):
    placed = (
        P(("dp", "fsdp"), None, None),
        P(("dp", "fsdp"), None, None),
        P(("dp", "fsdp")),
        P(("dp", "fsdp")),
        P(("dp", "fsdp"), None, None),
        P(("dp", "fsdp")),
        P(("dp", "fsdp")),
        P(("dp", "fsdp")),
    )
    return jax.shard_map(
        local,
        mesh=mesh,
        in_specs=placed,
        out_specs=(
            P(("dp", "fsdp"), None, None),
            P(("dp", "fsdp"), None, None),
            P(),
            P(("dp", "fsdp")),
            P(("dp", "fsdp")),
            P(("dp", "fsdp")),
        ),
        check_vma=False,
    )
```

```python
import functools
import math

import jax
import jax.numpy as jnp
from jax import lax
from jax.experimental import pallas as pl
from jax.experimental.pallas import tpu as pltpu
from jax.sharding import PartitionSpec as P

D = 768
HEADS = 12
HD = 64
FF = 3072
CTX = 1024
STEP = 5


NORM_EPS = 1e-06
BETA_ONE = 0.9
BETA_TWO = 0.999
ADAM_EPS = 1e-08
RATE = 0.03
DECAY = 0.01
CLIP = 500.0


def layout_sizes():
    return [
        (D, 9 * D),
        (9 * D,),
        (D, 3 * D),
        (D, D),
        (D,),
        (D, D),
        (CTX, 2 * D),
        (D, D),
        (D,),
        (D, FF),
        (FF,),
        (FF, D),
        (D,),
    ]


def unpack(flat_vector):
    pieces = []
    offset = 0
    for layout_shape in layout_sizes():
        number = math.prod(layout_shape)
        pieces.append(flat_vector[offset : offset + number].reshape(layout_shape))
        offset += number
    return pieces


def embed(steps_in):
    half_width = D // 2
    frequency = jnp.exp(-math.log(10000.0) * jnp.arange(half_width, dtype=jnp.float32) / half_width)
    angles = steps_in.astype(jnp.float32)[:, None] * frequency[None, :]
    return jnp.concatenate([jnp.cos(angles), jnp.sin(angles)], axis=1)


def normalize(hidden):
    centred = hidden - jnp.mean(hidden, axis=-1, keepdims=True)
    inverse = lax.rsqrt(jnp.mean(centred * centred, axis=-1, keepdims=True) + NORM_EPS)
    return (centred * inverse, inverse)


def norm_back(normed, inverse, grad_normed):
    return inverse * (
        grad_normed
        - jnp.mean(grad_normed, axis=-1, keepdims=True)
        - normed * jnp.mean(grad_normed * normed, axis=-1, keepdims=True)
    )


F32 = jnp.float32
BF = jnp.bfloat16
VMEM_LIMIT = 60 << 20


def nn(left_side, right_side):
    return lax.dot_general(
        left_side, right_side, (((1,), (0,)), ((), ())), preferred_element_type=F32
    )


def nt(left_side, right_side):
    return lax.dot_general(
        left_side, right_side, (((1,), (1,)), ((), ())), preferred_element_type=F32
    )


def tn(left_side, right_side):
    return lax.dot_general(
        left_side, right_side, (((0,), (0,)), ((), ())), preferred_element_type=F32
    )


def call(body, grid, in_specs, out_specs, out_shape, name, scratch=()):
    return pl.pallas_call(
        body,
        grid=grid,
        in_specs=in_specs,
        out_specs=out_specs,
        out_shape=out_shape,
        scratch_shapes=list(scratch),
        compiler_params=pltpu.CompilerParams(vmem_limit_bytes=VMEM_LIMIT),
        name=name,
    )


def struct(shape, dtype):
    return jax.ShapeDtypeStruct(shape, dtype)


def rows_spec(rows, width):
    return pl.BlockSpec((1, rows, width), lambda i, j: (i, j, 0))


def clip_spec(count, width):
    return pl.BlockSpec((1, count, width), lambda i, j: (i, 0, 0))


def whole_spec(shape):
    return pl.BlockSpec(shape, lambda *_: (0,) * len(shape))


def row_block(frames):
    for parts in (2, 3, 4, 6):
        if frames % (16 * parts) == 0:
            return frames // parts
    return frames


def add_to(ref, first, value):
    @pl.when(first)
    def _():
        ref[...] = value

    @pl.when(jnp.logical_not(first))
    def _():
        ref[...] += value


def column_sum(value):
    return jnp.sum(value, axis=0, keepdims=True)


def qkv_kernel(x_ref, mod_ref, w_ref, out_ref):
    normed, _ = normalize(x_ref[0].astype(F32))
    first_in = (normed * (1.0 + mod_ref[0, 1:2]) + mod_ref[0, 0:1]).astype(BF)
    out_ref[0] = nn(first_in, w_ref[...]).astype(BF)


def qkv_forward(latents, mod, weight):
    clips, frames, width = latents.shape
    rows = row_block(frames)
    wide = weight.shape[1]
    return call(
        qkv_kernel,
        (clips, frames // rows),
        [rows_spec(rows, width), clip_spec(9, width), whole_spec(weight.shape)],
        rows_spec(rows, wide),
        struct((clips, frames, wide), BF),
        "qkv_forward",
    )(latents, mod, weight)


def head_lanes():
    lane = lax.broadcasted_iota(jnp.int32, (1, 2 * HD), 1)
    return lane, lane < HD


def usable_bias(length, count):
    row = lax.broadcasted_iota(jnp.int32, (count, 2 * HD), 0)
    return jnp.where(row < length, 0.0, -1e30).astype(BF)


def attend_kernel(*refs, masked):
    if masked:
        len_ref, q_ref, k_ref, v_ref, o_ref, l_ref = refs
    else:
        q_ref, k_ref, v_ref, o_ref, l_ref = refs
    k, v = k_ref[0], v_ref[0]
    scaled = q_ref[0] * jnp.asarray(HD**-0.5, BF)
    lane, low = head_lanes()
    one = jnp.ones((), BF)
    zero = jnp.zeros((), BF)
    values = [jnp.where(low, v, one), jnp.where(low, one, v)]
    if masked:
        bias = usable_bias(len_ref[pl.program_id(0)], k.shape[0])
        tag = jnp.where(lane % HD == 0, one, zero)
        queries = [jnp.where(low, scaled, tag), jnp.where(low, tag, scaled)]
        keys = [jnp.where(low, k, bias), jnp.where(low, bias, k)]
    else:
        queries = [jnp.where(low, scaled, zero), jnp.where(low, zero, scaled)]
        keys = [k, k]
    tops, mixes = [], []
    for head in range(2):
        scores = nt(queries[head], keys[head])
        top = jnp.max(scores, axis=1, keepdims=True)
        mixes.append(nn(jnp.exp(scores - top).astype(BF), values[head]))
        tops.append(top)
    total = jnp.where(low, mixes[1], mixes[0])
    l_ref[0, 0] = jnp.where(low, tops[1], tops[0]) + jnp.log(total)
    o_ref[0] = (jnp.where(low, mixes[0], mixes[1]) / pltpu.roll(total, HD, 1)).astype(BF)


def pair_spec(rows, offset):
    return pl.BlockSpec((1, rows, 2 * HD), lambda i, j: (i, 0, j + offset))


def lse_spec(rows):
    return pl.BlockSpec((1, 1, rows, 2 * HD), lambda i, j: (i, j, 0, 0))


def attend_forward(queries, key_offset, pairs, value_offset, lengths, name):
    clips, frames = queries.shape[:2]
    slots = pairs.shape[1]
    groups = HEADS // 2
    masked = lengths is not None
    specs = [
        pair_spec(frames, 0),
        pair_spec(slots, key_offset),
        pair_spec(slots, value_offset),
    ]
    args = [queries, pairs, pairs]
    if masked:
        specs.insert(0, pl.BlockSpec(memory_space=pltpu.SMEM))
        args.insert(0, lengths)
    return call(
        functools.partial(attend_kernel, masked=masked),
        (clips, groups),
        specs,
        [pair_spec(frames, 0), lse_spec(frames)],
        [struct((clips, frames, D), BF), struct((clips, groups, frames, 2 * HD), F32)],
        name,
    )(*args)


def three_parts(value):
    high = value.astype(BF)
    rest = value - high.astype(F32)
    middle = rest.astype(BF)
    return high, middle, (rest - middle.astype(F32)).astype(BF)


def attend_back_kernel(*refs, masked):
    if masked:
        len_ref, q_ref, k_ref, v_ref, do_ref, o_ref, l_ref, dq_ref, dk_ref, dv_ref = refs
    else:
        q_ref, k_ref, v_ref, do_ref, o_ref, l_ref, dq_ref, dk_ref, dv_ref = refs
    k, v, grad = k_ref[0], v_ref[0], do_ref[0]
    scaled = q_ref[0] * jnp.asarray(HD**-0.5, BF)
    lane, low = head_lanes()
    spot = lane % HD
    one = jnp.ones((), BF)
    zero = jnp.zeros((), BF)
    product = grad.astype(F32) * o_ref[0].astype(F32)
    delta_low = jnp.sum(jnp.where(low, product, 0.0), axis=1, keepdims=True)
    delta_high = jnp.sum(jnp.where(low, 0.0, product), axis=1, keepdims=True)

    def negated(value, last):
        high, middle, rest = three_parts(-value)
        return jnp.where(
            spot == 0,
            high,
            jnp.where(spot == 1, middle, jnp.where(spot == 2, rest, last)),
        )

    tag = jnp.where(spot == 3, one, zero) if masked else zero
    lse_lanes = negated(l_ref[0, 0], tag)
    delta_lanes = negated(jnp.where(low, delta_high, delta_low), zero)
    ones = jnp.broadcast_to(jnp.where(spot < 3, one, zero), k.shape)
    key_lanes = ones
    if masked:
        bias = usable_bias(len_ref[pl.program_id(0)], k.shape[0])
        key_lanes = jnp.where(spot == 3, bias, ones)
    transposed = k.astype(F32).T.astype(BF)
    grad_queries, grad_keys, grad_values = [], [], []
    for head in range(2):

        def merge(own, other):
            return jnp.where(low, own, other) if head == 0 else jnp.where(low, other, own)

        probability = jnp.exp(nt(merge(k, key_lanes), merge(scaled, lse_lanes)))
        centred = nt(merge(v, ones), merge(grad, delta_lanes))
        grad_scores = (probability * centred).astype(BF)
        grad_values.append(nn(probability.astype(BF), grad))
        grad_keys.append(nn(grad_scores, scaled))
        grad_queries.append(nn(transposed[HD * head : HD * (head + 1)], grad_scores))
    dv_ref[0] = jnp.where(low, grad_values[0], grad_values[1]).astype(BF)
    dk_ref[0] = jnp.where(low, grad_keys[0], grad_keys[1]).astype(BF)
    dq_ref[0] = (jnp.concatenate(grad_queries, axis=0).T * HD**-0.5).astype(BF)


def attend_backward(queries, key_offset, pairs, value_offset, lengths, grad, mixed, lse, name):
    clips, frames = queries.shape[:2]
    slots = pairs.shape[1]
    groups = HEADS // 2
    masked = lengths is not None
    specs = [
        pair_spec(frames, 0),
        pair_spec(slots, key_offset),
        pair_spec(slots, value_offset),
        pair_spec(frames, 0),
        pair_spec(frames, 0),
        lse_spec(frames),
    ]
    args = [queries, pairs, pairs, grad, mixed, lse]
    if masked:
        specs.insert(0, pl.BlockSpec(memory_space=pltpu.SMEM))
        args.insert(0, lengths)
    return call(
        functools.partial(attend_back_kernel, masked=masked),
        (clips, groups),
        specs,
        [pair_spec(frames, 0), pair_spec(slots, 0), pair_spec(slots, 0)],
        [
            struct((clips, frames, D), BF),
            struct((clips, slots, D), BF),
            struct((clips, slots, D), BF),
        ],
        name,
    )(*args)


def after_self_kernel(o_ref, x_ref, mod_ref, wo_ref, bo_ref, wq_ref, z_ref, h_ref, q_ref):
    branch = nn(o_ref[0], wo_ref[...]) + bo_ref[...]
    hidden = x_ref[0].astype(F32) + mod_ref[0, 2:3] * branch
    normed, _ = normalize(hidden)
    second_in = (normed * (1.0 + mod_ref[0, 4:5]) + mod_ref[0, 3:4]).astype(BF)
    z_ref[0] = branch.astype(BF)
    h_ref[0] = hidden
    q_ref[0] = nn(second_in, wq_ref[...]).astype(BF)


def after_self(mixed, latents, mod, weight, bias, query_weight):
    clips, frames, width = latents.shape
    rows = row_block(frames)
    spec = rows_spec(rows, width)
    square = whole_spec((width, width))
    return call(
        after_self_kernel,
        (clips, frames // rows),
        [spec, spec, clip_spec(9, width), square, whole_spec((1, width)), square],
        [spec, spec, spec],
        [
            struct(latents.shape, BF),
            struct(latents.shape, F32),
            struct(latents.shape, BF),
        ],
        "after_self",
    )(mixed, latents, mod, weight, bias, query_weight)


def after_cross_kernel(o_ref, h_ref, mod_ref, wo_ref, bo_ref, z_ref, out_ref):
    branch = nn(o_ref[0], wo_ref[...]) + bo_ref[...]
    z_ref[0] = branch.astype(BF)
    out_ref[0] = h_ref[0] + mod_ref[0, 5:6] * branch


def after_cross(mixed, hidden, mod, weight, bias):
    clips, frames, width = hidden.shape
    rows = row_block(frames)
    spec = rows_spec(rows, width)
    return call(
        after_cross_kernel,
        (clips, frames // rows),
        [
            spec,
            spec,
            clip_spec(9, width),
            whole_spec((width, width)),
            whole_spec((1, width)),
        ],
        [spec, spec],
        [struct(hidden.shape, BF), struct(hidden.shape, F32)],
        "after_cross",
    )(mixed, hidden, mod, weight, bias)


GELU_ROOT = math.sqrt(2.0 / math.pi)


def feed_kernel(
    h_ref,
    dy_ref,
    mod_ref,
    up_ref,
    upb_ref,
    down_ref,
    downb_ref,
    out_ref,
    dh_ref,
    dup_ref,
    ddown_ref,
    dupb_ref,
    ddownb_ref,
    sums_ref,
    in_s,
    int_s,
    dz_s,
    dzt_s,
    z_s,
    *,
    clips,
    frames,
    rows,
):
    step = pl.program_id(0)
    last = pl.num_programs(0) - 1
    spans = [
        (clip, start, clip * frames + start)
        for clip in range(clips)
        for start in range(0, frames, rows)
    ]

    @pl.when(step == 0)
    def _():
        bias_sum = jnp.zeros((1, h_ref.shape[2]), F32)
        for clip, start, at in spans:
            normed, _ = normalize(h_ref[clip, start : start + rows])
            third_in = normed * (1.0 + mod_ref[clip, 7:8]) + mod_ref[clip, 6:7]
            dz = (mod_ref[clip, 8:9] * dy_ref[clip, start : start + rows].astype(F32)).astype(BF)
            in_s[at : at + rows] = third_in.astype(BF)
            dz_s[at : at + rows] = dz
            bias_sum += column_sum(dz.astype(F32))
        ddownb_ref[...] = bias_sum
        int_s[...] = in_s[...].T
        dzt_s[...] = dz_s[...].T

    up, down = up_ref[...], down_ref[...]
    grad_up = grad_down = grad_bias = None
    for clip, start, at in spans:
        here = pl.ds(at, rows)
        hidden = nn(in_s[here], up) + upb_ref[...]
        square = hidden * hidden
        tanh = jnp.tanh(GELU_ROOT * hidden * (1.0 + 0.044715 * square))
        half = 0.5 + 0.5 * tanh
        activated = (hidden * half).astype(BF)
        slope = half + hidden * half * (1.0 - tanh) * (
            GELU_ROOT * (1.0 + 3 * 0.044715 * square)
        )
        dz = dz_s[here]
        grad_hidden = (nt(dz, down) * slope).astype(BF)
        branch = nn(activated, down)
        grad_in = nt(grad_hidden, up)

        @pl.when(step == 0)
        def _(branch=branch, grad_in=grad_in, here=here, clip=clip, start=start):
            z_s[here] = branch
            dh_ref[clip, start : start + rows] = grad_in

        @pl.when(step > 0)
        def _(branch=branch, grad_in=grad_in, here=here, clip=clip, start=start):
            z_s[here] += branch
            dh_ref[clip, start : start + rows] += grad_in

        one_up = nn(int_s[:, at : at + rows], grad_hidden)
        one_down = nn(dzt_s[:, at : at + rows], activated)
        one_bias = column_sum(grad_hidden.astype(F32))
        grad_up = one_up if grad_up is None else grad_up + one_up
        grad_down = one_down if grad_down is None else grad_down + one_down
        grad_bias = one_bias if grad_bias is None else grad_bias + one_bias
    dup_ref[...] = grad_up.astype(BF)
    ddown_ref[...] = grad_down.T.astype(BF)
    dupb_ref[...] = grad_bias

    @pl.when(step == last)
    def _():
        for clip in range(clips):
            sums = None
            for start in range(0, frames, rows):
                at = clip * frames + start
                block = slice(start, start + rows)
                hidden = h_ref[clip, block]
                dy = dy_ref[clip, block].astype(F32)
                branch = z_s[at : at + rows] + downb_ref[...]
                out_ref[clip, block] = (hidden + mod_ref[clip, 8:9] * branch).astype(BF)
                normed, inverse = normalize(hidden)
                grad_in = dh_ref[clip, block]
                dh_ref[clip, block] = dy + norm_back(
                    normed, inverse, grad_in * (1.0 + mod_ref[clip, 7:8])
                )
                here = [
                    column_sum(grad_in),
                    column_sum(grad_in * normed),
                    column_sum(dy * branch),
                ]
                sums = here if sums is None else [a + b for a, b in zip(sums, here)]
            for index in range(3):
                sums_ref[clip, index : index + 1] = sums[index]


def feed(hidden, cotangent, mod, up, up_bias, down, down_bias, block=512):
    clips, frames, width = hidden.shape
    inner = up.shape[1]
    rows = row_block(frames)
    tokens = clips * frames

    def once(shape):
        return pl.BlockSpec(
            shape, lambda j: (0,) * len(shape), pipeline_mode=pl.Buffered(1)
        )

    def columns(count):
        return pl.BlockSpec((count, block), lambda j: (0, j))

    lines = pl.BlockSpec((block, width), lambda j: (j, 0))
    cube = once((clips, frames, width))
    return call(
        functools.partial(feed_kernel, clips=clips, frames=frames, rows=rows),
        (inner // block,),
        [
            cube,
            cube,
            once(mod.shape),
            columns(width),
            columns(1),
            lines,
            once((1, width)),
        ],
        [
            cube,
            cube,
            columns(width),
            lines,
            columns(1),
            once((1, width)),
            once((clips, 3, width)),
        ],
        [
            struct(hidden.shape, BF),
            struct(hidden.shape, F32),
            struct(up.shape, BF),
            struct(down.shape, BF),
            struct((1, inner), F32),
            struct((1, width), F32),
            struct((clips, 3, width), F32),
        ],
        "feed",
        [
            pltpu.VMEM((tokens, width), BF),
            pltpu.VMEM((width, tokens), BF),
            pltpu.VMEM((tokens, width), BF),
            pltpu.VMEM((width, tokens), BF),
            pltpu.VMEM((tokens, width), F32),
        ],
    )(hidden, cotangent, mod, up, up_bias, down, down_bias)


def ends():
    i, j = pl.program_id(0), pl.program_id(1)
    first = (i == 0) & (j == 0)
    last = (i == pl.num_programs(0) - 1) & (j == pl.num_programs(1) - 1)
    return j == 0, first, last


def before_cross_kernel(
    dh_ref, z_ref, o_ref, mod_ref, w_ref, do_ref, dw_ref, db_ref, sums_ref, dw_s
):
    new_clip, first, last = ends()
    dh = dh_ref[0]
    dz = (mod_ref[0, 5:6] * dh).astype(BF)
    add_to(sums_ref, new_clip, column_sum(dh * z_ref[0].astype(F32))[None])
    add_to(db_ref, first, column_sum(dz.astype(F32)))
    do_ref[0] = nt(dz, w_ref[...]).astype(BF)
    add_to(dw_s, first, tn(o_ref[0], dz))

    @pl.when(last)
    def _():
        dw_ref[...] = dw_s[...].astype(BF)


def before_cross(dh, branch, mixed, mod, weight):
    clips, frames, width = dh.shape
    rows = row_block(frames)
    spec = rows_spec(rows, width)
    square = whole_spec((width, width))
    return call(
        before_cross_kernel,
        (clips, frames // rows),
        [spec, spec, spec, clip_spec(9, width), square],
        [spec, square, whole_spec((1, width)), clip_spec(1, width)],
        [
            struct(dh.shape, BF),
            struct((width, width), BF),
            struct((1, width), F32),
            struct((clips, 1, width), F32),
        ],
        "before_cross",
        [pltpu.VMEM((width, width), F32)],
    )(dh, branch, mixed, mod, weight)


def before_self_kernel(
    dq_ref,
    h_ref,
    dh_ref,
    z_ref,
    o_ref,
    mod_ref,
    wq_ref,
    wo_ref,
    out_ref,
    do_ref,
    dwq_ref,
    dwo_ref,
    db_ref,
    sums_ref,
    dwq_s,
    dwo_s,
):
    new_clip, first, last = ends()
    normed, inverse = normalize(h_ref[0])
    second_in = (normed * (1.0 + mod_ref[0, 4:5]) + mod_ref[0, 3:4]).astype(BF)
    grad_query = dq_ref[0]
    add_to(dwq_s, first, tn(second_in, grad_query))
    grad_in = nt(grad_query, wq_ref[...])
    dh = dh_ref[0] + norm_back(normed, inverse, grad_in * (1.0 + mod_ref[0, 4:5]))
    out_ref[0] = dh
    dz = (mod_ref[0, 2:3] * dh).astype(BF)
    sums = jnp.concatenate(
        [
            column_sum(grad_in),
            column_sum(grad_in * normed),
            column_sum(dh * z_ref[0].astype(F32)),
        ],
        axis=0,
    )
    add_to(sums_ref, new_clip, sums[None])
    add_to(db_ref, first, column_sum(dz.astype(F32)))
    do_ref[0] = nt(dz, wo_ref[...]).astype(BF)
    add_to(dwo_s, first, tn(o_ref[0], dz))

    @pl.when(last)
    def _():
        dwq_ref[...] = dwq_s[...].astype(BF)
        dwo_ref[...] = dwo_s[...].astype(BF)


def before_self(grad_query, hidden, dh, branch, mixed, mod, query_weight, weight):
    clips, frames, width = dh.shape
    rows = row_block(frames)
    spec = rows_spec(rows, width)
    square = whole_spec((width, width))
    return call(
        before_self_kernel,
        (clips, frames // rows),
        [spec, spec, spec, spec, spec, clip_spec(9, width), square, square],
        [spec, spec, square, square, whole_spec((1, width)), clip_spec(3, width)],
        [
            struct(dh.shape, F32),
            struct(dh.shape, BF),
            struct((width, width), BF),
            struct((width, width), BF),
            struct((1, width), F32),
            struct((clips, 3, width), F32),
        ],
        "before_self",
        [pltpu.VMEM((width, width), F32), pltpu.VMEM((width, width), F32)],
    )(grad_query, hidden, dh, branch, mixed, mod, query_weight, weight)


def input_kernel(
    dq_ref, dk_ref, dv_ref, x_ref, dh_ref, mod_ref, w_ref, out_ref, dw_ref, sums_ref, dw_s
):
    new_clip, first, last = ends()
    width = x_ref.shape[2]
    normed, inverse = normalize(x_ref[0].astype(F32))
    first_in = (normed * (1.0 + mod_ref[0, 1:2]) + mod_ref[0, 0:1]).astype(BF)
    turned = first_in.T
    grad_in = None
    for index, ref in enumerate((dq_ref, dk_ref, dv_ref)):
        columns = slice(index * width, (index + 1) * width)
        grad = ref[0]
        part = nt(grad, w_ref[:, columns])
        grad_in = part if grad_in is None else grad_in + part
        add_to(dw_s.at[:, columns], first, nn(turned, grad))
    out_ref[0] = (
        dh_ref[0] + norm_back(normed, inverse, grad_in * (1.0 + mod_ref[0, 1:2]))
    ).astype(BF)
    sums = jnp.concatenate([column_sum(grad_in), column_sum(grad_in * normed)], axis=0)
    add_to(sums_ref, new_clip, sums[None])

    @pl.when(last)
    def _():
        dw_ref[...] = dw_s[...].astype(BF)


def input_back(grads, latents, dh, mod, weight):
    clips, frames, width = dh.shape
    rows = row_block(frames)
    spec = rows_spec(rows, width)
    return call(
        input_kernel,
        (clips, frames // rows),
        [spec] * 5 + [clip_spec(9, width), whole_spec(weight.shape)],
        [spec, whole_spec(weight.shape), clip_spec(2, width)],
        [
            struct(dh.shape, BF),
            struct(weight.shape, BF),
            struct((clips, 2, width), F32),
        ],
        "input_back",
        [pltpu.VMEM(weight.shape, F32)],
    )(*grads, latents, dh, mod, weight)


def block_pass(latents, captions, lengths, cotangent, mod, weights):
    (
        triple_weight,
        output_weight,
        output_bias,
        cross_query,
        cross_keyval,
        cross_output,
        cross_bias,
        up_weight,
        up_bias,
        down_weight,
        down_bias,
    ) = weights
    clips, frames, width = latents.shape
    slots = captions.shape[1]
    groups = HEADS // 2
    caption_flat = captions.reshape(clips * slots, captions.shape[2])
    triple = qkv_forward(latents, mod, triple_weight)
    mixed_one, lse_one = attend_forward(triple, groups, triple, 2 * groups, None, "self_forward")
    branch_one, hidden_one, cross_queries = after_self(
        mixed_one, latents, mod, output_weight, output_bias, cross_query
    )
    pairs = (
        jnp.dot(caption_flat, cross_keyval, preferred_element_type=F32)
        .astype(BF)
        .reshape(clips, slots, 2 * width)
    )
    mixed_two, lse_two = attend_forward(cross_queries, 0, pairs, groups, lengths, "cross_forward")
    branch_two, hidden_two = after_cross(mixed_two, hidden_one, mod, cross_output, cross_bias)
    output, dh_two, grad_up, grad_down, grad_up_bias, grad_down_bias, sums_three = feed(
        hidden_two, cotangent, mod, up_weight, up_bias, down_weight, down_bias
    )
    grad_mixed_two, grad_cross_output, grad_cross_bias, gate_two = before_cross(
        dh_two, branch_two, mixed_two, mod, cross_output
    )
    grad_cq, grad_ck, grad_cv = attend_backward(
        cross_queries, 0, pairs, groups, lengths, grad_mixed_two, mixed_two, lse_two, "cross_back"
    )
    grad_pairs = jnp.concatenate([grad_ck, grad_cv], axis=-1).reshape(clips * slots, 2 * width)
    grad_keyval = jnp.dot(caption_flat.T, grad_pairs, preferred_element_type=F32).astype(BF)
    dh_one, grad_mixed_one, grad_cross_query, grad_output, grad_output_bias, sums_two = before_self(
        grad_cq, hidden_one, dh_two, branch_one, mixed_one, mod, cross_query, output_weight
    )
    grads_one = attend_backward(
        triple,
        groups,
        triple,
        2 * groups,
        None,
        grad_mixed_one,
        mixed_one,
        lse_one,
        "self_back",
    )
    input_grad, grad_triple, sums_one = input_back(grads_one, latents, dh_one, mod, triple_weight)
    grad_mod = jnp.concatenate(
        [sums_one, sums_two[:, 2:], sums_two[:, :2], gate_two, sums_three], axis=1
    ).astype(BF)
    return (
        output,
        input_grad,
        grad_mod,
        [
            grad_triple,
            grad_output,
            grad_output_bias,
            grad_cross_query,
            grad_keyval,
            grad_cross_output,
            grad_cross_bias,
            grad_up,
            grad_up_bias,
            grad_down,
            grad_down_bias,
        ],
    )


LANE = 128
TILE = 16


def linear_layout():
    spots = []
    offset = 0
    for shape in layout_sizes():
        number = math.prod(shape) // LANE
        spots.append((offset, number, shape))
        offset += number
    return spots


class Plan:
    def __init__(self, devices, share):
        self.devices, self.share = devices, share
        spots = linear_layout()
        self.first_row = spots[2][0]
        self.rows = spots[-1][0] + spots[-1][1]
        self.lead = self.first_row // share
        self.padded = -(-share // TILE) * TILE
        self.lent = -(-(self.padded // 3) // TILE) * TILE
        self.kept = self.padded - self.lent
        self.chunk = 2 * self.lent
        self.base = (self.first_row - self.lead * share) // TILE * TILE

    def find(self, row):
        owner, at = divmod(row, self.share)
        if at < self.kept:
            base = self.base if owner == self.lead else 0
            return owner, at - base, self.kept - at
        if owner == self.lead:
            return self.lead - 1, at - self.kept, self.share - at
        lender = owner - self.lead - 1
        return lender // 2, (lender % 2) * self.lent + at - self.kept, self.share - at

    def segments(self, start, count):
        found = []
        row = start
        while row < start + count:
            chunk, place, left = self.find(row)
            take = min(left, start + count - row)
            found.append((chunk, place, row, take))
            row += take
        return found


def unpack_kernel(*refs, plan, indices, step):
    n = len(indices)
    spots = linear_layout()
    g_ref, outs, rest = refs[0], refs[1 : 1 + n], refs[1 + n :]
    lin, in_sem, out_sem = rest[0], rest[1], rest[2]
    stages, results = rest[3 : 3 + n], rest[3 + n :]
    loads = []
    for which, index in enumerate(indices):
        offset, number, _ = spots[index]
        place = 0
        mine = []
        for slot, (chunk, row, at, take) in enumerate(plan.segments(offset, number)):
            low = row // TILE * TILE
            high = -(-(row + take) // TILE) * TILE
            copy = pltpu.make_async_copy(
                g_ref.at[chunk, pl.ds(low, high - low)],
                stages[which].at[pl.ds(place, high - low)],
                in_sem.at[which, slot],
            )
            copy.start()
            mine.append((copy, place, row - low, high - low, at - offset, take))
            place += high - low
        loads.append(mine)
    stores = []
    for which, index in enumerate(indices):
        offset, number, shape = spots[index]
        for copy, place, skip, size, at, take in loads[which]:
            copy.wait()
            first = stages[which][place : place + TILE].astype(F32)
            lin[at : at + TILE - skip] = first[skip:]
            blocks, tail = divmod(size - TILE, step)

            def body(i, _, place=place, at=at, skip=skip, which=which):
                source = pl.multiple_of(place + TILE + i * step, TILE)
                lin[pl.ds(at + TILE - skip + i * step, step)] = stages[which][
                    pl.ds(source, step)
                ].astype(F32)
                return 0

            lax.fori_loop(0, blocks, body, 0)
            if tail:
                source = place + TILE + blocks * step
                target = at + TILE - skip + blocks * step
                lin[target : target + tail] = stages[which][source : source + tail].astype(F32)
        if len(shape) == 1:
            for c in range(number):
                results[which][0:1, c * LANE : (c + 1) * LANE] = lin[c : c + 1]
        else:
            high, wide = shape
            count = wide // LANE
            rows = 64

            def turn(i, _, which=which, count=count):
                top = pl.multiple_of(i * rows, rows)
                for c in range(count):
                    results[which][pl.ds(top, rows), c * LANE : (c + 1) * LANE] = lin[
                        pl.ds(top * count + c, rows, stride=count)
                    ].astype(BF)
                return 0

            lax.fori_loop(0, high // rows, turn, 0)
        copy = pltpu.make_async_copy(results[which], outs[which], out_sem.at[which])
        copy.start()
        stores.append(copy)
    for copy in stores:
        copy.wait()


def unpack_weights(gathered, plan, indices, step=128):
    spots = linear_layout()
    stage_shapes, result_shapes, most, tallest = [], [], 0, 0
    for index in indices:
        offset, number, shape = spots[index]
        found = plan.segments(offset, number)
        size = sum(-(-(r + t) // TILE) * TILE - r // TILE * TILE for _, r, _, t in found)
        stage_shapes.append(pltpu.VMEM((size, LANE), BF))
        most = max(most, len(found))
        tallest = max(tallest, number)
        result_shapes.append((shape, BF) if len(shape) == 2 else ((1, shape[0]), F32))
    anywhere = pl.BlockSpec(memory_space=pl.ANY)
    return pl.pallas_call(
        functools.partial(unpack_kernel, plan=plan, indices=indices, step=step),
        in_specs=[anywhere],
        out_specs=[anywhere] * len(indices),
        out_shape=[jax.ShapeDtypeStruct(s, t) for s, t in result_shapes],
        scratch_shapes=[
            pltpu.VMEM((tallest + 2 * TILE, LANE), F32),
            pltpu.SemaphoreType.DMA((len(indices), most)),
            pltpu.SemaphoreType.DMA((len(indices),)),
        ]
        + stage_shapes
        + [pltpu.VMEM(s, t) for s, t in result_shapes],
        compiler_params=pltpu.CompilerParams(vmem_limit_bytes=VMEM_LIMIT),
        name="unpack",
    )(gathered)


def pack_kernel(*refs, plan, indices, step):
    n = len(indices)
    spots = linear_layout()
    ins, out_ref, rest = refs[:n], refs[n], refs[n + 1 :]
    lin, stage, in_sem, out_sem = rest[:4]
    held = rest[4:]
    copies = []
    for which in range(n):
        copy = pltpu.make_async_copy(ins[which], held[which], in_sem.at[which])
        copy.start()
        copies.append(copy)
    stores = []
    begin = spots[indices[0]][0]
    total = spots[indices[-1]][0] + spots[indices[-1]][1] - begin
    pieces = plan.segments(begin, total)
    place = 0
    done = -TILE
    lin[0:TILE] = jnp.zeros((TILE, LANE), F32)
    slot = 0
    for which, index in enumerate(indices):
        offset, number, shape = spots[index]
        copies[which].wait()
        if len(shape) == 1:
            for c in range(number):
                lin[TILE + c : TILE + c + 1] = held[which][0:1, c * LANE : (c + 1) * LANE]
        else:
            high, wide = shape
            count = wide // LANE
            rows = 64

            def turn(i, _, which=which, count=count):
                top = pl.multiple_of(i * rows, rows)
                for c in range(count):
                    lin[pl.ds(TILE + top * count + c, rows, stride=count)] = held[which][
                        pl.ds(top, rows), c * LANE : (c + 1) * LANE
                    ].astype(F32)
                return 0

            lax.fori_loop(0, high // rows, turn, 0)
        low, high_row = offset - begin, offset - begin + number
        last = which == n - 1
        while slot < len(pieces):
            chunk, row, at, take = pieces[slot]
            at -= begin
            head = row - row // TILE * TILE
            start, stop = at - head, at + take
            ceil = start + -(-(stop - start) // TILE) * TILE
            first = max(start, done)
            whole = stop <= high_row
            end = ceil if whole else start + (high_row - start) // TILE * TILE
            if end > first:
                base = row - head + first - start
                blocks, tail = divmod(end - first, step)
                shift = TILE + first - low

                def body(i, _, place=place, shift=shift):
                    target = pl.multiple_of(place + i * step, TILE)
                    stage[pl.ds(target, step)] = lin[pl.ds(shift + i * step, step)].astype(BF)
                    return 0

                lax.fori_loop(0, blocks, body, 0)
                if tail:
                    source = shift + blocks * step
                    target = place + blocks * step
                    stage[target : target + tail] = lin[source : source + tail].astype(BF)
                copy = pltpu.make_async_copy(
                    stage.at[pl.ds(place, end - first)],
                    out_ref.at[chunk, pl.ds(base, end - first)],
                    out_sem.at[len(stores)],
                )
                copy.start()
                stores.append(copy)
                place += end - first
                done = end
            if not whole:
                break
            done = stop if slot + 1 == len(pieces) else min(done, stop)
            slot += 1
        if not last:
            lin[0:TILE] = lin[number : number + TILE]
    for copy in stores:
        copy.wait()


def pack_grads(grads, plan, indices, step=128):
    spots = linear_layout()
    tallest = max(spots[i][1] for i in indices)
    begin = spots[indices[0]][0]
    total = spots[indices[-1]][0] + spots[indices[-1]][1] - begin
    count = len(plan.segments(begin, total))
    anywhere = pl.BlockSpec(memory_space=pl.ANY)
    return pl.pallas_call(
        functools.partial(pack_kernel, plan=plan, indices=indices, step=step),
        in_specs=[anywhere] * len(indices),
        out_specs=anywhere,
        out_shape=jax.ShapeDtypeStruct((plan.devices, plan.chunk, LANE), BF),
        scratch_shapes=[
            pltpu.VMEM((tallest + 2 * TILE, LANE), F32),
            pltpu.VMEM((total + 2 * TILE * (count + len(indices)), LANE), BF),
            pltpu.SemaphoreType.DMA((len(indices),)),
            pltpu.SemaphoreType.DMA((count + len(indices),)),
        ]
        + [pltpu.VMEM(g.shape, g.dtype) for g in grads],
        compiler_params=pltpu.CompilerParams(vmem_limit_bytes=VMEM_LIMIT),
        name="pack",
    )(*grads)


MESH = pl.DeviceIdType.MESH
ROWS = 208


def place_of():
    dp, fs = lax.axis_index("dp"), lax.axis_index("fsdp")
    return dp, fs, dp // 2, dp % 2, fs // 2, fs % 2


def meet_all(me, devices, inner):
    barrier = pltpu.get_barrier_semaphore()

    def greet(i, _):
        other = (me + i) % devices
        pl.semaphore_signal(
            barrier, inc=1, device_id=(other // inner, other % inner), device_id_type=MESH
        )
        return 0

    lax.fori_loop(1, devices, greet, 0)
    pl.semaphore_wait(barrier, devices - 1)


def when_all(conditions):
    total = None
    for condition in conditions:
        if condition is not None:
            total = condition if total is None else total & condition
    return total


def guarded(condition, body):
    if condition is None:
        body()
    else:
        pl.when(condition)(body)


def gather_kernel(
    slot_ref, out_ref, own_sem, lend_send, lend_recv, send_sem, recv_sem, *, plan, inner
):
    dp, fs, y, x, z, c = place_of()
    me = dp * inner + fs
    lead, lent, kept = plan.lead, plan.lent, plan.kept
    levels = inner // 2
    meet_all(me, plan.devices, inner)

    def own_copy():
        start = pl.multiple_of(jnp.where(me == lead, plan.base, 0), TILE)
        return pltpu.make_async_copy(
            slot_ref.at[pl.ds(start, plan.chunk)], out_ref.at[me], own_sem
        )

    def lend(slot, target, part):
        return pltpu.make_async_remote_copy(
            src_ref=slot_ref.at[pl.ds(kept, lent)],
            dst_ref=out_ref.at[target, pl.ds(pl.multiple_of(part * lent, TILE), lent)],
            send_sem=lend_send.at[slot],
            recv_sem=lend_recv.at[part],
            device_id=(target // inner, target % inner),
            device_id_type=MESH,
        )

    lender = jnp.maximum(me - lead - 1, 0)

    @pl.when(me > lead)
    def _():
        lend(0, lender // 2, lender % 2).start()

    @pl.when(me == lead)
    def _():
        lend(0, lead - 1, 0).start()
        lend(1, lead - 1, 1).start()

    @pl.when(me >= lead)
    def _():
        own_copy().start()
        own_copy().wait()

    @pl.when(me < lead)
    def _():
        lend(0, lead - 1, 0).wait_recv()
        lend(0, lead - 1, 1).wait_recv()

    across = {
        "up": (dp, fs + 2),
        "down": (dp, fs - 2),
        "x": (dp + 1 - 2 * x, fs),
        "y": (dp + 2 - 4 * y, fs),
        "twin": (dp, fs + 1 - 2 * c),
    }
    kinds = tuple(across)
    pending = []

    def copy(kind, yy, xx, zz, part, cc=None):
        core = c if cc is None else cc
        column = yy * 2 + xx
        index = column * inner + zz * 2 + core
        rows = pl.ds(part * lent, lent)
        return pltpu.make_async_remote_copy(
            src_ref=out_ref.at[index, rows],
            dst_ref=out_ref.at[index, rows],
            send_sem=send_sem.at[kinds.index(kind), column * levels + zz, part],
            recv_sem=recv_sem.at[index, part],
            device_id=across[kind],
            device_id_type=MESH,
        )

    def send(condition, kind, yy, xx, zz, part):
        guarded(condition, lambda: copy(kind, yy, xx, zz, part).start())
        pending.append((condition, kind, yy, xx, zz, part))

    def arrive(condition, yy, xx, zz, part):
        guarded(condition, lambda: copy("x", yy, xx, zz, part).wait_recv())

    def spread(distance):
        for sign in (1, -1) if distance else (0,):
            zz = z + sign * distance
            inside = when_all(
                [zz < levels if sign > 0 else None, zz >= 0 if sign < 0 else None]
            )
            yield zz, sign, inside

    for turn in range(levels + 2):
        if turn < levels:
            for zz, sign, inside in spread(turn):
                for part in range(2):
                    if turn:
                        arrive(inside, y, x, zz, part)
                    if sign <= 0:
                        send(when_all([inside, z < levels - 1]), "up", y, x, zz, part)
                    if sign >= 0:
                        send(when_all([inside, z > 0]), "down", y, x, zz, part)
                    for kind in ("x", "y") if part else ("y", "x"):
                        send(inside, kind, y, x, zz, part)
                    send(inside, "twin", y, x, zz, part)
        if 1 <= turn <= levels:
            for zz, sign, inside in spread(turn - 1):
                arrive(inside, y, 1 - x, zz, 0)
                send(inside, "y", y, 1 - x, zz, 0)
                send(inside, "twin", y, 1 - x, zz, 0)
                arrive(inside, 1 - y, x, zz, 1)
                send(inside, "x", 1 - y, x, zz, 1)
                send(inside, "twin", 1 - y, x, zz, 1)
                arrive(inside, 1 - y, x, zz, 0)
                send(inside, "twin", 1 - y, x, zz, 0)
                arrive(inside, y, 1 - x, zz, 1)
                send(inside, "twin", y, 1 - x, zz, 1)
        if turn >= 2:
            for zz, sign, inside in spread(turn - 2):
                for part in range(2):
                    arrive(inside, 1 - y, 1 - x, zz, part)
                    send(inside, "twin", 1 - y, 1 - x, zz, part)

    def twin_arrivals(i, _):
        column, zz = i // levels, i % levels
        for part in range(2):
            copy("twin", column // 2, column % 2, zz, part, 1 - c).wait_recv()
        return 0

    lax.fori_loop(0, 4 * levels, twin_arrivals, 0)
    for condition, kind, yy, xx, zz, part in pending:
        guarded(condition, lambda: copy(kind, yy, xx, zz, part).wait_send())

    @pl.when(me >= lead)
    def _():
        lend(0, lead - 1, 0).wait_send()

    @pl.when(me == lead)
    def _():
        lend(1, lead - 1, 1).wait_send()


def gather_chunks(slot, plan, inner, collective):
    anywhere = pl.BlockSpec(memory_space=pl.ANY)
    dma = pltpu.SemaphoreType.DMA
    return pl.pallas_call(
        functools.partial(gather_kernel, plan=plan, inner=inner),
        in_specs=[anywhere],
        out_specs=anywhere,
        out_shape=jax.ShapeDtypeStruct((plan.devices, plan.chunk, LANE), BF),
        scratch_shapes=[
            dma,
            dma((2,)),
            dma((2,)),
            dma((5, plan.devices // 2, 2)),
            dma((plan.devices, 2)),
        ],
        compiler_params=pltpu.CompilerParams(collective_id=collective, has_side_effects=True),
        name="gather_chunks",
    )(slot)


def scatter_kernel(
    g_ref,
    out_ref,
    acc,
    twin,
    wide_y,
    wide_x,
    slim_x,
    slim_y,
    line,
    load_sem,
    twin_send,
    twin_recv,
    wide_send,
    wide_recv,
    slim_send,
    slim_recv,
    line_send,
    line_recv,
    own_sem,
    back_send,
    back_recv,
    *,
    plan,
    inner,
):
    dp, fs, y, x, z, c = place_of()
    me = dp * inner + fs
    lead, lent, kept = plan.lead, plan.lent, plan.kept
    levels = inner // 2
    x_mate = (dp + 1 - 2 * x, fs)
    y_mate = (dp + 2 - 4 * y, fs)
    meet_all(me, plan.devices, inner)

    def remote(source, target, send, receive, device):
        return pltpu.make_async_remote_copy(
            src_ref=source,
            dst_ref=target,
            send_sem=send,
            recv_sem=receive,
            device_id=device,
            device_id_type=MESH,
        )

    def slot_of(yy, xx, zz):
        return (yy * 2 + xx) * levels + zz

    def load(yy, xx, zz):
        slot = slot_of(yy, xx, zz)
        return pltpu.make_async_copy(
            g_ref.at[(yy * 2 + xx) * inner + zz * 2 + c], acc.at[slot], load_sem.at[slot]
        )

    def to_twin(yy, xx, zz):
        slot = slot_of(yy, xx, zz)
        return remote(
            g_ref.at[(yy * 2 + xx) * inner + zz * 2 + 1 - c],
            twin.at[slot],
            twin_send.at[slot],
            twin_recv.at[slot],
            (dp, fs + 1 - 2 * c),
        )

    def piece(slot, part):
        return acc.at[slot, pl.ds(part * lent, lent)]

    def wide(part, other, zz, yy=0, xx=0):
        buffer, device = (wide_x, x_mate) if part else (wide_y, y_mate)
        index = other * levels + zz
        return remote(
            piece(slot_of(yy, xx, zz), part),
            buffer.at[index],
            wide_send.at[part, index],
            wide_recv.at[part, index],
            device,
        )

    def slim(part, zz, yy=0, xx=0):
        buffer, device = (slim_y, y_mate) if part else (slim_x, x_mate)
        return remote(
            piece(slot_of(yy, xx, zz), part),
            buffer.at[zz],
            slim_send.at[part, zz],
            slim_recv.at[part, zz],
            device,
        )

    def along(upward, zz, part):
        way = 0 if upward else 1
        return remote(
            piece(slot_of(y, x, zz), part),
            line.at[way, zz, part],
            line_send.at[way, zz, part],
            line_recv.at[way, zz, part],
            (dp, fs + 2 if upward else fs - 2),
        )

    def add(slot, first, count, source):
        def body(i, _):
            at = pl.multiple_of(i * ROWS, TILE)
            to = pl.ds(pl.multiple_of(first + i * ROWS, TILE), ROWS)
            acc[slot, to] = (
                acc[slot, to].astype(F32) + source[pl.ds(at, ROWS)].astype(F32)
            ).astype(BF)
            return 0

        lax.fori_loop(0, count // ROWS, body, 0)

    def add_part(slot, part, source):
        add(slot, part * lent, lent, source)

    def level(k):
        return jnp.where(z < levels // 2, z + levels - 1 - k, z + 1 + k) % levels

    columns = ((1 - y, 1 - x), (1 - y, x), (y, 1 - x), (y, x))

    for yy, xx in columns:

        def begin(k, _, yy=yy, xx=xx):
            to_twin(yy, xx, level(k)).start()
            load(yy, xx, level(k)).start()
            return 0

        lax.fori_loop(0, levels, begin, 0)

    def settle(yy, xx, zz):
        slot = slot_of(yy, xx, zz)
        load(yy, xx, zz).wait()
        to_twin(yy, xx, zz).wait_recv()
        add(slot, 0, plan.chunk, twin.at[slot])

    def diagonal(k, _):
        zz = level(k)
        settle(1 - y, 1 - x, zz)
        wide(0, 1 - x, zz, 1 - y, 1 - x).start()
        wide(1, 1 - y, zz, 1 - y, 1 - x).start()
        return 0

    def sides(k, _):
        zz = level(k)
        settle(1 - y, x, zz)
        wide(0, x, zz, 1 - y, x).start()
        settle(y, 1 - x, zz)
        wide(1, y, zz, y, 1 - x).start()
        return 0

    def middle(k, _):
        zz = level(k)
        wide(0, 1 - x, zz).wait_recv()
        add_part(slot_of(y, 1 - x, zz), 0, wide_y.at[(1 - x) * levels + zz])
        slim(0, zz, y, 1 - x).start()
        wide(1, 1 - y, zz).wait_recv()
        add_part(slot_of(1 - y, x, zz), 1, wide_x.at[(1 - y) * levels + zz])
        slim(1, zz, 1 - y, x).start()
        return 0

    def home(k, _):
        zz = level(k)
        slot = slot_of(y, x, zz)
        settle(y, x, zz)
        wide(0, x, zz).wait_recv()
        add_part(slot, 0, wide_y.at[x * levels + zz])
        wide(1, y, zz).wait_recv()
        add_part(slot, 1, wide_x.at[y * levels + zz])
        return 0

    lax.fori_loop(0, levels, diagonal, 0)
    lax.fori_loop(0, levels, sides, 0)
    lax.fori_loop(0, levels, middle, 0)
    lax.fori_loop(0, levels, home, 0)

    def column_sum_of(zz):
        slot = slot_of(y, x, zz)
        slim(0, zz).wait_recv()
        add_part(slot, 0, slim_x.at[zz])
        slim(1, zz).wait_recv()
        add_part(slot, 1, slim_y.at[zz])

    def take(upward, zz, part):
        along(upward, zz, part).wait_recv()
        add_part(slot_of(y, x, zz), part, line.at[0 if upward else 1, zz, part])

    sent = []
    for distance in range(levels - 1, 0, -1):
        for upward in (True, False):
            zz = z + distance if upward else z - distance
            inside = zz < levels if upward else zz >= 0
            more = z > 0 if upward else z < levels - 1

            @pl.when(inside)
            def _(upward=upward, zz=zz, more=more):
                column_sum_of(zz)
                for part in range(2):

                    @pl.when(more)
                    def _(part=part):
                        take(upward, zz, part)

                    along(upward, zz, part).start()

            sent.append((inside, upward, zz))
    column_sum_of(z)
    for part in range(2):

        @pl.when(z > 0)
        def _(part=part):
            take(True, z, part)

        @pl.when(z < levels - 1)
        def _(part=part):
            take(False, z, part)

    mine = slot_of(y, x, z)

    def back(slot, part, owner):
        return remote(
            piece(mine, part),
            out_ref.at[pl.ds(kept, lent)],
            back_send.at[slot],
            back_recv,
            (owner // inner, owner % inner),
        )

    @pl.when(me < lead - 1)
    def _():
        back(0, 0, lead + 1 + 2 * me).start()
        back(1, 1, lead + 2 + 2 * me).start()

    @pl.when(me == lead - 1)
    def _():
        back(0, 0, me + 1).start()

    @pl.when(me == lead)
    def _():
        count = kept - plan.base
        copy = pltpu.make_async_copy(
            acc.at[mine, pl.ds(0, count)], out_ref.at[pl.ds(plan.base, count)], own_sem
        )
        copy.start()
        copy.wait()

    @pl.when(me > lead)
    def _():
        copy = pltpu.make_async_copy(
            acc.at[mine, pl.ds(0, kept)], out_ref.at[pl.ds(0, kept)], own_sem
        )
        copy.start()
        copy.wait()

    @pl.when(me >= lead)
    def _():
        back(0, 0, 0).wait_recv()

    for inside, upward, zz in sent:

        @pl.when(inside)
        def _(upward=upward, zz=zz):
            for part in range(2):
                along(upward, zz, part).wait_send()

    def finish(k, _):
        zz = level(k)
        for yy, xx in columns:
            to_twin(yy, xx, zz).wait_send()
        wide(0, 1 - x, zz).wait_send()
        wide(0, x, zz).wait_send()
        wide(1, 1 - y, zz).wait_send()
        wide(1, y, zz).wait_send()
        slim(0, zz).wait_send()
        slim(1, zz).wait_send()
        return 0

    lax.fori_loop(0, levels, finish, 0)

    @pl.when(me < lead)
    def _():
        back(0, 0, 0).wait_send()

    @pl.when(me < lead - 1)
    def _():
        back(1, 1, 0).wait_send()


def scatter_chunks(grads, plan, inner, collective):
    anywhere = pl.BlockSpec(memory_space=pl.ANY)
    dma = pltpu.SemaphoreType.DMA
    half, levels = plan.devices // 2, inner // 2
    part = (plan.lent, LANE)
    return pl.pallas_call(
        functools.partial(scatter_kernel, plan=plan, inner=inner),
        in_specs=[anywhere],
        out_specs=anywhere,
        out_shape=jax.ShapeDtypeStruct((plan.padded, LANE), BF),
        scratch_shapes=[
            pltpu.VMEM((half, plan.chunk, LANE), BF),
            pltpu.VMEM((half, plan.chunk, LANE), BF),
            pltpu.VMEM((2 * levels, *part), BF),
            pltpu.VMEM((2 * levels, *part), BF),
            pltpu.VMEM((levels, *part), BF),
            pltpu.VMEM((levels, *part), BF),
            pltpu.VMEM((2, levels, 2, *part), BF),
            dma((half,)),
            dma((half,)),
            dma((half,)),
            dma((2, 2 * levels)),
            dma((2, 2 * levels)),
            dma((2, levels)),
            dma((2, levels)),
            dma((2, levels, 2)),
            dma((2, levels, 2)),
            dma,
            dma((2,)),
            dma,
        ],
        compiler_params=pltpu.CompilerParams(
            collective_id=collective, has_side_effects=True, vmem_limit_bytes=VMEM_LIMIT
        ),
        name="scatter_chunks",
    )(grads)


def exchange_kernel(in_ref, out_ref, own_sem, send_sem, recv_sem, *, devices, inner, senders, receivers):
    me = lax.axis_index("dp") * inner + lax.axis_index("fsdp")
    meet_all(me, devices, inner)
    many = len(in_ref.shape) == 3

    def copy(source, target):
        return pltpu.make_async_remote_copy(
            src_ref=in_ref.at[target] if many else in_ref,
            dst_ref=out_ref.at[source],
            send_sem=send_sem.at[target],
            recv_sem=recv_sem.at[source],
            device_id=(target // inner, target % inner),
            device_id_type=MESH,
        )

    def each(i, _, act):
        other = (me + i) % devices
        act(other)
        return 0

    def start(other):
        pl.when((me < senders) & (other < receivers))(lambda: copy(me, other).start())

    def landed(other):
        pl.when((other < senders) & (me < receivers))(lambda: copy(other, other).wait_recv())

    def gone(other):
        pl.when((me < senders) & (other < receivers))(lambda: copy(me, other).wait_send())

    lax.fori_loop(1, devices, functools.partial(each, act=start), 0)

    @pl.when((me < senders) & (me < receivers))
    def _():
        own = pltpu.make_async_copy(in_ref.at[me] if many else in_ref, out_ref.at[me], own_sem)
        own.start()
        own.wait()

    lax.fori_loop(1, devices, functools.partial(each, act=landed), 0)
    lax.fori_loop(1, devices, functools.partial(each, act=gone), 0)


def exchange(value, devices, inner, senders, receivers, collective, name):
    anywhere = pl.BlockSpec(memory_space=pl.ANY)
    dma = pltpu.SemaphoreType.DMA
    return pl.pallas_call(
        functools.partial(
            exchange_kernel, devices=devices, inner=inner, senders=senders, receivers=receivers
        ),
        in_specs=[anywhere],
        out_specs=anywhere,
        out_shape=jax.ShapeDtypeStruct((senders, *value.shape[-2:]), value.dtype),
        scratch_shapes=[dma, dma((devices,)), dma((devices,))],
        compiler_params=pltpu.CompilerParams(collective_id=collective, has_side_effects=True),
        name=name,
    )(value)


HALF = 27
TALL = 72
SLAB = 112
CONDITION_ROWS = 832


def ada_spots(me, plan):
    lines = plan.share // HALF
    odd = me % 2
    limit = CONDITION_ROWS - TALL
    return [
        (odd, jnp.minimum((lines * me + odd) // 2, limit)),
        (1 - odd, jnp.minimum((lines * me - odd) // 2, limit)),
    ]


def ada_kernel(lin_ref, cond_ref, out_ref, *, plan, inner):
    me = lax.axis_index("dp") * inner + lax.axis_index("fsdp")
    for half, (shift, top) in enumerate(ada_spots(me, plan)):
        condition = cond_ref[pl.ds(top, TALL)].astype(BF)

        def body(c, _, half=half, shift=shift, condition=condition):
            rows = lin_ref[pl.ds(HALF * shift + c, TALL, stride=2 * HALF)].astype(BF)
            part = tn(condition, rows)
            count = plan.devices
            for clip in range(2):
                out_ref[pl.ds((2 * clip + half) * HALF + c, count, stride=SLAB)] = part[
                    clip * count : (clip + 1) * count
                ]
            return 0

        lax.fori_loop(0, HALF, body, 0)


def ada_partial(lin, cond, plan, inner):
    return pl.pallas_call(
        functools.partial(ada_kernel, plan=plan, inner=inner),
        out_shape=jax.ShapeDtypeStruct((plan.devices * SLAB, LANE), F32),
        compiler_params=pltpu.CompilerParams(vmem_limit_bytes=VMEM_LIMIT),
        name="ada_partial",
    )(lin, cond)


def own_grad_kernel(cond_ref, dmod_ref, rest_ref, g_ref, sums_ref, lin, *, plan, inner):
    me = lax.axis_index("dp") * inner + lax.axis_index("fsdp")
    count = plan.devices
    border = jnp.clip(plan.first_row - plan.share * me, 0, plan.share)
    for half, (shift, top) in enumerate(ada_spots(me, plan)):
        condition = cond_ref[pl.ds(top, TALL)].astype(BF)

        def body(c, _, half=half, shift=shift, condition=condition):
            grads = jnp.concatenate(
                [
                    dmod_ref[pl.ds((2 * clip + half) * HALF + c, count, stride=SLAB)]
                    for clip in range(2)
                ],
                axis=0,
            ).astype(BF)
            lin[pl.ds(HALF * shift + c, TALL, stride=2 * HALF)] = nn(condition, grads)
            return 0

        @pl.when(border > 0)
        def _(body=body):
            lax.fori_loop(0, HALF, body, 0)

    rows = 64

    def merge(i, total):
        at = pl.multiple_of(i * rows, rows)
        row = lax.broadcasted_iota(jnp.int32, (rows, LANE), 0) + at
        rest = jnp.where(row < plan.share, rest_ref[pl.ds(at, rows)].astype(F32), 0.0)
        value = jnp.where(row < border, lin[pl.ds(at, rows)], rest)
        g_ref[pl.ds(at, rows)] = value
        square = value * value
        return total + sum(square[k : k + 8] for k in range(0, rows, 8))

    sums_ref[...] = lax.fori_loop(0, plan.padded // rows, merge, jnp.zeros((8, LANE), F32))


def own_grad(cond, dmod, rest, plan, inner):
    return pl.pallas_call(
        functools.partial(own_grad_kernel, plan=plan, inner=inner),
        out_shape=[
            jax.ShapeDtypeStruct((plan.padded, LANE), F32),
            jax.ShapeDtypeStruct((8, LANE), F32),
        ],
        scratch_shapes=[pltpu.VMEM((2 * HALF * TALL, LANE), F32)],
        compiler_params=pltpu.CompilerParams(vmem_limit_bytes=VMEM_LIMIT),
        name="own_grad",
    )(cond, dmod, rest)


def fits(devices, inner, share):
    return inner == 8 and devices == 32 and share % (LANE * HALF) == 0


def local_fast(
    latents, captions, lengths, timesteps, cotangent, master, first_moment, second_moment
):
    clips, frames, width = latents.shape
    share = master.shape[0]
    inner = lax.axis_size("fsdp")
    devices = inner * lax.axis_size("dp")
    plan = Plan(devices, share // LANE)
    lead = plan.lead
    indices = tuple(range(2, 13))

    condition = jax.nn.silu(embed(timesteps)).astype(BF).astype(F32)
    conditions = exchange(
        jnp.pad(condition, ((0, 8 - clips), (0, 0))),
        devices,
        inner,
        devices,
        devices,
        1,
        "conditions",
    )
    columns = conditions[:, :clips].transpose(2, 1, 0).reshape(width, clips * devices)
    columns = jnp.concatenate(
        [
            columns,
            jnp.ones((1, clips * devices), F32),
            jnp.zeros((CONDITION_ROWS - width - 1, clips * devices), F32),
        ],
        axis=0,
    )
    rows = master.reshape(plan.share, LANE)
    lin = jnp.pad(rows, ((0, 2 * HALF * TALL - plan.share), (0, 0)))
    slabs = ada_partial(lin, columns, plan, inner).reshape(devices, SLAB, LANE)
    parts = exchange(slabs, devices, inner, lead + 1, devices, 2, "modulation")
    mod = jnp.sum(parts, axis=0)[: 54 * clips].reshape(clips, 9, width)

    slot = lin[: plan.padded].astype(BF)
    gathered = gather_chunks(slot, plan, inner, 3)
    weights = unpack_weights(gathered, plan, indices)
    output, input_grad, grad_mod, gradients = block_pass(
        latents, captions, lengths, cotangent, mod, weights
    )
    grad_rows = jnp.pad(
        grad_mod.astype(F32).reshape(54 * clips, LANE), ((0, SLAB - 54 * clips), (0, 0))
    )
    dmod = exchange(grad_rows, devices, inner, devices, lead + 1, 4, "modulation_grads")
    chunks = pack_grads(gradients, plan, indices)
    rest = scatter_chunks(chunks, plan, inner, 5)
    grads, squares = own_grad(
        columns, dmod.reshape(devices * SLAB, LANE), rest, plan, inner
    )
    squares = exchange(squares, devices, inner, devices, devices, 6, "squares")
    return (
        output,
        input_grad,
        grads[: plan.share].reshape(share),
        jnp.sum(squares),
    )


def local_any(
    latents, captions, lengths, timesteps, cotangent, master, first_moment, second_moment
):
    clips, frames, width = latents.shape
    share = master.shape[0]
    devices = lax.axis_size("dp") * lax.axis_size("fsdp")
    gathered = lax.all_gather(
        master.astype(BF).reshape(1, share), ("dp", "fsdp"), axis=0, tiled=True
    ).reshape(-1)
    weights = unpack(gathered)
    condition = jax.nn.silu(embed(timesteps)).astype(BF)
    mod = jnp.dot(condition, weights[0], preferred_element_type=F32) + weights[1].astype(F32)
    block_weights = [w.astype(F32).reshape(1, -1) if w.ndim == 1 else w for w in weights[2:]]
    output, input_grad, grad_mod, gradients = block_pass(
        latents, captions, lengths, cotangent, mod.reshape(clips, 9, width), block_weights
    )
    grad_mod = grad_mod.reshape(clips, 9 * width)
    grad_ada = jnp.dot(condition.T, grad_mod, preferred_element_type=F32)
    grad_list = [grad_ada, jnp.sum(grad_mod.astype(F32), axis=0)] + gradients
    flat = jnp.concatenate([piece.astype(F32).reshape(-1) for piece in grad_list])
    grad = lax.psum_scatter(
        flat.reshape(devices, share), ("dp", "fsdp"), scatter_dimension=0, tiled=True
    ).reshape(share)
    return output, input_grad, grad, lax.psum(jnp.sum(grad * grad), ("dp", "fsdp"))


def local(
    latents,
    captions,
    caption_lengths,
    timesteps,
    cotangent,
    master_weights,
    first_moment,
    second_moment,
):
    inner = lax.axis_size("fsdp")
    devices = inner * lax.axis_size("dp")
    run = local_fast if fits(devices, inner, master_weights.shape[0]) else local_any
    output, input_grad, grad_shard, squares = run(
        latents,
        captions,
        caption_lengths,
        timesteps,
        cotangent,
        master_weights,
        first_moment,
        second_moment,
    )
    grad_norm = jnp.sqrt(squares)
    clipped = grad_shard * (CLIP / jnp.maximum(grad_norm, CLIP))
    new_first = BETA_ONE * first_moment + (1.0 - BETA_ONE) * clipped
    new_second = BETA_TWO * second_moment + (1.0 - BETA_TWO) * clipped * clipped
    step_first = new_first / (1.0 - BETA_ONE**STEP)
    step_second = new_second / (1.0 - BETA_TWO**STEP)
    new_master = master_weights - RATE * (
        step_first / (jnp.sqrt(step_second) + ADAM_EPS) + DECAY * master_weights
    )
    return (output, input_grad, grad_norm, new_master, new_first, new_second)


def solution(mesh):
    placed = (
        P(("dp", "fsdp"), None, None),
        P(("dp", "fsdp"), None, None),
        P(("dp", "fsdp")),
        P(("dp", "fsdp")),
        P(("dp", "fsdp"), None, None),
        P(("dp", "fsdp")),
        P(("dp", "fsdp")),
        P(("dp", "fsdp")),
    )
    return jax.shard_map(
        local,
        mesh=mesh,
        in_specs=placed,
        out_specs=(
            P(("dp", "fsdp"), None, None),
            P(("dp", "fsdp"), None, None),
            P(),
            P(("dp", "fsdp")),
            P(("dp", "fsdp")),
            P(("dp", "fsdp")),
        ),
        check_vma=False,
    )
```

```python
import functools
import math

import jax
import jax.numpy as jnp
from jax import lax
from jax.experimental import pallas as pl
from jax.experimental.pallas import tpu as pltpu
from jax.sharding import PartitionSpec as P

D = 768
HEADS = 12
HD = 64
FF = 3072
CTX = 1024
STEP = 5


NORM_EPS = 1e-06
BETA_ONE = 0.9
BETA_TWO = 0.999
ADAM_EPS = 1e-08
RATE = 0.03
DECAY = 0.01
CLIP = 500.0


def layout_sizes():
    return [
        (D, 9 * D),
        (9 * D,),
        (D, 3 * D),
        (D, D),
        (D,),
        (D, D),
        (CTX, 2 * D),
        (D, D),
        (D,),
        (D, FF),
        (FF,),
        (FF, D),
        (D,),
    ]


def unpack(flat_vector):
    pieces = []
    offset = 0
    for layout_shape in layout_sizes():
        number = math.prod(layout_shape)
        pieces.append(flat_vector[offset : offset + number].reshape(layout_shape))
        offset += number
    return pieces


def embed(steps_in):
    half_width = D // 2
    frequency = jnp.exp(-math.log(10000.0) * jnp.arange(half_width, dtype=jnp.float32) / half_width)
    angles = steps_in.astype(jnp.float32)[:, None] * frequency[None, :]
    return jnp.concatenate([jnp.cos(angles), jnp.sin(angles)], axis=1)


def normalize(hidden):
    centred = hidden - jnp.mean(hidden, axis=-1, keepdims=True)
    inverse = lax.rsqrt(jnp.mean(centred * centred, axis=-1, keepdims=True) + NORM_EPS)
    return (centred * inverse, inverse)


def norm_back(normed, inverse, grad_normed):
    return inverse * (
        grad_normed
        - jnp.mean(grad_normed, axis=-1, keepdims=True)
        - normed * jnp.mean(grad_normed * normed, axis=-1, keepdims=True)
    )


F32 = jnp.float32
BF = jnp.bfloat16
VMEM_LIMIT = 60 << 20


def nn(left_side, right_side):
    return lax.dot_general(
        left_side, right_side, (((1,), (0,)), ((), ())), preferred_element_type=F32
    )


def nt(left_side, right_side):
    return lax.dot_general(
        left_side, right_side, (((1,), (1,)), ((), ())), preferred_element_type=F32
    )


def tn(left_side, right_side):
    return lax.dot_general(
        left_side, right_side, (((0,), (0,)), ((), ())), preferred_element_type=F32
    )


def call(body, grid, in_specs, out_specs, out_shape, name, scratch=()):
    return pl.pallas_call(
        body,
        grid=grid,
        in_specs=in_specs,
        out_specs=out_specs,
        out_shape=out_shape,
        scratch_shapes=list(scratch),
        compiler_params=pltpu.CompilerParams(vmem_limit_bytes=VMEM_LIMIT),
        name=name,
    )


def struct(shape, dtype):
    return jax.ShapeDtypeStruct(shape, dtype)


def rows_spec(rows, width):
    return pl.BlockSpec((1, rows, width), lambda i, j: (i, j, 0))


def clip_spec(count, width):
    return pl.BlockSpec((1, count, width), lambda i, j: (i, 0, 0))


def whole_spec(shape):
    return pl.BlockSpec(shape, lambda *_: (0,) * len(shape))


def row_block(frames):
    for parts in (2, 3, 4, 6):
        if frames % (16 * parts) == 0:
            return frames // parts
    return frames


def add_to(ref, first, value):
    @pl.when(first)
    def _():
        ref[...] = value

    @pl.when(jnp.logical_not(first))
    def _():
        ref[...] += value


def column_sum(value):
    return jnp.sum(value, axis=0, keepdims=True)


def qkv_kernel(x_ref, mod_ref, w_ref, out_ref):
    normed, _ = normalize(x_ref[0].astype(F32))
    first_in = (normed * (1.0 + mod_ref[0, 1:2]) + mod_ref[0, 0:1]).astype(BF)
    out_ref[0] = nn(first_in, w_ref[...]).astype(BF)


def qkv_forward(latents, mod, weight):
    clips, frames, width = latents.shape
    rows = row_block(frames)
    wide = weight.shape[1]
    return call(
        qkv_kernel,
        (clips, frames // rows),
        [rows_spec(rows, width), clip_spec(9, width), whole_spec(weight.shape)],
        rows_spec(rows, wide),
        struct((clips, frames, wide), BF),
        "qkv_forward",
    )(latents, mod, weight)


def head_lanes():
    lane = lax.broadcasted_iota(jnp.int32, (1, 2 * HD), 1)
    return lane, lane < HD


def usable_bias(length, count):
    row = lax.broadcasted_iota(jnp.int32, (count, 2 * HD), 0)
    return jnp.where(row < length, 0.0, -1e30).astype(BF)


def attend_kernel(*refs, masked):
    if masked:
        len_ref, q_ref, k_ref, v_ref, o_ref, l_ref = refs
    else:
        q_ref, k_ref, v_ref, o_ref, l_ref = refs
    k, v = k_ref[0], v_ref[0]
    scaled = q_ref[0] * jnp.asarray(HD**-0.5, BF)
    lane, low = head_lanes()
    one = jnp.ones((), BF)
    zero = jnp.zeros((), BF)
    values = [jnp.where(low, v, one), jnp.where(low, one, v)]
    if masked:
        bias = usable_bias(len_ref[pl.program_id(0)], k.shape[0])
        tag = jnp.where(lane % HD == 0, one, zero)
        queries = [jnp.where(low, scaled, tag), jnp.where(low, tag, scaled)]
        keys = [jnp.where(low, k, bias), jnp.where(low, bias, k)]
    else:
        queries = [jnp.where(low, scaled, zero), jnp.where(low, zero, scaled)]
        keys = [k, k]
    tops, mixes = [], []
    for head in range(2):
        scores = nt(queries[head], keys[head])
        top = jnp.max(scores, axis=1, keepdims=True)
        mixes.append(nn(jnp.exp(scores - top).astype(BF), values[head]))
        tops.append(top)
    total = jnp.where(low, mixes[1], mixes[0])
    l_ref[0, 0] = jnp.where(low, tops[1], tops[0]) + jnp.log(total)
    o_ref[0] = (jnp.where(low, mixes[0], mixes[1]) / pltpu.roll(total, HD, 1)).astype(BF)


def pair_spec(rows, offset):
    return pl.BlockSpec((1, rows, 2 * HD), lambda i, j: (i, 0, j + offset))


def lse_spec(rows):
    return pl.BlockSpec((1, 1, rows, 2 * HD), lambda i, j: (i, j, 0, 0))


def attend_forward(queries, key_offset, pairs, value_offset, lengths, name):
    clips, frames = queries.shape[:2]
    slots = pairs.shape[1]
    groups = HEADS // 2
    masked = lengths is not None
    specs = [
        pair_spec(frames, 0),
        pair_spec(slots, key_offset),
        pair_spec(slots, value_offset),
    ]
    args = [queries, pairs, pairs]
    if masked:
        specs.insert(0, pl.BlockSpec(memory_space=pltpu.SMEM))
        args.insert(0, lengths)
    return call(
        functools.partial(attend_kernel, masked=masked),
        (clips, groups),
        specs,
        [pair_spec(frames, 0), lse_spec(frames)],
        [struct((clips, frames, D), BF), struct((clips, groups, frames, 2 * HD), F32)],
        name,
    )(*args)


def three_parts(value):
    high = value.astype(BF)
    rest = value - high.astype(F32)
    middle = rest.astype(BF)
    return high, middle, (rest - middle.astype(F32)).astype(BF)


def attend_back_kernel(*refs, masked):
    if masked:
        len_ref, q_ref, k_ref, v_ref, do_ref, o_ref, l_ref, dq_ref, dk_ref, dv_ref = refs
    else:
        q_ref, k_ref, v_ref, do_ref, o_ref, l_ref, dq_ref, dk_ref, dv_ref = refs
    k, v, grad = k_ref[0], v_ref[0], do_ref[0]
    scaled = q_ref[0] * jnp.asarray(HD**-0.5, BF)
    lane, low = head_lanes()
    spot = lane % HD
    one = jnp.ones((), BF)
    zero = jnp.zeros((), BF)
    product = grad.astype(F32) * o_ref[0].astype(F32)
    delta_low = jnp.sum(jnp.where(low, product, 0.0), axis=1, keepdims=True)
    delta_high = jnp.sum(jnp.where(low, 0.0, product), axis=1, keepdims=True)

    def negated(value, last):
        high, middle, rest = three_parts(-value)
        return jnp.where(
            spot == 0,
            high,
            jnp.where(spot == 1, middle, jnp.where(spot == 2, rest, last)),
        )

    tag = jnp.where(spot == 3, one, zero) if masked else zero
    lse_lanes = negated(l_ref[0, 0], tag)
    delta_lanes = negated(jnp.where(low, delta_high, delta_low), zero)
    ones = jnp.broadcast_to(jnp.where(spot < 3, one, zero), k.shape)
    key_lanes = ones
    if masked:
        bias = usable_bias(len_ref[pl.program_id(0)], k.shape[0])
        key_lanes = jnp.where(spot == 3, bias, ones)
    transposed = k.astype(F32).T.astype(BF)
    grad_queries, grad_keys, grad_values = [], [], []
    for head in range(2):

        def merge(own, other):
            return jnp.where(low, own, other) if head == 0 else jnp.where(low, other, own)

        probability = jnp.exp(nt(merge(k, key_lanes), merge(scaled, lse_lanes)))
        centred = nt(merge(v, ones), merge(grad, delta_lanes))
        grad_scores = (probability * centred).astype(BF)
        grad_values.append(nn(probability.astype(BF), grad))
        grad_keys.append(nn(grad_scores, scaled))
        grad_queries.append(nn(transposed[HD * head : HD * (head + 1)], grad_scores))
    dv_ref[0] = jnp.where(low, grad_values[0], grad_values[1]).astype(BF)
    dk_ref[0] = jnp.where(low, grad_keys[0], grad_keys[1]).astype(BF)
    dq_ref[0] = (jnp.concatenate(grad_queries, axis=0).T * HD**-0.5).astype(BF)


def attend_backward(queries, key_offset, pairs, value_offset, lengths, grad, mixed, lse, name):
    clips, frames = queries.shape[:2]
    slots = pairs.shape[1]
    groups = HEADS // 2
    masked = lengths is not None
    specs = [
        pair_spec(frames, 0),
        pair_spec(slots, key_offset),
        pair_spec(slots, value_offset),
        pair_spec(frames, 0),
        pair_spec(frames, 0),
        lse_spec(frames),
    ]
    args = [queries, pairs, pairs, grad, mixed, lse]
    if masked:
        specs.insert(0, pl.BlockSpec(memory_space=pltpu.SMEM))
        args.insert(0, lengths)
    return call(
        functools.partial(attend_back_kernel, masked=masked),
        (clips, groups),
        specs,
        [pair_spec(frames, 0), pair_spec(slots, 0), pair_spec(slots, 0)],
        [
            struct((clips, frames, D), BF),
            struct((clips, slots, D), BF),
            struct((clips, slots, D), BF),
        ],
        name,
    )(*args)


def after_self_kernel(o_ref, x_ref, mod_ref, wo_ref, bo_ref, wq_ref, z_ref, h_ref, q_ref):
    branch = nn(o_ref[0], wo_ref[...]) + bo_ref[...]
    hidden = x_ref[0].astype(F32) + mod_ref[0, 2:3] * branch
    normed, _ = normalize(hidden)
    second_in = (normed * (1.0 + mod_ref[0, 4:5]) + mod_ref[0, 3:4]).astype(BF)
    z_ref[0] = branch.astype(BF)
    h_ref[0] = hidden
    q_ref[0] = nn(second_in, wq_ref[...]).astype(BF)


def after_self(mixed, latents, mod, weight, bias, query_weight):
    clips, frames, width = latents.shape
    rows = row_block(frames)
    spec = rows_spec(rows, width)
    square = whole_spec((width, width))
    return call(
        after_self_kernel,
        (clips, frames // rows),
        [spec, spec, clip_spec(9, width), square, whole_spec((1, width)), square],
        [spec, spec, spec],
        [
            struct(latents.shape, BF),
            struct(latents.shape, F32),
            struct(latents.shape, BF),
        ],
        "after_self",
    )(mixed, latents, mod, weight, bias, query_weight)


def after_cross_kernel(o_ref, h_ref, mod_ref, wo_ref, bo_ref, z_ref, out_ref):
    branch = nn(o_ref[0], wo_ref[...]) + bo_ref[...]
    z_ref[0] = branch.astype(BF)
    out_ref[0] = h_ref[0] + mod_ref[0, 5:6] * branch


def after_cross(mixed, hidden, mod, weight, bias):
    clips, frames, width = hidden.shape
    rows = row_block(frames)
    spec = rows_spec(rows, width)
    return call(
        after_cross_kernel,
        (clips, frames // rows),
        [
            spec,
            spec,
            clip_spec(9, width),
            whole_spec((width, width)),
            whole_spec((1, width)),
        ],
        [spec, spec],
        [struct(hidden.shape, BF), struct(hidden.shape, F32)],
        "after_cross",
    )(mixed, hidden, mod, weight, bias)


GELU_ROOT = math.sqrt(2.0 / math.pi)


def feed_kernel(
    h_ref,
    dy_ref,
    mod_ref,
    up_ref,
    upb_ref,
    down_ref,
    downb_ref,
    out_ref,
    dh_ref,
    dup_ref,
    ddown_ref,
    dupb_ref,
    ddownb_ref,
    sums_ref,
    in_s,
    int_s,
    dz_s,
    dzt_s,
    z_s,
    *,
    clips,
    frames,
    rows,
):
    step = pl.program_id(0)
    last = pl.num_programs(0) - 1
    spans = [
        (clip, start, clip * frames + start)
        for clip in range(clips)
        for start in range(0, frames, rows)
    ]

    @pl.when(step == 0)
    def _():
        bias_sum = jnp.zeros((1, h_ref.shape[2]), F32)
        for clip, start, at in spans:
            normed, _ = normalize(h_ref[clip, start : start + rows])
            third_in = normed * (1.0 + mod_ref[clip, 7:8]) + mod_ref[clip, 6:7]
            dz = (mod_ref[clip, 8:9] * dy_ref[clip, start : start + rows].astype(F32)).astype(BF)
            in_s[at : at + rows] = third_in.astype(BF)
            dz_s[at : at + rows] = dz
            bias_sum += column_sum(dz.astype(F32))
        ddownb_ref[...] = bias_sum
        int_s[...] = in_s[...].T
        dzt_s[...] = dz_s[...].T

    up, down = up_ref[...], down_ref[...]
    grad_up = grad_down = grad_bias = None
    for clip, start, at in spans:
        here = pl.ds(at, rows)
        hidden = nn(in_s[here], up) + upb_ref[...]
        square = hidden * hidden
        tanh = jnp.tanh(GELU_ROOT * hidden * (1.0 + 0.044715 * square))
        half = 0.5 + 0.5 * tanh
        activated = (hidden * half).astype(BF)
        slope = half + hidden * half * (1.0 - tanh) * (
            GELU_ROOT * (1.0 + 3 * 0.044715 * square)
        )
        dz = dz_s[here]
        grad_hidden = (nt(dz, down) * slope).astype(BF)
        branch = nn(activated, down)
        grad_in = nt(grad_hidden, up)

        @pl.when(step == 0)
        def _(branch=branch, grad_in=grad_in, here=here, clip=clip, start=start):
            z_s[here] = branch
            dh_ref[clip, start : start + rows] = grad_in

        @pl.when(step > 0)
        def _(branch=branch, grad_in=grad_in, here=here, clip=clip, start=start):
            z_s[here] += branch
            dh_ref[clip, start : start + rows] += grad_in

        one_up = nn(int_s[:, at : at + rows], grad_hidden)
        one_down = nn(dzt_s[:, at : at + rows], activated)
        one_bias = column_sum(grad_hidden.astype(F32))
        grad_up = one_up if grad_up is None else grad_up + one_up
        grad_down = one_down if grad_down is None else grad_down + one_down
        grad_bias = one_bias if grad_bias is None else grad_bias + one_bias
    dup_ref[...] = grad_up.astype(BF)
    ddown_ref[...] = grad_down.T.astype(BF)
    dupb_ref[...] = grad_bias

    @pl.when(step == last)
    def _():
        for clip in range(clips):
            sums = None
            for start in range(0, frames, rows):
                at = clip * frames + start
                block = slice(start, start + rows)
                hidden = h_ref[clip, block]
                dy = dy_ref[clip, block].astype(F32)
                branch = z_s[at : at + rows] + downb_ref[...]
                out_ref[clip, block] = (hidden + mod_ref[clip, 8:9] * branch).astype(BF)
                normed, inverse = normalize(hidden)
                grad_in = dh_ref[clip, block]
                dh_ref[clip, block] = dy + norm_back(
                    normed, inverse, grad_in * (1.0 + mod_ref[clip, 7:8])
                )
                here = [
                    column_sum(grad_in),
                    column_sum(grad_in * normed),
                    column_sum(dy * branch),
                ]
                sums = here if sums is None else [a + b for a, b in zip(sums, here)]
            for index in range(3):
                sums_ref[clip, index : index + 1] = sums[index]


def feed(hidden, cotangent, mod, up, up_bias, down, down_bias, block=512):
    clips, frames, width = hidden.shape
    inner = up.shape[1]
    rows = row_block(frames)
    tokens = clips * frames

    def once(shape):
        return pl.BlockSpec(
            shape, lambda j: (0,) * len(shape), pipeline_mode=pl.Buffered(1)
        )

    def columns(count):
        return pl.BlockSpec((count, block), lambda j: (0, j))

    lines = pl.BlockSpec((block, width), lambda j: (j, 0))
    cube = once((clips, frames, width))
    return call(
        functools.partial(feed_kernel, clips=clips, frames=frames, rows=rows),
        (inner // block,),
        [
            cube,
            cube,
            once(mod.shape),
            columns(width),
            columns(1),
            lines,
            once((1, width)),
        ],
        [
            cube,
            cube,
            columns(width),
            lines,
            columns(1),
            once((1, width)),
            once((clips, 3, width)),
        ],
        [
            struct(hidden.shape, BF),
            struct(hidden.shape, F32),
            struct(up.shape, BF),
            struct(down.shape, BF),
            struct((1, inner), F32),
            struct((1, width), F32),
            struct((clips, 3, width), F32),
        ],
        "feed",
        [
            pltpu.VMEM((tokens, width), BF),
            pltpu.VMEM((width, tokens), BF),
            pltpu.VMEM((tokens, width), BF),
            pltpu.VMEM((width, tokens), BF),
            pltpu.VMEM((tokens, width), F32),
        ],
    )(hidden, cotangent, mod, up, up_bias, down, down_bias)


def ends():
    i, j = pl.program_id(0), pl.program_id(1)
    first = (i == 0) & (j == 0)
    last = (i == pl.num_programs(0) - 1) & (j == pl.num_programs(1) - 1)
    return j == 0, first, last


def before_cross_kernel(
    dh_ref, z_ref, o_ref, mod_ref, w_ref, do_ref, dw_ref, db_ref, sums_ref, dw_s
):
    new_clip, first, last = ends()
    dh = dh_ref[0]
    dz = (mod_ref[0, 5:6] * dh).astype(BF)
    add_to(sums_ref, new_clip, column_sum(dh * z_ref[0].astype(F32))[None])
    add_to(db_ref, first, column_sum(dz.astype(F32)))
    do_ref[0] = nt(dz, w_ref[...]).astype(BF)
    add_to(dw_s, first, tn(o_ref[0], dz))

    @pl.when(last)
    def _():
        dw_ref[...] = dw_s[...].astype(BF)


def before_cross(dh, branch, mixed, mod, weight):
    clips, frames, width = dh.shape
    rows = row_block(frames)
    spec = rows_spec(rows, width)
    square = whole_spec((width, width))
    return call(
        before_cross_kernel,
        (clips, frames // rows),
        [spec, spec, spec, clip_spec(9, width), square],
        [spec, square, whole_spec((1, width)), clip_spec(1, width)],
        [
            struct(dh.shape, BF),
            struct((width, width), BF),
            struct((1, width), F32),
            struct((clips, 1, width), F32),
        ],
        "before_cross",
        [pltpu.VMEM((width, width), F32)],
    )(dh, branch, mixed, mod, weight)


def before_self_kernel(
    dq_ref,
    h_ref,
    dh_ref,
    z_ref,
    o_ref,
    mod_ref,
    wq_ref,
    wo_ref,
    out_ref,
    do_ref,
    dwq_ref,
    dwo_ref,
    db_ref,
    sums_ref,
    dwq_s,
    dwo_s,
):
    new_clip, first, last = ends()
    normed, inverse = normalize(h_ref[0])
    second_in = (normed * (1.0 + mod_ref[0, 4:5]) + mod_ref[0, 3:4]).astype(BF)
    grad_query = dq_ref[0]
    add_to(dwq_s, first, tn(second_in, grad_query))
    grad_in = nt(grad_query, wq_ref[...])
    dh = dh_ref[0] + norm_back(normed, inverse, grad_in * (1.0 + mod_ref[0, 4:5]))
    out_ref[0] = dh
    dz = (mod_ref[0, 2:3] * dh).astype(BF)
    sums = jnp.concatenate(
        [
            column_sum(grad_in),
            column_sum(grad_in * normed),
            column_sum(dh * z_ref[0].astype(F32)),
        ],
        axis=0,
    )
    add_to(sums_ref, new_clip, sums[None])
    add_to(db_ref, first, column_sum(dz.astype(F32)))
    do_ref[0] = nt(dz, wo_ref[...]).astype(BF)
    add_to(dwo_s, first, tn(o_ref[0], dz))

    @pl.when(last)
    def _():
        dwq_ref[...] = dwq_s[...].astype(BF)
        dwo_ref[...] = dwo_s[...].astype(BF)


def before_self(grad_query, hidden, dh, branch, mixed, mod, query_weight, weight):
    clips, frames, width = dh.shape
    rows = row_block(frames)
    spec = rows_spec(rows, width)
    square = whole_spec((width, width))
    return call(
        before_self_kernel,
        (clips, frames // rows),
        [spec, spec, spec, spec, spec, clip_spec(9, width), square, square],
        [spec, spec, square, square, whole_spec((1, width)), clip_spec(3, width)],
        [
            struct(dh.shape, F32),
            struct(dh.shape, BF),
            struct((width, width), BF),
            struct((width, width), BF),
            struct((1, width), F32),
            struct((clips, 3, width), F32),
        ],
        "before_self",
        [pltpu.VMEM((width, width), F32), pltpu.VMEM((width, width), F32)],
    )(grad_query, hidden, dh, branch, mixed, mod, query_weight, weight)


def input_kernel(
    dq_ref, dk_ref, dv_ref, x_ref, dh_ref, mod_ref, w_ref, out_ref, dw_ref, sums_ref, dw_s
):
    new_clip, first, last = ends()
    width = x_ref.shape[2]
    normed, inverse = normalize(x_ref[0].astype(F32))
    first_in = (normed * (1.0 + mod_ref[0, 1:2]) + mod_ref[0, 0:1]).astype(BF)
    turned = first_in.T
    grad_in = None
    for index, ref in enumerate((dq_ref, dk_ref, dv_ref)):
        columns = slice(index * width, (index + 1) * width)
        grad = ref[0]
        part = nt(grad, w_ref[:, columns])
        grad_in = part if grad_in is None else grad_in + part
        add_to(dw_s.at[:, columns], first, nn(turned, grad))
    out_ref[0] = (
        dh_ref[0] + norm_back(normed, inverse, grad_in * (1.0 + mod_ref[0, 1:2]))
    ).astype(BF)
    sums = jnp.concatenate([column_sum(grad_in), column_sum(grad_in * normed)], axis=0)
    add_to(sums_ref, new_clip, sums[None])

    @pl.when(last)
    def _():
        dw_ref[...] = dw_s[...].astype(BF)


def input_back(grads, latents, dh, mod, weight):
    clips, frames, width = dh.shape
    rows = row_block(frames)
    spec = rows_spec(rows, width)
    return call(
        input_kernel,
        (clips, frames // rows),
        [spec] * 5 + [clip_spec(9, width), whole_spec(weight.shape)],
        [spec, whole_spec(weight.shape), clip_spec(2, width)],
        [
            struct(dh.shape, BF),
            struct(weight.shape, BF),
            struct((clips, 2, width), F32),
        ],
        "input_back",
        [pltpu.VMEM(weight.shape, F32)],
    )(*grads, latents, dh, mod, weight)


def block_pass(latents, captions, lengths, cotangent, mod, weights):
    (
        triple_weight,
        output_weight,
        output_bias,
        cross_query,
        cross_keyval,
        cross_output,
        cross_bias,
        up_weight,
        up_bias,
        down_weight,
        down_bias,
    ) = weights
    clips, frames, width = latents.shape
    slots = captions.shape[1]
    groups = HEADS // 2
    caption_flat = captions.reshape(clips * slots, captions.shape[2])
    triple = qkv_forward(latents, mod, triple_weight)
    mixed_one, lse_one = attend_forward(triple, groups, triple, 2 * groups, None, "self_forward")
    branch_one, hidden_one, cross_queries = after_self(
        mixed_one, latents, mod, output_weight, output_bias, cross_query
    )
    pairs = (
        jnp.dot(caption_flat, cross_keyval, preferred_element_type=F32)
        .astype(BF)
        .reshape(clips, slots, 2 * width)
    )
    mixed_two, lse_two = attend_forward(cross_queries, 0, pairs, groups, lengths, "cross_forward")
    branch_two, hidden_two = after_cross(mixed_two, hidden_one, mod, cross_output, cross_bias)
    output, dh_two, grad_up, grad_down, grad_up_bias, grad_down_bias, sums_three = feed(
        hidden_two, cotangent, mod, up_weight, up_bias, down_weight, down_bias
    )
    grad_mixed_two, grad_cross_output, grad_cross_bias, gate_two = before_cross(
        dh_two, branch_two, mixed_two, mod, cross_output
    )
    grad_cq, grad_ck, grad_cv = attend_backward(
        cross_queries, 0, pairs, groups, lengths, grad_mixed_two, mixed_two, lse_two, "cross_back"
    )
    grad_pairs = jnp.concatenate([grad_ck, grad_cv], axis=-1).reshape(clips * slots, 2 * width)
    grad_keyval = jnp.dot(caption_flat.T, grad_pairs, preferred_element_type=F32).astype(BF)
    dh_one, grad_mixed_one, grad_cross_query, grad_output, grad_output_bias, sums_two = before_self(
        grad_cq, hidden_one, dh_two, branch_one, mixed_one, mod, cross_query, output_weight
    )
    grads_one = attend_backward(
        triple,
        groups,
        triple,
        2 * groups,
        None,
        grad_mixed_one,
        mixed_one,
        lse_one,
        "self_back",
    )
    input_grad, grad_triple, sums_one = input_back(grads_one, latents, dh_one, mod, triple_weight)
    grad_mod = jnp.concatenate(
        [sums_one, sums_two[:, 2:], sums_two[:, :2], gate_two, sums_three], axis=1
    ).astype(BF)
    return (
        output,
        input_grad,
        grad_mod,
        [
            grad_triple,
            grad_output,
            grad_output_bias,
            grad_cross_query,
            grad_keyval,
            grad_cross_output,
            grad_cross_bias,
            grad_up,
            grad_up_bias,
            grad_down,
            grad_down_bias,
        ],
    )


LANE = 128
TILE = 16


def linear_layout():
    spots = []
    offset = 0
    for shape in layout_sizes():
        number = math.prod(shape) // LANE
        spots.append((offset, number, shape))
        offset += number
    return spots


class Plan:
    def __init__(self, devices, share):
        self.devices, self.share = devices, share
        spots = linear_layout()
        self.first_row = spots[2][0]
        self.rows = spots[-1][0] + spots[-1][1]
        self.lead = self.first_row // share
        self.padded = -(-share // TILE) * TILE
        self.lent = -(-(self.padded // 3) // TILE) * TILE
        self.kept = self.padded - self.lent
        self.chunk = 2 * self.lent
        self.base = (self.first_row - self.lead * share) // TILE * TILE

    def find(self, row):
        owner, at = divmod(row, self.share)
        if at < self.kept:
            base = self.base if owner == self.lead else 0
            return owner, at - base, self.kept - at
        if owner == self.lead:
            return self.lead - 1, at - self.kept, self.share - at
        lender = owner - self.lead - 1
        return lender // 2, (lender % 2) * self.lent + at - self.kept, self.share - at

    def segments(self, start, count):
        found = []
        row = start
        while row < start + count:
            chunk, place, left = self.find(row)
            take = min(left, start + count - row)
            found.append((chunk, place, row, take))
            row += take
        return found


def unpack_kernel(*refs, plan, indices, step):
    n = len(indices)
    spots = linear_layout()
    g_ref, outs, rest = refs[0], refs[1 : 1 + n], refs[1 + n :]
    lin, in_sem, out_sem = rest[0], rest[1], rest[2]
    stages, results = rest[3 : 3 + n], rest[3 + n :]
    loads = []
    for which, index in enumerate(indices):
        offset, number, _ = spots[index]
        place = 0
        mine = []
        for slot, (chunk, row, at, take) in enumerate(plan.segments(offset, number)):
            low = row // TILE * TILE
            high = -(-(row + take) // TILE) * TILE
            copy = pltpu.make_async_copy(
                g_ref.at[chunk, pl.ds(low, high - low)],
                stages[which].at[pl.ds(place, high - low)],
                in_sem.at[which, slot],
            )
            copy.start()
            mine.append((copy, place, row - low, high - low, at - offset, take))
            place += high - low
        loads.append(mine)
    stores = []
    for which, index in enumerate(indices):
        offset, number, shape = spots[index]
        for copy, place, skip, size, at, take in loads[which]:
            copy.wait()
            first = stages[which][place : place + TILE].astype(F32)
            lin[at : at + TILE - skip] = first[skip:]
            blocks, tail = divmod(size - TILE, step)

            def body(i, _, place=place, at=at, skip=skip, which=which):
                source = pl.multiple_of(place + TILE + i * step, TILE)
                lin[pl.ds(at + TILE - skip + i * step, step)] = stages[which][
                    pl.ds(source, step)
                ].astype(F32)
                return 0

            lax.fori_loop(0, blocks, body, 0)
            if tail:
                source = place + TILE + blocks * step
                target = at + TILE - skip + blocks * step
                lin[target : target + tail] = stages[which][source : source + tail].astype(F32)
        if len(shape) == 1:
            for c in range(number):
                results[which][0:1, c * LANE : (c + 1) * LANE] = lin[c : c + 1]
        else:
            high, wide = shape
            count = wide // LANE
            rows = 64

            def turn(i, _, which=which, count=count):
                top = pl.multiple_of(i * rows, rows)
                for c in range(count):
                    results[which][pl.ds(top, rows), c * LANE : (c + 1) * LANE] = lin[
                        pl.ds(top * count + c, rows, stride=count)
                    ].astype(BF)
                return 0

            lax.fori_loop(0, high // rows, turn, 0)
        copy = pltpu.make_async_copy(results[which], outs[which], out_sem.at[which])
        copy.start()
        stores.append(copy)
    for copy in stores:
        copy.wait()


def unpack_weights(gathered, plan, indices, step=128):
    spots = linear_layout()
    stage_shapes, result_shapes, most, tallest = [], [], 0, 0
    for index in indices:
        offset, number, shape = spots[index]
        found = plan.segments(offset, number)
        size = sum(-(-(r + t) // TILE) * TILE - r // TILE * TILE for _, r, _, t in found)
        stage_shapes.append(pltpu.VMEM((size, LANE), BF))
        most = max(most, len(found))
        tallest = max(tallest, number)
        result_shapes.append((shape, BF) if len(shape) == 2 else ((1, shape[0]), F32))
    anywhere = pl.BlockSpec(memory_space=pl.ANY)
    return pl.pallas_call(
        functools.partial(unpack_kernel, plan=plan, indices=indices, step=step),
        in_specs=[anywhere],
        out_specs=[anywhere] * len(indices),
        out_shape=[jax.ShapeDtypeStruct(s, t) for s, t in result_shapes],
        scratch_shapes=[
            pltpu.VMEM((tallest + 2 * TILE, LANE), F32),
            pltpu.SemaphoreType.DMA((len(indices), most)),
            pltpu.SemaphoreType.DMA((len(indices),)),
        ]
        + stage_shapes
        + [pltpu.VMEM(s, t) for s, t in result_shapes],
        compiler_params=pltpu.CompilerParams(vmem_limit_bytes=VMEM_LIMIT),
        name="unpack",
    )(gathered)


def pack_kernel(*refs, plan, indices, step):
    n = len(indices)
    spots = linear_layout()
    ins, out_ref, rest = refs[:n], refs[n], refs[n + 1 :]
    lin, stage, in_sem, out_sem = rest[:4]
    held = rest[4:]
    copies = []
    for which in range(n):
        copy = pltpu.make_async_copy(ins[which], held[which], in_sem.at[which])
        copy.start()
        copies.append(copy)
    stores = []
    begin = spots[indices[0]][0]
    total = spots[indices[-1]][0] + spots[indices[-1]][1] - begin
    pieces = plan.segments(begin, total)
    place = 0
    done = -TILE
    lin[0:TILE] = jnp.zeros((TILE, LANE), F32)
    slot = 0
    for which, index in enumerate(indices):
        offset, number, shape = spots[index]
        copies[which].wait()
        if len(shape) == 1:
            for c in range(number):
                lin[TILE + c : TILE + c + 1] = held[which][0:1, c * LANE : (c + 1) * LANE]
        else:
            high, wide = shape
            count = wide // LANE
            rows = 64

            def turn(i, _, which=which, count=count):
                top = pl.multiple_of(i * rows, rows)
                for c in range(count):
                    lin[pl.ds(TILE + top * count + c, rows, stride=count)] = held[which][
                        pl.ds(top, rows), c * LANE : (c + 1) * LANE
                    ].astype(F32)
                return 0

            lax.fori_loop(0, high // rows, turn, 0)
        low, high_row = offset - begin, offset - begin + number
        last = which == n - 1
        while slot < len(pieces):
            chunk, row, at, take = pieces[slot]
            at -= begin
            head = row - row // TILE * TILE
            start, stop = at - head, at + take
            ceil = start + -(-(stop - start) // TILE) * TILE
            first = max(start, done)
            whole = stop <= high_row
            end = ceil if whole else start + (high_row - start) // TILE * TILE
            if end > first:
                base = row - head + first - start
                blocks, tail = divmod(end - first, step)
                shift = TILE + first - low

                def body(i, _, place=place, shift=shift):
                    target = pl.multiple_of(place + i * step, TILE)
                    stage[pl.ds(target, step)] = lin[pl.ds(shift + i * step, step)].astype(BF)
                    return 0

                lax.fori_loop(0, blocks, body, 0)
                if tail:
                    source = shift + blocks * step
                    target = place + blocks * step
                    stage[target : target + tail] = lin[source : source + tail].astype(BF)
                copy = pltpu.make_async_copy(
                    stage.at[pl.ds(place, end - first)],
                    out_ref.at[chunk, pl.ds(base, end - first)],
                    out_sem.at[len(stores)],
                )
                copy.start()
                stores.append(copy)
                place += end - first
                done = end
            if not whole:
                break
            done = stop if slot + 1 == len(pieces) else min(done, stop)
            slot += 1
        if not last:
            lin[0:TILE] = lin[number : number + TILE]
    for copy in stores:
        copy.wait()


def pack_grads(grads, plan, indices, step=128):
    spots = linear_layout()
    tallest = max(spots[i][1] for i in indices)
    begin = spots[indices[0]][0]
    total = spots[indices[-1]][0] + spots[indices[-1]][1] - begin
    count = len(plan.segments(begin, total))
    anywhere = pl.BlockSpec(memory_space=pl.ANY)
    return pl.pallas_call(
        functools.partial(pack_kernel, plan=plan, indices=indices, step=step),
        in_specs=[anywhere] * len(indices),
        out_specs=anywhere,
        out_shape=jax.ShapeDtypeStruct((plan.devices, plan.chunk, LANE), BF),
        scratch_shapes=[
            pltpu.VMEM((tallest + 2 * TILE, LANE), F32),
            pltpu.VMEM((total + 2 * TILE * (count + len(indices)), LANE), BF),
            pltpu.SemaphoreType.DMA((len(indices),)),
            pltpu.SemaphoreType.DMA((count + len(indices),)),
        ]
        + [pltpu.VMEM(g.shape, g.dtype) for g in grads],
        compiler_params=pltpu.CompilerParams(vmem_limit_bytes=VMEM_LIMIT),
        name="pack",
    )(*grads)


MESH = pl.DeviceIdType.MESH
ROWS = 208


def place_of():
    dp, fs = lax.axis_index("dp"), lax.axis_index("fsdp")
    return dp, fs, dp // 2, dp % 2, fs // 2, fs % 2


def meet_all(me, devices, inner):
    barrier = pltpu.get_barrier_semaphore()

    def greet(i, _):
        other = (me + i) % devices
        pl.semaphore_signal(
            barrier, inc=1, device_id=(other // inner, other % inner), device_id_type=MESH
        )
        return 0

    lax.fori_loop(1, devices, greet, 0)
    pl.semaphore_wait(barrier, devices - 1)


class Trade:
    def __init__(self, source, target, own_sem, send_sem, recv_sem, plan, inner, senders, receivers):
        self.source, self.target, self.own_sem = source, target, own_sem
        self.send_sem, self.recv_sem = send_sem, recv_sem
        self.devices, self.inner = plan.devices, inner
        self.senders, self.receivers = senders, receivers
        self.me = lax.axis_index("dp") * inner + lax.axis_index("fsdp")
        self.many = len(source.shape) == 3

    def piece(self, target):
        return self.source.at[target] if self.many else self.source

    def copy(self, source, target):
        return pltpu.make_async_remote_copy(
            src_ref=self.piece(target),
            dst_ref=self.target.at[source],
            send_sem=self.send_sem.at[target],
            recv_sem=self.recv_sem.at[source],
            device_id=(target // self.inner, target % self.inner),
            device_id_type=MESH,
        )

    def own(self):
        return pltpu.make_async_copy(
            self.piece(self.me), self.target.at[self.me], self.own_sem
        )

    def each(self, act):
        def body(i, _):
            act((self.me + i) % self.devices)
            return 0

        lax.fori_loop(1, self.devices, body, 0)

    def both(self):
        return (self.me < self.senders) & (self.me < self.receivers)

    def start(self):
        pl.when(self.both())(lambda: self.own().start())

        def act(other):
            ok = (self.me < self.senders) & (other < self.receivers)
            pl.when(ok)(lambda: self.copy(self.me, other).start())

        self.each(act)

    def wait(self):
        pl.when(self.both())(lambda: self.own().wait())

        def landed(other):
            ok = (other < self.senders) & (self.me < self.receivers)
            pl.when(ok)(lambda: self.copy(other, other).wait_recv())

        def gone(other):
            ok = (self.me < self.senders) & (other < self.receivers)
            pl.when(ok)(lambda: self.copy(self.me, other).wait_send())

        self.each(landed)
        self.each(gone)


def when_all(conditions):
    total = None
    for condition in conditions:
        if condition is not None:
            total = condition if total is None else total & condition
    return total


def guarded(condition, body):
    if condition is None:
        body()
    else:
        pl.when(condition)(body)


def start_kernel(
    cond_ref, slot_ref, all_ref, own_ref, own_sem, lend_send, lend_recv, send_sem, recv_sem,
    *, plan, inner
):
    dp, fs, _, _, _, _ = place_of()
    me = dp * inner + fs
    lead, lent, kept = plan.lead, plan.lent, plan.kept
    meet_all(me, plan.devices, inner)

    def own_copy():
        start = pl.multiple_of(jnp.where(me == lead, plan.base, 0), TILE)
        return pltpu.make_async_copy(
            slot_ref.at[pl.ds(start, plan.chunk)], own_ref, own_sem.at[0]
        )

    def lend(slot, target, part):
        return pltpu.make_async_remote_copy(
            src_ref=slot_ref.at[pl.ds(kept, lent)],
            dst_ref=own_ref.at[pl.ds(pl.multiple_of(part * lent, TILE), lent)],
            send_sem=lend_send.at[slot],
            recv_sem=lend_recv.at[part],
            device_id=(target // inner, target % inner),
            device_id_type=MESH,
        )

    lender = jnp.maximum(me - lead - 1, 0)

    @pl.when(me > lead)
    def _():
        lend(0, lender // 2, lender % 2).start()

    @pl.when(me == lead)
    def _():
        lend(0, lead - 1, 0).start()
        lend(1, lead - 1, 1).start()

    @pl.when(me >= lead)
    def _():
        own_copy().start()

    trade = Trade(
        cond_ref, all_ref, own_sem.at[1], send_sem, recv_sem, plan, inner, plan.devices, plan.devices
    )
    trade.start()
    trade.wait()

    @pl.when(me >= lead)
    def _():
        own_copy().wait()
        lend(0, lead - 1, 0).wait_send()

    @pl.when(me == lead)
    def _():
        lend(1, lead - 1, 1).wait_send()

    @pl.when(me < lead)
    def _():
        lend(0, lead - 1, 0).wait_recv()
        lend(0, lead - 1, 1).wait_recv()


def start_chunks(condition, slot, plan, inner, collective):
    anywhere = pl.BlockSpec(memory_space=pl.ANY)
    dma = pltpu.SemaphoreType.DMA
    return pl.pallas_call(
        functools.partial(start_kernel, plan=plan, inner=inner),
        in_specs=[anywhere] * 2,
        out_specs=[anywhere] * 2,
        out_shape=[
            jax.ShapeDtypeStruct((plan.devices, *condition.shape), condition.dtype),
            jax.ShapeDtypeStruct((plan.chunk, LANE), BF),
        ],
        scratch_shapes=[
            dma((2,)),
            dma((2,)),
            dma((2,)),
            dma((plan.devices,)),
            dma((plan.devices,)),
        ],
        compiler_params=pltpu.CompilerParams(collective_id=collective, has_side_effects=True),
        name="start_chunks",
    )(condition, slot)


def gather_kernel(
    chunk_ref, slab_ref, out_ref, parts_ref, own_sem, slab_send, slab_recv, send_sem, recv_sem,
    *, plan, inner
):
    dp, fs, y, x, z, c = place_of()
    me = dp * inner + fs
    lent = plan.lent
    levels = inner // 2
    meet_all(me, plan.devices, inner)
    own = pltpu.make_async_copy(chunk_ref, out_ref.at[me], own_sem.at[0])
    own.start()
    trade = Trade(
        slab_ref, parts_ref, own_sem.at[1], slab_send, slab_recv, plan, inner, plan.lead + 1, plan.devices
    )

    across = {
        "up": (dp, fs + 2),
        "down": (dp, fs - 2),
        "x": (dp + 1 - 2 * x, fs),
        "y": (dp + 2 - 4 * y, fs),
        "twin": (dp, fs + 1 - 2 * c),
    }
    kinds = tuple(across)
    pending = []

    def copy(kind, yy, xx, zz, part, cc=None, mine=False):
        core = c if cc is None else cc
        column = yy * 2 + xx
        index = column * inner + zz * 2 + core
        rows = pl.ds(part * lent, lent)
        return pltpu.make_async_remote_copy(
            src_ref=chunk_ref.at[rows] if mine else out_ref.at[index, rows],
            dst_ref=out_ref.at[index, rows],
            send_sem=send_sem.at[kinds.index(kind), column * levels + zz, part],
            recv_sem=recv_sem.at[index, part],
            device_id=across[kind],
            device_id_type=MESH,
        )

    def send(condition, kind, yy, xx, zz, part, mine=False):
        guarded(condition, lambda: copy(kind, yy, xx, zz, part, mine=mine).start())
        pending.append((condition, kind, yy, xx, zz, part))

    def arrive(condition, yy, xx, zz, part):
        guarded(condition, lambda: copy("x", yy, xx, zz, part).wait_recv())

    def spread(distance):
        for sign in (1, -1) if distance else (0,):
            zz = z + sign * distance
            inside = when_all(
                [zz < levels if sign > 0 else None, zz >= 0 if sign < 0 else None]
            )
            yield zz, sign, inside

    for turn in range(levels + 2):
        if turn < levels:
            for zz, sign, inside in spread(turn):
                for part in range(2):
                    if turn:
                        arrive(inside, y, x, zz, part)
                    if sign <= 0:
                        send(when_all([inside, z < levels - 1]), "up", y, x, zz, part, turn == 0)
                    if sign >= 0:
                        send(when_all([inside, z > 0]), "down", y, x, zz, part, turn == 0)
                    for kind in ("x", "y") if part else ("y", "x"):
                        send(inside, kind, y, x, zz, part, turn == 0)
                    send(inside, "twin", y, x, zz, part, turn == 0)
            if turn == 0:
                trade.start()
        if 1 <= turn <= levels:
            for zz, sign, inside in spread(turn - 1):
                arrive(inside, y, 1 - x, zz, 0)
                send(inside, "y", y, 1 - x, zz, 0)
                send(inside, "twin", y, 1 - x, zz, 0)
                arrive(inside, 1 - y, x, zz, 1)
                send(inside, "x", 1 - y, x, zz, 1)
                send(inside, "twin", 1 - y, x, zz, 1)
                arrive(inside, 1 - y, x, zz, 0)
                send(inside, "twin", 1 - y, x, zz, 0)
                arrive(inside, y, 1 - x, zz, 1)
                send(inside, "twin", y, 1 - x, zz, 1)
        if turn >= 2:
            for zz, sign, inside in spread(turn - 2):
                for part in range(2):
                    arrive(inside, 1 - y, 1 - x, zz, part)
                    send(inside, "twin", 1 - y, 1 - x, zz, part)

    def twin_arrivals(i, _):
        column, zz = i // levels, i % levels
        for part in range(2):
            copy("twin", column // 2, column % 2, zz, part, 1 - c).wait_recv()
        return 0

    lax.fori_loop(0, 4 * levels, twin_arrivals, 0)
    for condition, kind, yy, xx, zz, part in pending:
        guarded(condition, lambda: copy(kind, yy, xx, zz, part).wait_send())
    trade.wait()
    own.wait()


def gather_chunks(chunk, slabs, plan, inner, collective):
    anywhere = pl.BlockSpec(memory_space=pl.ANY)
    dma = pltpu.SemaphoreType.DMA
    return pl.pallas_call(
        functools.partial(gather_kernel, plan=plan, inner=inner),
        in_specs=[anywhere] * 2,
        out_specs=[anywhere] * 2,
        out_shape=[
            jax.ShapeDtypeStruct((plan.devices, plan.chunk, LANE), BF),
            jax.ShapeDtypeStruct((plan.lead + 1, *slabs.shape[1:]), slabs.dtype),
        ],
        scratch_shapes=[
            dma((2,)),
            dma((plan.devices,)),
            dma((plan.devices,)),
            dma((5, plan.devices // 2, 2)),
            dma((plan.devices, 2)),
        ],
        compiler_params=pltpu.CompilerParams(collective_id=collective, has_side_effects=True),
        name="gather_chunks",
    )(chunk, slabs)


def scatter_kernel(
    g_ref,
    rows_ref,
    out_ref,
    all_ref,
    acc,
    twin,
    wide_y,
    wide_x,
    slim_x,
    slim_y,
    line,
    load_sem,
    twin_send,
    twin_recv,
    wide_send,
    wide_recv,
    slim_send,
    slim_recv,
    line_send,
    line_recv,
    own_sem,
    back_send,
    back_recv,
    row_send,
    row_recv,
    *,
    plan,
    inner,
):
    dp, fs, y, x, z, c = place_of()
    me = dp * inner + fs
    lead, lent, kept = plan.lead, plan.lent, plan.kept
    levels = inner // 2
    x_mate = (dp + 1 - 2 * x, fs)
    y_mate = (dp + 2 - 4 * y, fs)
    meet_all(me, plan.devices, inner)

    def remote(source, target, send, receive, device):
        return pltpu.make_async_remote_copy(
            src_ref=source,
            dst_ref=target,
            send_sem=send,
            recv_sem=receive,
            device_id=device,
            device_id_type=MESH,
        )

    def slot_of(yy, xx, zz):
        return (yy * 2 + xx) * levels + zz

    def load(yy, xx, zz):
        slot = slot_of(yy, xx, zz)
        return pltpu.make_async_copy(
            g_ref.at[(yy * 2 + xx) * inner + zz * 2 + c], acc.at[slot], load_sem.at[slot]
        )

    def to_twin(yy, xx, zz):
        slot = slot_of(yy, xx, zz)
        return remote(
            g_ref.at[(yy * 2 + xx) * inner + zz * 2 + 1 - c],
            twin.at[slot],
            twin_send.at[slot],
            twin_recv.at[slot],
            (dp, fs + 1 - 2 * c),
        )

    def piece(slot, part):
        return acc.at[slot, pl.ds(part * lent, lent)]

    def wide(part, other, zz, yy=0, xx=0):
        buffer, device = (wide_x, x_mate) if part else (wide_y, y_mate)
        index = other * levels + zz
        return remote(
            piece(slot_of(yy, xx, zz), part),
            buffer.at[index],
            wide_send.at[part, index],
            wide_recv.at[part, index],
            device,
        )

    def slim(part, zz, yy=0, xx=0):
        buffer, device = (slim_y, y_mate) if part else (slim_x, x_mate)
        return remote(
            piece(slot_of(yy, xx, zz), part),
            buffer.at[zz],
            slim_send.at[part, zz],
            slim_recv.at[part, zz],
            device,
        )

    def along(upward, zz, part):
        way = 0 if upward else 1
        return remote(
            piece(slot_of(y, x, zz), part),
            line.at[way, zz, part],
            line_send.at[way, zz, part],
            line_recv.at[way, zz, part],
            (dp, fs + 2 if upward else fs - 2),
        )

    def add(slot, first, count, source):
        def body(i, _):
            at = pl.multiple_of(i * ROWS, TILE)
            to = pl.ds(pl.multiple_of(first + i * ROWS, TILE), ROWS)
            acc[slot, to] = acc[slot, to] + source[pl.ds(at, ROWS)]
            return 0

        lax.fori_loop(0, count // ROWS, body, 0)

    def add_part(slot, part, source):
        add(slot, part * lent, lent, source)

    def level(k):
        return jnp.where(z < levels // 2, z + levels - 1 - k, z + 1 + k) % levels

    columns = ((1 - y, 1 - x), (1 - y, x), (y, 1 - x), (y, x))

    for yy, xx in columns:

        def begin(k, _, yy=yy, xx=xx):
            to_twin(yy, xx, level(k)).start()
            load(yy, xx, level(k)).start()
            return 0

        lax.fori_loop(0, levels, begin, 0)

    trade = Trade(
        rows_ref, all_ref, own_sem.at[1], row_send, row_recv, plan, inner, plan.devices, lead + 1
    )

    def settle(yy, xx, zz):
        slot = slot_of(yy, xx, zz)
        load(yy, xx, zz).wait()
        to_twin(yy, xx, zz).wait_recv()
        add(slot, 0, plan.chunk, twin.at[slot])

    def diagonal(k):
        zz = level(k)
        settle(1 - y, 1 - x, zz)
        wide(0, 1 - x, zz, 1 - y, 1 - x).start()
        wide(1, 1 - y, zz, 1 - y, 1 - x).start()

    def sides(k):
        zz = level(k)
        settle(1 - y, x, zz)
        wide(0, x, zz, 1 - y, x).start()
        settle(y, 1 - x, zz)
        wide(1, y, zz, y, 1 - x).start()

    def middle(k):
        zz = level(k)
        wide(0, 1 - x, zz).wait_recv()
        add_part(slot_of(y, 1 - x, zz), 0, wide_y.at[(1 - x) * levels + zz])
        slim(0, zz, y, 1 - x).start()
        wide(1, 1 - y, zz).wait_recv()
        add_part(slot_of(1 - y, x, zz), 1, wide_x.at[(1 - y) * levels + zz])
        slim(1, zz, 1 - y, x).start()

    def home(k):
        zz = level(k)
        slot = slot_of(y, x, zz)
        settle(y, x, zz)
        wide(0, x, zz).wait_recv()
        add_part(slot, 0, wide_y.at[x * levels + zz])
        wide(1, y, zz).wait_recv()
        add_part(slot, 1, wide_x.at[y * levels + zz])
        slim(0, zz).wait_recv()
        add_part(slot, 0, slim_x.at[zz])
        slim(1, zz).wait_recv()
        add_part(slot, 1, slim_y.at[zz])

    def take(upward, zz, part):
        along(upward, zz, part).wait_recv()
        add_part(slot_of(y, x, zz), part, line.at[0 if upward else 1, zz, part])

    edge = (z == 0) | (z == levels - 1)
    sent = []

    def pass_on(k, allowed):
        zz = level(k)
        for upward in (True, False):
            inside = allowed & (zz > z if upward else zz < z)
            more = z > 0 if upward else z < levels - 1

            @pl.when(inside)
            def _(upward=upward, more=more):
                for part in range(2):

                    @pl.when(more)
                    def _(part=part):
                        take(upward, zz, part)

                    along(upward, zz, part).start()

            sent.append((inside, upward, zz))

    def once(k):
        diagonal(k)
        sides(k)

    once(0)
    once(1)
    middle(0)
    once(2)
    middle(1)
    home(0)
    pass_on(0, edge)
    once(3)
    middle(2)
    middle(3)
    trade.start()
    home(1)
    pass_on(1, z >= 0)
    home(2)
    pass_on(2, z >= 0)
    pass_on(0, jnp.logical_not(edge))
    home(3)
    for part in range(2):

        @pl.when(z > 0)
        def _(part=part):
            take(True, z, part)

        @pl.when(z < levels - 1)
        def _(part=part):
            take(False, z, part)

    mine = slot_of(y, x, z)

    def back(slot, part, owner):
        return remote(
            piece(mine, part),
            out_ref.at[pl.ds(kept, lent)],
            back_send.at[slot],
            back_recv,
            (owner // inner, owner % inner),
        )

    @pl.when(me < lead - 1)
    def _():
        back(0, 0, lead + 1 + 2 * me).start()
        back(1, 1, lead + 2 + 2 * me).start()

    @pl.when(me == lead - 1)
    def _():
        back(0, 0, me + 1).start()

    @pl.when(me == lead)
    def _():
        count = kept - plan.base
        copy = pltpu.make_async_copy(
            acc.at[mine, pl.ds(0, count)], out_ref.at[pl.ds(plan.base, count)], own_sem.at[0]
        )
        copy.start()
        copy.wait()

    @pl.when(me > lead)
    def _():
        copy = pltpu.make_async_copy(
            acc.at[mine, pl.ds(0, kept)], out_ref.at[pl.ds(0, kept)], own_sem.at[0]
        )
        copy.start()
        copy.wait()

    @pl.when(me >= lead)
    def _():
        back(0, 0, 0).wait_recv()

    for inside, upward, zz in sent:

        @pl.when(inside)
        def _(upward=upward, zz=zz):
            for part in range(2):
                along(upward, zz, part).wait_send()

    def finish(k, _):
        zz = level(k)
        for yy, xx in columns:
            to_twin(yy, xx, zz).wait_send()
        wide(0, 1 - x, zz).wait_send()
        wide(0, x, zz).wait_send()
        wide(1, 1 - y, zz).wait_send()
        wide(1, y, zz).wait_send()
        slim(0, zz).wait_send()
        slim(1, zz).wait_send()
        return 0

    lax.fori_loop(0, levels, finish, 0)

    @pl.when(me < lead)
    def _():
        back(0, 0, 0).wait_send()

    @pl.when(me < lead - 1)
    def _():
        back(1, 1, 0).wait_send()

    trade.wait()


def scatter_chunks(grads, rows, plan, inner, collective):
    anywhere = pl.BlockSpec(memory_space=pl.ANY)
    dma = pltpu.SemaphoreType.DMA
    half, levels = plan.devices // 2, inner // 2
    part = (plan.lent, LANE)
    return pl.pallas_call(
        functools.partial(scatter_kernel, plan=plan, inner=inner),
        in_specs=[anywhere] * 2,
        out_specs=[anywhere] * 2,
        out_shape=[
            jax.ShapeDtypeStruct((plan.padded, LANE), BF),
            jax.ShapeDtypeStruct((plan.devices, *rows.shape), rows.dtype),
        ],
        scratch_shapes=[
            pltpu.VMEM((half, plan.chunk, LANE), BF),
            pltpu.VMEM((half, plan.chunk, LANE), BF),
            pltpu.VMEM((2 * levels, *part), BF),
            pltpu.VMEM((2 * levels, *part), BF),
            pltpu.VMEM((levels, *part), BF),
            pltpu.VMEM((levels, *part), BF),
            pltpu.VMEM((2, levels, 2, *part), BF),
            dma((half,)),
            dma((half,)),
            dma((half,)),
            dma((2, 2 * levels)),
            dma((2, 2 * levels)),
            dma((2, levels)),
            dma((2, levels)),
            dma((2, levels, 2)),
            dma((2, levels, 2)),
            dma((2,)),
            dma((2,)),
            dma,
            dma((plan.devices,)),
            dma((plan.devices,)),
        ],
        compiler_params=pltpu.CompilerParams(
            collective_id=collective, has_side_effects=True, vmem_limit_bytes=VMEM_LIMIT
        ),
        name="scatter_chunks",
    )(grads, rows)


def exchange_kernel(in_ref, out_ref, own_sem, send_sem, recv_sem, *, plan, inner):
    me = lax.axis_index("dp") * inner + lax.axis_index("fsdp")
    meet_all(me, plan.devices, inner)
    trade = Trade(
        in_ref, out_ref, own_sem, send_sem, recv_sem, plan, inner, plan.devices, plan.devices
    )
    trade.start()
    trade.wait()


def exchange(value, plan, inner, collective, name):
    anywhere = pl.BlockSpec(memory_space=pl.ANY)
    dma = pltpu.SemaphoreType.DMA
    return pl.pallas_call(
        functools.partial(exchange_kernel, plan=plan, inner=inner),
        in_specs=[anywhere],
        out_specs=anywhere,
        out_shape=jax.ShapeDtypeStruct((plan.devices, *value.shape), value.dtype),
        scratch_shapes=[dma, dma((plan.devices,)), dma((plan.devices,))],
        compiler_params=pltpu.CompilerParams(collective_id=collective, has_side_effects=True),
        name=name,
    )(value)


HALF = 27
TALL = 72
SLAB = 112
CONDITION_ROWS = 832


def ada_spots(me, plan):
    lines = plan.share // HALF
    odd = me % 2
    limit = CONDITION_ROWS - TALL
    return [
        (odd, jnp.minimum((lines * me + odd) // 2, limit)),
        (1 - odd, jnp.minimum((lines * me - odd) // 2, limit)),
    ]


def ada_kernel(lin_ref, cond_ref, out_ref, *, plan, inner):
    me = lax.axis_index("dp") * inner + lax.axis_index("fsdp")
    for half, (shift, top) in enumerate(ada_spots(me, plan)):
        condition = cond_ref[pl.ds(top, TALL)].astype(BF)

        def body(c, _, half=half, shift=shift, condition=condition):
            rows = lin_ref[pl.ds(HALF * shift + c, TALL, stride=2 * HALF)].astype(BF)
            part = tn(condition, rows)
            count = plan.devices
            for clip in range(2):
                out_ref[pl.ds((2 * clip + half) * HALF + c, count, stride=SLAB)] = part[
                    clip * count : (clip + 1) * count
                ]
            return 0

        lax.fori_loop(0, HALF, body, 0, unroll=True)


def ada_partial(lin, cond, plan, inner):
    return pl.pallas_call(
        functools.partial(ada_kernel, plan=plan, inner=inner),
        out_shape=jax.ShapeDtypeStruct((plan.devices * SLAB, LANE), F32),
        compiler_params=pltpu.CompilerParams(vmem_limit_bytes=VMEM_LIMIT),
        name="ada_partial",
    )(lin, cond)


def own_grad_kernel(cond_ref, dmod_ref, rest_ref, g_ref, sums_ref, lin, *, plan, inner):
    me = lax.axis_index("dp") * inner + lax.axis_index("fsdp")
    count = plan.devices
    border = jnp.clip(plan.first_row - plan.share * me, 0, plan.share)
    for half, (shift, top) in enumerate(ada_spots(me, plan)):
        condition = cond_ref[pl.ds(top, TALL)].astype(BF)

        def body(c, _, half=half, shift=shift, condition=condition):
            grads = jnp.concatenate(
                [
                    dmod_ref[pl.ds((2 * clip + half) * HALF + c, count, stride=SLAB)]
                    for clip in range(2)
                ],
                axis=0,
            ).astype(BF)
            lin[pl.ds(HALF * shift + c, TALL, stride=2 * HALF)] = nn(condition, grads)
            return 0

        @pl.when(border > 0)
        def _(body=body):
            lax.fori_loop(0, HALF, body, 0, unroll=True)

    rows = 64

    def merge(i, total):
        at = pl.multiple_of(i * rows, rows)
        row = lax.broadcasted_iota(jnp.int32, (rows, LANE), 0) + at
        rest = jnp.where(row < plan.share, rest_ref[pl.ds(at, rows)].astype(F32), 0.0)
        value = jnp.where(row < border, lin[pl.ds(at, rows)], rest)
        g_ref[pl.ds(at, rows)] = value
        square = value * value
        return total + sum(square[k : k + 8] for k in range(0, rows, 8))

    sums_ref[...] = lax.fori_loop(0, plan.padded // rows, merge, jnp.zeros((8, LANE), F32))


def own_grad(cond, dmod, rest, plan, inner):
    return pl.pallas_call(
        functools.partial(own_grad_kernel, plan=plan, inner=inner),
        out_shape=[
            jax.ShapeDtypeStruct((plan.padded, LANE), F32),
            jax.ShapeDtypeStruct((8, LANE), F32),
        ],
        scratch_shapes=[pltpu.VMEM((2 * HALF * TALL, LANE), F32)],
        compiler_params=pltpu.CompilerParams(vmem_limit_bytes=VMEM_LIMIT),
        name="own_grad",
    )(cond, dmod, rest)


def fits(devices, inner, share):
    return inner == 8 and devices == 32 and share % (LANE * HALF) == 0


def local_fast(
    latents, captions, lengths, timesteps, cotangent, master, first_moment, second_moment
):
    clips, frames, width = latents.shape
    share = master.shape[0]
    inner = lax.axis_size("fsdp")
    devices = inner * lax.axis_size("dp")
    plan = Plan(devices, share // LANE)
    indices = tuple(range(2, 13))

    rows = master.reshape(plan.share, LANE)
    lin = jnp.pad(rows, ((0, 2 * HALF * TALL - plan.share), (0, 0)))
    steps, chunk = start_chunks(
        jnp.broadcast_to(
            jnp.pad(timesteps.astype(F32), (0, 8 - clips))[:, None], (8, LANE)
        ),
        lin[: plan.padded].astype(BF),
        plan,
        inner,
        1,
    )
    steps = steps[:, :clips, 0].T.reshape(devices * clips)
    columns = jax.nn.silu(embed(steps)).astype(BF).astype(F32).T
    columns = jnp.concatenate(
        [
            columns,
            jnp.ones((1, clips * devices), F32),
            jnp.zeros((CONDITION_ROWS - width - 1, clips * devices), F32),
        ],
        axis=0,
    )
    slabs = ada_partial(lin, columns, plan, inner).reshape(devices, SLAB, LANE)
    gathered, parts = gather_chunks(chunk, slabs, plan, inner, 2)
    mod = jnp.sum(parts, axis=0)[: 54 * clips].reshape(clips, 9, width)
    weights = unpack_weights(gathered, plan, indices)
    output, input_grad, grad_mod, gradients = block_pass(
        latents, captions, lengths, cotangent, mod, weights
    )
    grad_rows = jnp.pad(
        grad_mod.reshape(54 * clips, LANE), ((0, SLAB - 54 * clips), (0, 0))
    )
    chunks = pack_grads(gradients, plan, indices)
    rest, dmod = scatter_chunks(chunks, grad_rows, plan, inner, 3)
    grads, squares = own_grad(
        columns, dmod.reshape(devices * SLAB, LANE).astype(F32), rest, plan, inner
    )
    squares = exchange(squares, plan, inner, 4, "squares")
    return (
        output,
        input_grad,
        grads[: plan.share].reshape(share),
        jnp.sum(squares),
    )


def local_any(
    latents, captions, lengths, timesteps, cotangent, master, first_moment, second_moment
):
    clips, frames, width = latents.shape
    share = master.shape[0]
    devices = lax.axis_size("dp") * lax.axis_size("fsdp")
    gathered = lax.all_gather(
        master.astype(BF).reshape(1, share), ("dp", "fsdp"), axis=0, tiled=True
    ).reshape(-1)
    weights = unpack(gathered)
    condition = jax.nn.silu(embed(timesteps)).astype(BF)
    mod = jnp.dot(condition, weights[0], preferred_element_type=F32) + weights[1].astype(F32)
    block_weights = [w.astype(F32).reshape(1, -1) if w.ndim == 1 else w for w in weights[2:]]
    output, input_grad, grad_mod, gradients = block_pass(
        latents, captions, lengths, cotangent, mod.reshape(clips, 9, width), block_weights
    )
    grad_mod = grad_mod.reshape(clips, 9 * width)
    grad_ada = jnp.dot(condition.T, grad_mod, preferred_element_type=F32)
    grad_list = [grad_ada, jnp.sum(grad_mod.astype(F32), axis=0)] + gradients
    flat = jnp.concatenate([piece.astype(F32).reshape(-1) for piece in grad_list])
    grad = lax.psum_scatter(
        flat.reshape(devices, share), ("dp", "fsdp"), scatter_dimension=0, tiled=True
    ).reshape(share)
    return output, input_grad, grad, lax.psum(jnp.sum(grad * grad), ("dp", "fsdp"))


def local(
    latents,
    captions,
    caption_lengths,
    timesteps,
    cotangent,
    master_weights,
    first_moment,
    second_moment,
):
    inner = lax.axis_size("fsdp")
    devices = inner * lax.axis_size("dp")
    run = local_fast if fits(devices, inner, master_weights.shape[0]) else local_any
    output, input_grad, grad_shard, squares = run(
        latents,
        captions,
        caption_lengths,
        timesteps,
        cotangent,
        master_weights,
        first_moment,
        second_moment,
    )
    grad_norm = jnp.sqrt(squares)
    clipped = grad_shard * (CLIP / jnp.maximum(grad_norm, CLIP))
    new_first = BETA_ONE * first_moment + (1.0 - BETA_ONE) * clipped
    new_second = BETA_TWO * second_moment + (1.0 - BETA_TWO) * clipped * clipped
    step_first = new_first / (1.0 - BETA_ONE**STEP)
    step_second = new_second / (1.0 - BETA_TWO**STEP)
    new_master = master_weights - RATE * (
        step_first / (jnp.sqrt(step_second) + ADAM_EPS) + DECAY * master_weights
    )
    return (output, input_grad, grad_norm, new_master, new_first, new_second)


def solution(mesh):
    placed = (
        P(("dp", "fsdp"), None, None),
        P(("dp", "fsdp"), None, None),
        P(("dp", "fsdp")),
        P(("dp", "fsdp")),
        P(("dp", "fsdp"), None, None),
        P(("dp", "fsdp")),
        P(("dp", "fsdp")),
        P(("dp", "fsdp")),
    )
    return jax.shard_map(
        local,
        mesh=mesh,
        in_specs=placed,
        out_specs=(
            P(("dp", "fsdp"), None, None),
            P(("dp", "fsdp"), None, None),
            P(),
            P(("dp", "fsdp")),
            P(("dp", "fsdp")),
            P(("dp", "fsdp")),
        ),
        check_vma=False,
    )
```

```python
import functools
import math

import jax
import jax.numpy as jnp
from jax import lax
from jax.experimental import pallas as pl
from jax.experimental.pallas import tpu as pltpu
from jax.sharding import PartitionSpec as P

D = 768
HEADS = 12
HD = 64
FF = 3072
CTX = 1024
STEP = 5


NORM_EPS = 1e-06
BETA_ONE = 0.9
BETA_TWO = 0.999
ADAM_EPS = 1e-08
RATE = 0.03
DECAY = 0.01
CLIP = 500.0


def layout_sizes():
    return [
        (D, 9 * D),
        (9 * D,),
        (D, 3 * D),
        (D, D),
        (D,),
        (D, D),
        (CTX, 2 * D),
        (D, D),
        (D,),
        (D, FF),
        (FF,),
        (FF, D),
        (D,),
    ]


def unpack(flat_vector):
    pieces = []
    offset = 0
    for layout_shape in layout_sizes():
        number = math.prod(layout_shape)
        pieces.append(flat_vector[offset : offset + number].reshape(layout_shape))
        offset += number
    return pieces


def embed(steps_in):
    half_width = D // 2
    frequency = jnp.exp(-math.log(10000.0) * jnp.arange(half_width, dtype=jnp.float32) / half_width)
    angles = steps_in.astype(jnp.float32)[:, None] * frequency[None, :]
    return jnp.concatenate([jnp.cos(angles), jnp.sin(angles)], axis=1)


def normalize(hidden):
    centred = hidden - jnp.mean(hidden, axis=-1, keepdims=True)
    inverse = lax.rsqrt(jnp.mean(centred * centred, axis=-1, keepdims=True) + NORM_EPS)
    return (centred * inverse, inverse)


def norm_back(normed, inverse, grad_normed):
    return inverse * (
        grad_normed
        - jnp.mean(grad_normed, axis=-1, keepdims=True)
        - normed * jnp.mean(grad_normed * normed, axis=-1, keepdims=True)
    )


F32 = jnp.float32
BF = jnp.bfloat16
VMEM_LIMIT = 60 << 20


def nn(left_side, right_side):
    return lax.dot_general(
        left_side, right_side, (((1,), (0,)), ((), ())), preferred_element_type=F32
    )


def nt(left_side, right_side):
    return lax.dot_general(
        left_side, right_side, (((1,), (1,)), ((), ())), preferred_element_type=F32
    )


def tn(left_side, right_side):
    return lax.dot_general(
        left_side, right_side, (((0,), (0,)), ((), ())), preferred_element_type=F32
    )


def call(body, grid, in_specs, out_specs, out_shape, name, scratch=()):
    return pl.pallas_call(
        body,
        grid=grid,
        in_specs=in_specs,
        out_specs=out_specs,
        out_shape=out_shape,
        scratch_shapes=list(scratch),
        compiler_params=pltpu.CompilerParams(vmem_limit_bytes=VMEM_LIMIT),
        name=name,
    )


def struct(shape, dtype):
    return jax.ShapeDtypeStruct(shape, dtype)


def rows_spec(rows, width):
    return pl.BlockSpec((1, rows, width), lambda i, j: (i, j, 0))


def clip_spec(count, width):
    return pl.BlockSpec((1, count, width), lambda i, j: (i, 0, 0))


def whole_spec(shape):
    return pl.BlockSpec(shape, lambda *_: (0,) * len(shape))


def row_block(frames):
    for parts in (2, 3, 4, 6):
        if frames % (16 * parts) == 0:
            return frames // parts
    return frames


def add_to(ref, first, value):
    @pl.when(first)
    def _():
        ref[...] = value

    @pl.when(jnp.logical_not(first))
    def _():
        ref[...] += value


def span_of(rows):
    start = (pl.program_id(0) * pl.num_programs(1) + pl.program_id(1)) * rows
    return pl.ds(pl.multiple_of(start, rows), rows)


def clear_at(first, *refs):
    @pl.when(first)
    def _():
        for ref in refs:
            ref[...] = jnp.zeros_like(ref)


def column_sum(value):
    return jnp.sum(value, axis=0, keepdims=True)


def qkv_kernel(x_ref, mod_ref, w_ref, out_ref):
    normed, _ = normalize(x_ref[0].astype(F32))
    first_in = (normed * (1.0 + mod_ref[0, 1:2]) + mod_ref[0, 0:1]).astype(BF)
    out_ref[0] = nn(first_in, w_ref[...]).astype(BF)


def qkv_forward(latents, mod, weight):
    clips, frames, width = latents.shape
    rows = row_block(frames)
    wide = weight.shape[1]
    return call(
        qkv_kernel,
        (clips, frames // rows),
        [rows_spec(rows, width), clip_spec(9, width), whole_spec(weight.shape)],
        rows_spec(rows, wide),
        struct((clips, frames, wide), BF),
        "qkv_forward",
    )(latents, mod, weight)


def head_lanes():
    lane = lax.broadcasted_iota(jnp.int32, (1, 2 * HD), 1)
    return lane, lane < HD


def usable_bias(length, count):
    row = lax.broadcasted_iota(jnp.int32, (count, 2 * HD), 0)
    return jnp.where(row < length, 0.0, -1e30).astype(BF)


def attend_kernel(*refs, masked):
    if masked:
        len_ref, q_ref, k_ref, v_ref, o_ref, l_ref = refs
    else:
        q_ref, k_ref, v_ref, o_ref, l_ref = refs
    lane, low = head_lanes()
    for pair in range(l_ref.shape[1]):
        columns = slice(pair * 2 * HD, (pair + 1) * 2 * HD)
        length = len_ref[pl.program_id(0)] if masked else None
        attend_pair(
            lane,
            low,
            length,
            q_ref[0, :, columns],
            k_ref[0, :, columns],
            v_ref[0, :, columns],
            o_ref.at[0, :, columns],
            l_ref.at[0, pair],
        )


def attend_pair(lane, low, length, q, k, v, o_ref, l_ref):
    masked = length is not None
    scaled = q * jnp.asarray(HD**-0.5, BF)
    one = jnp.ones((), BF)
    zero = jnp.zeros((), BF)
    values = [jnp.where(low, v, one), jnp.where(low, one, v)]
    if masked:
        bias = usable_bias(length, k.shape[0])
        tag = jnp.where(lane % HD == 0, one, zero)
        queries = [jnp.where(low, scaled, tag), jnp.where(low, tag, scaled)]
        keys = [jnp.where(low, k, bias), jnp.where(low, bias, k)]
    else:
        queries = [jnp.where(low, scaled, zero), jnp.where(low, zero, scaled)]
        keys = [k, k]
    tops, mixes = [], []
    for head in range(2):
        scores = nt(queries[head], keys[head])
        top = jnp.max(scores, axis=1, keepdims=True)
        mixes.append(nn(jnp.exp(scores - top).astype(BF), values[head]))
        tops.append(top)
    total = jnp.where(low, mixes[1], mixes[0])
    l_ref[...] = jnp.where(low, tops[1], tops[0]) + jnp.log(total)
    o_ref[...] = (jnp.where(low, mixes[0], mixes[1]) / pltpu.roll(total, HD, 1)).astype(BF)


def pair_spec(rows, offset, pairs):
    return pl.BlockSpec((1, rows, 2 * HD * pairs), lambda i, j: (i, 0, j + offset // pairs))


def lse_spec(rows, pairs):
    return pl.BlockSpec((1, pairs, rows, 2 * HD), lambda i, j: (i, j, 0, 0))


def attend_forward(queries, key_offset, keyvals, value_offset, lengths, name, pairs=1):
    clips, frames = queries.shape[:2]
    slots = keyvals.shape[1]
    groups = HEADS // 2
    masked = lengths is not None
    specs = [
        pair_spec(frames, 0, pairs),
        pair_spec(slots, key_offset, pairs),
        pair_spec(slots, value_offset, pairs),
    ]
    args = [queries, keyvals, keyvals]
    if masked:
        specs.insert(0, pl.BlockSpec(memory_space=pltpu.SMEM))
        args.insert(0, lengths)
    return call(
        functools.partial(attend_kernel, masked=masked),
        (clips, groups // pairs),
        specs,
        [pair_spec(frames, 0, pairs), lse_spec(frames, pairs)],
        [struct((clips, frames, D), BF), struct((clips, groups, frames, 2 * HD), F32)],
        name,
    )(*args)


def three_parts(value):
    high = value.astype(BF)
    rest = value - high.astype(F32)
    middle = rest.astype(BF)
    return high, middle, (rest - middle.astype(F32)).astype(BF)


def attend_back_kernel(*refs, masked):
    if masked:
        len_ref, q_ref, k_ref, v_ref, do_ref, o_ref, l_ref, dq_ref, dk_ref, dv_ref = refs
    else:
        q_ref, k_ref, v_ref, do_ref, o_ref, l_ref, dq_ref, dk_ref, dv_ref = refs
    lane, low = head_lanes()
    for pair in range(l_ref.shape[1]):
        columns = slice(pair * 2 * HD, (pair + 1) * 2 * HD)
        length = len_ref[pl.program_id(0)] if masked else None
        attend_back_pair(
            lane,
            low,
            length,
            q_ref[0, :, columns],
            k_ref[0, :, columns],
            v_ref[0, :, columns],
            do_ref[0, :, columns],
            o_ref[0, :, columns],
            l_ref[0, pair],
            dq_ref.at[0, :, columns],
            dk_ref.at[0, :, columns],
            dv_ref.at[0, :, columns],
        )


def attend_back_pair(lane, low, length, q, k, v, grad, mixed, lse, dq_ref, dk_ref, dv_ref):
    masked = length is not None
    scaled = q * jnp.asarray(HD**-0.5, BF)
    spot = lane % HD
    one = jnp.ones((), BF)
    zero = jnp.zeros((), BF)
    product = grad.astype(F32) * mixed.astype(F32)
    delta_low = jnp.sum(jnp.where(low, product, 0.0), axis=1, keepdims=True)
    delta_high = jnp.sum(jnp.where(low, 0.0, product), axis=1, keepdims=True)

    def negated(value, last):
        high, middle, rest = three_parts(-value)
        return jnp.where(
            spot == 0,
            high,
            jnp.where(spot == 1, middle, jnp.where(spot == 2, rest, last)),
        )

    tag = jnp.where(spot == 3, one, zero) if masked else zero
    lse_lanes = negated(lse, tag)
    delta_lanes = negated(jnp.where(low, delta_high, delta_low), zero)
    ones = jnp.broadcast_to(jnp.where(spot < 3, one, zero), k.shape)
    key_lanes = ones
    if masked:
        bias = usable_bias(length, k.shape[0])
        key_lanes = jnp.where(spot == 3, bias, ones)
    transposed = k.astype(F32).T.astype(BF)
    grad_queries, grad_keys, grad_values = [], [], []
    for head in range(2):

        def merge(own, other):
            return jnp.where(low, own, other) if head == 0 else jnp.where(low, other, own)

        probability = jnp.exp(nt(merge(k, key_lanes), merge(scaled, lse_lanes)))
        centred = nt(merge(v, ones), merge(grad, delta_lanes))
        grad_scores = (probability * centred).astype(BF)
        grad_values.append(nn(probability.astype(BF), grad))
        grad_keys.append(nn(grad_scores, scaled))
        grad_queries.append(nn(transposed[HD * head : HD * (head + 1)], grad_scores))
    dv_ref[...] = jnp.where(low, grad_values[0], grad_values[1]).astype(BF)
    dk_ref[...] = jnp.where(low, grad_keys[0], grad_keys[1]).astype(BF)
    dq_ref[...] = (jnp.concatenate(grad_queries, axis=0).T * HD**-0.5).astype(BF)


def attend_backward(
    queries, key_offset, keyvals, value_offset, lengths, grad, mixed, lse, name, pairs=1
):
    clips, frames = queries.shape[:2]
    slots = keyvals.shape[1]
    groups = HEADS // 2
    masked = lengths is not None
    specs = [
        pair_spec(frames, 0, pairs),
        pair_spec(slots, key_offset, pairs),
        pair_spec(slots, value_offset, pairs),
        pair_spec(frames, 0, pairs),
        pair_spec(frames, 0, pairs),
        lse_spec(frames, pairs),
    ]
    args = [queries, keyvals, keyvals, grad, mixed, lse]
    if masked:
        specs.insert(0, pl.BlockSpec(memory_space=pltpu.SMEM))
        args.insert(0, lengths)
    return call(
        functools.partial(attend_back_kernel, masked=masked),
        (clips, groups // pairs),
        specs,
        [pair_spec(frames, 0, pairs), pair_spec(slots, 0, pairs), pair_spec(slots, 0, pairs)],
        [
            struct((clips, frames, D), BF),
            struct((clips, slots, D), BF),
            struct((clips, slots, D), BF),
        ],
        name,
    )(*args)


def after_self_kernel(o_ref, x_ref, mod_ref, wo_ref, bo_ref, wq_ref, z_ref, h_ref, q_ref):
    branch = nn(o_ref[0], wo_ref[...]) + bo_ref[...]
    hidden = x_ref[0].astype(F32) + mod_ref[0, 2:3] * branch
    normed, _ = normalize(hidden)
    second_in = (normed * (1.0 + mod_ref[0, 4:5]) + mod_ref[0, 3:4]).astype(BF)
    z_ref[0] = branch.astype(BF)
    h_ref[0] = hidden
    q_ref[0] = nn(second_in, wq_ref[...]).astype(BF)


def after_self(mixed, latents, mod, weight, bias, query_weight):
    clips, frames, width = latents.shape
    rows = row_block(frames)
    spec = rows_spec(rows, width)
    square = whole_spec((width, width))
    return call(
        after_self_kernel,
        (clips, frames // rows),
        [spec, spec, clip_spec(9, width), square, whole_spec((1, width)), square],
        [spec, spec, spec],
        [
            struct(latents.shape, BF),
            struct(latents.shape, F32),
            struct(latents.shape, BF),
        ],
        "after_self",
    )(mixed, latents, mod, weight, bias, query_weight)


def after_cross_kernel(o_ref, h_ref, mod_ref, wo_ref, bo_ref, z_ref, out_ref):
    branch = nn(o_ref[0], wo_ref[...]) + bo_ref[...]
    z_ref[0] = branch.astype(BF)
    out_ref[0] = h_ref[0] + mod_ref[0, 5:6] * branch


def after_cross(mixed, hidden, mod, weight, bias):
    clips, frames, width = hidden.shape
    rows = row_block(frames)
    spec = rows_spec(rows, width)
    return call(
        after_cross_kernel,
        (clips, frames // rows),
        [
            spec,
            spec,
            clip_spec(9, width),
            whole_spec((width, width)),
            whole_spec((1, width)),
        ],
        [spec, spec],
        [struct(hidden.shape, BF), struct(hidden.shape, F32)],
        "after_cross",
    )(mixed, hidden, mod, weight, bias)


GELU_ROOT = math.sqrt(2.0 / math.pi)


def feed_kernel(
    h_ref,
    dy_ref,
    mod_ref,
    up_ref,
    upb_ref,
    down_ref,
    downb_ref,
    out_ref,
    dh_ref,
    dup_ref,
    ddown_ref,
    dupb_ref,
    ddownb_ref,
    sums_ref,
    in_s,
    int_s,
    dz_s,
    dzt_s,
    z_s,
    act_s,
    du_s,
    *,
    clips,
    frames,
    rows,
):
    step = pl.program_id(0)
    last = pl.num_programs(0) - 1
    spans = [
        (clip, start, clip * frames + start)
        for clip in range(clips)
        for start in range(0, frames, rows)
    ]

    @pl.when(step == 0)
    def _():
        bias_sum = jnp.zeros((1, h_ref.shape[2]), F32)
        for clip, start, at in spans:
            normed, _ = normalize(h_ref[clip, start : start + rows])
            third_in = normed * (1.0 + mod_ref[clip, 7:8]) + mod_ref[clip, 6:7]
            dz = (mod_ref[clip, 8:9] * dy_ref[clip, start : start + rows].astype(F32)).astype(BF)
            in_s[at : at + rows] = third_in.astype(BF)
            dz_s[at : at + rows] = dz
            bias_sum += column_sum(dz.astype(F32))
        ddownb_ref[...] = bias_sum
        int_s[...] = in_s[...].T
        dzt_s[...] = dz_s[...].T
        z_s[...] = jnp.zeros_like(z_s)
        dh_ref[...] = jnp.zeros_like(dh_ref)

    up, down = up_ref[...], down_ref[...]
    for clip, start, at in spans:
        here = pl.ds(at, rows)
        hidden = nn(in_s[here], up) + upb_ref[...]
        square = hidden * hidden
        tanh = jnp.tanh(hidden * (GELU_ROOT + (GELU_ROOT * 0.044715) * square))
        half = 0.5 + 0.5 * tanh
        lifted = hidden * half
        activated = lifted.astype(BF)
        slope = half + lifted * (1.0 - tanh) * (
            GELU_ROOT + (GELU_ROOT * 3 * 0.044715) * square
        )
        grad_hidden = (nt(dz_s[here], down) * slope).astype(BF)
        z_s[here] += nn(activated, down)
        dh_ref[clip, start : start + rows] += nt(grad_hidden, up)
        act_s[here] = activated
        du_s[here] = grad_hidden
    dup_ref[...] = nn(int_s[...], du_s[...]).astype(BF)
    ddown_ref[...] = nn(dzt_s[...], act_s[...]).T.astype(BF)
    dupb_ref[...] = column_sum(du_s[...].astype(F32))

    @pl.when(step == last)
    def _():
        for clip in range(clips):
            sums = None
            for start in range(0, frames, rows):
                at = clip * frames + start
                block = slice(start, start + rows)
                hidden = h_ref[clip, block]
                dy = dy_ref[clip, block].astype(F32)
                branch = z_s[at : at + rows] + downb_ref[...]
                out_ref[clip, block] = (hidden + mod_ref[clip, 8:9] * branch).astype(BF)
                normed, inverse = normalize(hidden)
                grad_in = dh_ref[clip, block]
                dh_ref[clip, block] = dy + norm_back(
                    normed, inverse, grad_in * (1.0 + mod_ref[clip, 7:8])
                )
                here = [
                    column_sum(grad_in),
                    column_sum(grad_in * normed),
                    column_sum(dy * branch),
                ]
                sums = here if sums is None else [a + b for a, b in zip(sums, here)]
            for index in range(3):
                sums_ref[clip, index : index + 1] = sums[index]


def feed(hidden, cotangent, mod, up, up_bias, down, down_bias, block=768):
    clips, frames, width = hidden.shape
    inner = up.shape[1]
    rows = row_block(frames)
    tokens = clips * frames

    def once(shape):
        return pl.BlockSpec(
            shape, lambda j: (0,) * len(shape), pipeline_mode=pl.Buffered(1)
        )

    def columns(count):
        return pl.BlockSpec((count, block), lambda j: (0, j))

    lines = pl.BlockSpec((block, width), lambda j: (j, 0))
    cube = once((clips, frames, width))
    return call(
        functools.partial(feed_kernel, clips=clips, frames=frames, rows=rows),
        (inner // block,),
        [
            cube,
            cube,
            once(mod.shape),
            columns(width),
            columns(1),
            lines,
            once((1, width)),
        ],
        [
            cube,
            cube,
            columns(width),
            lines,
            columns(1),
            once((1, width)),
            once((clips, 3, width)),
        ],
        [
            struct(hidden.shape, BF),
            struct(hidden.shape, F32),
            struct(up.shape, BF),
            struct(down.shape, BF),
            struct((1, inner), F32),
            struct((1, width), F32),
            struct((clips, 3, width), F32),
        ],
        "feed",
        [
            pltpu.VMEM((tokens, width), BF),
            pltpu.VMEM((width, tokens), BF),
            pltpu.VMEM((tokens, width), BF),
            pltpu.VMEM((width, tokens), BF),
            pltpu.VMEM((tokens, width), F32),
            pltpu.VMEM((tokens, block), BF),
            pltpu.VMEM((tokens, block), BF),
        ],
    )(hidden, cotangent, mod, up, up_bias, down, down_bias)


def ends():
    i, j = pl.program_id(0), pl.program_id(1)
    first = (i == 0) & (j == 0)
    last = (i == pl.num_programs(0) - 1) & (j == pl.num_programs(1) - 1)
    return j == 0, first, last


def before_cross_kernel(
    dh_ref, z_ref, o_ref, mod_ref, w_ref, do_ref, dw_ref, db_ref, sums_ref, ot_s, dz_s
):
    new_clip, first, last = ends()
    clear_at(new_clip, sums_ref)
    clear_at(first, db_ref)
    dh = dh_ref[0]
    here = span_of(dh.shape[0])
    dz = (mod_ref[0, 5:6] * dh).astype(BF)
    dz_s[here] = dz
    ot_s[here] = o_ref[0]
    sums_ref[0] += column_sum(dh * z_ref[0].astype(F32))
    db_ref[...] += column_sum(dz.astype(F32))
    do_ref[0] = nt(dz, w_ref[...]).astype(BF)

    @pl.when(last)
    def _():
        dw_ref[...] = tn(ot_s[...], dz_s[...]).astype(BF)


def before_cross(dh, branch, mixed, mod, weight):
    clips, frames, width = dh.shape
    rows = row_block(frames)
    spec = rows_spec(rows, width)
    square = whole_spec((width, width))
    return call(
        before_cross_kernel,
        (clips, frames // rows),
        [spec, spec, spec, clip_spec(9, width), square],
        [spec, square, whole_spec((1, width)), clip_spec(1, width)],
        [
            struct(dh.shape, BF),
            struct((width, width), BF),
            struct((1, width), F32),
            struct((clips, 1, width), F32),
        ],
        "before_cross",
        [pltpu.VMEM((clips * frames, width), BF)] * 2,
    )(dh, branch, mixed, mod, weight)


def before_self_kernel(
    dq_ref,
    h_ref,
    dh_ref,
    z_ref,
    o_ref,
    mod_ref,
    wq_ref,
    wo_ref,
    out_ref,
    do_ref,
    dwq_ref,
    dwo_ref,
    db_ref,
    sums_ref,
    in_s,
    dq_s,
    o_s,
    dz_s,
):
    new_clip, first, last = ends()
    clear_at(new_clip, sums_ref)
    clear_at(first, db_ref)
    here = span_of(dq_ref.shape[1])
    normed, inverse = normalize(h_ref[0])
    in_s[here] = (normed * (1.0 + mod_ref[0, 4:5]) + mod_ref[0, 3:4]).astype(BF)
    grad_query = dq_ref[0]
    dq_s[here] = grad_query
    o_s[here] = o_ref[0]
    grad_in = nt(grad_query, wq_ref[...])
    dh = dh_ref[0] + norm_back(normed, inverse, grad_in * (1.0 + mod_ref[0, 4:5]))
    out_ref[0] = dh
    dz = (mod_ref[0, 2:3] * dh).astype(BF)
    dz_s[here] = dz
    sums_ref[0] += jnp.concatenate(
        [
            column_sum(grad_in),
            column_sum(grad_in * normed),
            column_sum(dh * z_ref[0].astype(F32)),
        ],
        axis=0,
    )
    db_ref[...] += column_sum(dz.astype(F32))
    do_ref[0] = nt(dz, wo_ref[...]).astype(BF)

    @pl.when(last)
    def _():
        dwq_ref[...] = tn(in_s[...], dq_s[...]).astype(BF)
        dwo_ref[...] = tn(o_s[...], dz_s[...]).astype(BF)


def before_self(grad_query, hidden, dh, branch, mixed, mod, query_weight, weight):
    clips, frames, width = dh.shape
    rows = row_block(frames)
    spec = rows_spec(rows, width)
    square = whole_spec((width, width))
    return call(
        before_self_kernel,
        (clips, frames // rows),
        [spec, spec, spec, spec, spec, clip_spec(9, width), square, square],
        [spec, spec, square, square, whole_spec((1, width)), clip_spec(3, width)],
        [
            struct(dh.shape, F32),
            struct(dh.shape, BF),
            struct((width, width), BF),
            struct((width, width), BF),
            struct((1, width), F32),
            struct((clips, 3, width), F32),
        ],
        "before_self",
        [pltpu.VMEM((clips * frames, width), BF)] * 4,
    )(grad_query, hidden, dh, branch, mixed, mod, query_weight, weight)


def input_kernel(
    dq_ref, dk_ref, dv_ref, x_ref, dh_ref, mod_ref, w_ref, out_ref, dw_ref, sums_ref, in_s, g_s
):
    new_clip, _, last = ends()
    width = x_ref.shape[2]
    clear_at(new_clip, sums_ref)
    here = span_of(x_ref.shape[1])
    normed, inverse = normalize(x_ref[0].astype(F32))
    in_s[here] = (normed * (1.0 + mod_ref[0, 1:2]) + mod_ref[0, 0:1]).astype(BF)
    grad_in = None
    for index, ref in enumerate((dq_ref, dk_ref, dv_ref)):
        columns = slice(index * width, (index + 1) * width)
        grad = ref[0]
        g_s[here, columns] = grad
        part = nt(grad, w_ref[:, columns])
        grad_in = part if grad_in is None else grad_in + part
    out_ref[0] = (
        dh_ref[0] + norm_back(normed, inverse, grad_in * (1.0 + mod_ref[0, 1:2]))
    ).astype(BF)
    sums_ref[0] += jnp.concatenate(
        [column_sum(grad_in), column_sum(grad_in * normed)], axis=0
    )

    @pl.when(last)
    def _():
        turned = in_s[...].T
        for index in range(3):
            columns = slice(index * width, (index + 1) * width)
            dw_ref[:, columns] = nn(turned, g_s[:, columns]).astype(BF)


def input_back(grads, latents, dh, mod, weight):
    clips, frames, width = dh.shape
    rows = row_block(frames)
    spec = rows_spec(rows, width)
    return call(
        input_kernel,
        (clips, frames // rows),
        [spec] * 5 + [clip_spec(9, width), whole_spec(weight.shape)],
        [spec, whole_spec(weight.shape), clip_spec(2, width)],
        [
            struct(dh.shape, BF),
            struct(weight.shape, BF),
            struct((clips, 2, width), F32),
        ],
        "input_back",
        [
            pltpu.VMEM((clips * frames, width), BF),
            pltpu.VMEM((clips * frames, weight.shape[1]), BF),
        ],
    )(*grads, latents, dh, mod, weight)


def block_pass(latents, captions, lengths, cotangent, mod, weights):
    (
        triple_weight,
        output_weight,
        output_bias,
        cross_query,
        cross_keyval,
        cross_output,
        cross_bias,
        up_weight,
        up_bias,
        down_weight,
        down_bias,
    ) = weights
    clips, frames, width = latents.shape
    slots = captions.shape[1]
    groups = HEADS // 2
    caption_flat = captions.reshape(clips * slots, captions.shape[2])
    triple = qkv_forward(latents, mod, triple_weight)
    mixed_one, lse_one = attend_forward(triple, groups, triple, 2 * groups, None, "self_forward", 2)
    branch_one, hidden_one, cross_queries = after_self(
        mixed_one, latents, mod, output_weight, output_bias, cross_query
    )
    pairs = (
        jnp.dot(caption_flat, cross_keyval, preferred_element_type=F32)
        .astype(BF)
        .reshape(clips, slots, 2 * width)
    )
    mixed_two, lse_two = attend_forward(cross_queries, 0, pairs, groups, lengths, "cross_forward")
    branch_two, hidden_two = after_cross(mixed_two, hidden_one, mod, cross_output, cross_bias)
    output, dh_two, grad_up, grad_down, grad_up_bias, grad_down_bias, sums_three = feed(
        hidden_two, cotangent, mod, up_weight, up_bias, down_weight, down_bias
    )
    grad_mixed_two, grad_cross_output, grad_cross_bias, gate_two = before_cross(
        dh_two, branch_two, mixed_two, mod, cross_output
    )
    grad_cq, grad_ck, grad_cv = attend_backward(
        cross_queries,
        0,
        pairs,
        groups,
        lengths,
        grad_mixed_two,
        mixed_two,
        lse_two,
        "cross_back",
        2,
    )
    grad_pairs = jnp.concatenate([grad_ck, grad_cv], axis=-1).reshape(clips * slots, 2 * width)
    grad_keyval = jnp.dot(caption_flat.T, grad_pairs, preferred_element_type=F32).astype(BF)
    dh_one, grad_mixed_one, grad_cross_query, grad_output, grad_output_bias, sums_two = before_self(
        grad_cq, hidden_one, dh_two, branch_one, mixed_one, mod, cross_query, output_weight
    )
    grads_one = attend_backward(
        triple,
        groups,
        triple,
        2 * groups,
        None,
        grad_mixed_one,
        mixed_one,
        lse_one,
        "self_back",
        2,
    )
    input_grad, grad_triple, sums_one = input_back(grads_one, latents, dh_one, mod, triple_weight)
    grad_mod = jnp.concatenate(
        [sums_one, sums_two[:, 2:], sums_two[:, :2], gate_two, sums_three], axis=1
    ).astype(BF)
    return (
        output,
        input_grad,
        grad_mod,
        [
            grad_triple,
            grad_output,
            grad_output_bias,
            grad_cross_query,
            grad_keyval,
            grad_cross_output,
            grad_cross_bias,
            grad_up,
            grad_up_bias,
            grad_down,
            grad_down_bias,
        ],
    )


LANE = 128
TILE = 16


def linear_layout():
    spots = []
    offset = 0
    for shape in layout_sizes():
        number = math.prod(shape) // LANE
        spots.append((offset, number, shape))
        offset += number
    return spots


class Plan:
    def __init__(self, devices, share):
        self.devices, self.share = devices, share
        spots = linear_layout()
        self.first_row = spots[2][0]
        self.rows = spots[-1][0] + spots[-1][1]
        self.lead = self.first_row // share
        self.padded = -(-share // TILE) * TILE
        self.lent = -(-(self.padded // 3) // TILE) * TILE
        self.kept = self.padded - self.lent
        self.chunk = 2 * self.lent
        self.base = (self.first_row - self.lead * share) // TILE * TILE

    def find(self, row):
        owner, at = divmod(row, self.share)
        if at < self.kept:
            base = self.base if owner == self.lead else 0
            return owner, at - base, self.kept - at
        if owner == self.lead:
            return self.lead - 1, at - self.kept, self.share - at
        lender = owner - self.lead - 1
        return lender // 2, (lender % 2) * self.lent + at - self.kept, self.share - at

    def segments(self, start, count):
        found = []
        row = start
        while row < start + count:
            chunk, place, left = self.find(row)
            take = min(left, start + count - row)
            found.append((chunk, place, row, take))
            row += take
        return found


def unpack_kernel(*refs, plan, indices, step):
    n = len(indices)
    spots = linear_layout()
    g_ref, outs, rest = refs[0], refs[1 : 1 + n], refs[1 + n :]
    lin, in_sem, out_sem = rest[0], rest[1], rest[2]
    stages, results = rest[3 : 3 + n], rest[3 + n :]
    loads = []
    for which, index in enumerate(indices):
        offset, number, _ = spots[index]
        place = 0
        mine = []
        for slot, (chunk, row, at, take) in enumerate(plan.segments(offset, number)):
            low = row // TILE * TILE
            high = -(-(row + take) // TILE) * TILE
            copy = pltpu.make_async_copy(
                g_ref.at[chunk, pl.ds(low, high - low)],
                stages[which].at[pl.ds(place, high - low)],
                in_sem.at[which, slot],
            )
            copy.start()
            mine.append((copy, place, row - low, high - low, at - offset, take))
            place += high - low
        loads.append(mine)
    stores = []
    for which, index in enumerate(indices):
        offset, number, shape = spots[index]
        for copy, place, skip, size, at, take in loads[which]:
            copy.wait()
            first = stages[which][place : place + TILE].astype(F32)
            lin[at : at + TILE - skip] = first[skip:]
            blocks, tail = divmod(size - TILE, step)

            def body(i, _, place=place, at=at, skip=skip, which=which):
                source = pl.multiple_of(place + TILE + i * step, TILE)
                lin[pl.ds(at + TILE - skip + i * step, step)] = stages[which][
                    pl.ds(source, step)
                ].astype(F32)
                return 0

            lax.fori_loop(0, blocks, body, 0)
            if tail:
                source = place + TILE + blocks * step
                target = at + TILE - skip + blocks * step
                lin[target : target + tail] = stages[which][source : source + tail].astype(F32)
        if len(shape) == 1:
            for c in range(number):
                results[which][0:1, c * LANE : (c + 1) * LANE] = lin[c : c + 1]
        else:
            high, wide = shape
            count = wide // LANE
            rows = 64

            def turn(i, _, which=which, count=count):
                top = pl.multiple_of(i * rows, rows)
                for c in range(count):
                    results[which][pl.ds(top, rows), c * LANE : (c + 1) * LANE] = lin[
                        pl.ds(top * count + c, rows, stride=count)
                    ].astype(BF)
                return 0

            lax.fori_loop(0, high // rows, turn, 0)
        copy = pltpu.make_async_copy(results[which], outs[which], out_sem.at[which])
        copy.start()
        stores.append(copy)
    for copy in stores:
        copy.wait()


def unpack_weights(gathered, plan, indices, step=128):
    spots = linear_layout()
    stage_shapes, result_shapes, most, tallest = [], [], 0, 0
    for index in indices:
        offset, number, shape = spots[index]
        found = plan.segments(offset, number)
        size = sum(-(-(r + t) // TILE) * TILE - r // TILE * TILE for _, r, _, t in found)
        stage_shapes.append(pltpu.VMEM((size, LANE), BF))
        most = max(most, len(found))
        tallest = max(tallest, number)
        result_shapes.append((shape, BF) if len(shape) == 2 else ((1, shape[0]), F32))
    anywhere = pl.BlockSpec(memory_space=pl.ANY)
    return pl.pallas_call(
        functools.partial(unpack_kernel, plan=plan, indices=indices, step=step),
        in_specs=[anywhere],
        out_specs=[anywhere] * len(indices),
        out_shape=[jax.ShapeDtypeStruct(s, t) for s, t in result_shapes],
        scratch_shapes=[
            pltpu.VMEM((tallest + 2 * TILE, LANE), F32),
            pltpu.SemaphoreType.DMA((len(indices), most)),
            pltpu.SemaphoreType.DMA((len(indices),)),
        ]
        + stage_shapes
        + [pltpu.VMEM(s, t) for s, t in result_shapes],
        compiler_params=pltpu.CompilerParams(vmem_limit_bytes=VMEM_LIMIT),
        name="unpack",
    )(gathered)


def pack_kernel(*refs, plan, indices, step):
    n = len(indices)
    spots = linear_layout()
    ins, out_ref, rest = refs[:n], refs[n], refs[n + 1 :]
    lin, stage, in_sem, out_sem = rest[:4]
    held = rest[4:]
    copies = []
    for which in range(n):
        copy = pltpu.make_async_copy(ins[which], held[which], in_sem.at[which])
        copy.start()
        copies.append(copy)
    stores = []
    begin = spots[indices[0]][0]
    total = spots[indices[-1]][0] + spots[indices[-1]][1] - begin
    pieces = plan.segments(begin, total)
    place = 0
    done = -TILE
    lin[0:TILE] = jnp.zeros((TILE, LANE), F32)
    slot = 0
    for which, index in enumerate(indices):
        offset, number, shape = spots[index]
        copies[which].wait()
        if len(shape) == 1:
            for c in range(number):
                lin[TILE + c : TILE + c + 1] = held[which][0:1, c * LANE : (c + 1) * LANE]
        else:
            high, wide = shape
            count = wide // LANE
            rows = 64

            def turn(i, _, which=which, count=count):
                top = pl.multiple_of(i * rows, rows)
                for c in range(count):
                    lin[pl.ds(TILE + top * count + c, rows, stride=count)] = held[which][
                        pl.ds(top, rows), c * LANE : (c + 1) * LANE
                    ].astype(F32)
                return 0

            lax.fori_loop(0, high // rows, turn, 0)
        low, high_row = offset - begin, offset - begin + number
        last = which == n - 1
        while slot < len(pieces):
            chunk, row, at, take = pieces[slot]
            at -= begin
            head = row - row // TILE * TILE
            start, stop = at - head, at + take
            ceil = start + -(-(stop - start) // TILE) * TILE
            first = max(start, done)
            whole = stop <= high_row
            end = ceil if whole else start + (high_row - start) // TILE * TILE
            if end > first:
                base = row - head + first - start
                blocks, tail = divmod(end - first, step)
                shift = TILE + first - low

                def body(i, _, place=place, shift=shift):
                    target = pl.multiple_of(place + i * step, TILE)
                    stage[pl.ds(target, step)] = lin[pl.ds(shift + i * step, step)].astype(BF)
                    return 0

                lax.fori_loop(0, blocks, body, 0)
                if tail:
                    source = shift + blocks * step
                    target = place + blocks * step
                    stage[target : target + tail] = lin[source : source + tail].astype(BF)
                copy = pltpu.make_async_copy(
                    stage.at[pl.ds(place, end - first)],
                    out_ref.at[chunk, pl.ds(base, end - first)],
                    out_sem.at[len(stores)],
                )
                copy.start()
                stores.append(copy)
                place += end - first
                done = end
            if not whole:
                break
            done = stop if slot + 1 == len(pieces) else min(done, stop)
            slot += 1
        if not last:
            lin[0:TILE] = lin[number : number + TILE]
    for copy in stores:
        copy.wait()


def pack_grads(grads, plan, indices, step=128):
    spots = linear_layout()
    tallest = max(spots[i][1] for i in indices)
    begin = spots[indices[0]][0]
    total = spots[indices[-1]][0] + spots[indices[-1]][1] - begin
    count = len(plan.segments(begin, total))
    anywhere = pl.BlockSpec(memory_space=pl.ANY)
    return pl.pallas_call(
        functools.partial(pack_kernel, plan=plan, indices=indices, step=step),
        in_specs=[anywhere] * len(indices),
        out_specs=anywhere,
        out_shape=jax.ShapeDtypeStruct((plan.devices, plan.chunk, LANE), BF),
        scratch_shapes=[
            pltpu.VMEM((tallest + 2 * TILE, LANE), F32),
            pltpu.VMEM((total + 2 * TILE * (count + len(indices)), LANE), BF),
            pltpu.SemaphoreType.DMA((len(indices),)),
            pltpu.SemaphoreType.DMA((count + len(indices),)),
        ]
        + [pltpu.VMEM(g.shape, g.dtype) for g in grads],
        compiler_params=pltpu.CompilerParams(vmem_limit_bytes=VMEM_LIMIT),
        name="pack",
    )(*grads)


MESH = pl.DeviceIdType.MESH
ROWS = 208


def place_of():
    dp, fs = lax.axis_index("dp"), lax.axis_index("fsdp")
    return dp, fs, dp // 2, dp % 2, fs // 2, fs % 2


def meet_all(me, devices, inner):
    barrier = pltpu.get_barrier_semaphore()

    def greet(i, _):
        other = (me + i) % devices
        pl.semaphore_signal(
            barrier, inc=1, device_id=(other // inner, other % inner), device_id_type=MESH
        )
        return 0

    lax.fori_loop(1, devices, greet, 0)
    pl.semaphore_wait(barrier, devices - 1)


class Trade:
    def __init__(self, source, target, own_sem, send_sem, recv_sem, plan, inner, senders, receivers):
        self.source, self.target, self.own_sem = source, target, own_sem
        self.send_sem, self.recv_sem = send_sem, recv_sem
        self.devices, self.inner = plan.devices, inner
        self.senders, self.receivers = senders, receivers
        self.me = lax.axis_index("dp") * inner + lax.axis_index("fsdp")
        self.many = len(source.shape) == 3

    def piece(self, target):
        return self.source.at[target] if self.many else self.source

    def copy(self, source, target):
        return pltpu.make_async_remote_copy(
            src_ref=self.piece(target),
            dst_ref=self.target.at[source],
            send_sem=self.send_sem.at[target],
            recv_sem=self.recv_sem.at[source],
            device_id=(target // self.inner, target % self.inner),
            device_id_type=MESH,
        )

    def own(self):
        return pltpu.make_async_copy(
            self.piece(self.me), self.target.at[self.me], self.own_sem
        )

    def each(self, act):
        def body(i, _):
            act((self.me + i) % self.devices)
            return 0

        lax.fori_loop(1, self.devices, body, 0)

    def both(self):
        return (self.me < self.senders) & (self.me < self.receivers)

    def start(self):
        pl.when(self.both())(lambda: self.own().start())

        def act(other):
            ok = (self.me < self.senders) & (other < self.receivers)
            pl.when(ok)(lambda: self.copy(self.me, other).start())

        self.each(act)

    def wait(self):
        pl.when(self.both())(lambda: self.own().wait())

        def landed(other):
            ok = (other < self.senders) & (self.me < self.receivers)
            pl.when(ok)(lambda: self.copy(other, other).wait_recv())

        def gone(other):
            ok = (self.me < self.senders) & (other < self.receivers)
            pl.when(ok)(lambda: self.copy(self.me, other).wait_send())

        self.each(landed)
        self.each(gone)


def when_all(conditions):
    total = None
    for condition in conditions:
        if condition is not None:
            total = condition if total is None else total & condition
    return total


def guarded(condition, body):
    if condition is None:
        body()
    else:
        pl.when(condition)(body)


def start_kernel(
    cond_ref, slot_ref, all_ref, own_ref, own_sem, lend_send, lend_recv, send_sem, recv_sem,
    *, plan, inner
):
    dp, fs, _, _, _, _ = place_of()
    me = dp * inner + fs
    lead, lent, kept = plan.lead, plan.lent, plan.kept
    meet_all(me, plan.devices, inner)

    def own_copy():
        start = pl.multiple_of(jnp.where(me == lead, plan.base, 0), TILE)
        return pltpu.make_async_copy(
            slot_ref.at[pl.ds(start, plan.chunk)], own_ref, own_sem.at[0]
        )

    def lend(slot, target, part):
        return pltpu.make_async_remote_copy(
            src_ref=slot_ref.at[pl.ds(kept, lent)],
            dst_ref=own_ref.at[pl.ds(pl.multiple_of(part * lent, TILE), lent)],
            send_sem=lend_send.at[slot],
            recv_sem=lend_recv.at[part],
            device_id=(target // inner, target % inner),
            device_id_type=MESH,
        )

    lender = jnp.maximum(me - lead - 1, 0)

    @pl.when(me > lead)
    def _():
        lend(0, lender // 2, lender % 2).start()

    @pl.when(me == lead)
    def _():
        lend(0, lead - 1, 0).start()
        lend(1, lead - 1, 1).start()

    @pl.when(me >= lead)
    def _():
        own_copy().start()

    trade = Trade(
        cond_ref, all_ref, own_sem.at[1], send_sem, recv_sem, plan, inner, plan.devices, plan.devices
    )
    trade.start()
    trade.wait()

    @pl.when(me >= lead)
    def _():
        own_copy().wait()
        lend(0, lead - 1, 0).wait_send()

    @pl.when(me == lead)
    def _():
        lend(1, lead - 1, 1).wait_send()

    @pl.when(me < lead)
    def _():
        lend(0, lead - 1, 0).wait_recv()
        lend(0, lead - 1, 1).wait_recv()


def start_chunks(condition, slot, plan, inner, collective):
    anywhere = pl.BlockSpec(memory_space=pl.ANY)
    dma = pltpu.SemaphoreType.DMA
    return pl.pallas_call(
        functools.partial(start_kernel, plan=plan, inner=inner),
        in_specs=[anywhere] * 2,
        out_specs=[anywhere] * 2,
        out_shape=[
            jax.ShapeDtypeStruct((plan.devices, *condition.shape), condition.dtype),
            jax.ShapeDtypeStruct((plan.chunk, LANE), BF),
        ],
        scratch_shapes=[
            dma((2,)),
            dma((2,)),
            dma((2,)),
            dma((plan.devices,)),
            dma((plan.devices,)),
        ],
        compiler_params=pltpu.CompilerParams(collective_id=collective, has_side_effects=True),
        name="start_chunks",
    )(condition, slot)


def gather_kernel(
    chunk_ref, slab_ref, out_ref, parts_ref, own_sem, slab_send, slab_recv, send_sem, recv_sem,
    *, plan, inner
):
    dp, fs, y, x, z, c = place_of()
    me = dp * inner + fs
    lent = plan.lent
    levels = inner // 2
    meet_all(me, plan.devices, inner)
    own = pltpu.make_async_copy(chunk_ref, out_ref.at[me], own_sem.at[0])
    own.start()
    trade = Trade(
        slab_ref, parts_ref, own_sem.at[1], slab_send, slab_recv, plan, inner, plan.lead + 1, plan.devices
    )

    across = {
        "up": (dp, fs + 2),
        "down": (dp, fs - 2),
        "x": (dp + 1 - 2 * x, fs),
        "y": (dp + 2 - 4 * y, fs),
        "twin": (dp, fs + 1 - 2 * c),
    }
    kinds = tuple(across)
    pending = []

    def copy(kind, yy, xx, zz, part, cc=None, mine=False):
        core = c if cc is None else cc
        column = yy * 2 + xx
        index = column * inner + zz * 2 + core
        rows = pl.ds(part * lent, lent)
        return pltpu.make_async_remote_copy(
            src_ref=chunk_ref.at[rows] if mine else out_ref.at[index, rows],
            dst_ref=out_ref.at[index, rows],
            send_sem=send_sem.at[kinds.index(kind), column * levels + zz, part],
            recv_sem=recv_sem.at[index, part],
            device_id=across[kind],
            device_id_type=MESH,
        )

    def send(condition, kind, yy, xx, zz, part, mine=False):
        guarded(condition, lambda: copy(kind, yy, xx, zz, part, mine=mine).start())
        pending.append((condition, kind, yy, xx, zz, part))

    def arrive(condition, yy, xx, zz, part):
        guarded(condition, lambda: copy("x", yy, xx, zz, part).wait_recv())

    def spread(distance):
        for sign in (1, -1) if distance else (0,):
            zz = z + sign * distance
            inside = when_all(
                [zz < levels if sign > 0 else None, zz >= 0 if sign < 0 else None]
            )
            yield zz, sign, inside

    for turn in range(levels + 2):
        if turn < levels:
            for zz, sign, inside in spread(turn):
                for part in range(2):
                    if turn:
                        arrive(inside, y, x, zz, part)
                    if sign <= 0:
                        send(when_all([inside, z < levels - 1]), "up", y, x, zz, part, turn == 0)
                    if sign >= 0:
                        send(when_all([inside, z > 0]), "down", y, x, zz, part, turn == 0)
                    for kind in ("x", "y") if part else ("y", "x"):
                        send(inside, kind, y, x, zz, part, turn == 0)
                    send(inside, "twin", y, x, zz, part, turn == 0)
            if turn == 0:
                trade.start()
        if 1 <= turn <= levels:
            for zz, sign, inside in spread(turn - 1):
                arrive(inside, y, 1 - x, zz, 0)
                send(inside, "y", y, 1 - x, zz, 0)
                send(inside, "twin", y, 1 - x, zz, 0)
                arrive(inside, 1 - y, x, zz, 1)
                send(inside, "x", 1 - y, x, zz, 1)
                send(inside, "twin", 1 - y, x, zz, 1)
                arrive(inside, 1 - y, x, zz, 0)
                send(inside, "twin", 1 - y, x, zz, 0)
                arrive(inside, y, 1 - x, zz, 1)
                send(inside, "twin", y, 1 - x, zz, 1)
        if turn >= 2:
            for zz, sign, inside in spread(turn - 2):
                for part in range(2):
                    arrive(inside, 1 - y, 1 - x, zz, part)
                    send(inside, "twin", 1 - y, 1 - x, zz, part)

    def twin_arrivals(i, _):
        column, zz = i // levels, i % levels
        for part in range(2):
            copy("twin", column // 2, column % 2, zz, part, 1 - c).wait_recv()
        return 0

    lax.fori_loop(0, 4 * levels, twin_arrivals, 0)
    for condition, kind, yy, xx, zz, part in pending:
        guarded(condition, lambda: copy(kind, yy, xx, zz, part).wait_send())
    trade.wait()
    own.wait()


def gather_chunks(chunk, slabs, plan, inner, collective):
    anywhere = pl.BlockSpec(memory_space=pl.ANY)
    dma = pltpu.SemaphoreType.DMA
    return pl.pallas_call(
        functools.partial(gather_kernel, plan=plan, inner=inner),
        in_specs=[anywhere] * 2,
        out_specs=[anywhere] * 2,
        out_shape=[
            jax.ShapeDtypeStruct((plan.devices, plan.chunk, LANE), BF),
            jax.ShapeDtypeStruct((plan.lead + 1, *slabs.shape[1:]), slabs.dtype),
        ],
        scratch_shapes=[
            dma((2,)),
            dma((plan.devices,)),
            dma((plan.devices,)),
            dma((5, plan.devices // 2, 2)),
            dma((plan.devices, 2)),
        ],
        compiler_params=pltpu.CompilerParams(collective_id=collective, has_side_effects=True),
        name="gather_chunks",
    )(chunk, slabs)


def scatter_kernel(
    g_ref,
    rows_ref,
    out_ref,
    all_ref,
    acc,
    twin,
    wide_y,
    wide_x,
    slim_x,
    slim_y,
    line,
    load_sem,
    twin_send,
    twin_recv,
    wide_send,
    wide_recv,
    slim_send,
    slim_recv,
    line_send,
    line_recv,
    own_sem,
    back_send,
    back_recv,
    row_send,
    row_recv,
    *,
    plan,
    inner,
):
    dp, fs, y, x, z, c = place_of()
    me = dp * inner + fs
    lead, lent, kept = plan.lead, plan.lent, plan.kept
    levels = inner // 2
    x_mate = (dp + 1 - 2 * x, fs)
    y_mate = (dp + 2 - 4 * y, fs)
    meet_all(me, plan.devices, inner)

    def remote(source, target, send, receive, device):
        return pltpu.make_async_remote_copy(
            src_ref=source,
            dst_ref=target,
            send_sem=send,
            recv_sem=receive,
            device_id=device,
            device_id_type=MESH,
        )

    def slot_of(yy, xx, zz):
        return (yy * 2 + xx) * levels + zz

    def load(yy, xx, zz):
        slot = slot_of(yy, xx, zz)
        return pltpu.make_async_copy(
            g_ref.at[(yy * 2 + xx) * inner + zz * 2 + c], acc.at[slot], load_sem.at[slot]
        )

    def to_twin(yy, xx, zz):
        slot = slot_of(yy, xx, zz)
        return remote(
            g_ref.at[(yy * 2 + xx) * inner + zz * 2 + 1 - c],
            twin.at[slot],
            twin_send.at[slot],
            twin_recv.at[slot],
            (dp, fs + 1 - 2 * c),
        )

    def piece(slot, part):
        return acc.at[slot, pl.ds(part * lent, lent)]

    def wide(part, other, zz, yy=0, xx=0):
        buffer, device = (wide_x, x_mate) if part else (wide_y, y_mate)
        index = other * levels + zz
        return remote(
            piece(slot_of(yy, xx, zz), part),
            buffer.at[index],
            wide_send.at[part, index],
            wide_recv.at[part, index],
            device,
        )

    def slim(part, zz, yy=0, xx=0):
        buffer, device = (slim_y, y_mate) if part else (slim_x, x_mate)
        return remote(
            piece(slot_of(yy, xx, zz), part),
            buffer.at[zz],
            slim_send.at[part, zz],
            slim_recv.at[part, zz],
            device,
        )

    def along(upward, zz, part):
        way = 0 if upward else 1
        return remote(
            piece(slot_of(y, x, zz), part),
            line.at[way, zz, part],
            line_send.at[way, zz, part],
            line_recv.at[way, zz, part],
            (dp, fs + 2 if upward else fs - 2),
        )

    def add(slot, first, count, source):
        def body(i, _):
            at = pl.multiple_of(i * ROWS, TILE)
            to = pl.ds(pl.multiple_of(first + i * ROWS, TILE), ROWS)
            acc[slot, to] = acc[slot, to] + source[pl.ds(at, ROWS)]
            return 0

        lax.fori_loop(0, count // ROWS, body, 0)

    def add_part(slot, part, source):
        add(slot, part * lent, lent, source)

    def level(k):
        return jnp.where(z < levels // 2, z + levels - 1 - k, z + 1 + k) % levels

    columns = ((1 - y, 1 - x), (1 - y, x), (y, 1 - x), (y, x))

    for k in range(levels):
        for yy, xx in columns:
            to_twin(yy, xx, level(k)).start()
            load(yy, xx, level(k)).start()

    trade = Trade(
        rows_ref, all_ref, own_sem.at[1], row_send, row_recv, plan, inner, plan.devices, lead + 1
    )

    def settle(yy, xx, zz):
        slot = slot_of(yy, xx, zz)
        load(yy, xx, zz).wait()
        to_twin(yy, xx, zz).wait_recv()
        add(slot, 0, plan.chunk, twin.at[slot])

    def diagonal(k):
        zz = level(k)
        settle(1 - y, 1 - x, zz)
        wide(0, 1 - x, zz, 1 - y, 1 - x).start()
        wide(1, 1 - y, zz, 1 - y, 1 - x).start()

    def sides(k):
        zz = level(k)
        settle(1 - y, x, zz)
        wide(0, x, zz, 1 - y, x).start()
        settle(y, 1 - x, zz)
        wide(1, y, zz, y, 1 - x).start()

    def middle(k):
        zz = level(k)
        wide(0, 1 - x, zz).wait_recv()
        add_part(slot_of(y, 1 - x, zz), 0, wide_y.at[(1 - x) * levels + zz])
        slim(0, zz, y, 1 - x).start()
        wide(1, 1 - y, zz).wait_recv()
        add_part(slot_of(1 - y, x, zz), 1, wide_x.at[(1 - y) * levels + zz])
        slim(1, zz, 1 - y, x).start()

    def home(k):
        zz = level(k)
        slot = slot_of(y, x, zz)
        settle(y, x, zz)
        wide(0, x, zz).wait_recv()
        add_part(slot, 0, wide_y.at[x * levels + zz])
        wide(1, y, zz).wait_recv()
        add_part(slot, 1, wide_x.at[y * levels + zz])
        slim(0, zz).wait_recv()
        add_part(slot, 0, slim_x.at[zz])
        slim(1, zz).wait_recv()
        add_part(slot, 1, slim_y.at[zz])

    def take(upward, zz, part):
        along(upward, zz, part).wait_recv()
        add_part(slot_of(y, x, zz), part, line.at[0 if upward else 1, zz, part])

    edge = (z == 0) | (z == levels - 1)
    sent = []

    def pass_on(k, allowed):
        zz = level(k)
        for upward in (True, False):
            inside = allowed & (zz > z if upward else zz < z)
            more = z > 0 if upward else z < levels - 1

            @pl.when(inside)
            def _(upward=upward, more=more):
                for part in range(2):

                    @pl.when(more)
                    def _(part=part):
                        take(upward, zz, part)

                    along(upward, zz, part).start()

            sent.append((inside, upward, zz))

    def once(k):
        diagonal(k)
        sides(k)

    once(0)
    once(1)
    middle(0)
    once(2)
    middle(1)
    home(0)
    pass_on(0, edge)
    once(3)
    middle(2)
    middle(3)
    trade.start()
    home(1)
    pass_on(1, z >= 0)
    home(2)
    pass_on(2, z >= 0)
    pass_on(0, jnp.logical_not(edge))
    home(3)
    for part in range(2):

        @pl.when(z > 0)
        def _(part=part):
            take(True, z, part)

        @pl.when(z < levels - 1)
        def _(part=part):
            take(False, z, part)

    mine = slot_of(y, x, z)

    def back(slot, part, owner):
        return remote(
            piece(mine, part),
            out_ref.at[pl.ds(kept, lent)],
            back_send.at[slot],
            back_recv,
            (owner // inner, owner % inner),
        )

    @pl.when(me < lead - 1)
    def _():
        back(0, 0, lead + 1 + 2 * me).start()
        back(1, 1, lead + 2 + 2 * me).start()

    @pl.when(me == lead - 1)
    def _():
        back(0, 0, me + 1).start()

    @pl.when(me == lead)
    def _():
        count = kept - plan.base
        copy = pltpu.make_async_copy(
            acc.at[mine, pl.ds(0, count)], out_ref.at[pl.ds(plan.base, count)], own_sem.at[0]
        )
        copy.start()
        copy.wait()

    @pl.when(me > lead)
    def _():
        copy = pltpu.make_async_copy(
            acc.at[mine, pl.ds(0, kept)], out_ref.at[pl.ds(0, kept)], own_sem.at[0]
        )
        copy.start()
        copy.wait()

    @pl.when(me >= lead)
    def _():
        back(0, 0, 0).wait_recv()

    for inside, upward, zz in sent:

        @pl.when(inside)
        def _(upward=upward, zz=zz):
            for part in range(2):
                along(upward, zz, part).wait_send()

    def finish(k, _):
        zz = level(k)
        for yy, xx in columns:
            to_twin(yy, xx, zz).wait_send()
        wide(0, 1 - x, zz).wait_send()
        wide(0, x, zz).wait_send()
        wide(1, 1 - y, zz).wait_send()
        wide(1, y, zz).wait_send()
        slim(0, zz).wait_send()
        slim(1, zz).wait_send()
        return 0

    lax.fori_loop(0, levels, finish, 0)

    @pl.when(me < lead)
    def _():
        back(0, 0, 0).wait_send()

    @pl.when(me < lead - 1)
    def _():
        back(1, 1, 0).wait_send()

    trade.wait()


def scatter_chunks(grads, rows, plan, inner, collective):
    anywhere = pl.BlockSpec(memory_space=pl.ANY)
    dma = pltpu.SemaphoreType.DMA
    half, levels = plan.devices // 2, inner // 2
    part = (plan.lent, LANE)
    return pl.pallas_call(
        functools.partial(scatter_kernel, plan=plan, inner=inner),
        in_specs=[anywhere] * 2,
        out_specs=[anywhere] * 2,
        out_shape=[
            jax.ShapeDtypeStruct((plan.padded, LANE), BF),
            jax.ShapeDtypeStruct((plan.devices, *rows.shape), rows.dtype),
        ],
        scratch_shapes=[
            pltpu.VMEM((half, plan.chunk, LANE), BF),
            pltpu.VMEM((half, plan.chunk, LANE), BF),
            pltpu.VMEM((2 * levels, *part), BF),
            pltpu.VMEM((2 * levels, *part), BF),
            pltpu.VMEM((levels, *part), BF),
            pltpu.VMEM((levels, *part), BF),
            pltpu.VMEM((2, levels, 2, *part), BF),
            dma((half,)),
            dma((half,)),
            dma((half,)),
            dma((2, 2 * levels)),
            dma((2, 2 * levels)),
            dma((2, levels)),
            dma((2, levels)),
            dma((2, levels, 2)),
            dma((2, levels, 2)),
            dma((2,)),
            dma((2,)),
            dma,
            dma((plan.devices,)),
            dma((plan.devices,)),
        ],
        compiler_params=pltpu.CompilerParams(
            collective_id=collective, has_side_effects=True, vmem_limit_bytes=VMEM_LIMIT
        ),
        name="scatter_chunks",
    )(grads, rows)


def exchange_kernel(in_ref, out_ref, own_sem, send_sem, recv_sem, *, plan, inner):
    me = lax.axis_index("dp") * inner + lax.axis_index("fsdp")
    meet_all(me, plan.devices, inner)
    trade = Trade(
        in_ref, out_ref, own_sem, send_sem, recv_sem, plan, inner, plan.devices, plan.devices
    )
    trade.start()
    trade.wait()


def exchange(value, plan, inner, collective, name):
    anywhere = pl.BlockSpec(memory_space=pl.ANY)
    dma = pltpu.SemaphoreType.DMA
    return pl.pallas_call(
        functools.partial(exchange_kernel, plan=plan, inner=inner),
        in_specs=[anywhere],
        out_specs=anywhere,
        out_shape=jax.ShapeDtypeStruct((plan.devices, *value.shape), value.dtype),
        scratch_shapes=[dma, dma((plan.devices,)), dma((plan.devices,))],
        compiler_params=pltpu.CompilerParams(collective_id=collective, has_side_effects=True),
        name=name,
    )(value)


HALF = 27
TALL = 72
SLAB = 112
CONDITION_ROWS = 832


def ada_spots(me, plan):
    lines = plan.share // HALF
    odd = me % 2
    limit = CONDITION_ROWS - TALL
    return [
        (odd, jnp.minimum((lines * me + odd) // 2, limit)),
        (1 - odd, jnp.minimum((lines * me - odd) // 2, limit)),
    ]


def ada_kernel(lin_ref, cond_ref, out_ref, *, plan, inner):
    me = lax.axis_index("dp") * inner + lax.axis_index("fsdp")
    for half, (shift, top) in enumerate(ada_spots(me, plan)):
        condition = cond_ref[pl.ds(top, TALL)].astype(BF)

        def body(c, _, half=half, shift=shift, condition=condition):
            rows = lin_ref[pl.ds(HALF * shift + c, TALL, stride=2 * HALF)].astype(BF)
            part = tn(condition, rows)
            count = plan.devices
            for clip in range(2):
                out_ref[pl.ds((2 * clip + half) * HALF + c, count, stride=SLAB)] = part[
                    clip * count : (clip + 1) * count
                ]
            return 0

        lax.fori_loop(0, HALF, body, 0, unroll=True)


def ada_partial(lin, cond, plan, inner):
    return pl.pallas_call(
        functools.partial(ada_kernel, plan=plan, inner=inner),
        out_shape=jax.ShapeDtypeStruct((plan.devices * SLAB, LANE), F32),
        compiler_params=pltpu.CompilerParams(vmem_limit_bytes=VMEM_LIMIT),
        name="ada_partial",
    )(lin, cond)


def own_grad_kernel(cond_ref, dmod_ref, rest_ref, g_ref, sums_ref, lin, *, plan, inner):
    me = lax.axis_index("dp") * inner + lax.axis_index("fsdp")
    count = plan.devices
    border = jnp.clip(plan.first_row - plan.share * me, 0, plan.share)
    for half, (shift, top) in enumerate(ada_spots(me, plan)):
        condition = cond_ref[pl.ds(top, TALL)].astype(BF)

        def body(c, _, half=half, shift=shift, condition=condition):
            grads = jnp.concatenate(
                [
                    dmod_ref[pl.ds((2 * clip + half) * HALF + c, count, stride=SLAB)]
                    for clip in range(2)
                ],
                axis=0,
            ).astype(BF)
            lin[pl.ds(HALF * shift + c, TALL, stride=2 * HALF)] = nn(condition, grads)
            return 0

        @pl.when(border > 0)
        def _(body=body):
            lax.fori_loop(0, HALF, body, 0, unroll=True)

    rows = 64

    def merge(i, total):
        at = pl.multiple_of(i * rows, rows)
        row = lax.broadcasted_iota(jnp.int32, (rows, LANE), 0) + at
        rest = jnp.where(row < plan.share, rest_ref[pl.ds(at, rows)].astype(F32), 0.0)
        value = jnp.where(row < border, lin[pl.ds(at, rows)], rest)
        g_ref[pl.ds(at, rows)] = value
        square = value * value
        return total + sum(square[k : k + 8] for k in range(0, rows, 8))

    sums_ref[...] = lax.fori_loop(0, plan.padded // rows, merge, jnp.zeros((8, LANE), F32))


def own_grad(cond, dmod, rest, plan, inner):
    return pl.pallas_call(
        functools.partial(own_grad_kernel, plan=plan, inner=inner),
        out_shape=[
            jax.ShapeDtypeStruct((plan.padded, LANE), F32),
            jax.ShapeDtypeStruct((8, LANE), F32),
        ],
        scratch_shapes=[pltpu.VMEM((2 * HALF * TALL, LANE), F32)],
        compiler_params=pltpu.CompilerParams(vmem_limit_bytes=VMEM_LIMIT),
        name="own_grad",
    )(cond, dmod, rest)


def fits(devices, inner, share):
    return inner == 8 and devices == 32 and share % (LANE * HALF) == 0


def local_fast(
    latents, captions, lengths, timesteps, cotangent, master, first_moment, second_moment
):
    clips, frames, width = latents.shape
    share = master.shape[0]
    inner = lax.axis_size("fsdp")
    devices = inner * lax.axis_size("dp")
    plan = Plan(devices, share // LANE)
    indices = tuple(range(2, 13))

    rows = master.reshape(plan.share, LANE)
    lin = jnp.pad(rows, ((0, 2 * HALF * TALL - plan.share), (0, 0)))
    steps, chunk = start_chunks(
        jnp.broadcast_to(
            jnp.pad(timesteps.astype(F32), (0, 8 - clips))[:, None], (8, LANE)
        ),
        lin[: plan.padded].astype(BF),
        plan,
        inner,
        1,
    )
    steps = steps[:, :clips, 0].T.reshape(devices * clips)
    columns = jax.nn.silu(embed(steps)).astype(BF).astype(F32).T
    columns = jnp.concatenate(
        [
            columns,
            jnp.ones((1, clips * devices), F32),
            jnp.zeros((CONDITION_ROWS - width - 1, clips * devices), F32),
        ],
        axis=0,
    )
    slabs = ada_partial(lin, columns, plan, inner).reshape(devices, SLAB, LANE)
    gathered, parts = gather_chunks(chunk, slabs, plan, inner, 2)
    mod = jnp.sum(parts, axis=0)[: 54 * clips].reshape(clips, 9, width)
    weights = unpack_weights(gathered, plan, indices)
    output, input_grad, grad_mod, gradients = block_pass(
        latents, captions, lengths, cotangent, mod, weights
    )
    grad_rows = jnp.pad(
        grad_mod.reshape(54 * clips, LANE), ((0, SLAB - 54 * clips), (0, 0))
    )
    chunks = pack_grads(gradients, plan, indices)
    rest, dmod = scatter_chunks(chunks, grad_rows, plan, inner, 3)
    grads, squares = own_grad(
        columns, dmod.reshape(devices * SLAB, LANE).astype(F32), rest, plan, inner
    )
    squares = exchange(squares, plan, inner, 4, "squares")
    return (
        output,
        input_grad,
        grads[: plan.share].reshape(share),
        jnp.sum(squares),
    )


def local_any(
    latents, captions, lengths, timesteps, cotangent, master, first_moment, second_moment
):
    clips, frames, width = latents.shape
    share = master.shape[0]
    devices = lax.axis_size("dp") * lax.axis_size("fsdp")
    gathered = lax.all_gather(
        master.astype(BF).reshape(1, share), ("dp", "fsdp"), axis=0, tiled=True
    ).reshape(-1)
    weights = unpack(gathered)
    condition = jax.nn.silu(embed(timesteps)).astype(BF)
    mod = jnp.dot(condition, weights[0], preferred_element_type=F32) + weights[1].astype(F32)
    block_weights = [w.astype(F32).reshape(1, -1) if w.ndim == 1 else w for w in weights[2:]]
    output, input_grad, grad_mod, gradients = block_pass(
        latents, captions, lengths, cotangent, mod.reshape(clips, 9, width), block_weights
    )
    grad_mod = grad_mod.reshape(clips, 9 * width)
    grad_ada = jnp.dot(condition.T, grad_mod, preferred_element_type=F32)
    grad_list = [grad_ada, jnp.sum(grad_mod.astype(F32), axis=0)] + gradients
    flat = jnp.concatenate([piece.astype(F32).reshape(-1) for piece in grad_list])
    grad = lax.psum_scatter(
        flat.reshape(devices, share), ("dp", "fsdp"), scatter_dimension=0, tiled=True
    ).reshape(share)
    return output, input_grad, grad, lax.psum(jnp.sum(grad * grad), ("dp", "fsdp"))


def local(
    latents,
    captions,
    caption_lengths,
    timesteps,
    cotangent,
    master_weights,
    first_moment,
    second_moment,
):
    inner = lax.axis_size("fsdp")
    devices = inner * lax.axis_size("dp")
    run = local_fast if fits(devices, inner, master_weights.shape[0]) else local_any
    output, input_grad, grad_shard, squares = run(
        latents,
        captions,
        caption_lengths,
        timesteps,
        cotangent,
        master_weights,
        first_moment,
        second_moment,
    )
    grad_norm = jnp.sqrt(squares)
    clipped = grad_shard * (CLIP / jnp.maximum(grad_norm, CLIP))
    new_first = BETA_ONE * first_moment + (1.0 - BETA_ONE) * clipped
    new_second = BETA_TWO * second_moment + (1.0 - BETA_TWO) * clipped * clipped
    step_first = new_first / (1.0 - BETA_ONE**STEP)
    step_second = new_second / (1.0 - BETA_TWO**STEP)
    new_master = master_weights - RATE * (
        step_first / (jnp.sqrt(step_second) + ADAM_EPS) + DECAY * master_weights
    )
    return (output, input_grad, grad_norm, new_master, new_first, new_second)


def solution(mesh):
    placed = (
        P(("dp", "fsdp"), None, None),
        P(("dp", "fsdp"), None, None),
        P(("dp", "fsdp")),
        P(("dp", "fsdp")),
        P(("dp", "fsdp"), None, None),
        P(("dp", "fsdp")),
        P(("dp", "fsdp")),
        P(("dp", "fsdp")),
    )
    return jax.shard_map(
        local,
        mesh=mesh,
        in_specs=placed,
        out_specs=(
            P(("dp", "fsdp"), None, None),
            P(("dp", "fsdp"), None, None),
            P(),
            P(("dp", "fsdp")),
            P(("dp", "fsdp")),
            P(("dp", "fsdp")),
        ),
        check_vma=False,
    )
```

```python
import functools
import math

import jax
import jax.numpy as jnp
from jax import lax
from jax.experimental import pallas as pl
from jax.experimental.pallas import tpu as pltpu
from jax.sharding import PartitionSpec as P

D = 768
HEADS = 12
HD = 64
FF = 3072
CTX = 1024
STEP = 5


NORM_EPS = 1e-06
BETA_ONE = 0.9
BETA_TWO = 0.999
ADAM_EPS = 1e-08
RATE = 0.03
DECAY = 0.01
CLIP = 500.0


def layout_sizes():
    return [
        (D, 9 * D),
        (9 * D,),
        (D, 3 * D),
        (D, D),
        (D,),
        (D, D),
        (CTX, 2 * D),
        (D, D),
        (D,),
        (D, FF),
        (FF,),
        (FF, D),
        (D,),
    ]


def unpack(flat_vector):
    pieces = []
    offset = 0
    for layout_shape in layout_sizes():
        number = math.prod(layout_shape)
        pieces.append(flat_vector[offset : offset + number].reshape(layout_shape))
        offset += number
    return pieces


def embed(steps_in):
    half_width = D // 2
    frequency = jnp.exp(-math.log(10000.0) * jnp.arange(half_width, dtype=jnp.float32) / half_width)
    angles = steps_in.astype(jnp.float32)[:, None] * frequency[None, :]
    return jnp.concatenate([jnp.cos(angles), jnp.sin(angles)], axis=1)


def normalize(hidden):
    centred = hidden - jnp.mean(hidden, axis=-1, keepdims=True)
    inverse = lax.rsqrt(jnp.mean(centred * centred, axis=-1, keepdims=True) + NORM_EPS)
    return (centred * inverse, inverse)


def norm_back(normed, inverse, grad_normed):
    return inverse * (
        grad_normed
        - jnp.mean(grad_normed, axis=-1, keepdims=True)
        - normed * jnp.mean(grad_normed * normed, axis=-1, keepdims=True)
    )


F32 = jnp.float32
BF = jnp.bfloat16
VMEM_LIMIT = 60 << 20


def nn(left_side, right_side):
    return lax.dot_general(
        left_side, right_side, (((1,), (0,)), ((), ())), preferred_element_type=F32
    )


def nt(left_side, right_side):
    return lax.dot_general(
        left_side, right_side, (((1,), (1,)), ((), ())), preferred_element_type=F32
    )


def tn(left_side, right_side):
    return lax.dot_general(
        left_side, right_side, (((0,), (0,)), ((), ())), preferred_element_type=F32
    )


def call(body, grid, in_specs, out_specs, out_shape, name, scratch=()):
    return pl.pallas_call(
        body,
        grid=grid,
        in_specs=in_specs,
        out_specs=out_specs,
        out_shape=out_shape,
        scratch_shapes=list(scratch),
        compiler_params=pltpu.CompilerParams(vmem_limit_bytes=VMEM_LIMIT),
        name=name,
    )


def struct(shape, dtype):
    return jax.ShapeDtypeStruct(shape, dtype)


def rows_spec(rows, width):
    return pl.BlockSpec((1, rows, width), lambda i, j: (i, j, 0))


def clip_spec(count, width):
    return pl.BlockSpec((1, count, width), lambda i, j: (i, 0, 0))


def whole_spec(shape):
    return pl.BlockSpec(shape, lambda *_: (0,) * len(shape))


def row_block(frames):
    for parts in (2, 3, 4, 6):
        if frames % (16 * parts) == 0:
            return frames // parts
    return frames


def add_to(ref, first, value):
    @pl.when(first)
    def _():
        ref[...] = value

    @pl.when(jnp.logical_not(first))
    def _():
        ref[...] += value


def span_of(rows):
    start = (pl.program_id(0) * pl.num_programs(1) + pl.program_id(1)) * rows
    return pl.ds(pl.multiple_of(start, rows), rows)


def clear_at(first, *refs):
    @pl.when(first)
    def _():
        for ref in refs:
            ref[...] = jnp.zeros_like(ref)


def column_sum(value):
    return jnp.sum(value, axis=0, keepdims=True)


def qkv_kernel(x_ref, mod_ref, w_ref, out_ref):
    normed, _ = normalize(x_ref[0].astype(F32))
    first_in = (normed * (1.0 + mod_ref[0, 1:2]) + mod_ref[0, 0:1]).astype(BF)
    out_ref[0] = nn(first_in, w_ref[...]).astype(BF)


def qkv_forward(latents, mod, weight):
    clips, frames, width = latents.shape
    rows = row_block(frames)
    wide = weight.shape[1]
    return call(
        qkv_kernel,
        (clips, frames // rows),
        [rows_spec(rows, width), clip_spec(9, width), whole_spec(weight.shape)],
        rows_spec(rows, wide),
        struct((clips, frames, wide), BF),
        "qkv_forward",
    )(latents, mod, weight)


def head_lanes():
    lane = lax.broadcasted_iota(jnp.int32, (1, 2 * HD), 1)
    return lane, lane < HD


def usable_bias(length, count):
    row = lax.broadcasted_iota(jnp.int32, (count, 2 * HD), 0)
    return jnp.where(row < length, 0.0, -1e30).astype(BF)


def attend_kernel(*refs, masked):
    if masked:
        len_ref, q_ref, k_ref, v_ref, o_ref, l_ref = refs
    else:
        q_ref, k_ref, v_ref, o_ref, l_ref = refs
    lane, low = head_lanes()
    for pair in range(l_ref.shape[1]):
        columns = slice(pair * 2 * HD, (pair + 1) * 2 * HD)
        length = len_ref[pl.program_id(0)] if masked else None
        attend_pair(
            lane,
            low,
            length,
            q_ref[0, :, columns],
            k_ref[0, :, columns],
            v_ref[0, :, columns],
            o_ref.at[0, :, columns],
            l_ref.at[0, pair],
        )


def attend_pair(lane, low, length, q, k, v, o_ref, l_ref):
    masked = length is not None
    scaled = q * jnp.asarray(HD**-0.5, BF)
    one = jnp.ones((), BF)
    zero = jnp.zeros((), BF)
    values = [jnp.where(low, v, one), jnp.where(low, one, v)]
    if masked:
        bias = usable_bias(length, k.shape[0])
        tag = jnp.where(lane % HD == 0, one, zero)
        queries = [jnp.where(low, scaled, tag), jnp.where(low, tag, scaled)]
        keys = [jnp.where(low, k, bias), jnp.where(low, bias, k)]
    else:
        queries = [jnp.where(low, scaled, zero), jnp.where(low, zero, scaled)]
        keys = [k, k]
    tops, mixes = [], []
    for head in range(2):
        scores = nt(queries[head], keys[head])
        top = jnp.max(scores, axis=1, keepdims=True)
        mixes.append(nn(jnp.exp(scores - top).astype(BF), values[head]))
        tops.append(top)
    total = jnp.where(low, mixes[1], mixes[0])
    l_ref[...] = jnp.where(low, tops[1], tops[0]) + jnp.log(total)
    o_ref[...] = (jnp.where(low, mixes[0], mixes[1]) / pltpu.roll(total, HD, 1)).astype(BF)


def pair_spec(rows, offset, pairs):
    return pl.BlockSpec((1, rows, 2 * HD * pairs), lambda i, j: (i, 0, j + offset // pairs))


def lse_spec(rows, pairs):
    return pl.BlockSpec((1, pairs, rows, 2 * HD), lambda i, j: (i, j, 0, 0))


def attend_forward(queries, key_offset, keyvals, value_offset, lengths, name, pairs=1):
    clips, frames = queries.shape[:2]
    slots = keyvals.shape[1]
    groups = HEADS // 2
    masked = lengths is not None
    specs = [
        pair_spec(frames, 0, pairs),
        pair_spec(slots, key_offset, pairs),
        pair_spec(slots, value_offset, pairs),
    ]
    args = [queries, keyvals, keyvals]
    if masked:
        specs.insert(0, pl.BlockSpec(memory_space=pltpu.SMEM))
        args.insert(0, lengths)
    return call(
        functools.partial(attend_kernel, masked=masked),
        (clips, groups // pairs),
        specs,
        [pair_spec(frames, 0, pairs), lse_spec(frames, pairs)],
        [struct((clips, frames, D), BF), struct((clips, groups, frames, 2 * HD), F32)],
        name,
    )(*args)


def three_parts(value):
    high = value.astype(BF)
    rest = value - high.astype(F32)
    middle = rest.astype(BF)
    return high, middle, (rest - middle.astype(F32)).astype(BF)


def attend_back_kernel(*refs, masked):
    if masked:
        len_ref, q_ref, k_ref, v_ref, do_ref, o_ref, l_ref, dq_ref, dk_ref, dv_ref = refs
    else:
        q_ref, k_ref, v_ref, do_ref, o_ref, l_ref, dq_ref, dk_ref, dv_ref = refs
    length = len_ref[pl.program_id(0)] if masked else None
    attend_back_step(
        length, q_ref, k_ref, v_ref, do_ref, o_ref, l_ref, dq_ref, dk_ref, dv_ref
    )


def attend_back_step(length, q_ref, k_ref, v_ref, do_ref, o_ref, l_ref, dq_ref, dk_ref, dv_ref):
    lane, low = head_lanes()
    for pair in range(l_ref.shape[1]):
        columns = slice(pair * 2 * HD, (pair + 1) * 2 * HD)
        attend_back_pair(
            lane,
            low,
            length,
            q_ref[0, :, columns],
            k_ref[0, :, columns],
            v_ref[0, :, columns],
            do_ref[0, :, columns],
            o_ref[0, :, columns],
            l_ref[0, pair],
            dq_ref.at[0, :, columns],
            dk_ref.at[0, :, columns],
            dv_ref.at[0, :, columns],
        )


def attend_back_pair(lane, low, length, q, k, v, grad, mixed, lse, dq_ref, dk_ref, dv_ref):
    masked = length is not None
    scaled = q * jnp.asarray(HD**-0.5, BF)
    spot = lane % HD
    one = jnp.ones((), BF)
    zero = jnp.zeros((), BF)
    product = grad.astype(F32) * mixed.astype(F32)
    delta_low = jnp.sum(jnp.where(low, product, 0.0), axis=1, keepdims=True)
    delta_high = jnp.sum(jnp.where(low, 0.0, product), axis=1, keepdims=True)

    def negated(value, last):
        high, middle, rest = three_parts(-value)
        return jnp.where(
            spot == 0,
            high,
            jnp.where(spot == 1, middle, jnp.where(spot == 2, rest, last)),
        )

    tag = jnp.where(spot == 3, one, zero) if masked else zero
    lse_lanes = negated(lse, tag)
    delta_lanes = negated(jnp.where(low, delta_high, delta_low), zero)
    ones = jnp.broadcast_to(jnp.where(spot < 3, one, zero), k.shape)
    key_lanes = ones
    if masked:
        bias = usable_bias(length, k.shape[0])
        key_lanes = jnp.where(spot == 3, bias, ones)
    transposed = k.astype(F32).T.astype(BF)
    grad_queries, grad_keys, grad_values = [], [], []
    for head in range(2):

        def merge(own, other):
            return jnp.where(low, own, other) if head == 0 else jnp.where(low, other, own)

        probability = jnp.exp(nt(merge(k, key_lanes), merge(scaled, lse_lanes)))
        centred = nt(merge(v, ones), merge(grad, delta_lanes))
        grad_scores = (probability * centred).astype(BF)
        grad_values.append(nn(probability.astype(BF), grad))
        grad_keys.append(nn(grad_scores, scaled))
        grad_queries.append(nn(transposed[HD * head : HD * (head + 1)], grad_scores))
    dv_ref[...] = jnp.where(low, grad_values[0], grad_values[1]).astype(BF)
    dk_ref[...] = jnp.where(low, grad_keys[0], grad_keys[1]).astype(BF)
    dq_ref[...] = (jnp.concatenate(grad_queries, axis=0).T * HD**-0.5).astype(BF)


def attend_backward(
    queries, key_offset, keyvals, value_offset, lengths, grad, mixed, lse, name, pairs=1
):
    clips, frames = queries.shape[:2]
    slots = keyvals.shape[1]
    groups = HEADS // 2
    masked = lengths is not None
    specs = [
        pair_spec(frames, 0, pairs),
        pair_spec(slots, key_offset, pairs),
        pair_spec(slots, value_offset, pairs),
        pair_spec(frames, 0, pairs),
        pair_spec(frames, 0, pairs),
        lse_spec(frames, pairs),
    ]
    args = [queries, keyvals, keyvals, grad, mixed, lse]
    if masked:
        specs.insert(0, pl.BlockSpec(memory_space=pltpu.SMEM))
        args.insert(0, lengths)
    return call(
        functools.partial(attend_back_kernel, masked=masked),
        (clips, groups // pairs),
        specs,
        [pair_spec(frames, 0, pairs), pair_spec(slots, 0, pairs), pair_spec(slots, 0, pairs)],
        [
            struct((clips, frames, D), BF),
            struct((clips, slots, D), BF),
            struct((clips, slots, D), BF),
        ],
        name,
    )(*args)


def after_self_kernel(o_ref, x_ref, mod_ref, wo_ref, bo_ref, wq_ref, z_ref, h_ref, q_ref):
    branch = nn(o_ref[0], wo_ref[...]) + bo_ref[...]
    hidden = x_ref[0].astype(F32) + mod_ref[0, 2:3] * branch
    normed, _ = normalize(hidden)
    second_in = (normed * (1.0 + mod_ref[0, 4:5]) + mod_ref[0, 3:4]).astype(BF)
    z_ref[0] = branch.astype(BF)
    h_ref[0] = hidden
    q_ref[0] = nn(second_in, wq_ref[...]).astype(BF)


def after_self(mixed, latents, mod, weight, bias, query_weight):
    clips, frames, width = latents.shape
    rows = row_block(frames)
    spec = rows_spec(rows, width)
    square = whole_spec((width, width))
    return call(
        after_self_kernel,
        (clips, frames // rows),
        [spec, spec, clip_spec(9, width), square, whole_spec((1, width)), square],
        [spec, spec, spec],
        [
            struct(latents.shape, BF),
            struct(latents.shape, F32),
            struct(latents.shape, BF),
        ],
        "after_self",
    )(mixed, latents, mod, weight, bias, query_weight)


def after_cross_kernel(o_ref, h_ref, mod_ref, wo_ref, bo_ref, z_ref, out_ref):
    branch = nn(o_ref[0], wo_ref[...]) + bo_ref[...]
    z_ref[0] = branch.astype(BF)
    out_ref[0] = h_ref[0] + mod_ref[0, 5:6] * branch


def after_cross(mixed, hidden, mod, weight, bias):
    clips, frames, width = hidden.shape
    rows = row_block(frames)
    spec = rows_spec(rows, width)
    return call(
        after_cross_kernel,
        (clips, frames // rows),
        [
            spec,
            spec,
            clip_spec(9, width),
            whole_spec((width, width)),
            whole_spec((1, width)),
        ],
        [spec, spec],
        [struct(hidden.shape, BF), struct(hidden.shape, F32)],
        "after_cross",
    )(mixed, hidden, mod, weight, bias)


GELU_ROOT = math.sqrt(2.0 / math.pi)


def feed_kernel(
    h_ref,
    dy_ref,
    mod_ref,
    up_ref,
    upb_ref,
    down_ref,
    downb_ref,
    out_ref,
    dh_ref,
    dup_ref,
    ddown_ref,
    dupb_ref,
    ddownb_ref,
    sums_ref,
    in_s,
    int_s,
    dz_s,
    dzt_s,
    z_s,
    act_s,
    du_s,
    *,
    clips,
    frames,
    rows,
):
    step = pl.program_id(0)
    last = pl.num_programs(0) - 1
    spans = [
        (clip, start, clip * frames + start)
        for clip in range(clips)
        for start in range(0, frames, rows)
    ]

    @pl.when(step == 0)
    def _():
        bias_sum = jnp.zeros((1, h_ref.shape[2]), F32)
        for clip, start, at in spans:
            normed, _ = normalize(h_ref[clip, start : start + rows])
            third_in = normed * (1.0 + mod_ref[clip, 7:8]) + mod_ref[clip, 6:7]
            dz = (mod_ref[clip, 8:9] * dy_ref[clip, start : start + rows].astype(F32)).astype(BF)
            in_s[at : at + rows] = third_in.astype(BF)
            dz_s[at : at + rows] = dz
            bias_sum += column_sum(dz.astype(F32))
        ddownb_ref[...] = bias_sum
        int_s[...] = in_s[...].T
        dzt_s[...] = dz_s[...].T
        z_s[...] = jnp.zeros_like(z_s)
        dh_ref[...] = jnp.zeros_like(dh_ref)

    up, down = up_ref[...], down_ref[...]

    per = frames // rows

    def one(index):
        at = pl.multiple_of(index * rows, rows)
        here = pl.ds(at, rows)
        hidden = nn(in_s[here], up) + upb_ref[...]
        square = hidden * hidden
        tanh = jnp.tanh(hidden * (GELU_ROOT + (GELU_ROOT * 0.044715) * square))
        half = 0.5 + 0.5 * tanh
        lifted = hidden * half
        activated = lifted.astype(BF)
        slope = half + lifted * (1.0 - tanh) * (
            GELU_ROOT + (GELU_ROOT * 3 * 0.044715) * square
        )
        grad_hidden = (nt(dz_s[here], down) * slope).astype(BF)
        z_s[here] += nn(activated, down)
        spot = pl.ds(pl.multiple_of(index % per * rows, rows), rows)
        dh_ref[index // per, spot] += nt(grad_hidden, up)
        act_s[here] = activated
        du_s[here] = grad_hidden

    def one_clip(clip, _):
        for part in range(per):
            one(clip * per + part)
        return 0

    lax.fori_loop(0, clips, one_clip, 0)
    dup_ref[...] = nn(int_s[...], du_s[...]).astype(BF)
    ddown_ref[...] = nn(dzt_s[...], act_s[...]).T.astype(BF)
    dupb_ref[...] = column_sum(du_s[...].astype(F32))

    @pl.when(step == last)
    def _():
        for clip in range(clips):
            sums = None
            for start in range(0, frames, rows):
                at = clip * frames + start
                block = slice(start, start + rows)
                hidden = h_ref[clip, block]
                dy = dy_ref[clip, block].astype(F32)
                branch = z_s[at : at + rows] + downb_ref[...]
                out_ref[clip, block] = (hidden + mod_ref[clip, 8:9] * branch).astype(BF)
                normed, inverse = normalize(hidden)
                grad_in = dh_ref[clip, block]
                dh_ref[clip, block] = dy + norm_back(
                    normed, inverse, grad_in * (1.0 + mod_ref[clip, 7:8])
                )
                here = [
                    column_sum(grad_in),
                    column_sum(grad_in * normed),
                    column_sum(dy * branch),
                ]
                sums = here if sums is None else [a + b for a, b in zip(sums, here)]
            for index in range(3):
                sums_ref[clip, index : index + 1] = sums[index]


def feed(hidden, cotangent, mod, up, up_bias, down, down_bias, block=768):
    clips, frames, width = hidden.shape
    inner = up.shape[1]
    rows = row_block(frames)
    tokens = clips * frames

    def once(shape):
        return pl.BlockSpec(
            shape, lambda j: (0,) * len(shape), pipeline_mode=pl.Buffered(1)
        )

    def columns(count):
        return pl.BlockSpec((count, block), lambda j: (0, j))

    lines = pl.BlockSpec((block, width), lambda j: (j, 0))
    cube = once((clips, frames, width))
    return call(
        functools.partial(feed_kernel, clips=clips, frames=frames, rows=rows),
        (inner // block,),
        [
            cube,
            cube,
            once(mod.shape),
            columns(width),
            columns(1),
            lines,
            once((1, width)),
        ],
        [
            cube,
            cube,
            columns(width),
            lines,
            columns(1),
            once((1, width)),
            once((clips, 3, width)),
        ],
        [
            struct(hidden.shape, BF),
            struct(hidden.shape, F32),
            struct(up.shape, BF),
            struct(down.shape, BF),
            struct((1, inner), F32),
            struct((1, width), F32),
            struct((clips, 3, width), F32),
        ],
        "feed",
        [
            pltpu.VMEM((tokens, width), BF),
            pltpu.VMEM((width, tokens), BF),
            pltpu.VMEM((tokens, width), BF),
            pltpu.VMEM((width, tokens), BF),
            pltpu.VMEM((tokens, width), F32),
            pltpu.VMEM((tokens, block), BF),
            pltpu.VMEM((tokens, block), BF),
        ],
    )(hidden, cotangent, mod, up, up_bias, down, down_bias)


def ends():
    i, j = pl.program_id(0), pl.program_id(1)
    first = (i == 0) & (j == 0)
    last = (i == pl.num_programs(0) - 1) & (j == pl.num_programs(1) - 1)
    return j == 0, first, last


def before_cross_kernel(
    dh_ref, z_ref, o_ref, mod_ref, w_ref, do_ref, dw_ref, db_ref, sums_ref, ot_s, dz_s
):
    new_clip, first, last = ends()
    clear_at(new_clip, sums_ref)
    clear_at(first, db_ref)
    dh = dh_ref[0]
    here = span_of(dh.shape[0])
    dz = (mod_ref[0, 5:6] * dh).astype(BF)
    dz_s[here] = dz
    ot_s[here] = o_ref[0]
    sums_ref[0] += column_sum(dh * z_ref[0].astype(F32))
    db_ref[...] += column_sum(dz.astype(F32))
    do_ref[0] = nt(dz, w_ref[...]).astype(BF)

    @pl.when(last)
    def _():
        dw_ref[...] = tn(ot_s[...], dz_s[...]).astype(BF)


def before_cross(dh, branch, mixed, mod, weight):
    clips, frames, width = dh.shape
    rows = row_block(frames)
    spec = rows_spec(rows, width)
    square = whole_spec((width, width))
    return call(
        before_cross_kernel,
        (clips, frames // rows),
        [spec, spec, spec, clip_spec(9, width), square],
        [spec, square, whole_spec((1, width)), clip_spec(1, width)],
        [
            struct(dh.shape, BF),
            struct((width, width), BF),
            struct((1, width), F32),
            struct((clips, 1, width), F32),
        ],
        "before_cross",
        [pltpu.VMEM((clips * frames, width), BF)] * 2,
    )(dh, branch, mixed, mod, weight)


def before_self_kernel(
    dq_ref,
    h_ref,
    dh_ref,
    z_ref,
    o_ref,
    mod_ref,
    wq_ref,
    wo_ref,
    out_ref,
    do_ref,
    dwq_ref,
    dwo_ref,
    db_ref,
    sums_ref,
    in_s,
    dq_s,
    o_s,
    dz_s,
):
    new_clip, first, last = ends()
    clear_at(new_clip, sums_ref)
    clear_at(first, db_ref)
    here = span_of(dq_ref.shape[1])
    normed, inverse = normalize(h_ref[0])
    in_s[here] = (normed * (1.0 + mod_ref[0, 4:5]) + mod_ref[0, 3:4]).astype(BF)
    grad_query = dq_ref[0]
    dq_s[here] = grad_query
    o_s[here] = o_ref[0]
    grad_in = nt(grad_query, wq_ref[...])
    dh = dh_ref[0] + norm_back(normed, inverse, grad_in * (1.0 + mod_ref[0, 4:5]))
    out_ref[0] = dh
    dz = (mod_ref[0, 2:3] * dh).astype(BF)
    dz_s[here] = dz
    sums_ref[0] += jnp.concatenate(
        [
            column_sum(grad_in),
            column_sum(grad_in * normed),
            column_sum(dh * z_ref[0].astype(F32)),
        ],
        axis=0,
    )
    db_ref[...] += column_sum(dz.astype(F32))
    do_ref[0] = nt(dz, wo_ref[...]).astype(BF)

    @pl.when(last)
    def _():
        dwq_ref[...] = tn(in_s[...], dq_s[...]).astype(BF)
        dwo_ref[...] = tn(o_s[...], dz_s[...]).astype(BF)


def before_self(grad_query, hidden, dh, branch, mixed, mod, query_weight, weight):
    clips, frames, width = dh.shape
    rows = row_block(frames)
    spec = rows_spec(rows, width)
    square = whole_spec((width, width))
    return call(
        before_self_kernel,
        (clips, frames // rows),
        [spec, spec, spec, spec, spec, clip_spec(9, width), square, square],
        [spec, spec, square, square, whole_spec((1, width)), clip_spec(3, width)],
        [
            struct(dh.shape, F32),
            struct(dh.shape, BF),
            struct((width, width), BF),
            struct((width, width), BF),
            struct((1, width), F32),
            struct((clips, 3, width), F32),
        ],
        "before_self",
        [pltpu.VMEM((clips * frames, width), BF)] * 4,
    )(grad_query, hidden, dh, branch, mixed, mod, query_weight, weight)


def input_kernel(
    dq_ref, dk_ref, dv_ref, x_ref, dh_ref, mod_ref, w_ref, out_ref, dw_ref, sums_ref, in_s, g_s
):
    new_clip, _, last = ends()
    width = x_ref.shape[2]
    clear_at(new_clip, sums_ref)
    here = span_of(x_ref.shape[1])
    normed, inverse = normalize(x_ref[0].astype(F32))
    in_s[here] = (normed * (1.0 + mod_ref[0, 1:2]) + mod_ref[0, 0:1]).astype(BF)
    grad_in = None
    for index, ref in enumerate((dq_ref, dk_ref, dv_ref)):
        columns = slice(index * width, (index + 1) * width)
        grad = ref[0]
        g_s[here, columns] = grad
        part = nt(grad, w_ref[:, columns])
        grad_in = part if grad_in is None else grad_in + part
    out_ref[0] = (
        dh_ref[0] + norm_back(normed, inverse, grad_in * (1.0 + mod_ref[0, 1:2]))
    ).astype(BF)
    sums_ref[0] += jnp.concatenate(
        [column_sum(grad_in), column_sum(grad_in * normed)], axis=0
    )

    @pl.when(last)
    def _():
        turned = in_s[...].T
        for index in range(3):
            columns = slice(index * width, (index + 1) * width)
            dw_ref[:, columns] = nn(turned, g_s[:, columns]).astype(BF)


def input_back(grads, latents, dh, mod, weight):
    clips, frames, width = dh.shape
    rows = row_block(frames)
    spec = rows_spec(rows, width)
    return call(
        input_kernel,
        (clips, frames // rows),
        [spec] * 5 + [clip_spec(9, width), whole_spec(weight.shape)],
        [spec, whole_spec(weight.shape), clip_spec(2, width)],
        [
            struct(dh.shape, BF),
            struct(weight.shape, BF),
            struct((clips, 2, width), F32),
        ],
        "input_back",
        [
            pltpu.VMEM((clips * frames, width), BF),
            pltpu.VMEM((clips * frames, weight.shape[1]), BF),
        ],
    )(*grads, latents, dh, mod, weight)


def block_pass(latents, captions, lengths, cotangent, mod, triple_weight, front, back):
    triple, mixed_one, lse_one, weights = front(latents, mod, triple_weight)
    (
        output_weight,
        output_bias,
        cross_query,
        cross_keyval,
        cross_output,
        cross_bias,
        up_weight,
        up_bias,
        down_weight,
        down_bias,
    ) = weights
    clips, frames, width = latents.shape
    slots = captions.shape[1]
    groups = HEADS // 2
    caption_flat = captions.reshape(clips * slots, captions.shape[2])
    branch_one, hidden_one, cross_queries = after_self(
        mixed_one, latents, mod, output_weight, output_bias, cross_query
    )
    pairs = (
        jnp.dot(caption_flat, cross_keyval, preferred_element_type=F32)
        .astype(BF)
        .reshape(clips, slots, 2 * width)
    )
    mixed_two, lse_two = attend_forward(cross_queries, 0, pairs, groups, lengths, "cross_forward")
    branch_two, hidden_two = after_cross(mixed_two, hidden_one, mod, cross_output, cross_bias)
    output, dh_two, grad_up, grad_down, grad_up_bias, grad_down_bias, sums_three = feed(
        hidden_two, cotangent, mod, up_weight, up_bias, down_weight, down_bias
    )
    grad_mixed_two, grad_cross_output, grad_cross_bias, gate_two = before_cross(
        dh_two, branch_two, mixed_two, mod, cross_output
    )
    grad_cq, grad_ck, grad_cv = attend_backward(
        cross_queries,
        0,
        pairs,
        groups,
        lengths,
        grad_mixed_two,
        mixed_two,
        lse_two,
        "cross_back",
        2,
    )
    grad_pairs = jnp.concatenate([grad_ck, grad_cv], axis=-1).reshape(clips * slots, 2 * width)
    grad_keyval = jnp.dot(caption_flat.T, grad_pairs, preferred_element_type=F32).astype(BF)
    dh_one, grad_mixed_one, grad_cross_query, grad_output, grad_output_bias, sums_two = before_self(
        grad_cq, hidden_one, dh_two, branch_one, mixed_one, mod, cross_query, output_weight
    )
    gradients = [
        grad_output,
        grad_output_bias,
        grad_cross_query,
        grad_keyval,
        grad_cross_output,
        grad_cross_bias,
        grad_up,
        grad_up_bias,
        grad_down,
        grad_down_bias,
    ]
    grads_one, rest = back(triple, grad_mixed_one, mixed_one, lse_one, gradients)
    input_grad, grad_triple, sums_one = input_back(grads_one, latents, dh_one, mod, triple_weight)
    grad_mod = jnp.concatenate(
        [sums_one, sums_two[:, 2:], sums_two[:, :2], gate_two, sums_three], axis=1
    ).astype(BF)
    return output, input_grad, grad_mod, grad_triple, gradients, rest


def plain_front(weights, latents, mod, triple_weight):
    groups = HEADS // 2
    triple = qkv_forward(latents, mod, triple_weight)
    mixed, lse = attend_forward(triple, groups, triple, 2 * groups, None, "self_forward", 2)
    return triple, mixed, lse, weights


def plain_back(triple, grad_mixed, mixed, lse, gradients):
    groups = HEADS // 2
    grads = attend_backward(
        triple, groups, triple, 2 * groups, None, grad_mixed, mixed, lse, "self_back", 2
    )
    return grads, None


LANE = 128
TILE = 16


def linear_layout():
    spots = []
    offset = 0
    for shape in layout_sizes():
        number = math.prod(shape) // LANE
        spots.append((offset, number, shape))
        offset += number
    return spots


class Group:
    def __init__(self, devices, inner, share, first, last):
        self.devices, self.share, self.first, self.last = devices, share, first, last
        self.padded = -(-share // TILE) * TILE
        owners, total = {}, 0
        for owner in range(first // share, (last - 1) // share + 1):
            low = max(first - owner * share, 0) // TILE
            high = -(-min(last - owner * share, share) // TILE)
            owners[owner] = [low, high]
            total += high - low
        self.tiles = 2 * -(-total // (2 * devices))
        self.chunk = self.tiles * TILE
        self.half = self.chunk // 2
        self.folds = next(
            n
            for n in range(1, 99)
            if self.half % (n * TILE) == 0 and self.half // n <= 512
        )
        room = [self.tiles] * devices
        self.pieces = []

        def give(owner, device):
            low, high = owners[owner]
            take = min(high - low, room[device])
            if take > 0:
                place = self.tiles - room[device]
                self.pieces.append((owner, device, low * TILE, place * TILE, take * TILE))
                room[device] -= take
                owners[owner][0] += take

        for flip in (0, 2 * inner, inner):
            for owner in owners:
                give(owner, owner ^ flip)
        for owner in owners:
            while owners[owner][0] < owners[owner][1]:
                give(owner, max(range(devices), key=lambda device: room[device]))

    def find(self, row):
        owner, at = divmod(row, self.share)
        for holder, device, start, place, count in self.pieces:
            if holder == owner and start <= at < start + count:
                return device, place + at - start, min(self.share, start + count) - at
        raise ValueError(row)

    def segments(self, start, count):
        found = []
        row = start
        while row < start + count:
            chunk, place, left = self.find(row)
            take = min(left, start + count - row)
            found.append((chunk, place, row, take))
            row += take
        return found

    def moves(self):
        return self.pieces


def unpack_kernel(*refs, plan, indices, step):
    n = len(indices)
    spots = linear_layout()
    g_ref, outs, rest = refs[0], refs[1 : 1 + n], refs[1 + n :]
    lin, in_sem, out_sem = rest[0], rest[1], rest[2]
    stages, results = rest[3 : 3 + n], rest[3 + n :]
    loads = []
    for which, index in enumerate(indices):
        offset, number, _ = spots[index]
        place = 0
        mine = []
        for slot, (chunk, row, at, take) in enumerate(plan.segments(offset, number)):
            low = row // TILE * TILE
            high = -(-(row + take) // TILE) * TILE
            copy = pltpu.make_async_copy(
                g_ref.at[chunk, pl.ds(low, high - low)],
                stages[which].at[pl.ds(place, high - low)],
                in_sem.at[which, slot],
            )
            copy.start()
            mine.append((copy, place, row - low, high - low, at - offset, take))
            place += high - low
        loads.append(mine)
    stores = []
    for which, index in enumerate(indices):
        offset, number, shape = spots[index]
        for copy, place, skip, size, at, take in loads[which]:
            copy.wait()
            first = stages[which][place : place + TILE].astype(F32)
            lin[at : at + TILE - skip] = first[skip:]
            blocks, tail = divmod(size - TILE, step)

            def body(i, _, place=place, at=at, skip=skip, which=which):
                source = pl.multiple_of(place + TILE + i * step, TILE)
                lin[pl.ds(at + TILE - skip + i * step, step)] = stages[which][
                    pl.ds(source, step)
                ].astype(F32)
                return 0

            lax.fori_loop(0, blocks, body, 0)
            if tail:
                source = place + TILE + blocks * step
                target = at + TILE - skip + blocks * step
                lin[target : target + tail] = stages[which][source : source + tail].astype(F32)
        if len(shape) == 1:
            for c in range(number):
                results[which][0:1, c * LANE : (c + 1) * LANE] = lin[c : c + 1]
        else:
            high, wide = shape
            count = wide // LANE
            rows = 64

            def turn(i, _, which=which, count=count):
                top = pl.multiple_of(i * rows, rows)
                for c in range(count):
                    results[which][pl.ds(top, rows), c * LANE : (c + 1) * LANE] = lin[
                        pl.ds(top * count + c, rows, stride=count)
                    ].astype(BF)
                return 0

            lax.fori_loop(0, high // rows, turn, 0)
        copy = pltpu.make_async_copy(results[which], outs[which], out_sem.at[which])
        copy.start()
        stores.append(copy)
    for copy in stores:
        copy.wait()


def unpack_weights(gathered, plan, indices, step=128):
    spots = linear_layout()
    stage_shapes, result_shapes, most, tallest = [], [], 0, 0
    for index in indices:
        offset, number, shape = spots[index]
        found = plan.segments(offset, number)
        size = sum(-(-(r + t) // TILE) * TILE - r // TILE * TILE for _, r, _, t in found)
        stage_shapes.append(pltpu.VMEM((size, LANE), BF))
        most = max(most, len(found))
        tallest = max(tallest, number)
        result_shapes.append((shape, BF) if len(shape) == 2 else ((1, shape[0]), F32))
    anywhere = pl.BlockSpec(memory_space=pl.ANY)
    return pl.pallas_call(
        functools.partial(unpack_kernel, plan=plan, indices=indices, step=step),
        in_specs=[anywhere],
        out_specs=[anywhere] * len(indices),
        out_shape=[jax.ShapeDtypeStruct(s, t) for s, t in result_shapes],
        scratch_shapes=[
            pltpu.VMEM((tallest + 2 * TILE, LANE), F32),
            pltpu.SemaphoreType.DMA((len(indices), most)),
            pltpu.SemaphoreType.DMA((len(indices),)),
        ]
        + stage_shapes
        + [pltpu.VMEM(s, t) for s, t in result_shapes],
        compiler_params=pltpu.CompilerParams(vmem_limit_bytes=VMEM_LIMIT),
        name="unpack",
    )(gathered)


def pack_kernel(*refs, plan, indices, step):
    n = len(indices)
    spots = linear_layout()
    ins, out_ref, rest = refs[:n], refs[n], refs[n + 1 :]
    lin, stage, in_sem, out_sem = rest[:4]
    held = rest[4:]
    copies = []
    for which in range(n):
        copy = pltpu.make_async_copy(ins[which], held[which], in_sem.at[which])
        copy.start()
        copies.append(copy)
    stores = []
    begin = spots[indices[0]][0]
    total = spots[indices[-1]][0] + spots[indices[-1]][1] - begin
    pieces = plan.segments(begin, total)
    place = 0
    done = -TILE
    lin[0:TILE] = jnp.zeros((TILE, LANE), F32)
    slot = 0
    for which, index in enumerate(indices):
        offset, number, shape = spots[index]
        copies[which].wait()
        if len(shape) == 1:
            for c in range(number):
                lin[TILE + c : TILE + c + 1] = held[which][0:1, c * LANE : (c + 1) * LANE]
        else:
            high, wide = shape
            count = wide // LANE
            rows = 64

            def turn(i, _, which=which, count=count):
                top = pl.multiple_of(i * rows, rows)
                for c in range(count):
                    lin[pl.ds(TILE + top * count + c, rows, stride=count)] = held[which][
                        pl.ds(top, rows), c * LANE : (c + 1) * LANE
                    ].astype(F32)
                return 0

            lax.fori_loop(0, high // rows, turn, 0)
        low, high_row = offset - begin, offset - begin + number
        last = which == n - 1
        while slot < len(pieces):
            chunk, row, at, take = pieces[slot]
            at -= begin
            head = row - row // TILE * TILE
            start, stop = at - head, at + take
            ceil = start + -(-(stop - start) // TILE) * TILE
            first = max(start, done)
            whole = stop <= high_row
            end = ceil if whole else start + (high_row - start) // TILE * TILE
            if end > first:
                base = row - head + first - start
                blocks, tail = divmod(end - first, step)
                shift = TILE + first - low

                def body(i, _, place=place, shift=shift):
                    target = pl.multiple_of(place + i * step, TILE)
                    stage[pl.ds(target, step)] = lin[pl.ds(shift + i * step, step)].astype(BF)
                    return 0

                lax.fori_loop(0, blocks, body, 0)
                if tail:
                    source = shift + blocks * step
                    target = place + blocks * step
                    stage[target : target + tail] = lin[source : source + tail].astype(BF)
                copy = pltpu.make_async_copy(
                    stage.at[pl.ds(place, end - first)],
                    out_ref.at[chunk, pl.ds(base, end - first)],
                    out_sem.at[len(stores)],
                )
                copy.start()
                stores.append(copy)
                place += end - first
                done = end
            if not whole:
                break
            done = stop if slot + 1 == len(pieces) else min(done, stop)
            slot += 1
        if not last:
            lin[0:TILE] = lin[number : number + TILE]
    for copy in stores:
        copy.wait()


def pack_grads(grads, plan, indices, step=128):
    spots = linear_layout()
    tallest = max(spots[i][1] for i in indices)
    begin = spots[indices[0]][0]
    total = spots[indices[-1]][0] + spots[indices[-1]][1] - begin
    count = len(plan.segments(begin, total))
    anywhere = pl.BlockSpec(memory_space=pl.ANY)
    return pl.pallas_call(
        functools.partial(pack_kernel, plan=plan, indices=indices, step=step),
        in_specs=[anywhere] * len(indices),
        out_specs=anywhere,
        out_shape=jax.ShapeDtypeStruct((plan.devices, plan.chunk, LANE), BF),
        scratch_shapes=[
            pltpu.VMEM((tallest + 2 * TILE, LANE), F32),
            pltpu.VMEM((total + 2 * TILE * (count + len(indices)), LANE), BF),
            pltpu.SemaphoreType.DMA((len(indices),)),
            pltpu.SemaphoreType.DMA((count + len(indices),)),
        ]
        + [pltpu.VMEM(g.shape, g.dtype) for g in grads],
        compiler_params=pltpu.CompilerParams(vmem_limit_bytes=VMEM_LIMIT),
        name="pack",
    )(*grads)


MESH = pl.DeviceIdType.MESH


def place_of():
    dp, fs = lax.axis_index("dp"), lax.axis_index("fsdp")
    return dp, fs, dp // 2, dp % 2, fs // 2, fs % 2


def meet_all(me, devices, inner):
    barrier = pltpu.get_barrier_semaphore()

    def greet(i, _):
        other = (me + i) % devices
        pl.semaphore_signal(
            barrier, inc=1, device_id=(other // inner, other % inner), device_id_type=MESH
        )
        return 0

    lax.fori_loop(1, devices, greet, 0)
    pl.semaphore_wait(barrier, devices - 1)


class Trade:
    def __init__(self, source, target, own_sem, send_sem, recv_sem, group, inner, senders, receivers):
        self.source, self.target, self.own_sem = source, target, own_sem
        self.send_sem, self.recv_sem = send_sem, recv_sem
        self.devices, self.inner = group.devices, inner
        self.senders, self.receivers = senders, receivers
        self.me = lax.axis_index("dp") * inner + lax.axis_index("fsdp")
        self.many = len(source.shape) == 3

    def piece(self, target):
        return self.source.at[target] if self.many else self.source

    def copy(self, source, target):
        return pltpu.make_async_remote_copy(
            src_ref=self.piece(target),
            dst_ref=self.target.at[source],
            send_sem=self.send_sem.at[target],
            recv_sem=self.recv_sem.at[source],
            device_id=(target // self.inner, target % self.inner),
            device_id_type=MESH,
        )

    def own(self):
        return pltpu.make_async_copy(
            self.piece(self.me), self.target.at[self.me], self.own_sem
        )

    def each(self, act):
        def body(i, _):
            act((self.me + i) % self.devices)
            return 0

        lax.fori_loop(1, self.devices, body, 0)

    def both(self):
        return (self.me < self.senders) & (self.me < self.receivers)

    def start(self):
        pl.when(self.both())(lambda: self.own().start())

        def act(other):
            ok = (self.me < self.senders) & (other < self.receivers)
            pl.when(ok)(lambda: self.copy(self.me, other).start())

        self.each(act)

    def wait(self):
        pl.when(self.both())(lambda: self.own().wait())

        def landed(other):
            ok = (other < self.senders) & (self.me < self.receivers)
            pl.when(ok)(lambda: self.copy(other, other).wait_recv())

        def gone(other):
            ok = (self.me < self.senders) & (other < self.receivers)
            pl.when(ok)(lambda: self.copy(self.me, other).wait_send())

        self.each(landed)
        self.each(gone)


def when_all(conditions):
    total = None
    for condition in conditions:
        if condition is not None:
            total = condition if total is None else total & condition
    return total


def guarded(condition, body):
    if condition is None:
        body()
    else:
        pl.when(condition)(body)


class Deal:
    def __init__(self, group, source, target, send_sem, recv_sem, inner, back):
        self.source, self.target, self.back = source, target, back
        self.send_sem, self.recv_sem, self.inner = send_sem, recv_sem, inner
        self.me = lax.axis_index("dp") * inner + lax.axis_index("fsdp")
        self.moves = []
        for owner, device, row, place, count in group.moves():
            if back:
                self.moves.append((device, owner, place, row, count))
            else:
                self.moves.append((owner, device, row, place, count))

    def copy(self, move):
        source, target, start, place, count = move
        out = [m for m in self.moves if m[0] == source].index(move)
        into = [m for m in self.moves if m[1] == target].index(move)
        from_ref = self.source.at[pl.ds(start, count)]
        to_ref = self.target.at[pl.ds(place, count)]
        if source == target:
            return pltpu.make_async_copy(from_ref, to_ref, self.recv_sem.at[into])
        return pltpu.make_async_remote_copy(
            src_ref=from_ref,
            dst_ref=to_ref,
            send_sem=self.send_sem.at[out],
            recv_sem=self.recv_sem.at[into],
            device_id=(target // self.inner, target % self.inner),
            device_id_type=MESH,
        )

    def each(self, key, act):
        for device in sorted({m[key] for m in self.moves}):
            mine = [m for m in self.moves if m[key] == device]

            @pl.when(self.me == device)
            def _(mine=mine):
                for move in mine:
                    act(move)

    def start(self):
        self.each(0, lambda move: self.copy(move).start())

    def landed(self):
        def act(move):
            if move[0] == move[1]:
                self.copy(move).wait()
            else:
                self.copy(move).wait_recv()

        self.each(1, act)

    def gone(self):
        def act(move):
            if move[0] != move[1]:
                self.copy(move).wait_send()

        self.each(0, act)

    @staticmethod
    def semaphores(group, back):
        sends = recvs = 0
        for device in range(group.devices):
            sends = max(sends, sum(1 for m in group.moves() if m[1 if back else 0] == device))
            recvs = max(recvs, sum(1 for m in group.moves() if m[0 if back else 1] == device))
        dma = pltpu.SemaphoreType.DMA
        return [dma((sends,)), dma((recvs,))]


def remote_call(body, in_specs, out_specs, out_shape, scratch, collective, name, grid=()):
    return pl.pallas_call(
        body,
        grid=grid,
        in_specs=in_specs,
        out_specs=out_specs,
        out_shape=out_shape,
        scratch_shapes=scratch,
        compiler_params=pltpu.CompilerParams(
            collective_id=collective, has_side_effects=True, vmem_limit_bytes=VMEM_LIMIT
        ),
        name=name,
    )


ANYWHERE = pl.BlockSpec(memory_space=pl.ANY)


def start_kernel(
    step_ref, slot_ref, all_ref, chunk_ref, own_sem, send_sem, recv_sem, deal_send, deal_recv,
    *, group, inner
):
    me = lax.axis_index("dp") * inner + lax.axis_index("fsdp")
    meet_all(me, group.devices, inner)
    deal = Deal(group, slot_ref, chunk_ref, deal_send, deal_recv, inner, False)
    trade = Trade(
        step_ref, all_ref, own_sem, send_sem, recv_sem, group, inner, group.devices, group.devices
    )
    trade.start()
    deal.start()
    trade.wait()
    deal.landed()
    deal.gone()


def start_chunks(steps, slot, group, inner, collective):
    dma = pltpu.SemaphoreType.DMA
    return remote_call(
        functools.partial(start_kernel, group=group, inner=inner),
        [ANYWHERE] * 2,
        [ANYWHERE] * 2,
        [
            jax.ShapeDtypeStruct((group.devices, *steps.shape), steps.dtype),
            jax.ShapeDtypeStruct((group.chunk, LANE), BF),
        ],
        [dma, dma((group.devices,)), dma((group.devices,))] + Deal.semaphores(group, False),
        collective,
        "start_chunks",
    )(steps, slot)


class Gather:
    def __init__(self, group, inner, chunk_ref, out_ref, own_sem, send_sem, recv_sem):
        self.group, self.inner = group, inner
        self.chunk_ref, self.out_ref = chunk_ref, out_ref
        self.send_sem, self.recv_sem = send_sem, recv_sem
        dp, fs, self.y, self.x, self.z, self.c = place_of()
        self.levels = inner // 2
        self.own = pltpu.make_async_copy(chunk_ref, out_ref.at[dp * inner + fs], own_sem)
        self.across = {
            "up": (dp, fs + 2),
            "down": (dp, fs - 2),
            "x": (dp + 1 - 2 * self.x, fs),
            "y": (dp + 2 - 4 * self.y, fs),
            "twin": (dp, fs + 1 - 2 * self.c),
        }
        self.kinds = tuple(self.across)
        self.closing = False

    @staticmethod
    def semaphores(group):
        dma = pltpu.SemaphoreType.DMA
        return [dma, dma((5, group.devices // 2, 2)), dma((group.devices, 2))]

    def copy(self, kind, yy, xx, zz, part, cc=None, mine=False):
        core = self.c if cc is None else cc
        column = yy * 2 + xx
        index = column * self.inner + zz * 2 + core
        rows = pl.ds(part * self.group.half, self.group.half)
        return pltpu.make_async_remote_copy(
            src_ref=self.chunk_ref.at[rows] if mine else self.out_ref.at[index, rows],
            dst_ref=self.out_ref.at[index, rows],
            send_sem=self.send_sem.at[
                self.kinds.index(kind), column * self.levels + zz, part
            ],
            recv_sem=self.recv_sem.at[index, part],
            device_id=self.across[kind],
            device_id_type=MESH,
        )

    def send(self, condition, kind, yy, xx, zz, part, mine=False):
        copy = functools.partial(self.copy, kind, yy, xx, zz, part, mine=mine)
        if self.closing:
            guarded(condition, lambda: copy().wait_send())
        else:
            guarded(condition, lambda: copy().start())

    def arrive(self, condition, yy, xx, zz, part):
        if self.closing:
            return
        guarded(condition, lambda: self.copy("x", yy, xx, zz, part).wait_recv())

    def spread(self, distance):
        for sign in (1, -1) if distance else (0,):
            zz = self.z + sign * distance
            inside = when_all(
                [zz < self.levels if sign > 0 else None, zz >= 0 if sign < 0 else None]
            )
            yield zz, sign, inside

    def turn(self, turn):
        y, x, z, levels = self.y, self.x, self.z, self.levels
        if turn == 0 and not self.closing:
            self.own.start()
        if turn < levels:
            for zz, sign, inside in self.spread(turn):
                mine = turn == 0
                for part in range(2):
                    if turn:
                        self.arrive(inside, y, x, zz, part)
                    if sign <= 0:
                        self.send(when_all([inside, z < levels - 1]), "up", y, x, zz, part, mine)
                    if sign >= 0:
                        self.send(when_all([inside, z > 0]), "down", y, x, zz, part, mine)
                    for kind in ("x", "y") if part else ("y", "x"):
                        self.send(inside, kind, y, x, zz, part, mine)
                    self.send(inside, "twin", y, x, zz, part, mine)
        if 1 <= turn <= levels:
            for zz, sign, inside in self.spread(turn - 1):
                self.arrive(inside, y, 1 - x, zz, 0)
                self.send(inside, "y", y, 1 - x, zz, 0)
                self.send(inside, "twin", y, 1 - x, zz, 0)
                self.arrive(inside, 1 - y, x, zz, 1)
                self.send(inside, "x", 1 - y, x, zz, 1)
                self.send(inside, "twin", 1 - y, x, zz, 1)
                self.arrive(inside, 1 - y, x, zz, 0)
                self.send(inside, "twin", 1 - y, x, zz, 0)
                self.arrive(inside, y, 1 - x, zz, 1)
                self.send(inside, "twin", y, 1 - x, zz, 1)
        if turn >= 2:
            for zz, sign, inside in self.spread(turn - 2):
                for part in range(2):
                    self.arrive(inside, 1 - y, 1 - x, zz, part)
                    self.send(inside, "twin", 1 - y, 1 - x, zz, part)

    def finish(self):
        def twin_arrivals(i, _):
            column, zz = i // self.levels, i % self.levels
            for part in range(2):
                self.copy("twin", column // 2, column % 2, zz, part, 1 - self.c).wait_recv()
            return 0

        lax.fori_loop(0, 4 * self.levels, twin_arrivals, 0)
        self.closing = True
        for turn in range(self.levels + 2):
            self.turn(turn)
        self.own.wait()


class PairTrade:
    def __init__(self, slab_ref, out_ref, mine, theirs, sems, inner, devices):
        self.slab_ref, self.out_ref, self.mine, self.theirs = slab_ref, out_ref, mine, theirs
        self.pair_sem, self.send_sem, self.recv_sem = sems
        self.inner, self.chips, self.senders = inner, devices // 2, out_ref.shape[0]
        dp, fs, _, _, _, self.core = place_of()
        self.twin = (dp, fs + 1 - 2 * self.core)
        self.chip = (dp * inner + fs) // 2

    def load(self):
        return pltpu.make_async_copy(self.slab_ref.at[self.core], self.mine, self.pair_sem.at[0])

    def pair(self):
        return pltpu.make_async_remote_copy(
            src_ref=self.slab_ref.at[1 - self.core],
            dst_ref=self.theirs,
            send_sem=self.pair_sem.at[1],
            recv_sem=self.pair_sem.at[2],
            device_id=self.twin,
            device_id_type=MESH,
        )

    def copy(self, source, target):
        device = 2 * target + self.core
        return pltpu.make_async_remote_copy(
            src_ref=self.mine.at[target],
            dst_ref=self.out_ref.at[source],
            send_sem=self.send_sem.at[target],
            recv_sem=self.recv_sem.at[source],
            device_id=(device // self.inner, device % self.inner),
            device_id_type=MESH,
        )

    def own(self):
        return pltpu.make_async_copy(
            self.mine.at[self.chip], self.out_ref.at[self.chip], self.pair_sem.at[3]
        )

    def each(self, act):
        def body(i, _):
            act((self.chip + i) % self.chips)
            return 0

        lax.fori_loop(1, self.chips, body, 0)

    def begin(self):
        @pl.when(self.chip < self.senders)
        def _():
            self.pair().start()
            self.load().start()

    def start(self):
        @pl.when(self.chip < self.senders)
        def _():
            self.load().wait()
            self.pair().wait_recv()

            def add(i, _):
                self.mine[i] = self.mine[i] + self.theirs[i]
                return 0

            lax.fori_loop(0, self.chips, add, 0)
            self.own().start()
            self.each(lambda other: self.copy(self.chip, other).start())

    def wait(self):
        def landed(other):
            pl.when(other < self.senders)(lambda: self.copy(other, other).wait_recv())

        self.each(landed)

        @pl.when(self.chip < self.senders)
        def _():
            self.own().wait()
            self.pair().wait_send()
            self.each(lambda other: self.copy(self.chip, other).wait_send())


def gather_kernel(
    chunk_ref, slab_ref, slot_ref, out_ref, parts_ref, next_ref, mine, theirs, *sems,
    group, later, inner
):
    me = lax.axis_index("dp") * inner + lax.axis_index("fsdp")
    meet_all(me, group.devices, inner)
    trade = PairTrade(slab_ref, parts_ref, mine, theirs, sems[:3], inner, group.devices)
    gather = Gather(group, inner, chunk_ref, out_ref, *sems[3:6])
    deal = Deal(later, slot_ref, next_ref, *sems[6:], inner, False)
    trade.begin()
    gather.turn(0)
    trade.start()
    gather.turn(1)
    deal.start()
    for turn in range(2, inner // 2 + 2):
        gather.turn(turn)
    gather.finish()
    trade.wait()
    deal.landed()
    deal.gone()


def gather_chunks(chunk, slabs, slot, group, later, inner, senders, collective):
    dma = pltpu.SemaphoreType.DMA
    return remote_call(
        functools.partial(gather_kernel, group=group, later=later, inner=inner),
        [ANYWHERE] * 3,
        [ANYWHERE] * 3,
        [
            jax.ShapeDtypeStruct((group.devices, group.chunk, LANE), BF),
            jax.ShapeDtypeStruct((senders // 2, *slabs.shape[2:]), slabs.dtype),
            jax.ShapeDtypeStruct((later.chunk, LANE), BF),
        ],
        [
            pltpu.VMEM(slabs.shape[1:], slabs.dtype),
            pltpu.VMEM(slabs.shape[1:], slabs.dtype),
            dma((4,)),
            dma((group.devices // 2,)),
            dma((group.devices // 2,)),
        ]
        + Gather.semaphores(group)
        + Deal.semaphores(later, False),
        collective,
        "gather_chunks",
    )(chunk, slabs, slot)


def scatter_stages(
    group,
    inner,
    g_ref,
    acc,
    twin,
    wide_y,
    wide_x,
    slim_x,
    slim_y,
    line,
    load_sem,
    twin_send,
    twin_recv,
    wide_send,
    wide_recv,
    slim_send,
    slim_recv,
    line_send,
    line_recv,
):
    dp, fs, y, x, z, c = place_of()
    me = dp * inner + fs
    lent = group.half
    levels = inner // 2
    x_mate = (dp + 1 - 2 * x, fs)
    y_mate = (dp + 2 - 4 * y, fs)

    def remote(source, target, send, receive, device):
        return pltpu.make_async_remote_copy(
            src_ref=source,
            dst_ref=target,
            send_sem=send,
            recv_sem=receive,
            device_id=device,
            device_id_type=MESH,
        )

    def slot_of(yy, xx, zz):
        return (yy * 2 + xx) * levels + zz

    def load(yy, xx, zz):
        slot = slot_of(yy, xx, zz)
        return pltpu.make_async_copy(
            g_ref.at[(yy * 2 + xx) * inner + zz * 2 + c], acc.at[slot], load_sem.at[slot]
        )

    def to_twin(yy, xx, zz):
        slot = slot_of(yy, xx, zz)
        return remote(
            g_ref.at[(yy * 2 + xx) * inner + zz * 2 + 1 - c],
            twin.at[slot],
            twin_send.at[slot],
            twin_recv.at[slot],
            (dp, fs + 1 - 2 * c),
        )

    def piece(slot, part):
        return acc.at[slot, pl.ds(part * lent, lent)]

    def wide(part, other, zz, yy=0, xx=0):
        buffer, device = (wide_x, x_mate) if part else (wide_y, y_mate)
        index = other * levels + zz
        return remote(
            piece(slot_of(yy, xx, zz), part),
            buffer.at[index],
            wide_send.at[part, index],
            wide_recv.at[part, index],
            device,
        )

    def slim(part, zz, yy=0, xx=0):
        buffer, device = (slim_y, y_mate) if part else (slim_x, x_mate)
        return remote(
            piece(slot_of(yy, xx, zz), part),
            buffer.at[zz],
            slim_send.at[part, zz],
            slim_recv.at[part, zz],
            device,
        )

    def along(upward, zz, part):
        way = 0 if upward else 1
        return remote(
            piece(slot_of(y, x, zz), part),
            line.at[way, zz, part],
            line_send.at[way, zz, part],
            line_recv.at[way, zz, part],
            (dp, fs + 2 if upward else fs - 2),
        )

    block = lent // group.folds

    def add(slot, first, count, source):
        def body(i, _):
            at = pl.multiple_of(i * block, TILE)
            to = pl.ds(pl.multiple_of(first + i * block, TILE), block)
            acc[slot, to] = acc[slot, to] + source[pl.ds(at, block)]
            return 0

        lax.fori_loop(0, count // block, body, 0)

    def add_part(slot, part, source):
        add(slot, part * lent, lent, source)

    def level(k):
        return jnp.where(z < levels // 2, z + levels - 1 - k, z + 1 + k) % levels

    columns = ((1 - y, 1 - x), (1 - y, x), (y, 1 - x), (y, x))

    def begin():
        for k in range(levels):
            for yy, xx in columns:
                to_twin(yy, xx, level(k)).start()
                load(yy, xx, level(k)).start()

    def settle(yy, xx, zz):
        slot = slot_of(yy, xx, zz)
        load(yy, xx, zz).wait()
        to_twin(yy, xx, zz).wait_recv()
        add(slot, 0, group.chunk, twin.at[slot])

    def diagonal(k):
        zz = level(k)
        settle(1 - y, 1 - x, zz)
        wide(0, 1 - x, zz, 1 - y, 1 - x).start()
        wide(1, 1 - y, zz, 1 - y, 1 - x).start()

    def sides(k):
        zz = level(k)
        settle(1 - y, x, zz)
        wide(0, x, zz, 1 - y, x).start()
        settle(y, 1 - x, zz)
        wide(1, y, zz, y, 1 - x).start()

    def middle(k):
        zz = level(k)
        wide(0, 1 - x, zz).wait_recv()
        add_part(slot_of(y, 1 - x, zz), 0, wide_y.at[(1 - x) * levels + zz])
        slim(0, zz, y, 1 - x).start()
        wide(1, 1 - y, zz).wait_recv()
        add_part(slot_of(1 - y, x, zz), 1, wide_x.at[(1 - y) * levels + zz])
        slim(1, zz, 1 - y, x).start()

    def home(k):
        zz = level(k)
        slot = slot_of(y, x, zz)
        settle(y, x, zz)
        wide(0, x, zz).wait_recv()
        add_part(slot, 0, wide_y.at[x * levels + zz])
        wide(1, y, zz).wait_recv()
        add_part(slot, 1, wide_x.at[y * levels + zz])
        slim(0, zz).wait_recv()
        add_part(slot, 0, slim_x.at[zz])
        slim(1, zz).wait_recv()
        add_part(slot, 1, slim_y.at[zz])

    def take(upward, zz, part):
        along(upward, zz, part).wait_recv()
        add_part(slot_of(y, x, zz), part, line.at[0 if upward else 1, zz, part])

    def ways(k, allowed):
        zz = level(k)
        for upward in (True, False):
            yield zz, upward, allowed() & (zz > z if upward else zz < z)

    def pass_on(k, allowed):
        more = {True: z > 0, False: z < levels - 1}
        for zz, upward, inside in ways(k, allowed):

            @pl.when(inside)
            def _(zz=zz, upward=upward):
                for part in range(2):

                    @pl.when(more[upward])
                    def _(part=part):
                        take(upward, zz, part)

                    along(upward, zz, part).start()

    def close_pass(k, allowed):
        for zz, upward, inside in ways(k, allowed):

            @pl.when(inside)
            def _(zz=zz, upward=upward):
                for part in range(2):
                    along(upward, zz, part).wait_send()

    def at_edge():
        return (z == 0) | (z == levels - 1)

    def off_edge():
        return (z > 0) & (z < levels - 1)

    def anywhere():
        return z >= 0

    def once(k):
        diagonal(k)
        sides(k)

    def final():
        for part in range(2):

            @pl.when(z > 0)
            def _(part=part):
                take(True, z, part)

            @pl.when(z < levels - 1)
            def _(part=part):
                take(False, z, part)

    stages = {
        "begin": begin,
        "once0": lambda: once(0),
        "once1": lambda: once(1),
        "middle0": lambda: middle(0),
        "once2": lambda: once(2),
        "middle1": lambda: middle(1),
        "home0": lambda: home(0),
        "pass0": lambda: pass_on(0, at_edge),
        "once3": lambda: once(3),
        "middle2": lambda: middle(2),
        "middle3": lambda: middle(3),
        "home1": lambda: home(1),
        "pass1": lambda: pass_on(1, anywhere),
        "home2": lambda: home(2),
        "pass2": lambda: pass_on(2, anywhere),
        "inner0": lambda: pass_on(0, off_edge),
        "home3": lambda: home(3),
        "final": final,
    }

    def finish():
        for k, allowed in ((0, at_edge), (1, anywhere), (2, anywhere), (0, off_edge)):
            close_pass(k, allowed)

        def close(k, _):
            zz = level(k)
            for yy, xx in columns:
                to_twin(yy, xx, zz).wait_send()
            wide(0, 1 - x, zz).wait_send()
            wide(0, x, zz).wait_send()
            wide(1, 1 - y, zz).wait_send()
            wide(1, y, zz).wait_send()
            slim(0, zz).wait_send()
            slim(1, zz).wait_send()
            return 0

        lax.fori_loop(0, levels, close, 0)

    return stages, finish, acc.at[slot_of(y, x, z)]


def scatter_scratch(group, inner):
    dma = pltpu.SemaphoreType.DMA
    half, levels = group.devices // 2, inner // 2
    part = (group.half, LANE)
    return [
        pltpu.VMEM((half, group.chunk, LANE), BF),
        pltpu.VMEM((half, group.chunk, LANE), BF),
        pltpu.VMEM((2 * levels, *part), BF),
        pltpu.VMEM((2 * levels, *part), BF),
        pltpu.VMEM((levels, *part), BF),
        pltpu.VMEM((levels, *part), BF),
        pltpu.VMEM((2, levels, 2, *part), BF),
        dma((half,)),
        dma((half,)),
        dma((half,)),
        dma((2, 2 * levels)),
        dma((2, 2 * levels)),
        dma((2, levels)),
        dma((2, levels)),
        dma((2, levels, 2)),
        dma((2, levels, 2)),
    ]


def scatter_kernel(
    g_ref, rows_ref, out_ref, all_ref, own_sem, row_send, row_recv, *rest, group, inner, receivers
):
    me = lax.axis_index("dp") * inner + lax.axis_index("fsdp")
    meet_all(me, group.devices, inner)
    stages, finish, total = scatter_stages(group, inner, g_ref, *rest[:-2])
    trade = Trade(
        rows_ref, all_ref, own_sem, row_send, row_recv, group, inner, group.devices, receivers
    )
    for name, stage in stages.items():
        stage()
        if name == "once0":
            trade.start()
    deal = Deal(group, total, out_ref, *rest[-2:], inner, True)
    deal.start()
    finish()
    trade.wait()
    deal.landed()
    deal.gone()


def scatter_chunks(grads, rows, group, inner, receivers, collective):
    dma = pltpu.SemaphoreType.DMA
    return remote_call(
        functools.partial(scatter_kernel, group=group, inner=inner, receivers=receivers),
        [ANYWHERE] * 2,
        [ANYWHERE] * 2,
        [
            jax.ShapeDtypeStruct((group.padded, LANE), BF),
            jax.ShapeDtypeStruct((group.devices, *rows.shape), rows.dtype),
        ],
        [dma, dma((group.devices,)), dma((group.devices,))]
        + scatter_scratch(group, inner)
        + Deal.semaphores(group, True),
        collective,
        "scatter_chunks",
    )(grads, rows)


def front_kernel(
    x_ref, mod_ref, w_ref, chunk_ref, qkv_ref, o_ref, l_ref, out_ref, qkv_s, *sems,
    group, inner, leads, pairs
):
    step = pl.program_id(0)
    last = pl.num_programs(0) - 1
    clips, frames, _ = qkv_s.shape
    rows = x_ref.shape[1]
    gather = Gather(group, inner, chunk_ref, out_ref, *sems)
    me = lax.axis_index("dp") * inner + lax.axis_index("fsdp")

    @pl.when(step == 0)
    def _():
        meet_all(me, group.devices, inner)
        gather.turn(0)

    for turn, at in ((1, leads), (2, leads + 2), (3, leads + 4)):

        @pl.when(step == at)
        def _(turn=turn):
            gather.turn(turn)

    @pl.when(step < leads)
    def _():
        normed, _ = normalize(x_ref[0].astype(F32))
        first_in = (normed * (1.0 + mod_ref[0, 1:2]) + mod_ref[0, 0:1]).astype(BF)
        block = nn(first_in, w_ref[...]).astype(BF)
        qkv_ref[0] = block
        start = pl.multiple_of(step * rows % frames, rows)
        qkv_s[step * rows // frames, pl.ds(start, rows)] = block

    @pl.when(step >= leads)
    def _():
        lane, low = head_lanes()
        count = HEADS // 2 // pairs
        clip, group_index = (step - leads) // count, (step - leads) % count
        for pair in range(pairs):

            def columns(part):
                at = (group_index * pairs + pair + part * HEADS // 2) * 2 * HD
                return qkv_s[clip, :, pl.ds(pl.multiple_of(at, 2 * HD), 2 * HD)]

            attend_pair(
                lane,
                low,
                None,
                columns(0),
                columns(1),
                columns(2),
                o_ref.at[0, :, pair * 2 * HD : (pair + 1) * 2 * HD],
                l_ref.at[0, pair],
            )

    @pl.when(step == last)
    def _():
        for turn in range(4, inner // 2 + 2):
            gather.turn(turn)
        gather.finish()


def front_and_gather(latents, mod, weight, chunk, group, inner, collective, pairs=2):
    clips, frames, width = latents.shape
    rows = row_block(frames)
    per = frames // rows
    leads = clips * per
    count = HEADS // 2 // pairs

    def lead(s):
        return jnp.minimum(s, leads - 1)

    def tail(s):
        return jnp.maximum(s - leads, 0)

    wide = weight.shape[1]
    return remote_call(
        functools.partial(front_kernel, group=group, inner=inner, leads=leads, pairs=pairs),
        [
            pl.BlockSpec((1, rows, width), lambda s: (lead(s) // per, lead(s) % per, 0)),
            pl.BlockSpec((1, 9, width), lambda s: (lead(s) // per, 0, 0)),
            whole_spec(weight.shape),
            ANYWHERE,
        ],
        [
            pl.BlockSpec((1, rows, wide), lambda s: (lead(s) // per, lead(s) % per, 0)),
            pl.BlockSpec(
                (1, frames, 2 * HD * pairs), lambda s: (tail(s) // count, 0, tail(s) % count)
            ),
            pl.BlockSpec(
                (1, pairs, frames, 2 * HD), lambda s: (tail(s) // count, tail(s) % count, 0, 0)
            ),
            ANYWHERE,
        ],
        [
            struct((clips, frames, wide), BF),
            struct((clips, frames, width), BF),
            struct((clips, HEADS // 2, frames, 2 * HD), F32),
            struct((group.devices, group.chunk, LANE), BF),
        ],
        [pltpu.VMEM((clips, frames, wide), BF)] + Gather.semaphores(group),
        collective,
        "front_and_gather",
        (leads + clips * count,),
    )(latents, mod, weight, chunk)


def back_kernel(
    q_ref, k_ref, v_ref, do_ref, o_ref, l_ref, g_ref, dq_ref, dk_ref, dv_ref, rest_ref, *scratch,
    group, inner
):
    step = pl.program_id(0)
    last = pl.num_programs(0) - 1
    stages, finish, total = scatter_stages(group, inner, g_ref, *scratch[:-2])
    deal = Deal(group, total, rest_ref, *scratch[-2:], inner, True)
    me = lax.axis_index("dp") * inner + lax.axis_index("fsdp")

    @pl.when(step == 0)
    def _():
        meet_all(me, group.devices, inner)

    plan = (
        (0, ("begin",)),
        (1, ("once0", "once1")),
        (2, ("middle0", "once2")),
        (3, ("middle1", "once3")),
        (4, ("home0", "pass0")),
        (5, ("middle2",)),
    )
    for at, names in plan:

        @pl.when(step == at)
        def _(names=names):
            for name in names:
                stages[name]()

    attend_back_step(
        None, q_ref, k_ref, v_ref, do_ref, o_ref, l_ref, dq_ref, dk_ref, dv_ref
    )

    @pl.when(step == last)
    def _():
        for name in (
            "middle3", "home1", "pass1", "home2", "pass2", "inner0", "home3", "final"
        ):
            stages[name]()
        deal.start()
        finish()
        deal.landed()
        deal.gone()


def back_and_scatter(queries, grad, mixed, lse, chunks, group, inner, collective, pairs=2):
    clips, frames, wide = queries.shape
    width = wide // 3
    count = HEADS // 2 // pairs

    def pair_at(part):
        return pl.BlockSpec(
            (1, frames, 2 * HD * pairs), lambda s: (s // count, 0, s % count + part * count)
        )

    lse_at = pl.BlockSpec((1, pairs, frames, 2 * HD), lambda s: (s // count, s % count, 0, 0))
    return remote_call(
        functools.partial(back_kernel, group=group, inner=inner),
        [pair_at(0), pair_at(1), pair_at(2), pair_at(0), pair_at(0), lse_at, ANYWHERE],
        [pair_at(0)] * 3 + [ANYWHERE],
        [struct((clips, frames, width), BF)] * 3 + [struct((group.padded, LANE), BF)],
        scatter_scratch(group, inner) + Deal.semaphores(group, True),
        collective,
        "back_and_scatter",
        (clips * count,),
    )(queries, queries, queries, grad, mixed, lse, chunks)


def exchange_kernel(in_ref, out_ref, own_sem, send_sem, recv_sem, *, group, inner):
    me = lax.axis_index("dp") * inner + lax.axis_index("fsdp")
    meet_all(me, group.devices, inner)
    trade = Trade(
        in_ref, out_ref, own_sem, send_sem, recv_sem, group, inner, group.devices, group.devices
    )
    trade.start()
    trade.wait()


def exchange(value, group, inner, collective, name):
    dma = pltpu.SemaphoreType.DMA
    return remote_call(
        functools.partial(exchange_kernel, group=group, inner=inner),
        [ANYWHERE],
        ANYWHERE,
        jax.ShapeDtypeStruct((group.devices, *value.shape), value.dtype),
        [dma, dma((group.devices,)), dma((group.devices,))],
        collective,
        name,
    )(value)


HALF = 27
TALL = 72
SLAB = 112
CONDITION_ROWS = 832


def ada_spots(me, group):
    lines = group.share // HALF
    odd = me % 2
    limit = CONDITION_ROWS - TALL
    return [
        (odd, jnp.minimum((lines * me + odd) // 2, limit)),
        (1 - odd, jnp.minimum((lines * me - odd) // 2, limit)),
    ]


def ada_kernel(lin_ref, cond_ref, out_ref, *, group, inner):
    me = lax.axis_index("dp") * inner + lax.axis_index("fsdp")
    for half, (shift, top) in enumerate(ada_spots(me, group)):
        condition = cond_ref[pl.ds(top, TALL)].astype(BF)

        def body(c, _, half=half, shift=shift, condition=condition):
            rows = lin_ref[pl.ds(HALF * shift + c, TALL, stride=2 * HALF)].astype(BF)
            part = tn(condition, rows)
            count = group.devices
            for clip in range(2):
                out_ref[pl.ds((2 * clip + half) * HALF + c, count, stride=SLAB)] = part[
                    clip * count : (clip + 1) * count
                ]
            return 0

        lax.fori_loop(0, HALF, body, 0, unroll=True)


def ada_partial(lin, cond, group, inner):
    return pl.pallas_call(
        functools.partial(ada_kernel, group=group, inner=inner),
        out_shape=jax.ShapeDtypeStruct((group.devices * SLAB, LANE), F32),
        compiler_params=pltpu.CompilerParams(vmem_limit_bytes=VMEM_LIMIT),
        name="ada_partial",
    )(lin, cond)


def own_grad_kernel(cond_ref, dmod_ref, early_ref, late_ref, g_ref, sums_ref, lin, *, group, inner):
    me = lax.axis_index("dp") * inner + lax.axis_index("fsdp")
    count = group.devices // 2
    border = jnp.clip(group.first - group.share * me, 0, group.share)
    middle = jnp.clip(group.last - group.share * me, 0, group.share)
    for half, (shift, top) in enumerate(ada_spots(me, group)):
        condition = cond_ref[pl.ds(top, TALL)].astype(BF)

        def body(c, _, half=half, shift=shift, condition=condition):
            grads = jnp.concatenate(
                [
                    dmod_ref[
                        pl.ds(core * SLAB + (2 * clip + half) * HALF + c, count, stride=2 * SLAB)
                    ]
                    for clip in range(2)
                    for core in range(2)
                ],
                axis=0,
            ).astype(BF)
            lin[pl.ds(HALF * shift + c, TALL, stride=2 * HALF)] = nn(condition, grads)
            return 0

        @pl.when(border > 0)
        def _(body=body):
            lax.fori_loop(0, HALF, body, 0, unroll=True)

    rows = 64

    def merge(i, total):
        at = pl.multiple_of(i * rows, rows)
        row = lax.broadcasted_iota(jnp.int32, (rows, LANE), 0) + at
        early = early_ref[pl.ds(at, rows)].astype(F32)
        late = jnp.where(row < group.share, late_ref[pl.ds(at, rows)].astype(F32), 0.0)
        value = jnp.where(
            row < border, lin[pl.ds(at, rows)], jnp.where(row < middle, early, late)
        )
        g_ref[pl.ds(at, rows)] = value
        square = value * value
        return total + sum(square[k : k + 8] for k in range(0, rows, 8))

    sums_ref[...] = lax.fori_loop(0, group.padded // rows, merge, jnp.zeros((8, LANE), F32))


def own_grad(cond, dmod, early, late, group, inner):
    return pl.pallas_call(
        functools.partial(own_grad_kernel, group=group, inner=inner),
        out_shape=[
            jax.ShapeDtypeStruct((group.padded, LANE), F32),
            jax.ShapeDtypeStruct((8, LANE), F32),
        ],
        scratch_shapes=[pltpu.VMEM((2 * HALF * TALL, LANE), F32)],
        compiler_params=pltpu.CompilerParams(vmem_limit_bytes=VMEM_LIMIT),
        name="own_grad",
    )(cond, dmod, early, late)


def fits(devices, inner, share):
    return inner == 8 and devices == 32 and share % (LANE * HALF) == 0


def local_fast(latents, captions, lengths, timesteps, cotangent, master):
    clips, frames, width = latents.shape
    share = master.shape[0]
    inner = lax.axis_size("fsdp")
    devices = inner * lax.axis_size("dp")
    spots = linear_layout()
    end = spots[-1][0] + spots[-1][1]
    early = Group(devices, inner, share // LANE, spots[2][0], spots[3][0])
    late = Group(devices, inner, share // LANE, spots[3][0], end)
    holders = spots[2][0] // early.share + 1

    lin = lax.optimization_barrier(
        jnp.pad(
            master.reshape(early.share, LANE), ((0, 2 * HALF * TALL - early.share), (0, 0))
        )
    )
    slot = lin[: early.padded].astype(BF)
    steps, chunk = start_chunks(
        jnp.broadcast_to(
            jnp.pad(timesteps.astype(F32), (0, 8 - clips))[:, None], (8, LANE)
        ),
        slot,
        early,
        inner,
        1,
    )
    steps = steps[:, :clips, 0].reshape(devices // 2, 2, clips).T.reshape(devices * clips)
    columns = jax.nn.silu(embed(steps)).astype(BF).astype(F32).T
    columns = jnp.concatenate(
        [
            columns,
            jnp.ones((1, clips * devices), F32),
            jnp.zeros((CONDITION_ROWS - width - 1, clips * devices), F32),
        ],
        axis=0,
    )
    slabs = ada_partial(lin, columns, early, inner).reshape(2, devices // 2, SLAB, LANE)
    gathered, parts, later_chunk = gather_chunks(
        chunk, slabs, slot, early, late, inner, holders, 2
    )
    mod = jnp.sum(parts, axis=0)[: 54 * clips].reshape(clips, 9, width)
    (triple_weight,) = unpack_weights(gathered, early, (2,))

    def front(latents, mod, triple_weight):
        triple, mixed, lse, later = front_and_gather(
            latents, mod, triple_weight, later_chunk, late, inner, 3
        )
        return triple, mixed, lse, unpack_weights(later, late, tuple(range(3, 13)))

    def back(triple, grad_mixed, mixed, lse, gradients):
        chunks = pack_grads(gradients, late, tuple(range(3, 13)))
        *grads, rest = back_and_scatter(
            triple, grad_mixed, mixed, lse, chunks, late, inner, 4
        )
        return grads, rest

    output, input_grad, grad_mod, grad_triple, _, late_grads = block_pass(
        latents, captions, lengths, cotangent, mod, triple_weight, front, back
    )
    grad_rows = jnp.pad(
        grad_mod.reshape(54 * clips, LANE), ((0, SLAB - 54 * clips), (0, 0))
    )
    chunks = pack_grads([grad_triple], early, (2,))
    early_grads, dmod = scatter_chunks(chunks, grad_rows, early, inner, holders, 5)
    grads, squares = own_grad(
        columns,
        dmod.reshape(devices * SLAB, LANE).astype(F32),
        early_grads,
        late_grads,
        early,
        inner,
    )
    squares = exchange(squares, early, inner, 6, "squares")
    return (
        output,
        input_grad,
        grads[: early.share].reshape(share),
        jnp.sum(squares),
    )


def local_any(latents, captions, lengths, timesteps, cotangent, master):
    clips, frames, width = latents.shape
    share = master.shape[0]
    devices = lax.axis_size("dp") * lax.axis_size("fsdp")
    gathered = lax.all_gather(
        master.astype(BF).reshape(1, share), ("dp", "fsdp"), axis=0, tiled=True
    ).reshape(-1)
    weights = unpack(gathered)
    condition = jax.nn.silu(embed(timesteps)).astype(BF)
    mod = jnp.dot(condition, weights[0], preferred_element_type=F32) + weights[1].astype(F32)
    block_weights = [w.astype(F32).reshape(1, -1) if w.ndim == 1 else w for w in weights[2:]]
    output, input_grad, grad_mod, grad_triple, gradients, _ = block_pass(
        latents,
        captions,
        lengths,
        cotangent,
        mod.reshape(clips, 9, width),
        block_weights[0],
        functools.partial(plain_front, block_weights[1:]),
        plain_back,
    )
    grad_mod = grad_mod.reshape(clips, 9 * width)
    grad_ada = jnp.dot(condition.T, grad_mod, preferred_element_type=F32)
    grad_list = [grad_ada, jnp.sum(grad_mod.astype(F32), axis=0), grad_triple] + gradients
    flat = jnp.concatenate([piece.astype(F32).reshape(-1) for piece in grad_list])
    grad = lax.psum_scatter(
        flat.reshape(devices, share), ("dp", "fsdp"), scatter_dimension=0, tiled=True
    ).reshape(share)
    return output, input_grad, grad, lax.psum(jnp.sum(grad * grad), ("dp", "fsdp"))


def local(
    latents,
    captions,
    caption_lengths,
    timesteps,
    cotangent,
    master_weights,
    first_moment,
    second_moment,
):
    inner = lax.axis_size("fsdp")
    devices = inner * lax.axis_size("dp")
    run = local_fast if fits(devices, inner, master_weights.shape[0]) else local_any
    output, input_grad, grad_shard, squares = run(
        latents,
        captions,
        caption_lengths,
        timesteps,
        cotangent,
        master_weights,
    )
    grad_norm = jnp.sqrt(squares)
    clipped = grad_shard * (CLIP / jnp.maximum(grad_norm, CLIP))
    new_first = BETA_ONE * first_moment + (1.0 - BETA_ONE) * clipped
    new_second = BETA_TWO * second_moment + (1.0 - BETA_TWO) * clipped * clipped
    step_first = new_first / (1.0 - BETA_ONE**STEP)
    step_second = new_second / (1.0 - BETA_TWO**STEP)
    new_master = master_weights - RATE * (
        step_first / (jnp.sqrt(step_second) + ADAM_EPS) + DECAY * master_weights
    )
    return (output, input_grad, grad_norm, new_master, new_first, new_second)


def solution(mesh):
    placed = (
        P(("dp", "fsdp"), None, None),
        P(("dp", "fsdp"), None, None),
        P(("dp", "fsdp")),
        P(("dp", "fsdp")),
        P(("dp", "fsdp"), None, None),
        P(("dp", "fsdp")),
        P(("dp", "fsdp")),
        P(("dp", "fsdp")),
    )
    return jax.shard_map(
        local,
        mesh=mesh,
        in_specs=placed,
        out_specs=(
            P(("dp", "fsdp"), None, None),
            P(("dp", "fsdp"), None, None),
            P(),
            P(("dp", "fsdp")),
            P(("dp", "fsdp")),
            P(("dp", "fsdp")),
        ),
        check_vma=False,
    )
```

```python
import functools
import math

import jax
import jax.numpy as jnp
from jax import lax
from jax.experimental import pallas as pl
from jax.experimental.pallas import tpu as pltpu
from jax.sharding import PartitionSpec as P

D = 768
HEADS = 12
HD = 64
FF = 3072
CTX = 1024
STEP = 5


NORM_EPS = 1e-06
BETA_ONE = 0.9
BETA_TWO = 0.999
ADAM_EPS = 1e-08
RATE = 0.03
DECAY = 0.01
CLIP = 500.0


def layout_sizes():
    return [
        (D, 9 * D),
        (9 * D,),
        (D, 3 * D),
        (D, D),
        (D,),
        (D, D),
        (CTX, 2 * D),
        (D, D),
        (D,),
        (D, FF),
        (FF,),
        (FF, D),
        (D,),
    ]


def unpack(flat_vector):
    pieces = []
    offset = 0
    for layout_shape in layout_sizes():
        number = math.prod(layout_shape)
        pieces.append(flat_vector[offset : offset + number].reshape(layout_shape))
        offset += number
    return pieces


def embed(steps_in):
    half_width = D // 2
    frequency = jnp.exp(-math.log(10000.0) * jnp.arange(half_width, dtype=jnp.float32) / half_width)
    angles = steps_in.astype(jnp.float32)[:, None] * frequency[None, :]
    return jnp.concatenate([jnp.cos(angles), jnp.sin(angles)], axis=1)


def normalize(hidden):
    centred = hidden - jnp.mean(hidden, axis=-1, keepdims=True)
    inverse = lax.rsqrt(jnp.mean(centred * centred, axis=-1, keepdims=True) + NORM_EPS)
    return (centred * inverse, inverse)


def norm_back(normed, inverse, grad_normed):
    return inverse * (
        grad_normed
        - jnp.mean(grad_normed, axis=-1, keepdims=True)
        - normed * jnp.mean(grad_normed * normed, axis=-1, keepdims=True)
    )


F32 = jnp.float32
BF = jnp.bfloat16
VMEM_LIMIT = 60 << 20


def nn(left_side, right_side):
    return lax.dot_general(
        left_side, right_side, (((1,), (0,)), ((), ())), preferred_element_type=F32
    )


def nt(left_side, right_side):
    return lax.dot_general(
        left_side, right_side, (((1,), (1,)), ((), ())), preferred_element_type=F32
    )


def tn(left_side, right_side):
    return lax.dot_general(
        left_side, right_side, (((0,), (0,)), ((), ())), preferred_element_type=F32
    )


def call(body, grid, in_specs, out_specs, out_shape, name, scratch=()):
    return pl.pallas_call(
        body,
        grid=grid,
        in_specs=in_specs,
        out_specs=out_specs,
        out_shape=out_shape,
        scratch_shapes=list(scratch),
        compiler_params=pltpu.CompilerParams(vmem_limit_bytes=VMEM_LIMIT),
        name=name,
    )


def struct(shape, dtype):
    return jax.ShapeDtypeStruct(shape, dtype)


def rows_spec(rows, width):
    return pl.BlockSpec((1, rows, width), lambda i, j: (i, j, 0))


def clip_spec(count, width):
    return pl.BlockSpec((1, count, width), lambda i, j: (i, 0, 0))


def whole_spec(shape):
    return pl.BlockSpec(shape, lambda *_: (0,) * len(shape))


def row_block(frames):
    for parts in (2, 3, 4, 6):
        if frames % (16 * parts) == 0:
            return frames // parts
    return frames


def add_to(ref, first, value):
    @pl.when(first)
    def _():
        ref[...] = value

    @pl.when(jnp.logical_not(first))
    def _():
        ref[...] += value


def span_of(rows):
    start = (pl.program_id(0) * pl.num_programs(1) + pl.program_id(1)) * rows
    return pl.ds(pl.multiple_of(start, rows), rows)


def clear_at(first, *refs):
    @pl.when(first)
    def _():
        for ref in refs:
            ref[...] = jnp.zeros_like(ref)


def column_sum(value):
    return jnp.sum(value, axis=0, keepdims=True)


def qkv_kernel(x_ref, mod_ref, w_ref, out_ref):
    normed, _ = normalize(x_ref[0].astype(F32))
    first_in = (normed * (1.0 + mod_ref[0, 1:2]) + mod_ref[0, 0:1]).astype(BF)
    out_ref[0] = nn(first_in, w_ref[...]).astype(BF)


def qkv_forward(latents, mod, weight):
    clips, frames, width = latents.shape
    rows = row_block(frames)
    wide = weight.shape[1]
    return call(
        qkv_kernel,
        (clips, frames // rows),
        [rows_spec(rows, width), clip_spec(9, width), whole_spec(weight.shape)],
        rows_spec(rows, wide),
        struct((clips, frames, wide), BF),
        "qkv_forward",
    )(latents, mod, weight)


def head_lanes():
    lane = lax.broadcasted_iota(jnp.int32, (1, 2 * HD), 1)
    return lane, lane < HD


def usable_bias(length, count):
    row = lax.broadcasted_iota(jnp.int32, (count, 2 * HD), 0)
    return jnp.where(row < length, 0.0, -1e30).astype(BF)


def attend_kernel(*refs, masked):
    if masked:
        len_ref, q_ref, k_ref, v_ref, o_ref, l_ref = refs
    else:
        q_ref, k_ref, v_ref, o_ref, l_ref = refs
    lane, low = head_lanes()
    for pair in range(l_ref.shape[1]):
        columns = slice(pair * 2 * HD, (pair + 1) * 2 * HD)
        length = len_ref[pl.program_id(0)] if masked else None
        attend_pair(
            lane,
            low,
            length,
            q_ref[0, :, columns],
            k_ref[0, :, columns],
            v_ref[0, :, columns],
            o_ref.at[0, :, columns],
            l_ref.at[0, pair],
        )


def attend_pair(lane, low, length, q, k, v, o_ref, l_ref):
    masked = length is not None
    scaled = q * jnp.asarray(HD**-0.5, BF)
    one = jnp.ones((), BF)
    zero = jnp.zeros((), BF)
    values = [jnp.where(low, v, one), jnp.where(low, one, v)]
    if masked:
        bias = usable_bias(length, k.shape[0])
        tag = jnp.where(lane % HD == 0, one, zero)
        queries = [jnp.where(low, scaled, tag), jnp.where(low, tag, scaled)]
        keys = [jnp.where(low, k, bias), jnp.where(low, bias, k)]
    else:
        queries = [jnp.where(low, scaled, zero), jnp.where(low, zero, scaled)]
        keys = [k, k]
    tops, mixes = [], []
    for head in range(2):
        scores = nt(queries[head], keys[head])
        top = jnp.max(scores, axis=1, keepdims=True)
        mixes.append(nn(jnp.exp(scores - top).astype(BF), values[head]))
        tops.append(top)
    total = jnp.where(low, mixes[1], mixes[0])
    l_ref[...] = jnp.where(low, tops[1], tops[0]) + jnp.log(total)
    o_ref[...] = (jnp.where(low, mixes[0], mixes[1]) / pltpu.roll(total, HD, 1)).astype(BF)


def pair_spec(rows, offset, pairs):
    return pl.BlockSpec((1, rows, 2 * HD * pairs), lambda i, j: (i, 0, j + offset // pairs))


def lse_spec(rows, pairs):
    return pl.BlockSpec((1, pairs, rows, 2 * HD), lambda i, j: (i, j, 0, 0))


def attend_forward(queries, key_offset, keyvals, value_offset, lengths, name, pairs=1):
    clips, frames = queries.shape[:2]
    slots = keyvals.shape[1]
    groups = HEADS // 2
    masked = lengths is not None
    specs = [
        pair_spec(frames, 0, pairs),
        pair_spec(slots, key_offset, pairs),
        pair_spec(slots, value_offset, pairs),
    ]
    args = [queries, keyvals, keyvals]
    if masked:
        specs.insert(0, pl.BlockSpec(memory_space=pltpu.SMEM))
        args.insert(0, lengths)
    return call(
        functools.partial(attend_kernel, masked=masked),
        (clips, groups // pairs),
        specs,
        [pair_spec(frames, 0, pairs), lse_spec(frames, pairs)],
        [struct((clips, frames, D), BF), struct((clips, groups, frames, 2 * HD), F32)],
        name,
    )(*args)


def three_parts(value):
    high = value.astype(BF)
    rest = value - high.astype(F32)
    middle = rest.astype(BF)
    return high, middle, (rest - middle.astype(F32)).astype(BF)


def attend_back_kernel(*refs, masked):
    if masked:
        len_ref, q_ref, k_ref, v_ref, do_ref, o_ref, l_ref, dq_ref, dk_ref, dv_ref = refs
    else:
        q_ref, k_ref, v_ref, do_ref, o_ref, l_ref, dq_ref, dk_ref, dv_ref = refs
    length = len_ref[pl.program_id(0)] if masked else None
    attend_back_step(
        length, q_ref, k_ref, v_ref, do_ref, o_ref, l_ref, dq_ref, dk_ref, dv_ref
    )


def attend_back_step(length, q_ref, k_ref, v_ref, do_ref, o_ref, l_ref, dq_ref, dk_ref, dv_ref):
    lane, low = head_lanes()
    for pair in range(l_ref.shape[1]):
        columns = slice(pair * 2 * HD, (pair + 1) * 2 * HD)
        attend_back_pair(
            lane,
            low,
            length,
            q_ref[0, :, columns],
            k_ref[0, :, columns],
            v_ref[0, :, columns],
            do_ref[0, :, columns],
            o_ref[0, :, columns],
            l_ref[0, pair],
            dq_ref.at[0, :, columns],
            dk_ref.at[0, :, columns],
            dv_ref.at[0, :, columns],
        )


def attend_back_pair(lane, low, length, q, k, v, grad, mixed, lse, dq_ref, dk_ref, dv_ref):
    masked = length is not None
    scaled = q * jnp.asarray(HD**-0.5, BF)
    spot = lane % HD
    one = jnp.ones((), BF)
    zero = jnp.zeros((), BF)
    product = grad.astype(F32) * mixed.astype(F32)
    delta_low = jnp.sum(jnp.where(low, product, 0.0), axis=1, keepdims=True)
    delta_high = jnp.sum(jnp.where(low, 0.0, product), axis=1, keepdims=True)

    def negated(value, last):
        high, middle, rest = three_parts(-value)
        return jnp.where(
            spot == 0,
            high,
            jnp.where(spot == 1, middle, jnp.where(spot == 2, rest, last)),
        )

    tag = jnp.where(spot == 3, one, zero) if masked else zero
    lse_lanes = negated(lse, tag)
    delta_lanes = negated(jnp.where(low, delta_high, delta_low), zero)
    ones = jnp.broadcast_to(jnp.where(spot < 3, one, zero), k.shape)
    key_lanes = ones
    if masked:
        bias = usable_bias(length, k.shape[0])
        key_lanes = jnp.where(spot == 3, bias, ones)
    transposed = k.astype(F32).T.astype(BF)
    grad_queries, grad_keys, grad_values = [], [], []
    for head in range(2):

        def merge(own, other):
            return jnp.where(low, own, other) if head == 0 else jnp.where(low, other, own)

        probability = jnp.exp(nt(merge(k, key_lanes), merge(scaled, lse_lanes)))
        centred = nt(merge(v, ones), merge(grad, delta_lanes))
        grad_scores = (probability * centred).astype(BF)
        grad_values.append(nn(probability.astype(BF), grad))
        grad_keys.append(nn(grad_scores, scaled))
        grad_queries.append(nn(transposed[HD * head : HD * (head + 1)], grad_scores))
    dv_ref[...] = jnp.where(low, grad_values[0], grad_values[1]).astype(BF)
    dk_ref[...] = jnp.where(low, grad_keys[0], grad_keys[1]).astype(BF)
    dq_ref[...] = (jnp.concatenate(grad_queries, axis=0).T * HD**-0.5).astype(BF)


def attend_backward(
    queries, key_offset, keyvals, value_offset, lengths, grad, mixed, lse, name, pairs=1
):
    clips, frames = queries.shape[:2]
    slots = keyvals.shape[1]
    groups = HEADS // 2
    masked = lengths is not None
    specs = [
        pair_spec(frames, 0, pairs),
        pair_spec(slots, key_offset, pairs),
        pair_spec(slots, value_offset, pairs),
        pair_spec(frames, 0, pairs),
        pair_spec(frames, 0, pairs),
        lse_spec(frames, pairs),
    ]
    args = [queries, keyvals, keyvals, grad, mixed, lse]
    if masked:
        specs.insert(0, pl.BlockSpec(memory_space=pltpu.SMEM))
        args.insert(0, lengths)
    return call(
        functools.partial(attend_back_kernel, masked=masked),
        (clips, groups // pairs),
        specs,
        [pair_spec(frames, 0, pairs), pair_spec(slots, 0, pairs), pair_spec(slots, 0, pairs)],
        [
            struct((clips, frames, D), BF),
            struct((clips, slots, D), BF),
            struct((clips, slots, D), BF),
        ],
        name,
    )(*args)


def after_self_kernel(o_ref, x_ref, mod_ref, wo_ref, bo_ref, wq_ref, z_ref, h_ref, q_ref):
    branch = nn(o_ref[0], wo_ref[...]) + bo_ref[...]
    hidden = x_ref[0].astype(F32) + mod_ref[0, 2:3] * branch
    normed, _ = normalize(hidden)
    second_in = (normed * (1.0 + mod_ref[0, 4:5]) + mod_ref[0, 3:4]).astype(BF)
    z_ref[0] = branch.astype(BF)
    h_ref[0] = hidden
    q_ref[0] = nn(second_in, wq_ref[...]).astype(BF)


def after_self(mixed, latents, mod, weight, bias, query_weight):
    clips, frames, width = latents.shape
    rows = row_block(frames)
    spec = rows_spec(rows, width)
    square = whole_spec((width, width))
    return call(
        after_self_kernel,
        (clips, frames // rows),
        [spec, spec, clip_spec(9, width), square, whole_spec((1, width)), square],
        [spec, spec, spec],
        [
            struct(latents.shape, BF),
            struct(latents.shape, F32),
            struct(latents.shape, BF),
        ],
        "after_self",
    )(mixed, latents, mod, weight, bias, query_weight)


def after_cross_kernel(o_ref, h_ref, mod_ref, wo_ref, bo_ref, z_ref, out_ref):
    branch = nn(o_ref[0], wo_ref[...]) + bo_ref[...]
    z_ref[0] = branch.astype(BF)
    out_ref[0] = h_ref[0] + mod_ref[0, 5:6] * branch


def after_cross(mixed, hidden, mod, weight, bias):
    clips, frames, width = hidden.shape
    rows = row_block(frames)
    spec = rows_spec(rows, width)
    return call(
        after_cross_kernel,
        (clips, frames // rows),
        [
            spec,
            spec,
            clip_spec(9, width),
            whole_spec((width, width)),
            whole_spec((1, width)),
        ],
        [spec, spec],
        [struct(hidden.shape, BF), struct(hidden.shape, F32)],
        "after_cross",
    )(mixed, hidden, mod, weight, bias)


GELU_ROOT = math.sqrt(2.0 / math.pi)


def feed_kernel(
    h_ref,
    dy_ref,
    mod_ref,
    up_ref,
    upb_ref,
    down_ref,
    downb_ref,
    out_ref,
    dh_ref,
    dup_ref,
    ddown_ref,
    dupb_ref,
    ddownb_ref,
    sums_ref,
    in_s,
    int_s,
    dz_s,
    dzt_s,
    z_s,
    act_s,
    du_s,
    *,
    clips,
    frames,
    rows,
):
    step = pl.program_id(0)
    last = pl.num_programs(0) - 1
    spans = [
        (clip, start, clip * frames + start)
        for clip in range(clips)
        for start in range(0, frames, rows)
    ]

    @pl.when(step == 0)
    def _():
        bias_sum = jnp.zeros((1, h_ref.shape[2]), F32)
        for clip, start, at in spans:
            normed, _ = normalize(h_ref[clip, start : start + rows])
            third_in = normed * (1.0 + mod_ref[clip, 7:8]) + mod_ref[clip, 6:7]
            dz = (mod_ref[clip, 8:9] * dy_ref[clip, start : start + rows].astype(F32)).astype(BF)
            in_s[at : at + rows] = third_in.astype(BF)
            dz_s[at : at + rows] = dz
            bias_sum += column_sum(dz.astype(F32))
        ddownb_ref[...] = bias_sum
        int_s[...] = in_s[...].T
        dzt_s[...] = dz_s[...].T
        z_s[...] = jnp.zeros_like(z_s)
        dh_ref[...] = jnp.zeros_like(dh_ref)

    up, down = up_ref[...], down_ref[...]

    per = frames // rows

    def one(index):
        at = pl.multiple_of(index * rows, rows)
        here = pl.ds(at, rows)
        hidden = nn(in_s[here], up) + upb_ref[...]
        square = hidden * hidden
        tanh = jnp.tanh(hidden * (GELU_ROOT + (GELU_ROOT * 0.044715) * square))
        half = 0.5 + 0.5 * tanh
        lifted = hidden * half
        activated = lifted.astype(BF)
        slope = half + lifted * (1.0 - tanh) * (
            GELU_ROOT + (GELU_ROOT * 3 * 0.044715) * square
        )
        grad_hidden = (nt(dz_s[here], down) * slope).astype(BF)
        z_s[here] += nn(activated, down)
        spot = pl.ds(pl.multiple_of(index % per * rows, rows), rows)
        dh_ref[index // per, spot] += nt(grad_hidden, up)
        act_s[here] = activated
        du_s[here] = grad_hidden

    def one_clip(clip, _):
        for part in range(per):
            one(clip * per + part)
        return 0

    lax.fori_loop(0, clips, one_clip, 0)
    dup_ref[...] = nn(int_s[...], du_s[...]).astype(BF)
    ddown_ref[...] = nn(dzt_s[...], act_s[...]).T.astype(BF)
    dupb_ref[...] = column_sum(du_s[...].astype(F32))

    @pl.when(step == last)
    def _():
        for clip in range(clips):
            sums = None
            for start in range(0, frames, rows):
                at = clip * frames + start
                block = slice(start, start + rows)
                hidden = h_ref[clip, block]
                dy = dy_ref[clip, block].astype(F32)
                branch = z_s[at : at + rows] + downb_ref[...]
                out_ref[clip, block] = (hidden + mod_ref[clip, 8:9] * branch).astype(BF)
                normed, inverse = normalize(hidden)
                grad_in = dh_ref[clip, block]
                dh_ref[clip, block] = dy + norm_back(
                    normed, inverse, grad_in * (1.0 + mod_ref[clip, 7:8])
                )
                here = [
                    column_sum(grad_in),
                    column_sum(grad_in * normed),
                    column_sum(dy * branch),
                ]
                sums = here if sums is None else [a + b for a, b in zip(sums, here)]
            for index in range(3):
                sums_ref[clip, index : index + 1] = sums[index]


def feed(hidden, cotangent, mod, up, up_bias, down, down_bias, block=768):
    clips, frames, width = hidden.shape
    inner = up.shape[1]
    rows = row_block(frames)
    tokens = clips * frames

    def once(shape):
        return pl.BlockSpec(
            shape, lambda j: (0,) * len(shape), pipeline_mode=pl.Buffered(1)
        )

    def columns(count):
        return pl.BlockSpec((count, block), lambda j: (0, j))

    lines = pl.BlockSpec((block, width), lambda j: (j, 0))
    cube = once((clips, frames, width))
    return call(
        functools.partial(feed_kernel, clips=clips, frames=frames, rows=rows),
        (inner // block,),
        [
            cube,
            cube,
            once(mod.shape),
            columns(width),
            columns(1),
            lines,
            once((1, width)),
        ],
        [
            cube,
            cube,
            columns(width),
            lines,
            columns(1),
            once((1, width)),
            once((clips, 3, width)),
        ],
        [
            struct(hidden.shape, BF),
            struct(hidden.shape, F32),
            struct(up.shape, BF),
            struct(down.shape, BF),
            struct((1, inner), F32),
            struct((1, width), F32),
            struct((clips, 3, width), F32),
        ],
        "feed",
        [
            pltpu.VMEM((tokens, width), BF),
            pltpu.VMEM((width, tokens), BF),
            pltpu.VMEM((tokens, width), BF),
            pltpu.VMEM((width, tokens), BF),
            pltpu.VMEM((tokens, width), F32),
            pltpu.VMEM((tokens, block), BF),
            pltpu.VMEM((tokens, block), BF),
        ],
    )(hidden, cotangent, mod, up, up_bias, down, down_bias)


def ends():
    i, j = pl.program_id(0), pl.program_id(1)
    first = (i == 0) & (j == 0)
    last = (i == pl.num_programs(0) - 1) & (j == pl.num_programs(1) - 1)
    return j == 0, first, last


def before_cross_kernel(
    dh_ref, z_ref, o_ref, mod_ref, w_ref, do_ref, dw_ref, db_ref, sums_ref, ot_s, dz_s
):
    new_clip, first, last = ends()
    clear_at(new_clip, sums_ref)
    clear_at(first, db_ref)
    dh = dh_ref[0]
    here = span_of(dh.shape[0])
    dz = (mod_ref[0, 5:6] * dh).astype(BF)
    dz_s[here] = dz
    ot_s[here] = o_ref[0]
    sums_ref[0] += column_sum(dh * z_ref[0].astype(F32))
    db_ref[...] += column_sum(dz.astype(F32))
    do_ref[0] = nt(dz, w_ref[...]).astype(BF)

    @pl.when(last)
    def _():
        dw_ref[...] = tn(ot_s[...], dz_s[...]).astype(BF)


def before_cross(dh, branch, mixed, mod, weight):
    clips, frames, width = dh.shape
    rows = row_block(frames)
    spec = rows_spec(rows, width)
    square = whole_spec((width, width))
    return call(
        before_cross_kernel,
        (clips, frames // rows),
        [spec, spec, spec, clip_spec(9, width), square],
        [spec, square, whole_spec((1, width)), clip_spec(1, width)],
        [
            struct(dh.shape, BF),
            struct((width, width), BF),
            struct((1, width), F32),
            struct((clips, 1, width), F32),
        ],
        "before_cross",
        [pltpu.VMEM((clips * frames, width), BF)] * 2,
    )(dh, branch, mixed, mod, weight)


def before_self_kernel(
    dq_ref,
    h_ref,
    dh_ref,
    z_ref,
    o_ref,
    mod_ref,
    wq_ref,
    wo_ref,
    out_ref,
    do_ref,
    dwq_ref,
    dwo_ref,
    db_ref,
    sums_ref,
    in_s,
    dq_s,
    o_s,
    dz_s,
):
    new_clip, first, last = ends()
    clear_at(new_clip, sums_ref)
    clear_at(first, db_ref)
    here = span_of(dq_ref.shape[1])
    normed, inverse = normalize(h_ref[0])
    in_s[here] = (normed * (1.0 + mod_ref[0, 4:5]) + mod_ref[0, 3:4]).astype(BF)
    grad_query = dq_ref[0]
    dq_s[here] = grad_query
    o_s[here] = o_ref[0]
    grad_in = nt(grad_query, wq_ref[...])
    dh = dh_ref[0] + norm_back(normed, inverse, grad_in * (1.0 + mod_ref[0, 4:5]))
    out_ref[0] = dh
    dz = (mod_ref[0, 2:3] * dh).astype(BF)
    dz_s[here] = dz
    sums_ref[0] += jnp.concatenate(
        [
            column_sum(grad_in),
            column_sum(grad_in * normed),
            column_sum(dh * z_ref[0].astype(F32)),
        ],
        axis=0,
    )
    db_ref[...] += column_sum(dz.astype(F32))
    do_ref[0] = nt(dz, wo_ref[...]).astype(BF)

    @pl.when(last)
    def _():
        dwq_ref[...] = tn(in_s[...], dq_s[...]).astype(BF)
        dwo_ref[...] = tn(o_s[...], dz_s[...]).astype(BF)


def before_self(grad_query, hidden, dh, branch, mixed, mod, query_weight, weight):
    clips, frames, width = dh.shape
    rows = row_block(frames)
    spec = rows_spec(rows, width)
    square = whole_spec((width, width))
    return call(
        before_self_kernel,
        (clips, frames // rows),
        [spec, spec, spec, spec, spec, clip_spec(9, width), square, square],
        [spec, spec, square, square, whole_spec((1, width)), clip_spec(3, width)],
        [
            struct(dh.shape, F32),
            struct(dh.shape, BF),
            struct((width, width), BF),
            struct((width, width), BF),
            struct((1, width), F32),
            struct((clips, 3, width), F32),
        ],
        "before_self",
        [pltpu.VMEM((clips * frames, width), BF)] * 4,
    )(grad_query, hidden, dh, branch, mixed, mod, query_weight, weight)


def input_kernel(
    dq_ref, dk_ref, dv_ref, x_ref, dh_ref, mod_ref, w_ref, out_ref, dw_ref, sums_ref, in_s, g_s
):
    new_clip, _, last = ends()
    width = x_ref.shape[2]
    clear_at(new_clip, sums_ref)
    here = span_of(x_ref.shape[1])
    normed, inverse = normalize(x_ref[0].astype(F32))
    in_s[here] = (normed * (1.0 + mod_ref[0, 1:2]) + mod_ref[0, 0:1]).astype(BF)
    grad_in = None
    for index, ref in enumerate((dq_ref, dk_ref, dv_ref)):
        columns = slice(index * width, (index + 1) * width)
        grad = ref[0]
        g_s[here, columns] = grad
        part = nt(grad, w_ref[:, columns])
        grad_in = part if grad_in is None else grad_in + part
    out_ref[0] = (
        dh_ref[0] + norm_back(normed, inverse, grad_in * (1.0 + mod_ref[0, 1:2]))
    ).astype(BF)
    sums_ref[0] += jnp.concatenate(
        [column_sum(grad_in), column_sum(grad_in * normed)], axis=0
    )

    @pl.when(last)
    def _():
        turned = in_s[...].T
        for index in range(3):
            columns = slice(index * width, (index + 1) * width)
            dw_ref[:, columns] = nn(turned, g_s[:, columns]).astype(BF)


def input_back(grads, latents, dh, mod, weight):
    clips, frames, width = dh.shape
    rows = row_block(frames)
    spec = rows_spec(rows, width)
    return call(
        input_kernel,
        (clips, frames // rows),
        [spec] * 5 + [clip_spec(9, width), whole_spec(weight.shape)],
        [spec, whole_spec(weight.shape), clip_spec(2, width)],
        [
            struct(dh.shape, BF),
            struct(weight.shape, BF),
            struct((clips, 2, width), F32),
        ],
        "input_back",
        [
            pltpu.VMEM((clips * frames, width), BF),
            pltpu.VMEM((clips * frames, weight.shape[1]), BF),
        ],
    )(*grads, latents, dh, mod, weight)


def block_pass(latents, captions, lengths, cotangent, mod, triple_weight, front, back):
    triple, mixed_one, lse_one, weights = front(latents, mod, triple_weight)
    (
        output_weight,
        output_bias,
        cross_query,
        cross_keyval,
        cross_output,
        cross_bias,
        up_weight,
        up_bias,
        down_weight,
        down_bias,
    ) = weights
    clips, frames, width = latents.shape
    slots = captions.shape[1]
    groups = HEADS // 2
    caption_flat = captions.reshape(clips * slots, captions.shape[2])
    branch_one, hidden_one, cross_queries = after_self(
        mixed_one, latents, mod, output_weight, output_bias, cross_query
    )
    pairs = (
        jnp.dot(caption_flat, cross_keyval, preferred_element_type=F32)
        .astype(BF)
        .reshape(clips, slots, 2 * width)
    )
    mixed_two, lse_two = attend_forward(cross_queries, 0, pairs, groups, lengths, "cross_forward")
    branch_two, hidden_two = after_cross(mixed_two, hidden_one, mod, cross_output, cross_bias)
    output, dh_two, grad_up, grad_down, grad_up_bias, grad_down_bias, sums_three = feed(
        hidden_two, cotangent, mod, up_weight, up_bias, down_weight, down_bias
    )
    grad_mixed_two, grad_cross_output, grad_cross_bias, gate_two = before_cross(
        dh_two, branch_two, mixed_two, mod, cross_output
    )
    grad_cq, grad_ck, grad_cv = attend_backward(
        cross_queries,
        0,
        pairs,
        groups,
        lengths,
        grad_mixed_two,
        mixed_two,
        lse_two,
        "cross_back",
        2,
    )
    grad_pairs = jnp.concatenate([grad_ck, grad_cv], axis=-1).reshape(clips * slots, 2 * width)
    grad_keyval = jnp.dot(caption_flat.T, grad_pairs, preferred_element_type=F32).astype(BF)
    dh_one, grad_mixed_one, grad_cross_query, grad_output, grad_output_bias, sums_two = before_self(
        grad_cq, hidden_one, dh_two, branch_one, mixed_one, mod, cross_query, output_weight
    )
    gradients = [
        grad_output,
        grad_output_bias,
        grad_cross_query,
        grad_keyval,
        grad_cross_output,
        grad_cross_bias,
        grad_up,
        grad_up_bias,
        grad_down,
        grad_down_bias,
    ]
    input_grad, grad_triple, sums_one, rest = back(
        triple, grad_mixed_one, mixed_one, lse_one, latents, dh_one, mod, triple_weight, gradients
    )
    grad_mod = jnp.concatenate(
        [sums_one, sums_two[:, 2:], sums_two[:, :2], gate_two, sums_three], axis=1
    ).astype(BF)
    return output, input_grad, grad_mod, grad_triple, gradients, rest


def plain_front(weights, latents, mod, triple_weight):
    groups = HEADS // 2
    triple = qkv_forward(latents, mod, triple_weight)
    mixed, lse = attend_forward(triple, groups, triple, 2 * groups, None, "self_forward", 2)
    return triple, mixed, lse, weights


def plain_back(triple, grad_mixed, mixed, lse, latents, dh, mod, triple_weight, gradients):
    groups = HEADS // 2
    grads = attend_backward(
        triple, groups, triple, 2 * groups, None, grad_mixed, mixed, lse, "self_back", 2
    )
    return *input_back(grads, latents, dh, mod, triple_weight), None


LANE = 128
TILE = 16


def linear_layout():
    spots = []
    offset = 0
    for shape in layout_sizes():
        number = math.prod(shape) // LANE
        spots.append((offset, number, shape))
        offset += number
    return spots


class Group:
    def __init__(self, devices, inner, share, first, last):
        self.devices, self.share, self.first, self.last = devices, share, first, last
        self.padded = -(-share // TILE) * TILE
        owners, total = {}, 0
        for owner in range(first // share, (last - 1) // share + 1):
            low = max(first - owner * share, 0) // TILE
            high = -(-min(last - owner * share, share) // TILE)
            owners[owner] = [low, high]
            total += high - low
        self.tiles = 2 * -(-total // (2 * devices))
        self.chunk = self.tiles * TILE
        self.half = self.chunk // 2
        self.folds = next(
            n
            for n in range(1, 99)
            if self.half % (n * TILE) == 0 and self.half // n <= 512
        )
        room = [self.tiles] * devices
        self.pieces = []

        def give(owner, device):
            low, high = owners[owner]
            take = min(high - low, room[device])
            if take > 0:
                place = self.tiles - room[device]
                self.pieces.append((owner, device, low * TILE, place * TILE, take * TILE))
                room[device] -= take
                owners[owner][0] += take

        for flip in (0, 2 * inner, inner):
            for owner in owners:
                give(owner, owner ^ flip)
        for owner in owners:
            while owners[owner][0] < owners[owner][1]:
                give(owner, max(range(devices), key=lambda device: room[device]))

    def find(self, row):
        owner, at = divmod(row, self.share)
        for holder, device, start, place, count in self.pieces:
            if holder == owner and start <= at < start + count:
                return device, place + at - start, min(self.share, start + count) - at
        raise ValueError(row)

    def segments(self, start, count):
        found = []
        row = start
        while row < start + count:
            chunk, place, left = self.find(row)
            take = min(left, start + count - row)
            found.append((chunk, place, row, take))
            row += take
        return found

    def moves(self):
        return self.pieces


def unpack_kernel(*refs, plan, indices, step):
    n = len(indices)
    spots = linear_layout()
    g_ref, outs, rest = refs[0], refs[1 : 1 + n], refs[1 + n :]
    lin, in_sem, out_sem = rest[0], rest[1], rest[2]
    stages, results = rest[3 : 3 + n], rest[3 + n :]
    loads = []
    for which, index in enumerate(indices):
        offset, number, _ = spots[index]
        place = 0
        mine = []
        for slot, (chunk, row, at, take) in enumerate(plan.segments(offset, number)):
            low = row // TILE * TILE
            high = -(-(row + take) // TILE) * TILE
            copy = pltpu.make_async_copy(
                g_ref.at[chunk, pl.ds(low, high - low)],
                stages[which].at[pl.ds(place, high - low)],
                in_sem.at[which, slot],
            )
            copy.start()
            mine.append((copy, place, row - low, high - low, at - offset, take))
            place += high - low
        loads.append(mine)
    stores = []
    for which, index in enumerate(indices):
        offset, number, shape = spots[index]
        for copy, place, skip, size, at, take in loads[which]:
            copy.wait()
            first = stages[which][place : place + TILE].astype(F32)
            lin[at : at + TILE - skip] = first[skip:]
            blocks, tail = divmod(size - TILE, step)

            def body(i, _, place=place, at=at, skip=skip, which=which):
                source = pl.multiple_of(place + TILE + i * step, TILE)
                lin[pl.ds(at + TILE - skip + i * step, step)] = stages[which][
                    pl.ds(source, step)
                ].astype(F32)
                return 0

            lax.fori_loop(0, blocks, body, 0)
            if tail:
                source = place + TILE + blocks * step
                target = at + TILE - skip + blocks * step
                lin[target : target + tail] = stages[which][source : source + tail].astype(F32)
        if len(shape) == 1:
            for c in range(number):
                results[which][0:1, c * LANE : (c + 1) * LANE] = lin[c : c + 1]
        else:
            high, wide = shape
            count = wide // LANE
            rows = 64

            def turn(i, _, which=which, count=count):
                top = pl.multiple_of(i * rows, rows)
                for c in range(count):
                    results[which][pl.ds(top, rows), c * LANE : (c + 1) * LANE] = lin[
                        pl.ds(top * count + c, rows, stride=count)
                    ].astype(BF)
                return 0

            lax.fori_loop(0, high // rows, turn, 0)
        copy = pltpu.make_async_copy(results[which], outs[which], out_sem.at[which])
        copy.start()
        stores.append(copy)
    for copy in stores:
        copy.wait()


def unpack_weights(gathered, plan, indices, step=128):
    spots = linear_layout()
    stage_shapes, result_shapes, most, tallest = [], [], 0, 0
    for index in indices:
        offset, number, shape = spots[index]
        found = plan.segments(offset, number)
        size = sum(-(-(r + t) // TILE) * TILE - r // TILE * TILE for _, r, _, t in found)
        stage_shapes.append(pltpu.VMEM((size, LANE), BF))
        most = max(most, len(found))
        tallest = max(tallest, number)
        result_shapes.append((shape, BF) if len(shape) == 2 else ((1, shape[0]), F32))
    anywhere = pl.BlockSpec(memory_space=pl.ANY)
    return pl.pallas_call(
        functools.partial(unpack_kernel, plan=plan, indices=indices, step=step),
        in_specs=[anywhere],
        out_specs=[anywhere] * len(indices),
        out_shape=[jax.ShapeDtypeStruct(s, t) for s, t in result_shapes],
        scratch_shapes=[
            pltpu.VMEM((tallest + 2 * TILE, LANE), F32),
            pltpu.SemaphoreType.DMA((len(indices), most)),
            pltpu.SemaphoreType.DMA((len(indices),)),
        ]
        + stage_shapes
        + [pltpu.VMEM(s, t) for s, t in result_shapes],
        compiler_params=pltpu.CompilerParams(vmem_limit_bytes=VMEM_LIMIT),
        name="unpack",
    )(gathered)


def pack_kernel(*refs, plan, indices, step):
    n = len(indices)
    spots = linear_layout()
    ins, out_ref, rest = refs[:n], refs[n], refs[n + 1 :]
    lin, stage, in_sem, out_sem = rest[:4]
    held = rest[4:]
    copies = []
    for which in range(n):
        copy = pltpu.make_async_copy(ins[which], held[which], in_sem.at[which])
        copy.start()
        copies.append(copy)
    stores = []
    begin = spots[indices[0]][0]
    total = spots[indices[-1]][0] + spots[indices[-1]][1] - begin
    pieces = plan.segments(begin, total)
    place = 0
    done = -TILE
    lin[0:TILE] = jnp.zeros((TILE, LANE), F32)
    slot = 0
    for which, index in enumerate(indices):
        offset, number, shape = spots[index]
        copies[which].wait()
        if len(shape) == 1:
            for c in range(number):
                lin[TILE + c : TILE + c + 1] = held[which][0:1, c * LANE : (c + 1) * LANE]
        else:
            high, wide = shape
            count = wide // LANE
            rows = 64

            def turn(i, _, which=which, count=count):
                top = pl.multiple_of(i * rows, rows)
                for c in range(count):
                    lin[pl.ds(TILE + top * count + c, rows, stride=count)] = held[which][
                        pl.ds(top, rows), c * LANE : (c + 1) * LANE
                    ].astype(F32)
                return 0

            lax.fori_loop(0, high // rows, turn, 0)
        low, high_row = offset - begin, offset - begin + number
        last = which == n - 1
        while slot < len(pieces):
            chunk, row, at, take = pieces[slot]
            at -= begin
            head = row - row // TILE * TILE
            start, stop = at - head, at + take
            ceil = start + -(-(stop - start) // TILE) * TILE
            first = max(start, done)
            whole = stop <= high_row
            end = ceil if whole else start + (high_row - start) // TILE * TILE
            if end > first:
                base = row - head + first - start
                blocks, tail = divmod(end - first, step)
                shift = TILE + first - low

                def body(i, _, place=place, shift=shift):
                    target = pl.multiple_of(place + i * step, TILE)
                    stage[pl.ds(target, step)] = lin[pl.ds(shift + i * step, step)].astype(BF)
                    return 0

                lax.fori_loop(0, blocks, body, 0)
                if tail:
                    source = shift + blocks * step
                    target = place + blocks * step
                    stage[target : target + tail] = lin[source : source + tail].astype(BF)
                copy = pltpu.make_async_copy(
                    stage.at[pl.ds(place, end - first)],
                    out_ref.at[chunk, pl.ds(base, end - first)],
                    out_sem.at[len(stores)],
                )
                copy.start()
                stores.append(copy)
                place += end - first
                done = end
            if not whole:
                break
            done = stop if slot + 1 == len(pieces) else min(done, stop)
            slot += 1
        if not last:
            lin[0:TILE] = lin[number : number + TILE]
    for copy in stores:
        copy.wait()


def pack_grads(grads, plan, indices, step=128):
    spots = linear_layout()
    tallest = max(spots[i][1] for i in indices)
    begin = spots[indices[0]][0]
    total = spots[indices[-1]][0] + spots[indices[-1]][1] - begin
    count = len(plan.segments(begin, total))
    anywhere = pl.BlockSpec(memory_space=pl.ANY)
    return pl.pallas_call(
        functools.partial(pack_kernel, plan=plan, indices=indices, step=step),
        in_specs=[anywhere] * len(indices),
        out_specs=anywhere,
        out_shape=jax.ShapeDtypeStruct((plan.devices, plan.chunk, LANE), BF),
        scratch_shapes=[
            pltpu.VMEM((tallest + 2 * TILE, LANE), F32),
            pltpu.VMEM((total + 2 * TILE * (count + len(indices)), LANE), BF),
            pltpu.SemaphoreType.DMA((len(indices),)),
            pltpu.SemaphoreType.DMA((count + len(indices),)),
        ]
        + [pltpu.VMEM(g.shape, g.dtype) for g in grads],
        compiler_params=pltpu.CompilerParams(vmem_limit_bytes=VMEM_LIMIT),
        name="pack",
    )(*grads)


MESH = pl.DeviceIdType.MESH


def place_of():
    dp, fs = lax.axis_index("dp"), lax.axis_index("fsdp")
    return dp, fs, dp // 2, dp % 2, fs // 2, fs % 2


def meet_all(me, devices, inner):
    barrier = pltpu.get_barrier_semaphore()

    def greet(i, _):
        other = (me + i) % devices
        pl.semaphore_signal(
            barrier, inc=1, device_id=(other // inner, other % inner), device_id_type=MESH
        )
        return 0

    lax.fori_loop(1, devices, greet, 0)
    pl.semaphore_wait(barrier, devices - 1)


class Trade:
    def __init__(self, source, target, own_sem, send_sem, recv_sem, group, inner, senders, receivers):
        self.source, self.target, self.own_sem = source, target, own_sem
        self.send_sem, self.recv_sem = send_sem, recv_sem
        self.devices, self.inner = group.devices, inner
        self.senders, self.receivers = senders, receivers
        self.me = lax.axis_index("dp") * inner + lax.axis_index("fsdp")
        self.many = len(source.shape) == 3

    def piece(self, target):
        return self.source.at[target] if self.many else self.source

    def copy(self, source, target):
        return pltpu.make_async_remote_copy(
            src_ref=self.piece(target),
            dst_ref=self.target.at[source],
            send_sem=self.send_sem.at[target],
            recv_sem=self.recv_sem.at[source],
            device_id=(target // self.inner, target % self.inner),
            device_id_type=MESH,
        )

    def own(self):
        return pltpu.make_async_copy(
            self.piece(self.me), self.target.at[self.me], self.own_sem
        )

    def each(self, act):
        def body(i, _):
            act((self.me + i) % self.devices)
            return 0

        lax.fori_loop(1, self.devices, body, 0)

    def both(self):
        return (self.me < self.senders) & (self.me < self.receivers)

    def start(self):
        pl.when(self.both())(lambda: self.own().start())

        def act(other):
            ok = (self.me < self.senders) & (other < self.receivers)
            pl.when(ok)(lambda: self.copy(self.me, other).start())

        self.each(act)

    def wait(self):
        pl.when(self.both())(lambda: self.own().wait())

        def landed(other):
            ok = (other < self.senders) & (self.me < self.receivers)
            pl.when(ok)(lambda: self.copy(other, other).wait_recv())

        def gone(other):
            ok = (self.me < self.senders) & (other < self.receivers)
            pl.when(ok)(lambda: self.copy(self.me, other).wait_send())

        self.each(landed)
        self.each(gone)


def when_all(conditions):
    total = None
    for condition in conditions:
        if condition is not None:
            total = condition if total is None else total & condition
    return total


def guarded(condition, body):
    if condition is None:
        body()
    else:
        pl.when(condition)(body)


class Deal:
    def __init__(self, group, source, target, send_sem, recv_sem, inner, back):
        self.source, self.target, self.back = source, target, back
        self.send_sem, self.recv_sem, self.inner = send_sem, recv_sem, inner
        self.me = lax.axis_index("dp") * inner + lax.axis_index("fsdp")
        self.moves = []
        for owner, device, row, place, count in group.moves():
            if back:
                self.moves.append((device, owner, place, row, count))
            else:
                self.moves.append((owner, device, row, place, count))

    def copy(self, move):
        source, target, start, place, count = move
        out = [m for m in self.moves if m[0] == source].index(move)
        into = [m for m in self.moves if m[1] == target].index(move)
        from_ref = self.source.at[pl.ds(start, count)]
        to_ref = self.target.at[pl.ds(place, count)]
        if source == target:
            return pltpu.make_async_copy(from_ref, to_ref, self.recv_sem.at[into])
        return pltpu.make_async_remote_copy(
            src_ref=from_ref,
            dst_ref=to_ref,
            send_sem=self.send_sem.at[out],
            recv_sem=self.recv_sem.at[into],
            device_id=(target // self.inner, target % self.inner),
            device_id_type=MESH,
        )

    def each(self, key, act):
        for device in sorted({m[key] for m in self.moves}):
            mine = [m for m in self.moves if m[key] == device]

            @pl.when(self.me == device)
            def _(mine=mine):
                for move in mine:
                    act(move)

    def start(self):
        self.each(0, lambda move: self.copy(move).start())

    def landed(self):
        def act(move):
            if move[0] == move[1]:
                self.copy(move).wait()
            else:
                self.copy(move).wait_recv()

        self.each(1, act)

    def gone(self):
        def act(move):
            if move[0] != move[1]:
                self.copy(move).wait_send()

        self.each(0, act)

    @staticmethod
    def semaphores(group, back):
        sends = recvs = 0
        for device in range(group.devices):
            sends = max(sends, sum(1 for m in group.moves() if m[1 if back else 0] == device))
            recvs = max(recvs, sum(1 for m in group.moves() if m[0 if back else 1] == device))
        dma = pltpu.SemaphoreType.DMA
        return [dma((sends,)), dma((recvs,))]


def remote_call(body, in_specs, out_specs, out_shape, scratch, collective, name, grid=()):
    return pl.pallas_call(
        body,
        grid=grid,
        in_specs=in_specs,
        out_specs=out_specs,
        out_shape=out_shape,
        scratch_shapes=scratch,
        compiler_params=pltpu.CompilerParams(
            collective_id=collective, has_side_effects=True, vmem_limit_bytes=VMEM_LIMIT
        ),
        name=name,
    )


ANYWHERE = pl.BlockSpec(memory_space=pl.ANY)


def start_kernel(
    step_ref, slot_ref, all_ref, chunk_ref, own_sem, send_sem, recv_sem, deal_send, deal_recv,
    *, group, inner
):
    me = lax.axis_index("dp") * inner + lax.axis_index("fsdp")
    meet_all(me, group.devices, inner)
    deal = Deal(group, slot_ref, chunk_ref, deal_send, deal_recv, inner, False)
    trade = Trade(
        step_ref, all_ref, own_sem, send_sem, recv_sem, group, inner, group.devices, group.devices
    )
    trade.start()
    deal.start()
    trade.wait()
    deal.landed()
    deal.gone()


def start_chunks(steps, slot, group, inner, collective):
    dma = pltpu.SemaphoreType.DMA
    return remote_call(
        functools.partial(start_kernel, group=group, inner=inner),
        [ANYWHERE] * 2,
        [ANYWHERE] * 2,
        [
            jax.ShapeDtypeStruct((group.devices, *steps.shape), steps.dtype),
            jax.ShapeDtypeStruct((group.chunk, LANE), BF),
        ],
        [dma, dma((group.devices,)), dma((group.devices,))] + Deal.semaphores(group, False),
        collective,
        "start_chunks",
    )(steps, slot)


class Gather:
    def __init__(self, group, inner, chunk_ref, out_ref, own_sem, send_sem, recv_sem):
        self.group, self.inner = group, inner
        self.chunk_ref, self.out_ref = chunk_ref, out_ref
        self.send_sem, self.recv_sem = send_sem, recv_sem
        dp, fs, self.y, self.x, self.z, self.c = place_of()
        self.levels = inner // 2
        self.own = pltpu.make_async_copy(chunk_ref, out_ref.at[dp * inner + fs], own_sem)
        self.across = {
            "up": (dp, fs + 2),
            "down": (dp, fs - 2),
            "x": (dp + 1 - 2 * self.x, fs),
            "y": (dp + 2 - 4 * self.y, fs),
            "twin": (dp, fs + 1 - 2 * self.c),
        }
        self.kinds = tuple(self.across)
        self.closing = False

    @staticmethod
    def semaphores(group):
        dma = pltpu.SemaphoreType.DMA
        return [dma, dma((5, group.devices // 2, 2)), dma((group.devices, 2))]

    def copy(self, kind, yy, xx, zz, part, cc=None, mine=False):
        core = self.c if cc is None else cc
        column = yy * 2 + xx
        index = column * self.inner + zz * 2 + core
        rows = pl.ds(part * self.group.half, self.group.half)
        return pltpu.make_async_remote_copy(
            src_ref=self.chunk_ref.at[rows] if mine else self.out_ref.at[index, rows],
            dst_ref=self.out_ref.at[index, rows],
            send_sem=self.send_sem.at[
                self.kinds.index(kind), column * self.levels + zz, part
            ],
            recv_sem=self.recv_sem.at[index, part],
            device_id=self.across[kind],
            device_id_type=MESH,
        )

    def send(self, condition, kind, yy, xx, zz, part, mine=False):
        copy = functools.partial(self.copy, kind, yy, xx, zz, part, mine=mine)
        if self.closing:
            guarded(condition, lambda: copy().wait_send())
        else:
            guarded(condition, lambda: copy().start())

    def arrive(self, condition, yy, xx, zz, part):
        if self.closing:
            return
        guarded(condition, lambda: self.copy("x", yy, xx, zz, part).wait_recv())

    def spread(self, distance):
        for sign in (1, -1) if distance else (0,):
            zz = self.z + sign * distance
            inside = when_all(
                [zz < self.levels if sign > 0 else None, zz >= 0 if sign < 0 else None]
            )
            yield zz, sign, inside

    def turn(self, turn):
        y, x, z, levels = self.y, self.x, self.z, self.levels
        if turn == 0 and not self.closing:
            self.own.start()
        if turn < levels:
            for zz, sign, inside in self.spread(turn):
                mine = turn == 0
                for part in range(2):
                    if turn:
                        self.arrive(inside, y, x, zz, part)
                    if sign <= 0:
                        self.send(when_all([inside, z < levels - 1]), "up", y, x, zz, part, mine)
                    if sign >= 0:
                        self.send(when_all([inside, z > 0]), "down", y, x, zz, part, mine)
                    for kind in ("x", "y") if part else ("y", "x"):
                        self.send(inside, kind, y, x, zz, part, mine)
                    self.send(inside, "twin", y, x, zz, part, mine)
        if 1 <= turn <= levels:
            for zz, sign, inside in self.spread(turn - 1):
                self.arrive(inside, y, 1 - x, zz, 0)
                self.send(inside, "y", y, 1 - x, zz, 0)
                self.send(inside, "twin", y, 1 - x, zz, 0)
                self.arrive(inside, 1 - y, x, zz, 1)
                self.send(inside, "x", 1 - y, x, zz, 1)
                self.send(inside, "twin", 1 - y, x, zz, 1)
                self.arrive(inside, 1 - y, x, zz, 0)
                self.send(inside, "twin", 1 - y, x, zz, 0)
                self.arrive(inside, y, 1 - x, zz, 1)
                self.send(inside, "twin", y, 1 - x, zz, 1)
        if turn >= 2:
            for zz, sign, inside in self.spread(turn - 2):
                for part in range(2):
                    self.arrive(inside, 1 - y, 1 - x, zz, part)
                    self.send(inside, "twin", 1 - y, 1 - x, zz, part)

    def finish(self):
        def twin_arrivals(i, _):
            column, zz = i // self.levels, i % self.levels
            for part in range(2):
                self.copy("twin", column // 2, column % 2, zz, part, 1 - self.c).wait_recv()
            return 0

        lax.fori_loop(0, 4 * self.levels, twin_arrivals, 0)
        self.closing = True
        for turn in range(self.levels + 2):
            self.turn(turn)
        self.own.wait()


class ShortGather:
    def __init__(self, group, inner, chunk_ref, out_ref, own_sem, send_sem, recv_sem):
        self.group, self.inner = group, inner
        self.chunk_ref, self.out_ref = chunk_ref, out_ref
        self.send_sem, self.recv_sem = send_sem, recv_sem
        dp, fs, self.y, self.x, self.z, self.c = place_of()
        self.levels = inner // 2
        self.own = pltpu.make_async_copy(chunk_ref, out_ref.at[dp * inner + fs], own_sem)
        self.across = {
            "z1": (dp, self.level(-1) * 2 + self.c),
            "z2": (dp, self.level(-2) * 2 + self.c),
            "z3": (dp, self.level(-3) * 2 + self.c),
            "x": (dp + 1 - 2 * self.x, fs),
            "y": (dp + 2 - 4 * self.y, fs),
            "twin": (dp, fs + 1 - 2 * self.c),
        }
        self.kinds = tuple(self.across)
        self.closing = False

    @staticmethod
    def semaphores(group):
        dma = pltpu.SemaphoreType.DMA
        return [dma, dma((6, group.devices // 2, 2)), dma((group.devices, 2))]

    def copy(self, kind, yy, xx, zz, part, cc=None, mine=False):
        core = self.c if cc is None else cc
        column = yy * 2 + xx
        index = column * self.inner + zz * 2 + core
        rows = pl.ds(part * self.group.half, self.group.half)
        return pltpu.make_async_remote_copy(
            src_ref=self.chunk_ref.at[rows] if mine else self.out_ref.at[index, rows],
            dst_ref=self.out_ref.at[index, rows],
            send_sem=self.send_sem.at[
                self.kinds.index(kind), column * self.levels + zz, part
            ],
            recv_sem=self.recv_sem.at[index, part],
            device_id=self.across[kind],
            device_id_type=MESH,
        )

    def level(self, back):
        return (self.z - back + self.levels) % self.levels

    def send(self, kind, yy, xx, zz, part, mine=False):
        copy = self.copy(kind, yy, xx, zz, part, mine=mine)
        if self.closing:
            copy.wait_send()
        else:
            copy.start()

    def arrive(self, yy, xx, zz, part):
        if not self.closing:
            self.copy("x", yy, xx, zz, part).wait_recv()

    def turn(self, turn):
        y, x, levels = self.y, self.x, self.levels
        if turn == 0 and not self.closing:
            self.own.start()
        if turn < levels:
            zz = self.level(turn)
            for part in range(2):
                if turn:
                    self.arrive(y, x, zz, part)
                for kind in ("x", "y") if part else ("y", "x"):
                    self.send(kind, y, x, zz, part, turn == 0)
                if turn == 0:
                    for kind in ("z1", "z2", "z3"):
                        self.send(kind, y, x, zz, part, True)
                self.send("twin", y, x, zz, part, turn == 0)
        if 1 <= turn <= levels:
            zz = self.level(turn - 1)
            self.arrive(y, 1 - x, zz, 0)
            self.send("y", y, 1 - x, zz, 0)
            self.send("twin", y, 1 - x, zz, 0)
            self.arrive(1 - y, x, zz, 1)
            self.send("x", 1 - y, x, zz, 1)
            self.send("twin", 1 - y, x, zz, 1)
            self.arrive(1 - y, x, zz, 0)
            self.send("twin", 1 - y, x, zz, 0)
            self.arrive(y, 1 - x, zz, 1)
            self.send("twin", y, 1 - x, zz, 1)
        if turn >= 2:
            zz = self.level(turn - 2)
            for part in range(2):
                self.arrive(1 - y, 1 - x, zz, part)
                self.send("twin", 1 - y, 1 - x, zz, part)

    def finish(self):
        def twin_arrivals(i, _):
            column, zz = i // self.levels, i % self.levels
            for part in range(2):
                self.copy("twin", column // 2, column % 2, zz, part, 1 - self.c).wait_recv()
            return 0

        lax.fori_loop(0, 4 * self.levels, twin_arrivals, 0)
        self.closing = True
        for turn in range(self.levels + 2):
            self.turn(turn)
        self.own.wait()


class PairTrade:
    def __init__(self, slab_ref, out_ref, mine, theirs, sems, inner, devices):
        self.slab_ref, self.out_ref, self.mine, self.theirs = slab_ref, out_ref, mine, theirs
        self.pair_sem, self.send_sem, self.recv_sem = sems
        self.inner, self.chips, self.senders = inner, devices // 2, out_ref.shape[0]
        dp, fs, _, _, _, self.core = place_of()
        self.twin = (dp, fs + 1 - 2 * self.core)
        self.chip = (dp * inner + fs) // 2

    def load(self):
        return pltpu.make_async_copy(self.slab_ref.at[self.core], self.mine, self.pair_sem.at[0])

    def pair(self):
        return pltpu.make_async_remote_copy(
            src_ref=self.slab_ref.at[1 - self.core],
            dst_ref=self.theirs,
            send_sem=self.pair_sem.at[1],
            recv_sem=self.pair_sem.at[2],
            device_id=self.twin,
            device_id_type=MESH,
        )

    def copy(self, source, target):
        device = 2 * target + self.core
        return pltpu.make_async_remote_copy(
            src_ref=self.mine.at[target],
            dst_ref=self.out_ref.at[source],
            send_sem=self.send_sem.at[target],
            recv_sem=self.recv_sem.at[source],
            device_id=(device // self.inner, device % self.inner),
            device_id_type=MESH,
        )

    def own(self):
        return pltpu.make_async_copy(
            self.mine.at[self.chip], self.out_ref.at[self.chip], self.pair_sem.at[3]
        )

    def each(self, act):
        def body(i, _):
            act((self.chip + i) % self.chips)
            return 0

        lax.fori_loop(1, self.chips, body, 0)

    def begin(self):
        @pl.when(self.chip < self.senders)
        def _():
            self.pair().start()
            self.load().start()

    def start(self):
        @pl.when(self.chip < self.senders)
        def _():
            self.load().wait()
            self.pair().wait_recv()

            def add(i, _):
                self.mine[i] = self.mine[i] + self.theirs[i]
                return 0

            lax.fori_loop(0, self.chips, add, 0)
            self.own().start()
            self.each(lambda other: self.copy(self.chip, other).start())

    def wait(self):
        def landed(other):
            pl.when(other < self.senders)(lambda: self.copy(other, other).wait_recv())

        self.each(landed)

        @pl.when(self.chip < self.senders)
        def _():
            self.own().wait()
            self.pair().wait_send()
            self.each(lambda other: self.copy(self.chip, other).wait_send())


def gather_kernel(
    chunk_ref, slab_ref, slot_ref, out_ref, parts_ref, next_ref, mine, theirs, *sems,
    group, later, inner
):
    me = lax.axis_index("dp") * inner + lax.axis_index("fsdp")
    meet_all(me, group.devices, inner)
    trade = PairTrade(slab_ref, parts_ref, mine, theirs, sems[:3], inner, group.devices)
    gather = ShortGather(group, inner, chunk_ref, out_ref, *sems[3:6])
    deal = Deal(later, slot_ref, next_ref, *sems[6:], inner, False)
    trade.begin()
    gather.turn(0)
    trade.start()
    gather.turn(1)
    deal.start()
    for turn in range(2, inner // 2 + 2):
        gather.turn(turn)
    gather.finish()
    trade.wait()
    deal.landed()
    deal.gone()


def gather_chunks(chunk, slabs, slot, group, later, inner, senders, collective):
    dma = pltpu.SemaphoreType.DMA
    return remote_call(
        functools.partial(gather_kernel, group=group, later=later, inner=inner),
        [ANYWHERE] * 3,
        [ANYWHERE] * 3,
        [
            jax.ShapeDtypeStruct((group.devices, group.chunk, LANE), BF),
            jax.ShapeDtypeStruct((senders // 2, *slabs.shape[2:]), slabs.dtype),
            jax.ShapeDtypeStruct((later.chunk, LANE), BF),
        ],
        [
            pltpu.VMEM(slabs.shape[1:], slabs.dtype),
            pltpu.VMEM(slabs.shape[1:], slabs.dtype),
            dma((4,)),
            dma((group.devices // 2,)),
            dma((group.devices // 2,)),
        ]
        + ShortGather.semaphores(group)
        + Deal.semaphores(later, False),
        collective,
        "gather_chunks",
    )(chunk, slabs, slot)


def scatter_stages(
    group,
    inner,
    g_ref,
    acc,
    twin,
    wide_y,
    wide_x,
    slim_x,
    slim_y,
    line,
    load_sem,
    twin_send,
    twin_recv,
    wide_send,
    wide_recv,
    slim_send,
    slim_recv,
    line_send,
    line_recv,
):
    dp, fs, y, x, z, c = place_of()
    me = dp * inner + fs
    lent = group.half
    levels = inner // 2
    x_mate = (dp + 1 - 2 * x, fs)
    y_mate = (dp + 2 - 4 * y, fs)

    def remote(source, target, send, receive, device):
        return pltpu.make_async_remote_copy(
            src_ref=source,
            dst_ref=target,
            send_sem=send,
            recv_sem=receive,
            device_id=device,
            device_id_type=MESH,
        )

    def slot_of(yy, xx, zz):
        return (yy * 2 + xx) * levels + zz

    def load(yy, xx, zz):
        slot = slot_of(yy, xx, zz)
        return pltpu.make_async_copy(
            g_ref.at[(yy * 2 + xx) * inner + zz * 2 + c], acc.at[slot], load_sem.at[slot]
        )

    def to_twin(yy, xx, zz):
        slot = slot_of(yy, xx, zz)
        return remote(
            g_ref.at[(yy * 2 + xx) * inner + zz * 2 + 1 - c],
            twin.at[slot],
            twin_send.at[slot],
            twin_recv.at[slot],
            (dp, fs + 1 - 2 * c),
        )

    def piece(slot, part):
        return acc.at[slot, pl.ds(part * lent, lent)]

    def wide(part, other, zz, yy=0, xx=0):
        buffer, device = (wide_x, x_mate) if part else (wide_y, y_mate)
        index = other * levels + zz
        return remote(
            piece(slot_of(yy, xx, zz), part),
            buffer.at[index],
            wide_send.at[part, index],
            wide_recv.at[part, index],
            device,
        )

    def slim(part, zz, yy=0, xx=0):
        buffer, device = (slim_y, y_mate) if part else (slim_x, x_mate)
        return remote(
            piece(slot_of(yy, xx, zz), part),
            buffer.at[zz],
            slim_send.at[part, zz],
            slim_recv.at[part, zz],
            device,
        )

    def along(upward, zz, part):
        way = 0 if upward else 1
        return remote(
            piece(slot_of(y, x, zz), part),
            line.at[way, zz, part],
            line_send.at[way, zz, part],
            line_recv.at[way, zz, part],
            (dp, fs + 2 if upward else fs - 2),
        )

    block = lent // group.folds

    def add(slot, first, count, source):
        def body(i, _):
            at = pl.multiple_of(i * block, TILE)
            to = pl.ds(pl.multiple_of(first + i * block, TILE), block)
            acc[slot, to] = acc[slot, to] + source[pl.ds(at, block)]
            return 0

        lax.fori_loop(0, count // block, body, 0)

    def add_part(slot, part, source):
        add(slot, part * lent, lent, source)

    def level(k):
        return jnp.where(z < levels // 2, z + levels - 1 - k, z + 1 + k) % levels

    columns = ((1 - y, 1 - x), (1 - y, x), (y, 1 - x), (y, x))

    def begin():
        for k in range(levels):
            for yy, xx in columns:
                to_twin(yy, xx, level(k)).start()
                load(yy, xx, level(k)).start()

    def settle(yy, xx, zz):
        slot = slot_of(yy, xx, zz)
        load(yy, xx, zz).wait()
        to_twin(yy, xx, zz).wait_recv()
        add(slot, 0, group.chunk, twin.at[slot])

    def diagonal(k):
        zz = level(k)
        settle(1 - y, 1 - x, zz)
        wide(0, 1 - x, zz, 1 - y, 1 - x).start()
        wide(1, 1 - y, zz, 1 - y, 1 - x).start()

    def sides(k):
        zz = level(k)
        settle(1 - y, x, zz)
        wide(0, x, zz, 1 - y, x).start()
        settle(y, 1 - x, zz)
        wide(1, y, zz, y, 1 - x).start()

    def middle(k):
        zz = level(k)
        wide(0, 1 - x, zz).wait_recv()
        add_part(slot_of(y, 1 - x, zz), 0, wide_y.at[(1 - x) * levels + zz])
        slim(0, zz, y, 1 - x).start()
        wide(1, 1 - y, zz).wait_recv()
        add_part(slot_of(1 - y, x, zz), 1, wide_x.at[(1 - y) * levels + zz])
        slim(1, zz, 1 - y, x).start()

    def home(k):
        zz = level(k)
        slot = slot_of(y, x, zz)
        settle(y, x, zz)
        wide(0, x, zz).wait_recv()
        add_part(slot, 0, wide_y.at[x * levels + zz])
        wide(1, y, zz).wait_recv()
        add_part(slot, 1, wide_x.at[y * levels + zz])
        slim(0, zz).wait_recv()
        add_part(slot, 0, slim_x.at[zz])
        slim(1, zz).wait_recv()
        add_part(slot, 1, slim_y.at[zz])

    def take(upward, zz, part):
        along(upward, zz, part).wait_recv()
        add_part(slot_of(y, x, zz), part, line.at[0 if upward else 1, zz, part])

    def ways(k, allowed):
        zz = level(k)
        for upward in (True, False):
            yield zz, upward, allowed() & (zz > z if upward else zz < z)

    def pass_on(k, allowed):
        more = {True: z > 0, False: z < levels - 1}
        for zz, upward, inside in ways(k, allowed):

            @pl.when(inside)
            def _(zz=zz, upward=upward):
                for part in range(2):

                    @pl.when(more[upward])
                    def _(part=part):
                        take(upward, zz, part)

                    along(upward, zz, part).start()

    def close_pass(k, allowed):
        for zz, upward, inside in ways(k, allowed):

            @pl.when(inside)
            def _(zz=zz, upward=upward):
                for part in range(2):
                    along(upward, zz, part).wait_send()

    def at_edge():
        return (z == 0) | (z == levels - 1)

    def off_edge():
        return (z > 0) & (z < levels - 1)

    def anywhere():
        return z >= 0

    def once(k):
        diagonal(k)
        sides(k)

    def final():
        for part in range(2):

            @pl.when(z > 0)
            def _(part=part):
                take(True, z, part)

            @pl.when(z < levels - 1)
            def _(part=part):
                take(False, z, part)

    stages = {
        "begin": begin,
        "once0": lambda: once(0),
        "once1": lambda: once(1),
        "middle0": lambda: middle(0),
        "once2": lambda: once(2),
        "middle1": lambda: middle(1),
        "home0": lambda: home(0),
        "pass0": lambda: pass_on(0, at_edge),
        "once3": lambda: once(3),
        "middle2": lambda: middle(2),
        "middle3": lambda: middle(3),
        "home1": lambda: home(1),
        "pass1": lambda: pass_on(1, anywhere),
        "home2": lambda: home(2),
        "pass2": lambda: pass_on(2, anywhere),
        "inner0": lambda: pass_on(0, off_edge),
        "home3": lambda: home(3),
        "final": final,
    }

    def finish():
        for k, allowed in ((0, at_edge), (1, anywhere), (2, anywhere), (0, off_edge)):
            close_pass(k, allowed)

        def close(k, _):
            zz = level(k)
            for yy, xx in columns:
                to_twin(yy, xx, zz).wait_send()
            wide(0, 1 - x, zz).wait_send()
            wide(0, x, zz).wait_send()
            wide(1, 1 - y, zz).wait_send()
            wide(1, y, zz).wait_send()
            slim(0, zz).wait_send()
            slim(1, zz).wait_send()
            return 0

        lax.fori_loop(0, levels, close, 0)

    return stages, finish, acc.at[slot_of(y, x, z)]


def scatter_scratch(group, inner):
    dma = pltpu.SemaphoreType.DMA
    half, levels = group.devices // 2, inner // 2
    part = (group.half, LANE)
    return [
        pltpu.VMEM((half, group.chunk, LANE), BF),
        pltpu.VMEM((half, group.chunk, LANE), BF),
        pltpu.VMEM((2 * levels, *part), BF),
        pltpu.VMEM((2 * levels, *part), BF),
        pltpu.VMEM((levels, *part), BF),
        pltpu.VMEM((levels, *part), BF),
        pltpu.VMEM((2, levels, 2, *part), BF),
        dma((half,)),
        dma((half,)),
        dma((half,)),
        dma((2, 2 * levels)),
        dma((2, 2 * levels)),
        dma((2, levels)),
        dma((2, levels)),
        dma((2, levels, 2)),
        dma((2, levels, 2)),
    ]


def scatter_kernel(
    g_ref, rows_ref, out_ref, all_ref, own_sem, row_send, row_recv, *rest, group, inner, receivers
):
    me = lax.axis_index("dp") * inner + lax.axis_index("fsdp")
    meet_all(me, group.devices, inner)
    stages, finish, total = scatter_stages(group, inner, g_ref, *rest[:-2])
    trade = Trade(
        rows_ref, all_ref, own_sem, row_send, row_recv, group, inner, group.devices, receivers
    )
    for name, stage in stages.items():
        stage()
        if name == "once0":
            trade.start()
    deal = Deal(group, total, out_ref, *rest[-2:], inner, True)
    deal.start()
    finish()
    trade.wait()
    deal.landed()
    deal.gone()


def scatter_chunks(grads, rows, group, inner, receivers, collective):
    dma = pltpu.SemaphoreType.DMA
    return remote_call(
        functools.partial(scatter_kernel, group=group, inner=inner, receivers=receivers),
        [ANYWHERE] * 2,
        [ANYWHERE] * 2,
        [
            jax.ShapeDtypeStruct((group.padded, LANE), BF),
            jax.ShapeDtypeStruct((group.devices, *rows.shape), rows.dtype),
        ],
        [dma, dma((group.devices,)), dma((group.devices,))]
        + scatter_scratch(group, inner)
        + Deal.semaphores(group, True),
        collective,
        "scatter_chunks",
    )(grads, rows)


def front_kernel(
    x_ref, mod_ref, w_ref, chunk_ref, qkv_ref, o_ref, l_ref, out_ref, qkv_s, *sems,
    group, inner, leads, pairs
):
    step = pl.program_id(0)
    last = pl.num_programs(0) - 1
    clips, frames, _ = qkv_s.shape
    rows = x_ref.shape[1]
    gather = Gather(group, inner, chunk_ref, out_ref, *sems)
    me = lax.axis_index("dp") * inner + lax.axis_index("fsdp")

    @pl.when(step == 0)
    def _():
        meet_all(me, group.devices, inner)
        gather.turn(0)

    for turn, at in ((1, leads), (2, leads + 2), (3, leads + 4)):

        @pl.when(step == at)
        def _(turn=turn):
            gather.turn(turn)

    @pl.when(step < leads)
    def _():
        normed, _ = normalize(x_ref[0].astype(F32))
        first_in = (normed * (1.0 + mod_ref[0, 1:2]) + mod_ref[0, 0:1]).astype(BF)
        block = nn(first_in, w_ref[...]).astype(BF)
        qkv_ref[0] = block
        start = pl.multiple_of(step * rows % frames, rows)
        qkv_s[step * rows // frames, pl.ds(start, rows)] = block

    @pl.when(step >= leads)
    def _():
        lane, low = head_lanes()
        count = HEADS // 2 // pairs
        clip, group_index = (step - leads) // count, (step - leads) % count
        for pair in range(pairs):

            def columns(part):
                at = (group_index * pairs + pair + part * HEADS // 2) * 2 * HD
                return qkv_s[clip, :, pl.ds(pl.multiple_of(at, 2 * HD), 2 * HD)]

            attend_pair(
                lane,
                low,
                None,
                columns(0),
                columns(1),
                columns(2),
                o_ref.at[0, :, pair * 2 * HD : (pair + 1) * 2 * HD],
                l_ref.at[0, pair],
            )

    @pl.when(step == last)
    def _():
        for turn in range(4, inner // 2 + 2):
            gather.turn(turn)
        gather.finish()


def front_and_gather(latents, mod, weight, chunk, group, inner, collective, pairs=2):
    clips, frames, width = latents.shape
    rows = row_block(frames)
    per = frames // rows
    leads = clips * per
    count = HEADS // 2 // pairs

    def lead(s):
        return jnp.minimum(s, leads - 1)

    def tail(s):
        return jnp.maximum(s - leads, 0)

    wide = weight.shape[1]
    return remote_call(
        functools.partial(front_kernel, group=group, inner=inner, leads=leads, pairs=pairs),
        [
            pl.BlockSpec((1, rows, width), lambda s: (lead(s) // per, lead(s) % per, 0)),
            pl.BlockSpec((1, 9, width), lambda s: (lead(s) // per, 0, 0)),
            whole_spec(weight.shape),
            ANYWHERE,
        ],
        [
            pl.BlockSpec((1, rows, wide), lambda s: (lead(s) // per, lead(s) % per, 0)),
            pl.BlockSpec(
                (1, frames, 2 * HD * pairs), lambda s: (tail(s) // count, 0, tail(s) % count)
            ),
            pl.BlockSpec(
                (1, pairs, frames, 2 * HD), lambda s: (tail(s) // count, tail(s) % count, 0, 0)
            ),
            ANYWHERE,
        ],
        [
            struct((clips, frames, wide), BF),
            struct((clips, frames, width), BF),
            struct((clips, HEADS // 2, frames, 2 * HD), F32),
            struct((group.devices, group.chunk, LANE), BF),
        ],
        [pltpu.VMEM((clips, frames, wide), BF)] + Gather.semaphores(group),
        collective,
        "front_and_gather",
        (leads + clips * count,),
    )(latents, mod, weight, chunk)


def back_kernel(
    q_ref, k_ref, v_ref, do_ref, o_ref, l_ref, x_ref, dh_ref, mod_ref, w_ref, g_ref,
    out_ref, dw_ref, sums_ref, rest_ref, grad_s, in_s, *scratch,
    group, inner, pairs, period
):
    step = pl.program_id(0)
    last = pl.num_programs(0) - 1
    clip, turn = step // period, step % period
    width = x_ref.shape[2]
    rows = x_ref.shape[1]
    stages, finish, total = scatter_stages(group, inner, g_ref, *scratch[:-2])
    deal = Deal(group, total, rest_ref, *scratch[-2:], inner, True)
    me = lax.axis_index("dp") * inner + lax.axis_index("fsdp")

    @pl.when(step == 0)
    def _():
        meet_all(me, group.devices, inner)

    plan = (
        (0, ("begin",)),
        (1, ("once0", "once1")),
        (3, ("middle0", "once2")),
        (5, ("middle1", "once3")),
        (7, ("home0", "pass0")),
        (8, ("middle2",)),
        (11, ("middle3",)),
        (12, ("home1", "pass1")),
        (14, ("home2", "pass2")),
        (16, ("inner0",)),
    )
    for at, names in plan:

        @pl.when(step == at)
        def _(names=names):
            for name in names:
                stages[name]()

    @pl.when(turn < pairs)
    def _():
        lane, low = head_lanes()

        def columns(part):
            at = pl.multiple_of(turn * 2 * HD, 2 * HD)
            return grad_s.at[:, pl.ds(part * width + at, 2 * HD)]

        attend_back_pair(
            lane,
            low,
            None,
            q_ref[0],
            k_ref[0],
            v_ref[0],
            do_ref[0],
            o_ref[0],
            l_ref[0, 0],
            columns(0),
            columns(1),
            columns(2),
        )

    clear_at(turn == pairs, sums_ref)

    @pl.when(turn >= pairs)
    def _():
        here = pl.ds(pl.multiple_of((turn - pairs) * rows, rows), rows)
        normed, inverse = normalize(x_ref[0].astype(F32))
        in_s[here] = (normed * (1.0 + mod_ref[0, 1:2]) + mod_ref[0, 0:1]).astype(BF)
        grad_in = None
        for index in range(3):
            part = slice(index * width, (index + 1) * width)
            product = nt(grad_s[here, part], w_ref[:, part])
            grad_in = product if grad_in is None else grad_in + product
        out_ref[0] = (
            dh_ref[0] + norm_back(normed, inverse, grad_in * (1.0 + mod_ref[0, 1:2]))
        ).astype(BF)
        sums_ref[0] += jnp.concatenate(
            [column_sum(grad_in), column_sum(grad_in * normed)], axis=0
        )

    @pl.when(turn == period - 1)
    def _():
        turned = in_s[...].T
        for index in range(3):
            part = slice(index * width, (index + 1) * width)
            product = nn(turned, grad_s[:, part])

            @pl.when(clip == 0)
            def _(product=product, part=part):
                dw_ref[:, part] = product.astype(BF)

            @pl.when(clip > 0)
            def _(product=product, part=part):
                dw_ref[:, part] = (dw_ref[:, part].astype(F32) + product).astype(BF)

    @pl.when(step == last)
    def _():
        for name in ("home3", "final"):
            stages[name]()
        deal.start()
        finish()
        deal.landed()
        deal.gone()


def back_and_scatter(
    queries, grad, mixed, lse, latents, dh, mod, weight, chunks, group, inner, collective
):
    clips, frames, wide = queries.shape
    width = wide // 3
    pairs = HEADS // 2
    rows = frames // 3
    period = pairs + frames // rows

    def pair_at(part):
        return pl.BlockSpec(
            (1, frames, 2 * HD),
            lambda s: (s // period, 0, jnp.minimum(s % period, pairs - 1) + part * pairs),
        )

    lse_at = pl.BlockSpec(
        (1, 1, frames, 2 * HD),
        lambda s: (s // period, jnp.minimum(s % period, pairs - 1), 0, 0),
    )
    rows_at = pl.BlockSpec(
        (1, rows, width), lambda s: (s // period, jnp.maximum(s % period - pairs, 0), 0)
    )

    def clip_at(count):
        return pl.BlockSpec((1, count, width), lambda s: (s // period, 0, 0))

    whole = pl.BlockSpec(weight.shape, lambda s: (0, 0), pipeline_mode=pl.Buffered(1))
    return remote_call(
        functools.partial(back_kernel, group=group, inner=inner, pairs=pairs, period=period),
        [
            pair_at(0),
            pair_at(1),
            pair_at(2),
            pair_at(0),
            pair_at(0),
            lse_at,
            rows_at,
            rows_at,
            clip_at(9),
            whole,
            ANYWHERE,
        ],
        [rows_at, whole, clip_at(2), ANYWHERE],
        [
            struct((clips, frames, width), BF),
            struct(weight.shape, BF),
            struct((clips, 2, width), F32),
            struct((group.padded, LANE), BF),
        ],
        [pltpu.VMEM((frames, wide), BF), pltpu.VMEM((frames, width), BF)]
        + scatter_scratch(group, inner)
        + Deal.semaphores(group, True),
        collective,
        "back_and_scatter",
        (clips * period,),
    )(queries, queries, queries, grad, mixed, lse, latents, dh, mod, weight, chunks)


def exchange_kernel(in_ref, out_ref, own_sem, send_sem, recv_sem, *, group, inner):
    me = lax.axis_index("dp") * inner + lax.axis_index("fsdp")
    meet_all(me, group.devices, inner)
    trade = Trade(
        in_ref, out_ref, own_sem, send_sem, recv_sem, group, inner, group.devices, group.devices
    )
    trade.start()
    trade.wait()


def exchange(value, group, inner, collective, name):
    dma = pltpu.SemaphoreType.DMA
    return remote_call(
        functools.partial(exchange_kernel, group=group, inner=inner),
        [ANYWHERE],
        ANYWHERE,
        jax.ShapeDtypeStruct((group.devices, *value.shape), value.dtype),
        [dma, dma((group.devices,)), dma((group.devices,))],
        collective,
        name,
    )(value)


HALF = 27
TALL = 72
SLAB = 112
CONDITION_ROWS = 832


def ada_spots(me, group):
    lines = group.share // HALF
    odd = me % 2
    limit = CONDITION_ROWS - TALL
    return [
        (odd, jnp.minimum((lines * me + odd) // 2, limit)),
        (1 - odd, jnp.minimum((lines * me - odd) // 2, limit)),
    ]


def ada_kernel(lin_ref, cond_ref, out_ref, *, group, inner):
    me = lax.axis_index("dp") * inner + lax.axis_index("fsdp")
    for half, (shift, top) in enumerate(ada_spots(me, group)):
        condition = cond_ref[pl.ds(top, TALL)].astype(BF)

        def body(c, _, half=half, shift=shift, condition=condition):
            rows = lin_ref[pl.ds(HALF * shift + c, TALL, stride=2 * HALF)].astype(BF)
            part = tn(condition, rows)
            count = group.devices
            for clip in range(2):
                out_ref[pl.ds((2 * clip + half) * HALF + c, count, stride=SLAB)] = part[
                    clip * count : (clip + 1) * count
                ]
            return 0

        lax.fori_loop(0, HALF, body, 0, unroll=True)


def ada_partial(lin, cond, group, inner):
    return pl.pallas_call(
        functools.partial(ada_kernel, group=group, inner=inner),
        out_shape=jax.ShapeDtypeStruct((group.devices * SLAB, LANE), F32),
        compiler_params=pltpu.CompilerParams(vmem_limit_bytes=VMEM_LIMIT),
        name="ada_partial",
    )(lin, cond)


def own_grad_kernel(
    cond_ref, given_ref, early_ref, late_ref, g_ref, sums_ref, lin, dmod_ref, *, group, inner
):
    me = lax.axis_index("dp") * inner + lax.axis_index("fsdp")
    count = group.devices // 2
    border = jnp.clip(group.first - group.share * me, 0, group.share)
    middle = jnp.clip(group.last - group.share * me, 0, group.share)

    @pl.when(border > 0)
    def _():
        dmod_ref[...] = given_ref[...].astype(F32)

    for half, (shift, top) in enumerate(ada_spots(me, group)):
        condition = cond_ref[pl.ds(top, TALL)].astype(BF)

        def body(c, _, half=half, shift=shift, condition=condition):
            grads = jnp.concatenate(
                [
                    dmod_ref[
                        pl.ds(core * SLAB + (2 * clip + half) * HALF + c, count, stride=2 * SLAB)
                    ]
                    for clip in range(2)
                    for core in range(2)
                ],
                axis=0,
            ).astype(BF)
            lin[pl.ds(HALF * shift + c, TALL, stride=2 * HALF)] = nn(condition, grads)
            return 0

        @pl.when(border > 0)
        def _(body=body):
            lax.fori_loop(0, HALF, body, 0, unroll=True)

    rows = 64

    def merge(i, total):
        at = pl.multiple_of(i * rows, rows)
        row = lax.broadcasted_iota(jnp.int32, (rows, LANE), 0) + at
        early = early_ref[pl.ds(at, rows)].astype(F32)
        late = jnp.where(row < group.share, late_ref[pl.ds(at, rows)].astype(F32), 0.0)
        value = jnp.where(
            row < border, lin[pl.ds(at, rows)], jnp.where(row < middle, early, late)
        )
        g_ref[pl.ds(at, rows)] = value
        square = value * value
        return total + sum(square[k : k + 8] for k in range(0, rows, 8))

    sums_ref[...] = lax.fori_loop(0, group.padded // rows, merge, jnp.zeros((8, LANE), F32))


def own_grad(cond, dmod, early, late, group, inner):
    return pl.pallas_call(
        functools.partial(own_grad_kernel, group=group, inner=inner),
        out_shape=[
            jax.ShapeDtypeStruct((group.padded, LANE), F32),
            jax.ShapeDtypeStruct((8, LANE), F32),
        ],
        scratch_shapes=[
            pltpu.VMEM((2 * HALF * TALL, LANE), F32),
            pltpu.VMEM(dmod.shape, F32),
        ],
        compiler_params=pltpu.CompilerParams(vmem_limit_bytes=VMEM_LIMIT),
        name="own_grad",
    )(cond, dmod, early, late)


def fits(devices, inner, share):
    return inner == 8 and devices == 32 and share % (LANE * HALF) == 0


def local_fast(latents, captions, lengths, timesteps, cotangent, master):
    clips, frames, width = latents.shape
    share = master.shape[0]
    inner = lax.axis_size("fsdp")
    devices = inner * lax.axis_size("dp")
    spots = linear_layout()
    end = spots[-1][0] + spots[-1][1]
    early = Group(devices, inner, share // LANE, spots[2][0], spots[3][0])
    late = Group(devices, inner, share // LANE, spots[3][0], end)
    holders = spots[2][0] // early.share + 1

    lin = lax.optimization_barrier(
        jnp.pad(
            master.reshape(early.share, LANE), ((0, 2 * HALF * TALL - early.share), (0, 0))
        )
    )
    slot = lin[: early.padded].astype(BF)
    steps, chunk = start_chunks(
        jnp.broadcast_to(
            jnp.pad(timesteps.astype(F32), (0, 8 - clips))[:, None], (8, LANE)
        ),
        slot,
        early,
        inner,
        1,
    )
    steps = steps[:, :clips, 0].reshape(devices // 2, 2, clips).T.reshape(devices * clips)
    columns = jax.nn.silu(embed(steps)).astype(BF).astype(F32).T
    columns = jnp.concatenate(
        [
            columns,
            jnp.ones((1, clips * devices), F32),
            jnp.zeros((CONDITION_ROWS - width - 1, clips * devices), F32),
        ],
        axis=0,
    )
    slabs = ada_partial(lin, columns, early, inner).reshape(2, devices // 2, SLAB, LANE)
    gathered, parts, later_chunk = gather_chunks(
        chunk, slabs, slot, early, late, inner, holders, 2
    )
    mod = jnp.sum(parts, axis=0)[: 54 * clips].reshape(clips, 9, width)
    (triple_weight,) = unpack_weights(gathered, early, (2,))

    def front(latents, mod, triple_weight):
        triple, mixed, lse, later = front_and_gather(
            latents, mod, triple_weight, later_chunk, late, inner, 3
        )
        return triple, mixed, lse, unpack_weights(later, late, tuple(range(3, 13)))

    def back(triple, grad_mixed, mixed, lse, latents, dh, mod, triple_weight, gradients):
        chunks = pack_grads(gradients, late, tuple(range(3, 13)))
        return back_and_scatter(
            triple,
            grad_mixed,
            mixed,
            lse,
            latents,
            dh,
            mod,
            triple_weight,
            chunks,
            late,
            inner,
            4,
        )

    output, input_grad, grad_mod, grad_triple, _, late_grads = block_pass(
        latents, captions, lengths, cotangent, mod, triple_weight, front, back
    )
    grad_rows = jnp.pad(
        grad_mod.reshape(54 * clips, LANE), ((0, SLAB - 54 * clips), (0, 0))
    )
    chunks = pack_grads([grad_triple], early, (2,))
    early_grads, dmod = scatter_chunks(chunks, grad_rows, early, inner, holders, 5)
    grads, squares = own_grad(
        columns,
        dmod.reshape(devices * SLAB, LANE),
        early_grads,
        late_grads,
        early,
        inner,
    )
    squares = exchange(squares, early, inner, 6, "squares")
    return (
        output,
        input_grad,
        grads[: early.share].reshape(share),
        jnp.sum(squares),
    )


def local_any(latents, captions, lengths, timesteps, cotangent, master):
    clips, frames, width = latents.shape
    share = master.shape[0]
    devices = lax.axis_size("dp") * lax.axis_size("fsdp")
    gathered = lax.all_gather(
        master.astype(BF).reshape(1, share), ("dp", "fsdp"), axis=0, tiled=True
    ).reshape(-1)
    weights = unpack(gathered)
    condition = jax.nn.silu(embed(timesteps)).astype(BF)
    mod = jnp.dot(condition, weights[0], preferred_element_type=F32) + weights[1].astype(F32)
    block_weights = [w.astype(F32).reshape(1, -1) if w.ndim == 1 else w for w in weights[2:]]
    output, input_grad, grad_mod, grad_triple, gradients, _ = block_pass(
        latents,
        captions,
        lengths,
        cotangent,
        mod.reshape(clips, 9, width),
        block_weights[0],
        functools.partial(plain_front, block_weights[1:]),
        plain_back,
    )
    grad_mod = grad_mod.reshape(clips, 9 * width)
    grad_ada = jnp.dot(condition.T, grad_mod, preferred_element_type=F32)
    grad_list = [grad_ada, jnp.sum(grad_mod.astype(F32), axis=0), grad_triple] + gradients
    flat = jnp.concatenate([piece.astype(F32).reshape(-1) for piece in grad_list])
    grad = lax.psum_scatter(
        flat.reshape(devices, share), ("dp", "fsdp"), scatter_dimension=0, tiled=True
    ).reshape(share)
    return output, input_grad, grad, lax.psum(jnp.sum(grad * grad), ("dp", "fsdp"))


def local(
    latents,
    captions,
    caption_lengths,
    timesteps,
    cotangent,
    master_weights,
    first_moment,
    second_moment,
):
    inner = lax.axis_size("fsdp")
    devices = inner * lax.axis_size("dp")
    run = local_fast if fits(devices, inner, master_weights.shape[0]) else local_any
    output, input_grad, grad_shard, squares = run(
        latents,
        captions,
        caption_lengths,
        timesteps,
        cotangent,
        master_weights,
    )
    grad_norm = jnp.sqrt(squares)
    clipped = grad_shard * (CLIP / jnp.maximum(grad_norm, CLIP))
    new_first = BETA_ONE * first_moment + (1.0 - BETA_ONE) * clipped
    new_second = BETA_TWO * second_moment + (1.0 - BETA_TWO) * clipped * clipped
    step_first = new_first / (1.0 - BETA_ONE**STEP)
    step_second = new_second / (1.0 - BETA_TWO**STEP)
    new_master = master_weights - RATE * (
        step_first / (jnp.sqrt(step_second) + ADAM_EPS) + DECAY * master_weights
    )
    return (output, input_grad, grad_norm, new_master, new_first, new_second)


def solution(mesh):
    placed = (
        P(("dp", "fsdp"), None, None),
        P(("dp", "fsdp"), None, None),
        P(("dp", "fsdp")),
        P(("dp", "fsdp")),
        P(("dp", "fsdp"), None, None),
        P(("dp", "fsdp")),
        P(("dp", "fsdp")),
        P(("dp", "fsdp")),
    )
    return jax.shard_map(
        local,
        mesh=mesh,
        in_specs=placed,
        out_specs=(
            P(("dp", "fsdp"), None, None),
            P(("dp", "fsdp"), None, None),
            P(),
            P(("dp", "fsdp")),
            P(("dp", "fsdp")),
            P(("dp", "fsdp")),
        ),
        check_vma=False,
    )
```

```python
import functools
import math

import jax
import jax.numpy as jnp
from jax import lax
from jax.experimental import pallas as pl
from jax.experimental.pallas import tpu as pltpu
from jax.sharding import PartitionSpec as P

D = 768
HEADS = 12
HD = 64
FF = 3072
CTX = 1024
STEP = 5


NORM_EPS = 1e-06
BETA_ONE = 0.9
BETA_TWO = 0.999
ADAM_EPS = 1e-08
RATE = 0.03
DECAY = 0.01
CLIP = 500.0


def layout_sizes():
    return [
        (D, 9 * D),
        (9 * D,),
        (D, 3 * D),
        (D, D),
        (D,),
        (D, D),
        (CTX, 2 * D),
        (D, D),
        (D,),
        (D, FF),
        (FF,),
        (FF, D),
        (D,),
    ]


def unpack(flat_vector):
    pieces = []
    offset = 0
    for layout_shape in layout_sizes():
        number = math.prod(layout_shape)
        pieces.append(flat_vector[offset : offset + number].reshape(layout_shape))
        offset += number
    return pieces


def embed(steps_in):
    half_width = D // 2
    frequency = jnp.exp(-math.log(10000.0) * jnp.arange(half_width, dtype=jnp.float32) / half_width)
    angles = steps_in.astype(jnp.float32)[:, None] * frequency[None, :]
    return jnp.concatenate([jnp.cos(angles), jnp.sin(angles)], axis=1)


def normalize(hidden):
    centred = hidden - jnp.mean(hidden, axis=-1, keepdims=True)
    inverse = lax.rsqrt(jnp.mean(centred * centred, axis=-1, keepdims=True) + NORM_EPS)
    return (centred * inverse, inverse)


def norm_back(normed, inverse, grad_normed):
    return inverse * (
        grad_normed
        - jnp.mean(grad_normed, axis=-1, keepdims=True)
        - normed * jnp.mean(grad_normed * normed, axis=-1, keepdims=True)
    )


F32 = jnp.float32
BF = jnp.bfloat16
VMEM_LIMIT = 60 << 20


def nn(left_side, right_side):
    return lax.dot_general(
        left_side, right_side, (((1,), (0,)), ((), ())), preferred_element_type=F32
    )


def nt(left_side, right_side):
    return lax.dot_general(
        left_side, right_side, (((1,), (1,)), ((), ())), preferred_element_type=F32
    )


def tn(left_side, right_side):
    return lax.dot_general(
        left_side, right_side, (((0,), (0,)), ((), ())), preferred_element_type=F32
    )


def call(body, grid, in_specs, out_specs, out_shape, name, scratch=()):
    return pl.pallas_call(
        body,
        grid=grid,
        in_specs=in_specs,
        out_specs=out_specs,
        out_shape=out_shape,
        scratch_shapes=list(scratch),
        compiler_params=pltpu.CompilerParams(vmem_limit_bytes=VMEM_LIMIT),
        name=name,
    )


def struct(shape, dtype):
    return jax.ShapeDtypeStruct(shape, dtype)


def rows_spec(rows, width):
    return pl.BlockSpec((1, rows, width), lambda i, j: (i, j, 0))


def clip_spec(count, width):
    return pl.BlockSpec((1, count, width), lambda i, j: (i, 0, 0))


def whole_spec(shape):
    return pl.BlockSpec(shape, lambda *_: (0,) * len(shape))


def row_block(frames):
    for parts in (2, 3, 4, 6):
        if frames % (16 * parts) == 0:
            return frames // parts
    return frames


def add_to(ref, first, value):
    @pl.when(first)
    def _():
        ref[...] = value

    @pl.when(jnp.logical_not(first))
    def _():
        ref[...] += value


def span_of(rows):
    start = (pl.program_id(0) * pl.num_programs(1) + pl.program_id(1)) * rows
    return pl.ds(pl.multiple_of(start, rows), rows)


def clear_at(first, *refs):
    @pl.when(first)
    def _():
        for ref in refs:
            ref[...] = jnp.zeros_like(ref)


def column_sum(value):
    return jnp.sum(value, axis=0, keepdims=True)


def qkv_kernel(x_ref, mod_ref, w_ref, out_ref):
    normed, _ = normalize(x_ref[0].astype(F32))
    first_in = (normed * (1.0 + mod_ref[0, 1:2]) + mod_ref[0, 0:1]).astype(BF)
    out_ref[0] = nn(first_in, w_ref[...]).astype(BF)


def qkv_forward(latents, mod, weight):
    clips, frames, width = latents.shape
    rows = row_block(frames)
    wide = weight.shape[1]
    return call(
        qkv_kernel,
        (clips, frames // rows),
        [rows_spec(rows, width), clip_spec(9, width), whole_spec(weight.shape)],
        rows_spec(rows, wide),
        struct((clips, frames, wide), BF),
        "qkv_forward",
    )(latents, mod, weight)


def head_lanes():
    lane = lax.broadcasted_iota(jnp.int32, (1, 2 * HD), 1)
    return lane, lane < HD


def usable_bias(length, count):
    row = lax.broadcasted_iota(jnp.int32, (count, 2 * HD), 0)
    return jnp.where(row < length, 0.0, -1e30).astype(BF)


def attend_kernel(*refs, masked):
    if masked:
        len_ref, q_ref, k_ref, v_ref, o_ref, l_ref = refs
    else:
        q_ref, k_ref, v_ref, o_ref, l_ref = refs
    lane, low = head_lanes()
    for pair in range(l_ref.shape[1]):
        columns = slice(pair * 2 * HD, (pair + 1) * 2 * HD)
        length = len_ref[pl.program_id(0)] if masked else None
        attend_pair(
            lane,
            low,
            length,
            q_ref[0, :, columns],
            k_ref[0, :, columns],
            v_ref[0, :, columns],
            o_ref.at[0, :, columns],
            l_ref.at[0, pair],
        )


def attend_pair(lane, low, length, q, k, v, o_ref, l_ref):
    masked = length is not None
    scaled = q * jnp.asarray(HD**-0.5, BF)
    one = jnp.ones((), BF)
    zero = jnp.zeros((), BF)
    values = [jnp.where(low, v, one), jnp.where(low, one, v)]
    if masked:
        bias = usable_bias(length, k.shape[0])
        tag = jnp.where(lane % HD == 0, one, zero)
        queries = [jnp.where(low, scaled, tag), jnp.where(low, tag, scaled)]
        keys = [jnp.where(low, k, bias), jnp.where(low, bias, k)]
    else:
        queries = [jnp.where(low, scaled, zero), jnp.where(low, zero, scaled)]
        keys = [k, k]
    tops, mixes = [], []
    for head in range(2):
        scores = nt(queries[head], keys[head])
        top = jnp.max(scores, axis=1, keepdims=True)
        mixes.append(nn(jnp.exp(scores - top).astype(BF), values[head]))
        tops.append(top)
    total = jnp.where(low, mixes[1], mixes[0])
    l_ref[...] = jnp.where(low, tops[1], tops[0]) + jnp.log(total)
    o_ref[...] = (jnp.where(low, mixes[0], mixes[1]) / pltpu.roll(total, HD, 1)).astype(BF)


def pair_spec(rows, offset, pairs):
    return pl.BlockSpec((1, rows, 2 * HD * pairs), lambda i, j: (i, 0, j + offset // pairs))


def lse_spec(rows, pairs):
    return pl.BlockSpec((1, pairs, rows, 2 * HD), lambda i, j: (i, j, 0, 0))


def attend_forward(queries, key_offset, keyvals, value_offset, lengths, name, pairs=1):
    clips, frames = queries.shape[:2]
    slots = keyvals.shape[1]
    groups = HEADS // 2
    masked = lengths is not None
    specs = [
        pair_spec(frames, 0, pairs),
        pair_spec(slots, key_offset, pairs),
        pair_spec(slots, value_offset, pairs),
    ]
    args = [queries, keyvals, keyvals]
    if masked:
        specs.insert(0, pl.BlockSpec(memory_space=pltpu.SMEM))
        args.insert(0, lengths)
    return call(
        functools.partial(attend_kernel, masked=masked),
        (clips, groups // pairs),
        specs,
        [pair_spec(frames, 0, pairs), lse_spec(frames, pairs)],
        [struct((clips, frames, D), BF), struct((clips, groups, frames, 2 * HD), F32)],
        name,
    )(*args)


def three_parts(value):
    high = value.astype(BF)
    rest = value - high.astype(F32)
    middle = rest.astype(BF)
    return high, middle, (rest - middle.astype(F32)).astype(BF)


def attend_back_kernel(*refs, masked):
    if masked:
        len_ref, q_ref, k_ref, v_ref, do_ref, o_ref, l_ref, dq_ref, dk_ref, dv_ref = refs
    else:
        q_ref, k_ref, v_ref, do_ref, o_ref, l_ref, dq_ref, dk_ref, dv_ref = refs
    length = len_ref[pl.program_id(0)] if masked else None
    attend_back_step(
        length, q_ref, k_ref, v_ref, do_ref, o_ref, l_ref, dq_ref, dk_ref, dv_ref
    )


def attend_back_step(length, q_ref, k_ref, v_ref, do_ref, o_ref, l_ref, dq_ref, dk_ref, dv_ref):
    lane, low = head_lanes()
    for pair in range(l_ref.shape[1]):
        columns = slice(pair * 2 * HD, (pair + 1) * 2 * HD)
        attend_back_pair(
            lane,
            low,
            length,
            q_ref[0, :, columns],
            k_ref[0, :, columns],
            v_ref[0, :, columns],
            do_ref[0, :, columns],
            o_ref[0, :, columns],
            l_ref[0, pair],
            dq_ref.at[0, :, columns],
            dk_ref.at[0, :, columns],
            dv_ref.at[0, :, columns],
        )


def attend_back_pair(lane, low, length, q, k, v, grad, mixed, lse, dq_ref, dk_ref, dv_ref):
    masked = length is not None
    scaled = q * jnp.asarray(HD**-0.5, BF)
    spot = lane % HD
    one = jnp.ones((), BF)
    zero = jnp.zeros((), BF)
    product = grad.astype(F32) * mixed.astype(F32)
    delta_low = jnp.sum(jnp.where(low, product, 0.0), axis=1, keepdims=True)
    delta_high = jnp.sum(jnp.where(low, 0.0, product), axis=1, keepdims=True)

    def negated(value, last):
        high, middle, rest = three_parts(-value)
        return jnp.where(
            spot == 0,
            high,
            jnp.where(spot == 1, middle, jnp.where(spot == 2, rest, last)),
        )

    tag = jnp.where(spot == 3, one, zero) if masked else zero
    lse_lanes = negated(lse, tag)
    delta_lanes = negated(jnp.where(low, delta_high, delta_low), zero)
    ones = jnp.broadcast_to(jnp.where(spot < 3, one, zero), k.shape)
    key_lanes = ones
    if masked:
        bias = usable_bias(length, k.shape[0])
        key_lanes = jnp.where(spot == 3, bias, ones)
    transposed = k.astype(F32).T.astype(BF)
    grad_queries, grad_keys, grad_values = [], [], []
    for head in range(2):

        def merge(own, other):
            return jnp.where(low, own, other) if head == 0 else jnp.where(low, other, own)

        probability = jnp.exp(nt(merge(k, key_lanes), merge(scaled, lse_lanes)))
        centred = nt(merge(v, ones), merge(grad, delta_lanes))
        grad_scores = (probability * centred).astype(BF)
        grad_values.append(nn(probability.astype(BF), grad))
        grad_keys.append(nn(grad_scores, scaled))
        grad_queries.append(nn(transposed[HD * head : HD * (head + 1)], grad_scores))
    dv_ref[...] = jnp.where(low, grad_values[0], grad_values[1]).astype(BF)
    dk_ref[...] = jnp.where(low, grad_keys[0], grad_keys[1]).astype(BF)
    dq_ref[...] = (jnp.concatenate(grad_queries, axis=0).T * HD**-0.5).astype(BF)


def attend_backward(
    queries, key_offset, keyvals, value_offset, lengths, grad, mixed, lse, name, pairs=1
):
    clips, frames = queries.shape[:2]
    slots = keyvals.shape[1]
    groups = HEADS // 2
    masked = lengths is not None
    specs = [
        pair_spec(frames, 0, pairs),
        pair_spec(slots, key_offset, pairs),
        pair_spec(slots, value_offset, pairs),
        pair_spec(frames, 0, pairs),
        pair_spec(frames, 0, pairs),
        lse_spec(frames, pairs),
    ]
    args = [queries, keyvals, keyvals, grad, mixed, lse]
    if masked:
        specs.insert(0, pl.BlockSpec(memory_space=pltpu.SMEM))
        args.insert(0, lengths)
    return call(
        functools.partial(attend_back_kernel, masked=masked),
        (clips, groups // pairs),
        specs,
        [pair_spec(frames, 0, pairs), pair_spec(slots, 0, pairs), pair_spec(slots, 0, pairs)],
        [
            struct((clips, frames, D), BF),
            struct((clips, slots, D), BF),
            struct((clips, slots, D), BF),
        ],
        name,
    )(*args)


def after_self_kernel(
    o_ref, x_ref, mod_ref, wo_ref, bo_ref, wq_ref, cap_ref, wkv_ref, z_ref, h_ref, q_ref, kv_ref
):
    @pl.when(pl.program_id(1) == 0)
    def _():
        kv_ref[0] = nn(cap_ref[0], wkv_ref[...]).astype(BF)

    branch = nn(o_ref[0], wo_ref[...]) + bo_ref[...]
    hidden = x_ref[0].astype(F32) + mod_ref[0, 2:3] * branch
    normed, _ = normalize(hidden)
    second_in = (normed * (1.0 + mod_ref[0, 4:5]) + mod_ref[0, 3:4]).astype(BF)
    z_ref[0] = branch.astype(BF)
    h_ref[0] = hidden
    q_ref[0] = nn(second_in, wq_ref[...]).astype(BF)


def after_self(mixed, latents, mod, weight, bias, query_weight, captions, keyval_weight):
    clips, frames, width = latents.shape
    slots, context = captions.shape[1:]
    wide = keyval_weight.shape[1]
    rows = row_block(frames)
    spec = rows_spec(rows, width)
    square = whole_spec((width, width))
    return call(
        after_self_kernel,
        (clips, frames // rows),
        [
            spec,
            spec,
            clip_spec(9, width),
            square,
            whole_spec((1, width)),
            square,
            clip_spec(slots, context),
            whole_spec(keyval_weight.shape),
        ],
        [spec, spec, spec, clip_spec(slots, wide)],
        [
            struct(latents.shape, BF),
            struct(latents.shape, F32),
            struct(latents.shape, BF),
            struct((clips, slots, wide), BF),
        ],
        "after_self",
    )(mixed, latents, mod, weight, bias, query_weight, captions, keyval_weight)


def after_cross_kernel(o_ref, h_ref, mod_ref, wo_ref, bo_ref, z_ref, out_ref):
    branch = nn(o_ref[0], wo_ref[...]) + bo_ref[...]
    z_ref[0] = branch.astype(BF)
    out_ref[0] = h_ref[0] + mod_ref[0, 5:6] * branch


def after_cross(mixed, hidden, mod, weight, bias):
    clips, frames, width = hidden.shape
    rows = row_block(frames)
    spec = rows_spec(rows, width)
    return call(
        after_cross_kernel,
        (clips, frames // rows),
        [
            spec,
            spec,
            clip_spec(9, width),
            whole_spec((width, width)),
            whole_spec((1, width)),
        ],
        [spec, spec],
        [struct(hidden.shape, BF), struct(hidden.shape, F32)],
        "after_cross",
    )(mixed, hidden, mod, weight, bias)


GELU_ROOT = math.sqrt(2.0 / math.pi)


def feed_kernel(
    h_ref,
    dy_ref,
    mod_ref,
    up_ref,
    upb_ref,
    down_ref,
    downb_ref,
    out_ref,
    dh_ref,
    dup_ref,
    ddown_ref,
    dupb_ref,
    ddownb_ref,
    sums_ref,
    in_s,
    int_s,
    dz_s,
    dzt_s,
    z_s,
    act_s,
    du_s,
    *,
    clips,
    frames,
    rows,
):
    step = pl.program_id(0)
    last = pl.num_programs(0) - 1
    spans = [
        (clip, start, clip * frames + start)
        for clip in range(clips)
        for start in range(0, frames, rows)
    ]

    @pl.when(step == 0)
    def _():
        bias_sum = jnp.zeros((1, h_ref.shape[2]), F32)
        for clip, start, at in spans:
            normed, _ = normalize(h_ref[clip, start : start + rows])
            third_in = normed * (1.0 + mod_ref[clip, 7:8]) + mod_ref[clip, 6:7]
            dz = (mod_ref[clip, 8:9] * dy_ref[clip, start : start + rows].astype(F32)).astype(BF)
            in_s[at : at + rows] = third_in.astype(BF)
            dz_s[at : at + rows] = dz
            bias_sum += column_sum(dz.astype(F32))
        ddownb_ref[...] = bias_sum
        int_s[...] = in_s[...].T
        dzt_s[...] = dz_s[...].T
        z_s[...] = jnp.zeros_like(z_s)
        dh_ref[...] = jnp.zeros_like(dh_ref)

    up, down = up_ref[...], down_ref[...]

    per = frames // rows

    def one(index):
        at = pl.multiple_of(index * rows, rows)
        here = pl.ds(at, rows)
        hidden = nn(in_s[here], up) + upb_ref[...]
        square = hidden * hidden
        tanh = jnp.tanh(hidden * (GELU_ROOT + (GELU_ROOT * 0.044715) * square))
        half = 0.5 + 0.5 * tanh
        lifted = hidden * half
        activated = lifted.astype(BF)
        slope = half + lifted * (1.0 - tanh) * (
            GELU_ROOT + (GELU_ROOT * 3 * 0.044715) * square
        )
        grad_hidden = (nt(dz_s[here], down) * slope).astype(BF)
        z_s[here] += nn(activated, down)
        spot = pl.ds(pl.multiple_of(index % per * rows, rows), rows)
        dh_ref[index // per, spot] += nt(grad_hidden, up)
        act_s[here] = activated
        du_s[here] = grad_hidden

    def one_clip(clip, _):
        for part in range(per):
            one(clip * per + part)
        return 0

    lax.fori_loop(0, clips, one_clip, 0)
    dup_ref[...] = nn(int_s[...], du_s[...]).astype(BF)
    ddown_ref[...] = nn(dzt_s[...], act_s[...]).T.astype(BF)
    dupb_ref[...] = column_sum(du_s[...].astype(F32))

    @pl.when(step == last)
    def _():
        for clip in range(clips):
            sums = None
            for start in range(0, frames, rows):
                at = clip * frames + start
                block = slice(start, start + rows)
                hidden = h_ref[clip, block]
                dy = dy_ref[clip, block].astype(F32)
                branch = z_s[at : at + rows] + downb_ref[...]
                out_ref[clip, block] = (hidden + mod_ref[clip, 8:9] * branch).astype(BF)
                normed, inverse = normalize(hidden)
                grad_in = dh_ref[clip, block]
                dh_ref[clip, block] = dy + norm_back(
                    normed, inverse, grad_in * (1.0 + mod_ref[clip, 7:8])
                )
                here = [
                    column_sum(grad_in),
                    column_sum(grad_in * normed),
                    column_sum(dy * branch),
                ]
                sums = here if sums is None else [a + b for a, b in zip(sums, here)]
            for index in range(3):
                sums_ref[clip, index : index + 1] = sums[index]


def feed(hidden, cotangent, mod, up, up_bias, down, down_bias, block=768):
    clips, frames, width = hidden.shape
    inner = up.shape[1]
    rows = row_block(frames)
    tokens = clips * frames

    def once(shape):
        return pl.BlockSpec(
            shape, lambda j: (0,) * len(shape), pipeline_mode=pl.Buffered(1)
        )

    def columns(count):
        return pl.BlockSpec((count, block), lambda j: (0, j))

    lines = pl.BlockSpec((block, width), lambda j: (j, 0))
    cube = once((clips, frames, width))
    return call(
        functools.partial(feed_kernel, clips=clips, frames=frames, rows=rows),
        (inner // block,),
        [
            cube,
            cube,
            once(mod.shape),
            columns(width),
            columns(1),
            lines,
            once((1, width)),
        ],
        [
            cube,
            cube,
            columns(width),
            lines,
            columns(1),
            once((1, width)),
            once((clips, 3, width)),
        ],
        [
            struct(hidden.shape, BF),
            struct(hidden.shape, F32),
            struct(up.shape, BF),
            struct(down.shape, BF),
            struct((1, inner), F32),
            struct((1, width), F32),
            struct((clips, 3, width), F32),
        ],
        "feed",
        [
            pltpu.VMEM((tokens, width), BF),
            pltpu.VMEM((width, tokens), BF),
            pltpu.VMEM((tokens, width), BF),
            pltpu.VMEM((width, tokens), BF),
            pltpu.VMEM((tokens, width), F32),
            pltpu.VMEM((tokens, block), BF),
            pltpu.VMEM((tokens, block), BF),
        ],
    )(hidden, cotangent, mod, up, up_bias, down, down_bias)


def ends():
    i, j = pl.program_id(0), pl.program_id(1)
    first = (i == 0) & (j == 0)
    last = (i == pl.num_programs(0) - 1) & (j == pl.num_programs(1) - 1)
    return j == 0, first, last


def before_cross_kernel(
    dh_ref, z_ref, o_ref, mod_ref, w_ref, do_ref, dw_ref, db_ref, sums_ref, ot_s, dz_s
):
    new_clip, first, last = ends()
    clear_at(new_clip, sums_ref)
    clear_at(first, db_ref)
    dh = dh_ref[0]
    here = span_of(dh.shape[0])
    dz = (mod_ref[0, 5:6] * dh).astype(BF)
    dz_s[here] = dz
    ot_s[here] = o_ref[0]
    sums_ref[0] += column_sum(dh * z_ref[0].astype(F32))
    db_ref[...] += column_sum(dz.astype(F32))
    do_ref[0] = nt(dz, w_ref[...]).astype(BF)

    @pl.when(last)
    def _():
        dw_ref[...] = tn(ot_s[...], dz_s[...]).astype(BF)


def before_cross(dh, branch, mixed, mod, weight):
    clips, frames, width = dh.shape
    rows = row_block(frames)
    spec = rows_spec(rows, width)
    square = whole_spec((width, width))
    return call(
        before_cross_kernel,
        (clips, frames // rows),
        [spec, spec, spec, clip_spec(9, width), square],
        [spec, square, whole_spec((1, width)), clip_spec(1, width)],
        [
            struct(dh.shape, BF),
            struct((width, width), BF),
            struct((1, width), F32),
            struct((clips, 1, width), F32),
        ],
        "before_cross",
        [pltpu.VMEM((clips * frames, width), BF)] * 2,
    )(dh, branch, mixed, mod, weight)


def before_self_kernel(
    dq_ref,
    h_ref,
    dh_ref,
    z_ref,
    o_ref,
    mod_ref,
    wq_ref,
    wo_ref,
    cap_ref,
    dk_ref,
    dv_ref,
    out_ref,
    do_ref,
    dwq_ref,
    dwo_ref,
    db_ref,
    sums_ref,
    dkv_ref,
    in_s,
    dq_s,
    o_s,
    dz_s,
):
    new_clip, first, last = ends()
    clear_at(new_clip, sums_ref)
    clear_at(first, db_ref)
    here = span_of(dq_ref.shape[1])
    normed, inverse = normalize(h_ref[0])
    in_s[here] = (normed * (1.0 + mod_ref[0, 4:5]) + mod_ref[0, 3:4]).astype(BF)
    grad_query = dq_ref[0]
    dq_s[here] = grad_query
    o_s[here] = o_ref[0]
    grad_in = nt(grad_query, wq_ref[...])
    dh = dh_ref[0] + norm_back(normed, inverse, grad_in * (1.0 + mod_ref[0, 4:5]))
    out_ref[0] = dh
    dz = (mod_ref[0, 2:3] * dh).astype(BF)
    dz_s[here] = dz
    sums_ref[0] += jnp.concatenate(
        [
            column_sum(grad_in),
            column_sum(grad_in * normed),
            column_sum(dh * z_ref[0].astype(F32)),
        ],
        axis=0,
    )
    db_ref[...] += column_sum(dz.astype(F32))
    do_ref[0] = nt(dz, wo_ref[...]).astype(BF)

    @pl.when(last)
    def _():
        dwq_ref[...] = tn(in_s[...], dq_s[...]).astype(BF)
        dwo_ref[...] = tn(o_s[...], dz_s[...]).astype(BF)
        turned = cap_ref[...].T
        half = dk_ref.shape[1]
        dkv_ref[:, :half] = nn(turned, dk_ref[...]).astype(BF)
        dkv_ref[:, half:] = nn(turned, dv_ref[...]).astype(BF)


def before_self(
    grad_query, hidden, dh, branch, mixed, mod, query_weight, weight, captions, grad_k, grad_v
):
    clips, frames, width = dh.shape
    captions, grad_k, grad_v = [t.reshape(-1, t.shape[2]) for t in (captions, grad_k, grad_v)]
    keyval_shape = (captions.shape[1], 2 * width)
    rows = row_block(frames)
    spec = rows_spec(rows, width)
    square = whole_spec((width, width))
    return call(
        before_self_kernel,
        (clips, frames // rows),
        [spec, spec, spec, spec, spec, clip_spec(9, width), square, square]
        + [whole_spec(t.shape) for t in (captions, grad_k, grad_v)],
        [
            spec,
            spec,
            square,
            square,
            whole_spec((1, width)),
            clip_spec(3, width),
            whole_spec(keyval_shape),
        ],
        [
            struct(dh.shape, F32),
            struct(dh.shape, BF),
            struct((width, width), BF),
            struct((width, width), BF),
            struct((1, width), F32),
            struct((clips, 3, width), F32),
            struct(keyval_shape, BF),
        ],
        "before_self",
        [pltpu.VMEM((clips * frames, width), BF)] * 4,
    )(
        grad_query,
        hidden,
        dh,
        branch,
        mixed,
        mod,
        query_weight,
        weight,
        captions,
        grad_k,
        grad_v,
    )


def input_kernel(
    dq_ref, dk_ref, dv_ref, x_ref, dh_ref, mod_ref, w_ref, out_ref, dw_ref, sums_ref, in_s, g_s
):
    new_clip, _, last = ends()
    width = x_ref.shape[2]
    clear_at(new_clip, sums_ref)
    here = span_of(x_ref.shape[1])
    normed, inverse = normalize(x_ref[0].astype(F32))
    in_s[here] = (normed * (1.0 + mod_ref[0, 1:2]) + mod_ref[0, 0:1]).astype(BF)
    grad_in = None
    for index, ref in enumerate((dq_ref, dk_ref, dv_ref)):
        columns = slice(index * width, (index + 1) * width)
        grad = ref[0]
        g_s[here, columns] = grad
        part = nt(grad, w_ref[:, columns])
        grad_in = part if grad_in is None else grad_in + part
    out_ref[0] = (
        dh_ref[0] + norm_back(normed, inverse, grad_in * (1.0 + mod_ref[0, 1:2]))
    ).astype(BF)
    sums_ref[0] += jnp.concatenate(
        [column_sum(grad_in), column_sum(grad_in * normed)], axis=0
    )

    @pl.when(last)
    def _():
        turned = in_s[...].T
        for index in range(3):
            columns = slice(index * width, (index + 1) * width)
            dw_ref[:, columns] = nn(turned, g_s[:, columns]).astype(BF)


def input_back(grads, latents, dh, mod, weight):
    clips, frames, width = dh.shape
    rows = row_block(frames)
    spec = rows_spec(rows, width)
    return call(
        input_kernel,
        (clips, frames // rows),
        [spec] * 5 + [clip_spec(9, width), whole_spec(weight.shape)],
        [spec, whole_spec(weight.shape), clip_spec(2, width)],
        [
            struct(dh.shape, BF),
            struct(weight.shape, BF),
            struct((clips, 2, width), F32),
        ],
        "input_back",
        [
            pltpu.VMEM((clips * frames, width), BF),
            pltpu.VMEM((clips * frames, weight.shape[1]), BF),
        ],
    )(*grads, latents, dh, mod, weight)


def block_pass(latents, captions, lengths, cotangent, mod, triple_weight, front, back):
    triple, mixed_one, lse_one, weights = front(latents, mod, triple_weight)
    (
        output_weight,
        output_bias,
        cross_query,
        cross_keyval,
        cross_output,
        cross_bias,
        up_weight,
        up_bias,
        down_weight,
        down_bias,
    ) = weights
    groups = HEADS // 2
    branch_one, hidden_one, cross_queries, pairs = after_self(
        mixed_one, latents, mod, output_weight, output_bias, cross_query, captions, cross_keyval
    )
    mixed_two, lse_two = attend_forward(cross_queries, 0, pairs, groups, lengths, "cross_forward")
    branch_two, hidden_two = after_cross(mixed_two, hidden_one, mod, cross_output, cross_bias)
    output, dh_two, grad_up, grad_down, grad_up_bias, grad_down_bias, sums_three = feed(
        hidden_two, cotangent, mod, up_weight, up_bias, down_weight, down_bias
    )
    grad_mixed_two, grad_cross_output, grad_cross_bias, gate_two = before_cross(
        dh_two, branch_two, mixed_two, mod, cross_output
    )
    grad_cq, grad_ck, grad_cv = attend_backward(
        cross_queries,
        0,
        pairs,
        groups,
        lengths,
        grad_mixed_two,
        mixed_two,
        lse_two,
        "cross_back",
        2,
    )
    (
        dh_one,
        grad_mixed_one,
        grad_cross_query,
        grad_output,
        grad_output_bias,
        sums_two,
        grad_keyval,
    ) = before_self(
        grad_cq,
        hidden_one,
        dh_two,
        branch_one,
        mixed_one,
        mod,
        cross_query,
        output_weight,
        captions,
        grad_ck,
        grad_cv,
    )
    gradients = [
        grad_output,
        grad_output_bias,
        grad_cross_query,
        grad_keyval,
        grad_cross_output,
        grad_cross_bias,
        grad_up,
        grad_up_bias,
        grad_down,
        grad_down_bias,
    ]
    input_grad, grad_triple, sums_one, rest = back(
        triple, grad_mixed_one, mixed_one, lse_one, latents, dh_one, mod, triple_weight, gradients
    )
    grad_mod = jnp.concatenate(
        [sums_one, sums_two[:, 2:], sums_two[:, :2], gate_two, sums_three], axis=1
    ).astype(BF)
    return output, input_grad, grad_mod, grad_triple, gradients, rest


def plain_front(weights, latents, mod, triple_weight):
    groups = HEADS // 2
    triple = qkv_forward(latents, mod, triple_weight)
    mixed, lse = attend_forward(triple, groups, triple, 2 * groups, None, "self_forward", 2)
    return triple, mixed, lse, weights


def plain_back(triple, grad_mixed, mixed, lse, latents, dh, mod, triple_weight, gradients):
    groups = HEADS // 2
    grads = attend_backward(
        triple, groups, triple, 2 * groups, None, grad_mixed, mixed, lse, "self_back", 2
    )
    return *input_back(grads, latents, dh, mod, triple_weight), None


LANE = 128
TILE = 16


def linear_layout():
    spots = []
    offset = 0
    for shape in layout_sizes():
        number = math.prod(shape) // LANE
        spots.append((offset, number, shape))
        offset += number
    return spots


class Group:
    def __init__(self, devices, inner, share, first, last):
        self.devices, self.share, self.first, self.last = devices, share, first, last
        self.padded = -(-share // TILE) * TILE
        owners, total = {}, 0
        for owner in range(first // share, (last - 1) // share + 1):
            low = max(first - owner * share, 0) // TILE
            high = -(-min(last - owner * share, share) // TILE)
            owners[owner] = [low, high]
            total += high - low
        self.tiles = 2 * -(-total // (2 * devices))
        self.chunk = self.tiles * TILE
        self.half = self.chunk // 2
        small = self.tiles // 9 * TILE
        large = self.half - small
        self.parts = (
            (0, large),
            (large, large),
            (2 * large, small),
            (2 * large + small, small),
        )
        self.folds = next(
            n
            for n in range(1, 99)
            if self.half % (n * TILE) == 0 and self.half // n <= 512
        )
        room = [self.tiles] * devices
        self.pieces = []

        def give(owner, device):
            low, high = owners[owner]
            take = min(high - low, room[device])
            if take > 0:
                place = self.tiles - room[device]
                self.pieces.append((owner, device, low * TILE, place * TILE, take * TILE))
                room[device] -= take
                owners[owner][0] += take

        for flip in (0, 2 * inner, inner):
            for owner in owners:
                give(owner, owner ^ flip)
        for owner in owners:
            while owners[owner][0] < owners[owner][1]:
                give(owner, max(range(devices), key=lambda device: room[device]))

    def find(self, row):
        owner, at = divmod(row, self.share)
        for holder, device, start, place, count in self.pieces:
            if holder == owner and start <= at < start + count:
                return device, place + at - start, min(self.share, start + count) - at
        raise ValueError(row)

    def segments(self, start, count):
        found = []
        row = start
        while row < start + count:
            chunk, place, left = self.find(row)
            take = min(left, start + count - row)
            found.append((chunk, place, row, take))
            row += take
        return found

    def moves(self):
        return self.pieces


def unpack_kernel(*refs, plan, indices, step):
    n = len(indices)
    spots = linear_layout()
    g_ref, outs, rest = refs[0], refs[1 : 1 + n], refs[1 + n :]
    lin, in_sem, out_sem = rest[0], rest[1], rest[2]
    stages, results = rest[3 : 3 + n], rest[3 + n :]
    loads = []
    for which, index in enumerate(indices):
        offset, number, _ = spots[index]
        place = 0
        mine = []
        for slot, (chunk, row, at, take) in enumerate(plan.segments(offset, number)):
            low = row // TILE * TILE
            high = -(-(row + take) // TILE) * TILE
            copy = pltpu.make_async_copy(
                g_ref.at[chunk, pl.ds(low, high - low)],
                stages[which].at[pl.ds(place, high - low)],
                in_sem.at[which, slot],
            )
            copy.start()
            mine.append((copy, place, row - low, high - low, at - offset, take))
            place += high - low
        loads.append(mine)
    stores = []
    for which, index in enumerate(indices):
        offset, number, shape = spots[index]
        for copy, place, skip, size, at, take in loads[which]:
            copy.wait()
            first = stages[which][place : place + TILE].astype(F32)
            lin[at : at + TILE - skip] = first[skip:]
            blocks, tail = divmod(size - TILE, step)

            def body(i, _, place=place, at=at, skip=skip, which=which):
                source = pl.multiple_of(place + TILE + i * step, TILE)
                lin[pl.ds(at + TILE - skip + i * step, step)] = stages[which][
                    pl.ds(source, step)
                ].astype(F32)
                return 0

            lax.fori_loop(0, blocks, body, 0)
            if tail:
                source = place + TILE + blocks * step
                target = at + TILE - skip + blocks * step
                lin[target : target + tail] = stages[which][source : source + tail].astype(F32)
        if len(shape) == 1:
            for c in range(number):
                results[which][0:1, c * LANE : (c + 1) * LANE] = lin[c : c + 1]
        else:
            high, wide = shape
            count = wide // LANE
            rows = 64

            def turn(i, _, which=which, count=count):
                top = pl.multiple_of(i * rows, rows)
                for c in range(count):
                    results[which][pl.ds(top, rows), c * LANE : (c + 1) * LANE] = lin[
                        pl.ds(top * count + c, rows, stride=count)
                    ].astype(BF)
                return 0

            lax.fori_loop(0, high // rows, turn, 0)
        copy = pltpu.make_async_copy(results[which], outs[which], out_sem.at[which])
        copy.start()
        stores.append(copy)
    for copy in stores:
        copy.wait()


def unpack_weights(gathered, plan, indices, step=128):
    spots = linear_layout()
    stage_shapes, result_shapes, most, tallest = [], [], 0, 0
    for index in indices:
        offset, number, shape = spots[index]
        found = plan.segments(offset, number)
        size = sum(-(-(r + t) // TILE) * TILE - r // TILE * TILE for _, r, _, t in found)
        stage_shapes.append(pltpu.VMEM((size, LANE), BF))
        most = max(most, len(found))
        tallest = max(tallest, number)
        result_shapes.append((shape, BF) if len(shape) == 2 else ((1, shape[0]), F32))
    anywhere = pl.BlockSpec(memory_space=pl.ANY)
    return pl.pallas_call(
        functools.partial(unpack_kernel, plan=plan, indices=indices, step=step),
        in_specs=[anywhere],
        out_specs=[anywhere] * len(indices),
        out_shape=[jax.ShapeDtypeStruct(s, t) for s, t in result_shapes],
        scratch_shapes=[
            pltpu.VMEM((tallest + 2 * TILE, LANE), F32),
            pltpu.SemaphoreType.DMA((len(indices), most)),
            pltpu.SemaphoreType.DMA((len(indices),)),
        ]
        + stage_shapes
        + [pltpu.VMEM(s, t) for s, t in result_shapes],
        compiler_params=pltpu.CompilerParams(vmem_limit_bytes=VMEM_LIMIT),
        name="unpack",
    )(gathered)


def pack_kernel(*refs, plan, indices, step):
    n = len(indices)
    spots = linear_layout()
    ins, out_ref, rest = refs[:n], refs[n], refs[n + 1 :]
    lin, stage, in_sem, out_sem = rest[:4]
    held = rest[4:]
    copies = []
    for which in range(n):
        copy = pltpu.make_async_copy(ins[which], held[which], in_sem.at[which])
        copy.start()
        copies.append(copy)
    stores = []
    begin = spots[indices[0]][0]
    total = spots[indices[-1]][0] + spots[indices[-1]][1] - begin
    pieces = plan.segments(begin, total)
    place = 0
    done = -TILE
    lin[0:TILE] = jnp.zeros((TILE, LANE), F32)
    slot = 0
    for which, index in enumerate(indices):
        offset, number, shape = spots[index]
        copies[which].wait()
        if len(shape) == 1:
            for c in range(number):
                lin[TILE + c : TILE + c + 1] = held[which][0:1, c * LANE : (c + 1) * LANE]
        else:
            high, wide = shape
            count = wide // LANE
            rows = 64

            def turn(i, _, which=which, count=count):
                top = pl.multiple_of(i * rows, rows)
                for c in range(count):
                    lin[pl.ds(TILE + top * count + c, rows, stride=count)] = held[which][
                        pl.ds(top, rows), c * LANE : (c + 1) * LANE
                    ].astype(F32)
                return 0

            lax.fori_loop(0, high // rows, turn, 0)
        low, high_row = offset - begin, offset - begin + number
        last = which == n - 1
        while slot < len(pieces):
            chunk, row, at, take = pieces[slot]
            at -= begin
            head = row - row // TILE * TILE
            start, stop = at - head, at + take
            ceil = start + -(-(stop - start) // TILE) * TILE
            first = max(start, done)
            whole = stop <= high_row
            end = ceil if whole else start + (high_row - start) // TILE * TILE
            if end > first:
                base = row - head + first - start
                blocks, tail = divmod(end - first, step)
                shift = TILE + first - low

                def body(i, _, place=place, shift=shift):
                    target = pl.multiple_of(place + i * step, TILE)
                    stage[pl.ds(target, step)] = lin[pl.ds(shift + i * step, step)].astype(BF)
                    return 0

                lax.fori_loop(0, blocks, body, 0)
                if tail:
                    source = shift + blocks * step
                    target = place + blocks * step
                    stage[target : target + tail] = lin[source : source + tail].astype(BF)
                copy = pltpu.make_async_copy(
                    stage.at[pl.ds(place, end - first)],
                    out_ref.at[chunk, pl.ds(base, end - first)],
                    out_sem.at[len(stores)],
                )
                copy.start()
                stores.append(copy)
                place += end - first
                done = end
            if not whole:
                break
            done = stop if slot + 1 == len(pieces) else min(done, stop)
            slot += 1
        if not last:
            lin[0:TILE] = lin[number : number + TILE]
    for copy in stores:
        copy.wait()


def pack_grads(grads, plan, indices, step=128):
    spots = linear_layout()
    tallest = max(spots[i][1] for i in indices)
    begin = spots[indices[0]][0]
    total = spots[indices[-1]][0] + spots[indices[-1]][1] - begin
    count = len(plan.segments(begin, total))
    anywhere = pl.BlockSpec(memory_space=pl.ANY)
    return pl.pallas_call(
        functools.partial(pack_kernel, plan=plan, indices=indices, step=step),
        in_specs=[anywhere] * len(indices),
        out_specs=anywhere,
        out_shape=jax.ShapeDtypeStruct((plan.devices, plan.chunk, LANE), BF),
        scratch_shapes=[
            pltpu.VMEM((tallest + 2 * TILE, LANE), F32),
            pltpu.VMEM((total + 2 * TILE * (count + len(indices)), LANE), BF),
            pltpu.SemaphoreType.DMA((len(indices),)),
            pltpu.SemaphoreType.DMA((count + len(indices),)),
        ]
        + [pltpu.VMEM(g.shape, g.dtype) for g in grads],
        compiler_params=pltpu.CompilerParams(vmem_limit_bytes=VMEM_LIMIT),
        name="pack",
    )(*grads)


MESH = pl.DeviceIdType.MESH


def place_of():
    dp, fs = lax.axis_index("dp"), lax.axis_index("fsdp")
    return dp, fs, dp // 2, dp % 2, fs // 2, fs % 2


def meet_all(me, devices, inner):
    barrier = pltpu.get_barrier_semaphore()

    def greet(i, _):
        other = (me + i) % devices
        pl.semaphore_signal(
            barrier, inc=1, device_id=(other // inner, other % inner), device_id_type=MESH
        )
        return 0

    lax.fori_loop(1, devices, greet, 0)
    pl.semaphore_wait(barrier, devices - 1)


class Trade:
    def __init__(self, source, target, own_sem, send_sem, recv_sem, group, inner, senders, receivers):
        self.source, self.target, self.own_sem = source, target, own_sem
        self.send_sem, self.recv_sem = send_sem, recv_sem
        self.devices, self.inner = group.devices, inner
        self.senders, self.receivers = senders, receivers
        self.me = lax.axis_index("dp") * inner + lax.axis_index("fsdp")
        self.many = len(source.shape) == 3

    def piece(self, target):
        return self.source.at[target] if self.many else self.source

    def copy(self, source, target):
        return pltpu.make_async_remote_copy(
            src_ref=self.piece(target),
            dst_ref=self.target.at[source],
            send_sem=self.send_sem.at[target],
            recv_sem=self.recv_sem.at[source],
            device_id=(target // self.inner, target % self.inner),
            device_id_type=MESH,
        )

    def own(self):
        return pltpu.make_async_copy(
            self.piece(self.me), self.target.at[self.me], self.own_sem
        )

    def each(self, act):
        def body(i, _):
            act((self.me + i) % self.devices)
            return 0

        lax.fori_loop(1, self.devices, body, 0)

    def both(self):
        return (self.me < self.senders) & (self.me < self.receivers)

    def start(self):
        pl.when(self.both())(lambda: self.own().start())

        def act(other):
            ok = (self.me < self.senders) & (other < self.receivers)
            pl.when(ok)(lambda: self.copy(self.me, other).start())

        self.each(act)

    def wait(self):
        pl.when(self.both())(lambda: self.own().wait())

        def landed(other):
            ok = (other < self.senders) & (self.me < self.receivers)
            pl.when(ok)(lambda: self.copy(other, other).wait_recv())

        def gone(other):
            ok = (self.me < self.senders) & (other < self.receivers)
            pl.when(ok)(lambda: self.copy(self.me, other).wait_send())

        self.each(landed)
        self.each(gone)


def when_all(conditions):
    total = None
    for condition in conditions:
        if condition is not None:
            total = condition if total is None else total & condition
    return total


def guarded(condition, body):
    if condition is None:
        body()
    else:
        pl.when(condition)(body)


class Deal:
    def __init__(self, group, source, target, send_sem, recv_sem, inner, back):
        self.source, self.target, self.back = source, target, back
        self.send_sem, self.recv_sem, self.inner = send_sem, recv_sem, inner
        self.me = lax.axis_index("dp") * inner + lax.axis_index("fsdp")
        self.moves = []
        for owner, device, row, place, count in group.moves():
            if back:
                self.moves.append((device, owner, place, row, count))
            else:
                self.moves.append((owner, device, row, place, count))

    def copy(self, move):
        source, target, start, place, count = move
        out = [m for m in self.moves if m[0] == source].index(move)
        into = [m for m in self.moves if m[1] == target].index(move)
        from_ref = self.source.at[pl.ds(start, count)]
        to_ref = self.target.at[pl.ds(place, count)]
        if source == target:
            return pltpu.make_async_copy(from_ref, to_ref, self.recv_sem.at[into])
        return pltpu.make_async_remote_copy(
            src_ref=from_ref,
            dst_ref=to_ref,
            send_sem=self.send_sem.at[out],
            recv_sem=self.recv_sem.at[into],
            device_id=(target // self.inner, target % self.inner),
            device_id_type=MESH,
        )

    def each(self, key, act):
        for device in sorted({m[key] for m in self.moves}):
            mine = [m for m in self.moves if m[key] == device]

            @pl.when(self.me == device)
            def _(mine=mine):
                for move in mine:
                    act(move)

    def start(self):
        self.each(0, lambda move: self.copy(move).start())

    def landed(self):
        def act(move):
            if move[0] == move[1]:
                self.copy(move).wait()
            else:
                self.copy(move).wait_recv()

        self.each(1, act)

    def gone(self):
        def act(move):
            if move[0] != move[1]:
                self.copy(move).wait_send()

        self.each(0, act)

    @staticmethod
    def semaphores(group, back):
        sends = recvs = 0
        for device in range(group.devices):
            sends = max(sends, sum(1 for m in group.moves() if m[1 if back else 0] == device))
            recvs = max(recvs, sum(1 for m in group.moves() if m[0 if back else 1] == device))
        dma = pltpu.SemaphoreType.DMA
        return [dma((sends,)), dma((recvs,))]


def remote_call(body, in_specs, out_specs, out_shape, scratch, collective, name, grid=()):
    return pl.pallas_call(
        body,
        grid=grid,
        in_specs=in_specs,
        out_specs=out_specs,
        out_shape=out_shape,
        scratch_shapes=scratch,
        compiler_params=pltpu.CompilerParams(
            collective_id=collective, has_side_effects=True, vmem_limit_bytes=VMEM_LIMIT
        ),
        name=name,
    )


ANYWHERE = pl.BlockSpec(memory_space=pl.ANY)


def start_kernel(
    step_ref, slot_ref, all_ref, chunk_ref, own_sem, send_sem, recv_sem, deal_send, deal_recv,
    *, group, inner
):
    me = lax.axis_index("dp") * inner + lax.axis_index("fsdp")
    meet_all(me, group.devices, inner)
    deal = Deal(group, slot_ref, chunk_ref, deal_send, deal_recv, inner, False)
    trade = Trade(
        step_ref, all_ref, own_sem, send_sem, recv_sem, group, inner, group.devices, group.devices
    )
    trade.start()
    deal.start()
    trade.wait()
    deal.landed()
    deal.gone()


def start_chunks(steps, slot, group, inner, collective):
    dma = pltpu.SemaphoreType.DMA
    return remote_call(
        functools.partial(start_kernel, group=group, inner=inner),
        [ANYWHERE] * 2,
        [ANYWHERE] * 2,
        [
            jax.ShapeDtypeStruct((group.devices, *steps.shape), steps.dtype),
            jax.ShapeDtypeStruct((group.chunk, LANE), BF),
        ],
        [dma, dma((group.devices,)), dma((group.devices,))] + Deal.semaphores(group, False),
        collective,
        "start_chunks",
    )(steps, slot)


class Gather:
    def __init__(self, group, inner, chunk_ref, out_ref, own_sem, send_sem, recv_sem):
        self.group, self.inner = group, inner
        self.chunk_ref, self.out_ref = chunk_ref, out_ref
        self.send_sem, self.recv_sem = send_sem, recv_sem
        dp, fs, self.y, self.x, self.z, self.c = place_of()
        self.levels = inner // 2
        self.own = pltpu.make_async_copy(chunk_ref, out_ref.at[dp * inner + fs], own_sem)
        self.across = {
            "up": (dp, fs + 2),
            "down": (dp, fs - 2),
            "x": (dp + 1 - 2 * self.x, fs),
            "y": (dp + 2 - 4 * self.y, fs),
            "twin": (dp, fs + 1 - 2 * self.c),
        }
        self.kinds = tuple(self.across)
        self.closing = False

    @staticmethod
    def semaphores(group):
        dma = pltpu.SemaphoreType.DMA
        return [dma, dma((5, group.devices // 2, 4)), dma((group.devices, 4))]

    def copy(self, kind, yy, xx, zz, part, cc=None, mine=False):
        core = self.c if cc is None else cc
        column = yy * 2 + xx
        index = column * self.inner + zz * 2 + core
        rows = pl.ds(*self.group.parts[part])
        return pltpu.make_async_remote_copy(
            src_ref=self.chunk_ref.at[rows] if mine else self.out_ref.at[index, rows],
            dst_ref=self.out_ref.at[index, rows],
            send_sem=self.send_sem.at[
                self.kinds.index(kind), column * self.levels + zz, part
            ],
            recv_sem=self.recv_sem.at[index, part],
            device_id=self.across[kind],
            device_id_type=MESH,
        )

    def send(self, condition, kind, yy, xx, zz, part, mine=False):
        copy = functools.partial(self.copy, kind, yy, xx, zz, part, mine=mine)
        if self.closing:
            guarded(condition, lambda: copy().wait_send())
        else:
            guarded(condition, lambda: copy().start())

    def arrive(self, condition, yy, xx, zz, part):
        if self.closing:
            return
        guarded(condition, lambda: self.copy("x", yy, xx, zz, part).wait_recv())

    def spread(self, distance):
        for sign in (1, -1) if distance else (0,):
            zz = self.z + sign * distance
            inside = when_all(
                [zz < self.levels if sign > 0 else None, zz >= 0 if sign < 0 else None]
            )
            yield zz, sign, inside

    def relay(self, distance, sign, inside, yy, xx, zz):
        own = yy is self.y and xx is self.x
        for part in (2, 3):
            mine = own and distance == 0
            if not mine:
                self.arrive(inside, yy, xx, zz, part)
            if distance == 0:
                if own:
                    kinds = ("x", "y") if part == 2 else ("y", "x")
                elif part == 2 and yy is self.y:
                    kinds = ("y",)
                elif part == 3 and xx is self.x:
                    kinds = ("x",)
                else:
                    kinds = ()
                for kind in kinds:
                    self.send(inside, kind, yy, xx, zz, part, mine)
            if sign <= 0:
                on = when_all([inside, self.z < self.levels - 1])
                self.send(on, "up", yy, xx, zz, part, mine)
            if sign >= 0:
                self.send(when_all([inside, self.z > 0]), "down", yy, xx, zz, part, mine)
            self.send(inside, "twin", yy, xx, zz, part, mine)

    def turn(self, turn):
        y, x, z, levels = self.y, self.x, self.z, self.levels
        if turn == 0 and not self.closing:
            self.own.start()
        if turn < levels:
            for zz, sign, inside in self.spread(turn):
                mine = turn == 0
                for part in range(2):
                    if turn:
                        self.arrive(inside, y, x, zz, part)
                    if sign <= 0:
                        self.send(when_all([inside, z < levels - 1]), "up", y, x, zz, part, mine)
                    if sign >= 0:
                        self.send(when_all([inside, z > 0]), "down", y, x, zz, part, mine)
                    for kind in ("x", "y") if part else ("y", "x"):
                        self.send(inside, kind, y, x, zz, part, mine)
                    self.send(inside, "twin", y, x, zz, part, mine)
                self.relay(turn, sign, inside, y, x, zz)
        if 1 <= turn <= levels:
            for zz, sign, inside in self.spread(turn - 1):
                self.arrive(inside, y, 1 - x, zz, 0)
                self.send(inside, "y", y, 1 - x, zz, 0)
                self.send(inside, "twin", y, 1 - x, zz, 0)
                self.arrive(inside, 1 - y, x, zz, 1)
                self.send(inside, "x", 1 - y, x, zz, 1)
                self.send(inside, "twin", 1 - y, x, zz, 1)
                self.arrive(inside, 1 - y, x, zz, 0)
                self.send(inside, "twin", 1 - y, x, zz, 0)
                self.arrive(inside, y, 1 - x, zz, 1)
                self.send(inside, "twin", y, 1 - x, zz, 1)
                self.relay(turn - 1, sign, inside, y, 1 - x, zz)
                self.relay(turn - 1, sign, inside, 1 - y, x, zz)
        if turn >= 2:
            for zz, sign, inside in self.spread(turn - 2):
                for part in range(2):
                    self.arrive(inside, 1 - y, 1 - x, zz, part)
                    self.send(inside, "twin", 1 - y, 1 - x, zz, part)
                self.relay(turn - 2, sign, inside, 1 - y, 1 - x, zz)

    def finish(self):
        def twin_arrivals(i, _):
            column, zz = i // self.levels, i % self.levels
            for part in range(4):
                self.copy("twin", column // 2, column % 2, zz, part, 1 - self.c).wait_recv()
            return 0

        lax.fori_loop(0, 4 * self.levels, twin_arrivals, 0)
        self.closing = True
        for turn in range(self.levels + 2):
            self.turn(turn)
        self.own.wait()


class ShortGather:
    def __init__(self, group, inner, chunk_ref, out_ref, own_sem, send_sem, recv_sem):
        self.group, self.inner = group, inner
        self.chunk_ref, self.out_ref = chunk_ref, out_ref
        self.send_sem, self.recv_sem = send_sem, recv_sem
        dp, fs, self.y, self.x, self.z, self.c = place_of()
        self.levels = inner // 2
        self.own = pltpu.make_async_copy(chunk_ref, out_ref.at[dp * inner + fs], own_sem)
        self.across = {
            "z1": (dp, self.level(-1) * 2 + self.c),
            "z2": (dp, self.level(-2) * 2 + self.c),
            "z3": (dp, self.level(-3) * 2 + self.c),
            "x": (dp + 1 - 2 * self.x, fs),
            "y": (dp + 2 - 4 * self.y, fs),
            "twin": (dp, fs + 1 - 2 * self.c),
        }
        self.kinds = tuple(self.across)
        self.closing = False

    @staticmethod
    def semaphores(group):
        dma = pltpu.SemaphoreType.DMA
        return [dma, dma((6, group.devices // 2, 2)), dma((group.devices, 2))]

    def copy(self, kind, yy, xx, zz, part, cc=None, mine=False):
        core = self.c if cc is None else cc
        column = yy * 2 + xx
        index = column * self.inner + zz * 2 + core
        rows = pl.ds(part * self.group.half, self.group.half)
        return pltpu.make_async_remote_copy(
            src_ref=self.chunk_ref.at[rows] if mine else self.out_ref.at[index, rows],
            dst_ref=self.out_ref.at[index, rows],
            send_sem=self.send_sem.at[
                self.kinds.index(kind), column * self.levels + zz, part
            ],
            recv_sem=self.recv_sem.at[index, part],
            device_id=self.across[kind],
            device_id_type=MESH,
        )

    def level(self, back):
        return (self.z - back + self.levels) % self.levels

    def send(self, kind, yy, xx, zz, part, mine=False):
        copy = self.copy(kind, yy, xx, zz, part, mine=mine)
        if self.closing:
            copy.wait_send()
        else:
            copy.start()

    def arrive(self, yy, xx, zz, part):
        if not self.closing:
            self.copy("x", yy, xx, zz, part).wait_recv()

    def turn(self, turn):
        y, x, levels = self.y, self.x, self.levels
        if turn == 0 and not self.closing:
            self.own.start()
        if turn < levels:
            zz = self.level(turn)
            for part in range(2):
                if turn:
                    self.arrive(y, x, zz, part)
                for kind in ("x", "y") if part else ("y", "x"):
                    self.send(kind, y, x, zz, part, turn == 0)
                if turn == 0:
                    for kind in ("z1", "z2", "z3"):
                        self.send(kind, y, x, zz, part, True)
                self.send("twin", y, x, zz, part, turn == 0)
        if 1 <= turn <= levels:
            zz = self.level(turn - 1)
            self.arrive(y, 1 - x, zz, 0)
            self.send("y", y, 1 - x, zz, 0)
            self.send("twin", y, 1 - x, zz, 0)
            self.arrive(1 - y, x, zz, 1)
            self.send("x", 1 - y, x, zz, 1)
            self.send("twin", 1 - y, x, zz, 1)
            self.arrive(1 - y, x, zz, 0)
            self.send("twin", 1 - y, x, zz, 0)
            self.arrive(y, 1 - x, zz, 1)
            self.send("twin", y, 1 - x, zz, 1)
        if turn >= 2:
            zz = self.level(turn - 2)
            for part in range(2):
                self.arrive(1 - y, 1 - x, zz, part)
                self.send("twin", 1 - y, 1 - x, zz, part)

    def finish(self):
        def twin_arrivals(i, _):
            column, zz = i // self.levels, i % self.levels
            for part in range(2):
                self.copy("twin", column // 2, column % 2, zz, part, 1 - self.c).wait_recv()
            return 0

        lax.fori_loop(0, 4 * self.levels, twin_arrivals, 0)
        self.closing = True
        for turn in range(self.levels + 2):
            self.turn(turn)
        self.own.wait()


class PairTrade:
    def __init__(self, slab_ref, out_ref, mine, theirs, sems, inner, devices):
        self.slab_ref, self.out_ref, self.mine, self.theirs = slab_ref, out_ref, mine, theirs
        self.pair_sem, self.send_sem, self.recv_sem = sems
        self.inner, self.chips, self.senders = inner, devices // 2, out_ref.shape[0]
        dp, fs, _, _, _, self.core = place_of()
        self.twin = (dp, fs + 1 - 2 * self.core)
        self.chip = (dp * inner + fs) // 2

    def load(self):
        return pltpu.make_async_copy(self.slab_ref.at[self.core], self.mine, self.pair_sem.at[0])

    def pair(self):
        return pltpu.make_async_remote_copy(
            src_ref=self.slab_ref.at[1 - self.core],
            dst_ref=self.theirs,
            send_sem=self.pair_sem.at[1],
            recv_sem=self.pair_sem.at[2],
            device_id=self.twin,
            device_id_type=MESH,
        )

    def copy(self, source, target):
        device = 2 * target + self.core
        return pltpu.make_async_remote_copy(
            src_ref=self.mine.at[target],
            dst_ref=self.out_ref.at[source],
            send_sem=self.send_sem.at[target],
            recv_sem=self.recv_sem.at[source],
            device_id=(device // self.inner, device % self.inner),
            device_id_type=MESH,
        )

    def own(self):
        return pltpu.make_async_copy(
            self.mine.at[self.chip], self.out_ref.at[self.chip], self.pair_sem.at[3]
        )

    def each(self, act):
        def body(i, _):
            act((self.chip + i) % self.chips)
            return 0

        lax.fori_loop(1, self.chips, body, 0)

    def begin(self):
        @pl.when(self.chip < self.senders)
        def _():
            self.pair().start()
            self.load().start()

    def start(self):
        @pl.when(self.chip < self.senders)
        def _():
            self.load().wait()
            self.pair().wait_recv()

            def add(i, _):
                self.mine[i] = self.mine[i] + self.theirs[i]
                return 0

            lax.fori_loop(0, self.chips, add, 0)
            self.own().start()
            self.each(lambda other: self.copy(self.chip, other).start())

    def wait(self):
        def landed(other):
            pl.when(other < self.senders)(lambda: self.copy(other, other).wait_recv())

        self.each(landed)

        @pl.when(self.chip < self.senders)
        def _():
            self.own().wait()
            self.pair().wait_send()
            self.each(lambda other: self.copy(self.chip, other).wait_send())


def gather_kernel(
    chunk_ref, slab_ref, slot_ref, out_ref, parts_ref, next_ref, mine, theirs, *sems,
    group, later, inner
):
    me = lax.axis_index("dp") * inner + lax.axis_index("fsdp")
    meet_all(me, group.devices, inner)
    trade = PairTrade(slab_ref, parts_ref, mine, theirs, sems[:3], inner, group.devices)
    gather = ShortGather(group, inner, chunk_ref, out_ref, *sems[3:6])
    deal = Deal(later, slot_ref, next_ref, *sems[6:], inner, False)
    trade.begin()
    gather.turn(0)
    trade.start()
    gather.turn(1)
    deal.start()
    for turn in range(2, inner // 2 + 2):
        gather.turn(turn)
    gather.finish()
    trade.wait()
    deal.landed()
    deal.gone()


def gather_chunks(chunk, slabs, slot, group, later, inner, senders, collective):
    dma = pltpu.SemaphoreType.DMA
    return remote_call(
        functools.partial(gather_kernel, group=group, later=later, inner=inner),
        [ANYWHERE] * 3,
        [ANYWHERE] * 3,
        [
            jax.ShapeDtypeStruct((group.devices, group.chunk, LANE), BF),
            jax.ShapeDtypeStruct((senders // 2, *slabs.shape[2:]), slabs.dtype),
            jax.ShapeDtypeStruct((later.chunk, LANE), BF),
        ],
        [
            pltpu.VMEM(slabs.shape[1:], slabs.dtype),
            pltpu.VMEM(slabs.shape[1:], slabs.dtype),
            dma((4,)),
            dma((group.devices // 2,)),
            dma((group.devices // 2,)),
        ]
        + ShortGather.semaphores(group)
        + Deal.semaphores(later, False),
        collective,
        "gather_chunks",
    )(chunk, slabs, slot)


def scatter_stages(
    group,
    inner,
    g_ref,
    acc,
    twin,
    wide_y,
    wide_x,
    slim_x,
    slim_y,
    line,
    load_sem,
    twin_send,
    twin_recv,
    wide_send,
    wide_recv,
    slim_send,
    slim_recv,
    line_send,
    line_recv,
):
    dp, fs, y, x, z, c = place_of()
    me = dp * inner + fs
    lent = group.half
    levels = inner // 2
    x_mate = (dp + 1 - 2 * x, fs)
    y_mate = (dp + 2 - 4 * y, fs)

    def remote(source, target, send, receive, device):
        return pltpu.make_async_remote_copy(
            src_ref=source,
            dst_ref=target,
            send_sem=send,
            recv_sem=receive,
            device_id=device,
            device_id_type=MESH,
        )

    def slot_of(yy, xx, zz):
        return (yy * 2 + xx) * levels + zz

    def load(yy, xx, zz):
        slot = slot_of(yy, xx, zz)
        return pltpu.make_async_copy(
            g_ref.at[(yy * 2 + xx) * inner + zz * 2 + c], acc.at[slot], load_sem.at[slot]
        )

    def to_twin(yy, xx, zz):
        slot = slot_of(yy, xx, zz)
        return remote(
            g_ref.at[(yy * 2 + xx) * inner + zz * 2 + 1 - c],
            twin.at[slot],
            twin_send.at[slot],
            twin_recv.at[slot],
            (dp, fs + 1 - 2 * c),
        )

    def piece(slot, part):
        return acc.at[slot, pl.ds(part * lent, lent)]

    def wide(part, other, zz, yy=0, xx=0):
        buffer, device = (wide_x, x_mate) if part else (wide_y, y_mate)
        index = other * levels + zz
        return remote(
            piece(slot_of(yy, xx, zz), part),
            buffer.at[index],
            wide_send.at[part, index],
            wide_recv.at[part, index],
            device,
        )

    def slim(part, zz, yy=0, xx=0):
        buffer, device = (slim_y, y_mate) if part else (slim_x, x_mate)
        return remote(
            piece(slot_of(yy, xx, zz), part),
            buffer.at[zz],
            slim_send.at[part, zz],
            slim_recv.at[part, zz],
            device,
        )

    def along(upward, zz, part):
        way = 0 if upward else 1
        return remote(
            piece(slot_of(y, x, zz), part),
            line.at[way, zz, part],
            line_send.at[way, zz, part],
            line_recv.at[way, zz, part],
            (dp, fs + 2 if upward else fs - 2),
        )

    block = lent // group.folds

    def add(slot, first, count, source):
        def body(i, _):
            at = pl.multiple_of(i * block, TILE)
            to = pl.ds(pl.multiple_of(first + i * block, TILE), block)
            acc[slot, to] = acc[slot, to] + source[pl.ds(at, block)]
            return 0

        lax.fori_loop(0, count // block, body, 0)

    def add_part(slot, part, source):
        add(slot, part * lent, lent, source)

    def level(k):
        return jnp.where(z < levels // 2, z + levels - 1 - k, z + 1 + k) % levels

    columns = ((1 - y, 1 - x), (1 - y, x), (y, 1 - x), (y, x))

    def begin():
        for k in range(levels):
            for yy, xx in columns:
                to_twin(yy, xx, level(k)).start()
                load(yy, xx, level(k)).start()

    def settle(yy, xx, zz):
        slot = slot_of(yy, xx, zz)
        load(yy, xx, zz).wait()
        to_twin(yy, xx, zz).wait_recv()
        add(slot, 0, group.chunk, twin.at[slot])

    def diagonal(k):
        zz = level(k)
        settle(1 - y, 1 - x, zz)
        wide(0, 1 - x, zz, 1 - y, 1 - x).start()
        wide(1, 1 - y, zz, 1 - y, 1 - x).start()

    def sides(k):
        zz = level(k)
        settle(1 - y, x, zz)
        wide(0, x, zz, 1 - y, x).start()
        settle(y, 1 - x, zz)
        wide(1, y, zz, y, 1 - x).start()

    def middle(k):
        zz = level(k)
        wide(0, 1 - x, zz).wait_recv()
        add_part(slot_of(y, 1 - x, zz), 0, wide_y.at[(1 - x) * levels + zz])
        slim(0, zz, y, 1 - x).start()
        wide(1, 1 - y, zz).wait_recv()
        add_part(slot_of(1 - y, x, zz), 1, wide_x.at[(1 - y) * levels + zz])
        slim(1, zz, 1 - y, x).start()

    def home(k):
        zz = level(k)
        slot = slot_of(y, x, zz)
        settle(y, x, zz)
        wide(0, x, zz).wait_recv()
        add_part(slot, 0, wide_y.at[x * levels + zz])
        wide(1, y, zz).wait_recv()
        add_part(slot, 1, wide_x.at[y * levels + zz])
        slim(0, zz).wait_recv()
        add_part(slot, 0, slim_x.at[zz])
        slim(1, zz).wait_recv()
        add_part(slot, 1, slim_y.at[zz])

    def take(upward, zz, part):
        along(upward, zz, part).wait_recv()
        add_part(slot_of(y, x, zz), part, line.at[0 if upward else 1, zz, part])

    def ways(k, allowed):
        zz = level(k)
        for upward in (True, False):
            yield zz, upward, allowed() & (zz > z if upward else zz < z)

    def pass_on(k, allowed):
        more = {True: z > 0, False: z < levels - 1}
        for zz, upward, inside in ways(k, allowed):

            @pl.when(inside)
            def _(zz=zz, upward=upward):
                for part in range(2):

                    @pl.when(more[upward])
                    def _(part=part):
                        take(upward, zz, part)

                    along(upward, zz, part).start()

    def close_pass(k, allowed):
        for zz, upward, inside in ways(k, allowed):

            @pl.when(inside)
            def _(zz=zz, upward=upward):
                for part in range(2):
                    along(upward, zz, part).wait_send()

    def at_edge():
        return (z == 0) | (z == levels - 1)

    def off_edge():
        return (z > 0) & (z < levels - 1)

    def anywhere():
        return z >= 0

    def once(k):
        diagonal(k)
        sides(k)

    def final():
        for part in range(2):

            @pl.when(z > 0)
            def _(part=part):
                take(True, z, part)

            @pl.when(z < levels - 1)
            def _(part=part):
                take(False, z, part)

    stages = {
        "begin": begin,
        "once0": lambda: once(0),
        "once1": lambda: once(1),
        "middle0": lambda: middle(0),
        "once2": lambda: once(2),
        "middle1": lambda: middle(1),
        "home0": lambda: home(0),
        "pass0": lambda: pass_on(0, at_edge),
        "once3": lambda: once(3),
        "middle2": lambda: middle(2),
        "middle3": lambda: middle(3),
        "home1": lambda: home(1),
        "pass1": lambda: pass_on(1, anywhere),
        "home2": lambda: home(2),
        "pass2": lambda: pass_on(2, anywhere),
        "inner0": lambda: pass_on(0, off_edge),
        "home3": lambda: home(3),
        "final": final,
    }

    def finish():
        for k, allowed in ((0, at_edge), (1, anywhere), (2, anywhere), (0, off_edge)):
            close_pass(k, allowed)

        def close(k, _):
            zz = level(k)
            for yy, xx in columns:
                to_twin(yy, xx, zz).wait_send()
            wide(0, 1 - x, zz).wait_send()
            wide(0, x, zz).wait_send()
            wide(1, 1 - y, zz).wait_send()
            wide(1, y, zz).wait_send()
            slim(0, zz).wait_send()
            slim(1, zz).wait_send()
            return 0

        lax.fori_loop(0, levels, close, 0)

    return stages, finish, acc.at[slot_of(y, x, z)]


def scatter_scratch(group, inner):
    dma = pltpu.SemaphoreType.DMA
    half, levels = group.devices // 2, inner // 2
    part = (group.half, LANE)
    return [
        pltpu.VMEM((half, group.chunk, LANE), BF),
        pltpu.VMEM((half, group.chunk, LANE), BF),
        pltpu.VMEM((2 * levels, *part), BF),
        pltpu.VMEM((2 * levels, *part), BF),
        pltpu.VMEM((levels, *part), BF),
        pltpu.VMEM((levels, *part), BF),
        pltpu.VMEM((2, levels, 2, *part), BF),
        dma((half,)),
        dma((half,)),
        dma((half,)),
        dma((2, 2 * levels)),
        dma((2, 2 * levels)),
        dma((2, levels)),
        dma((2, levels)),
        dma((2, levels, 2)),
        dma((2, levels, 2)),
    ]


def scatter_kernel(
    g_ref, rows_ref, out_ref, all_ref, own_sem, row_send, row_recv, *rest, group, inner, receivers
):
    me = lax.axis_index("dp") * inner + lax.axis_index("fsdp")
    meet_all(me, group.devices, inner)
    stages, finish, total = scatter_stages(group, inner, g_ref, *rest[:-2])
    trade = Trade(
        rows_ref, all_ref, own_sem, row_send, row_recv, group, inner, group.devices, receivers
    )
    for name, stage in stages.items():
        stage()
        if name == "once0":
            trade.start()
    deal = Deal(group, total, out_ref, *rest[-2:], inner, True)
    deal.start()
    finish()
    trade.wait()
    deal.landed()
    deal.gone()


def scatter_chunks(grads, rows, group, inner, receivers, collective):
    dma = pltpu.SemaphoreType.DMA
    return remote_call(
        functools.partial(scatter_kernel, group=group, inner=inner, receivers=receivers),
        [ANYWHERE] * 2,
        [ANYWHERE] * 2,
        [
            jax.ShapeDtypeStruct((group.padded, LANE), BF),
            jax.ShapeDtypeStruct((group.devices, *rows.shape), rows.dtype),
        ],
        [dma, dma((group.devices,)), dma((group.devices,))]
        + scatter_scratch(group, inner)
        + Deal.semaphores(group, True),
        collective,
        "scatter_chunks",
    )(grads, rows)


def front_kernel(
    x_ref, mod_ref, w_ref, chunk_ref, qkv_ref, o_ref, l_ref, out_ref, qkv_s, *sems,
    group, inner, leads, pairs
):
    step = pl.program_id(0)
    last = pl.num_programs(0) - 1
    clips, frames, _ = qkv_s.shape
    rows = x_ref.shape[1]
    gather = Gather(group, inner, chunk_ref, out_ref, *sems)
    me = lax.axis_index("dp") * inner + lax.axis_index("fsdp")

    @pl.when(step == 0)
    def _():
        meet_all(me, group.devices, inner)
        gather.turn(0)

    for turn, at in ((1, leads + 1), (2, leads + 3), (3, leads + 5)):

        @pl.when(step == at)
        def _(turn=turn):
            gather.turn(turn)

    @pl.when(step < leads)
    def _():
        normed, _ = normalize(x_ref[0].astype(F32))
        first_in = (normed * (1.0 + mod_ref[0, 1:2]) + mod_ref[0, 0:1]).astype(BF)
        block = nn(first_in, w_ref[...]).astype(BF)
        qkv_ref[0] = block
        start = pl.multiple_of(step * rows % frames, rows)
        qkv_s[step * rows // frames, pl.ds(start, rows)] = block

    @pl.when(step >= leads)
    def _():
        lane, low = head_lanes()
        count = HEADS // 2 // pairs
        clip, group_index = (step - leads) // count, (step - leads) % count
        for pair in range(pairs):

            def columns(part):
                at = (group_index * pairs + pair + part * HEADS // 2) * 2 * HD
                return qkv_s[clip, :, pl.ds(pl.multiple_of(at, 2 * HD), 2 * HD)]

            attend_pair(
                lane,
                low,
                None,
                columns(0),
                columns(1),
                columns(2),
                o_ref.at[0, :, pair * 2 * HD : (pair + 1) * 2 * HD],
                l_ref.at[0, pair],
            )

    @pl.when(step == last)
    def _():
        for turn in range(4, inner // 2 + 2):
            gather.turn(turn)
        gather.finish()


def front_and_gather(latents, mod, weight, chunk, group, inner, collective, pairs=2):
    clips, frames, width = latents.shape
    rows = row_block(frames)
    per = frames // rows
    leads = clips * per
    count = HEADS // 2 // pairs

    def lead(s):
        return jnp.minimum(s, leads - 1)

    def tail(s):
        return jnp.maximum(s - leads, 0)

    wide = weight.shape[1]
    return remote_call(
        functools.partial(front_kernel, group=group, inner=inner, leads=leads, pairs=pairs),
        [
            pl.BlockSpec((1, rows, width), lambda s: (lead(s) // per, lead(s) % per, 0)),
            pl.BlockSpec((1, 9, width), lambda s: (lead(s) // per, 0, 0)),
            whole_spec(weight.shape),
            ANYWHERE,
        ],
        [
            pl.BlockSpec((1, rows, wide), lambda s: (lead(s) // per, lead(s) % per, 0)),
            pl.BlockSpec(
                (1, frames, 2 * HD * pairs), lambda s: (tail(s) // count, 0, tail(s) % count)
            ),
            pl.BlockSpec(
                (1, pairs, frames, 2 * HD), lambda s: (tail(s) // count, tail(s) % count, 0, 0)
            ),
            ANYWHERE,
        ],
        [
            struct((clips, frames, wide), BF),
            struct((clips, frames, width), BF),
            struct((clips, HEADS // 2, frames, 2 * HD), F32),
            struct((group.devices, group.chunk, LANE), BF),
        ],
        [pltpu.VMEM((clips, frames, wide), BF)] + Gather.semaphores(group),
        collective,
        "front_and_gather",
        (leads + clips * count,),
    )(latents, mod, weight, chunk)


def back_kernel(
    q_ref, k_ref, v_ref, do_ref, o_ref, l_ref, x_ref, dh_ref, mod_ref, w_ref, g_ref,
    out_ref, dw_ref, sums_ref, rest_ref, grad_s, in_s, *scratch,
    group, inner, pairs, period
):
    step = pl.program_id(0)
    last = pl.num_programs(0) - 1
    clip, turn = step // period, step % period
    width = x_ref.shape[2]
    rows = x_ref.shape[1]
    stages, finish, total = scatter_stages(group, inner, g_ref, *scratch[:-2])
    deal = Deal(group, total, rest_ref, *scratch[-2:], inner, True)
    me = lax.axis_index("dp") * inner + lax.axis_index("fsdp")

    @pl.when(step == 0)
    def _():
        meet_all(me, group.devices, inner)

    plan = (
        (0, ("begin",)),
        (1, ("once0", "once1")),
        (3, ("middle0", "once2")),
        (5, ("middle1", "once3")),
        (7, ("home0", "pass0")),
        (8, ("middle2",)),
        (11, ("middle3",)),
        (12, ("home1", "pass1")),
        (14, ("home2", "pass2")),
        (16, ("inner0",)),
    )
    for at, names in plan:

        @pl.when(step == at)
        def _(names=names):
            for name in names:
                stages[name]()

    @pl.when(turn < pairs)
    def _():
        lane, low = head_lanes()

        def columns(part):
            at = pl.multiple_of(turn * 2 * HD, 2 * HD)
            return grad_s.at[:, pl.ds(part * width + at, 2 * HD)]

        attend_back_pair(
            lane,
            low,
            None,
            q_ref[0],
            k_ref[0],
            v_ref[0],
            do_ref[0],
            o_ref[0],
            l_ref[0, 0],
            columns(0),
            columns(1),
            columns(2),
        )

    clear_at(turn == pairs, sums_ref)

    @pl.when(turn >= pairs)
    def _():
        here = pl.ds(pl.multiple_of((turn - pairs) * rows, rows), rows)
        normed, inverse = normalize(x_ref[0].astype(F32))
        in_s[here] = (normed * (1.0 + mod_ref[0, 1:2]) + mod_ref[0, 0:1]).astype(BF)
        grad_in = None
        for index in range(3):
            part = slice(index * width, (index + 1) * width)
            product = nt(grad_s[here, part], w_ref[:, part])
            grad_in = product if grad_in is None else grad_in + product
        out_ref[0] = (
            dh_ref[0] + norm_back(normed, inverse, grad_in * (1.0 + mod_ref[0, 1:2]))
        ).astype(BF)
        sums_ref[0] += jnp.concatenate(
            [column_sum(grad_in), column_sum(grad_in * normed)], axis=0
        )

    @pl.when(turn == period - 1)
    def _():
        turned = in_s[...].T
        for index in range(3):
            part = slice(index * width, (index + 1) * width)
            product = nn(turned, grad_s[:, part])

            @pl.when(clip == 0)
            def _(product=product, part=part):
                dw_ref[:, part] = product.astype(BF)

            @pl.when(clip > 0)
            def _(product=product, part=part):
                dw_ref[:, part] = (dw_ref[:, part].astype(F32) + product).astype(BF)

    @pl.when(step == last)
    def _():
        for name in ("home3", "final"):
            stages[name]()
        deal.start()
        finish()
        deal.landed()
        deal.gone()


def back_and_scatter(
    queries, grad, mixed, lse, latents, dh, mod, weight, chunks, group, inner, collective
):
    clips, frames, wide = queries.shape
    width = wide // 3
    pairs = HEADS // 2
    rows = frames // 3
    period = pairs + frames // rows

    def pair_at(part):
        return pl.BlockSpec(
            (1, frames, 2 * HD),
            lambda s: (s // period, 0, jnp.minimum(s % period, pairs - 1) + part * pairs),
        )

    lse_at = pl.BlockSpec(
        (1, 1, frames, 2 * HD),
        lambda s: (s // period, jnp.minimum(s % period, pairs - 1), 0, 0),
    )
    rows_at = pl.BlockSpec(
        (1, rows, width), lambda s: (s // period, jnp.maximum(s % period - pairs, 0), 0)
    )

    def clip_at(count):
        return pl.BlockSpec((1, count, width), lambda s: (s // period, 0, 0))

    whole = pl.BlockSpec(weight.shape, lambda s: (0, 0), pipeline_mode=pl.Buffered(1))
    return remote_call(
        functools.partial(back_kernel, group=group, inner=inner, pairs=pairs, period=period),
        [
            pair_at(0),
            pair_at(1),
            pair_at(2),
            pair_at(0),
            pair_at(0),
            lse_at,
            rows_at,
            rows_at,
            clip_at(9),
            whole,
            ANYWHERE,
        ],
        [rows_at, whole, clip_at(2), ANYWHERE],
        [
            struct((clips, frames, width), BF),
            struct(weight.shape, BF),
            struct((clips, 2, width), F32),
            struct((group.padded, LANE), BF),
        ],
        [pltpu.VMEM((frames, wide), BF), pltpu.VMEM((frames, width), BF)]
        + scatter_scratch(group, inner)
        + Deal.semaphores(group, True),
        collective,
        "back_and_scatter",
        (clips * period,),
    )(queries, queries, queries, grad, mixed, lse, latents, dh, mod, weight, chunks)


def exchange_kernel(in_ref, out_ref, own_sem, send_sem, recv_sem, *, group, inner):
    me = lax.axis_index("dp") * inner + lax.axis_index("fsdp")
    meet_all(me, group.devices, inner)
    trade = Trade(
        in_ref, out_ref, own_sem, send_sem, recv_sem, group, inner, group.devices, group.devices
    )
    trade.start()
    trade.wait()


def exchange(value, group, inner, collective, name):
    dma = pltpu.SemaphoreType.DMA
    return remote_call(
        functools.partial(exchange_kernel, group=group, inner=inner),
        [ANYWHERE],
        ANYWHERE,
        jax.ShapeDtypeStruct((group.devices, *value.shape), value.dtype),
        [dma, dma((group.devices,)), dma((group.devices,))],
        collective,
        name,
    )(value)


HALF = 27
TALL = 72
SLAB = 112
CONDITION_ROWS = 832


def ada_spots(me, group):
    lines = group.share // HALF
    odd = me % 2
    limit = CONDITION_ROWS - TALL
    return [
        (odd, jnp.minimum((lines * me + odd) // 2, limit)),
        (1 - odd, jnp.minimum((lines * me - odd) // 2, limit)),
    ]


def ada_kernel(lin_ref, cond_ref, out_ref, *, group, inner):
    me = lax.axis_index("dp") * inner + lax.axis_index("fsdp")
    for half, (shift, top) in enumerate(ada_spots(me, group)):
        condition = cond_ref[pl.ds(top, TALL)].astype(BF)

        def body(c, _, half=half, shift=shift, condition=condition):
            rows = lin_ref[pl.ds(HALF * shift + c, TALL, stride=2 * HALF)].astype(BF)
            part = tn(condition, rows)
            count = group.devices
            for clip in range(2):
                out_ref[pl.ds((2 * clip + half) * HALF + c, count, stride=SLAB)] = part[
                    clip * count : (clip + 1) * count
                ]
            return 0

        lax.fori_loop(0, HALF, body, 0, unroll=True)


def ada_partial(lin, cond, group, inner):
    return pl.pallas_call(
        functools.partial(ada_kernel, group=group, inner=inner),
        out_shape=jax.ShapeDtypeStruct((group.devices * SLAB, LANE), F32),
        compiler_params=pltpu.CompilerParams(vmem_limit_bytes=VMEM_LIMIT),
        name="ada_partial",
    )(lin, cond)


def own_grad_kernel(
    cond_ref, given_ref, early_ref, late_ref, g_ref, sums_ref, lin, dmod_ref, *, group, inner
):
    me = lax.axis_index("dp") * inner + lax.axis_index("fsdp")
    count = group.devices // 2
    border = jnp.clip(group.first - group.share * me, 0, group.share)
    middle = jnp.clip(group.last - group.share * me, 0, group.share)

    @pl.when(border > 0)
    def _():
        dmod_ref[...] = given_ref[...].astype(F32)

    for half, (shift, top) in enumerate(ada_spots(me, group)):
        condition = cond_ref[pl.ds(top, TALL)].astype(BF)

        def body(c, _, half=half, shift=shift, condition=condition):
            grads = jnp.concatenate(
                [
                    dmod_ref[
                        pl.ds(core * SLAB + (2 * clip + half) * HALF + c, count, stride=2 * SLAB)
                    ]
                    for clip in range(2)
                    for core in range(2)
                ],
                axis=0,
            ).astype(BF)
            lin[pl.ds(HALF * shift + c, TALL, stride=2 * HALF)] = nn(condition, grads)
            return 0

        @pl.when(border > 0)
        def _(body=body):
            lax.fori_loop(0, HALF, body, 0, unroll=True)

    rows = 64

    def merge(i, total):
        at = pl.multiple_of(i * rows, rows)
        row = lax.broadcasted_iota(jnp.int32, (rows, LANE), 0) + at
        early = early_ref[pl.ds(at, rows)].astype(F32)
        late = jnp.where(row < group.share, late_ref[pl.ds(at, rows)].astype(F32), 0.0)
        value = jnp.where(
            row < border, lin[pl.ds(at, rows)], jnp.where(row < middle, early, late)
        )
        g_ref[pl.ds(at, rows)] = value
        square = value * value
        return total + sum(square[k : k + 8] for k in range(0, rows, 8))

    sums_ref[...] = lax.fori_loop(0, group.padded // rows, merge, jnp.zeros((8, LANE), F32))


def own_grad(cond, dmod, early, late, group, inner):
    return pl.pallas_call(
        functools.partial(own_grad_kernel, group=group, inner=inner),
        out_shape=[
            jax.ShapeDtypeStruct((group.padded, LANE), F32),
            jax.ShapeDtypeStruct((8, LANE), F32),
        ],
        scratch_shapes=[
            pltpu.VMEM((2 * HALF * TALL, LANE), F32),
            pltpu.VMEM(dmod.shape, F32),
        ],
        compiler_params=pltpu.CompilerParams(vmem_limit_bytes=VMEM_LIMIT),
        name="own_grad",
    )(cond, dmod, early, late)


def fits(devices, inner, share):
    return inner == 8 and devices == 32 and share % (LANE * HALF) == 0


def local_fast(latents, captions, lengths, timesteps, cotangent, master):
    clips, frames, width = latents.shape
    share = master.shape[0]
    inner = lax.axis_size("fsdp")
    devices = inner * lax.axis_size("dp")
    spots = linear_layout()
    end = spots[-1][0] + spots[-1][1]
    early = Group(devices, inner, share // LANE, spots[2][0], spots[3][0])
    late = Group(devices, inner, share // LANE, spots[3][0], end)
    holders = spots[2][0] // early.share + 1

    lin = lax.optimization_barrier(
        jnp.pad(
            master.reshape(early.share, LANE), ((0, 2 * HALF * TALL - early.share), (0, 0))
        )
    )
    slot = lin[: early.padded].astype(BF)
    steps, chunk = start_chunks(
        jnp.broadcast_to(
            jnp.pad(timesteps.astype(F32), (0, 8 - clips))[:, None], (8, LANE)
        ),
        slot,
        early,
        inner,
        1,
    )
    steps = steps[:, :clips, 0].reshape(devices // 2, 2, clips).T.reshape(devices * clips)
    columns = jax.nn.silu(embed(steps)).astype(BF).astype(F32).T
    columns = jnp.concatenate(
        [
            columns,
            jnp.ones((1, clips * devices), F32),
            jnp.zeros((CONDITION_ROWS - width - 1, clips * devices), F32),
        ],
        axis=0,
    )
    slabs = ada_partial(lin, columns, early, inner).reshape(2, devices // 2, SLAB, LANE)
    gathered, parts, later_chunk = gather_chunks(
        chunk, slabs, slot, early, late, inner, holders, 2
    )
    mod = jnp.sum(parts, axis=0)[: 54 * clips].reshape(clips, 9, width)
    (triple_weight,) = unpack_weights(gathered, early, (2,))

    def front(latents, mod, triple_weight):
        triple, mixed, lse, later = front_and_gather(
            latents, mod, triple_weight, later_chunk, late, inner, 3
        )
        return triple, mixed, lse, unpack_weights(later, late, tuple(range(3, 13)))

    def back(triple, grad_mixed, mixed, lse, latents, dh, mod, triple_weight, gradients):
        chunks = pack_grads(gradients, late, tuple(range(3, 13)))
        return back_and_scatter(
            triple,
            grad_mixed,
            mixed,
            lse,
            latents,
            dh,
            mod,
            triple_weight,
            chunks,
            late,
            inner,
            4,
        )

    output, input_grad, grad_mod, grad_triple, _, late_grads = block_pass(
        latents, captions, lengths, cotangent, mod, triple_weight, front, back
    )
    grad_rows = jnp.pad(
        grad_mod.reshape(54 * clips, LANE), ((0, SLAB - 54 * clips), (0, 0))
    )
    chunks = pack_grads([grad_triple], early, (2,))
    early_grads, dmod = scatter_chunks(chunks, grad_rows, early, inner, holders, 5)
    grads, squares = own_grad(
        columns,
        dmod.reshape(devices * SLAB, LANE),
        early_grads,
        late_grads,
        early,
        inner,
    )
    squares = exchange(squares, early, inner, 6, "squares")
    return (
        output,
        input_grad,
        grads[: early.share].reshape(share),
        jnp.sum(squares),
    )


def local_any(latents, captions, lengths, timesteps, cotangent, master):
    clips, frames, width = latents.shape
    share = master.shape[0]
    devices = lax.axis_size("dp") * lax.axis_size("fsdp")
    gathered = lax.all_gather(
        master.astype(BF).reshape(1, share), ("dp", "fsdp"), axis=0, tiled=True
    ).reshape(-1)
    weights = unpack(gathered)
    condition = jax.nn.silu(embed(timesteps)).astype(BF)
    mod = jnp.dot(condition, weights[0], preferred_element_type=F32) + weights[1].astype(F32)
    block_weights = [w.astype(F32).reshape(1, -1) if w.ndim == 1 else w for w in weights[2:]]
    output, input_grad, grad_mod, grad_triple, gradients, _ = block_pass(
        latents,
        captions,
        lengths,
        cotangent,
        mod.reshape(clips, 9, width),
        block_weights[0],
        functools.partial(plain_front, block_weights[1:]),
        plain_back,
    )
    grad_mod = grad_mod.reshape(clips, 9 * width)
    grad_ada = jnp.dot(condition.T, grad_mod, preferred_element_type=F32)
    grad_list = [grad_ada, jnp.sum(grad_mod.astype(F32), axis=0), grad_triple] + gradients
    flat = jnp.concatenate([piece.astype(F32).reshape(-1) for piece in grad_list])
    grad = lax.psum_scatter(
        flat.reshape(devices, share), ("dp", "fsdp"), scatter_dimension=0, tiled=True
    ).reshape(share)
    return output, input_grad, grad, lax.psum(jnp.sum(grad * grad), ("dp", "fsdp"))


def local(
    latents,
    captions,
    caption_lengths,
    timesteps,
    cotangent,
    master_weights,
    first_moment,
    second_moment,
):
    inner = lax.axis_size("fsdp")
    devices = inner * lax.axis_size("dp")
    run = local_fast if fits(devices, inner, master_weights.shape[0]) else local_any
    output, input_grad, grad_shard, squares = run(
        latents,
        captions,
        caption_lengths,
        timesteps,
        cotangent,
        master_weights,
    )
    grad_norm = jnp.sqrt(squares)
    clipped = grad_shard * (CLIP / jnp.maximum(grad_norm, CLIP))
    new_first = BETA_ONE * first_moment + (1.0 - BETA_ONE) * clipped
    new_second = BETA_TWO * second_moment + (1.0 - BETA_TWO) * clipped * clipped
    step_first = new_first / (1.0 - BETA_ONE**STEP)
    step_second = new_second / (1.0 - BETA_TWO**STEP)
    new_master = master_weights - RATE * (
        step_first / (jnp.sqrt(step_second) + ADAM_EPS) + DECAY * master_weights
    )
    return (output, input_grad, grad_norm, new_master, new_first, new_second)


def solution(mesh):
    placed = (
        P(("dp", "fsdp"), None, None),
        P(("dp", "fsdp"), None, None),
        P(("dp", "fsdp")),
        P(("dp", "fsdp")),
        P(("dp", "fsdp"), None, None),
        P(("dp", "fsdp")),
        P(("dp", "fsdp")),
        P(("dp", "fsdp")),
    )
    return jax.shard_map(
        local,
        mesh=mesh,
        in_specs=placed,
        out_specs=(
            P(("dp", "fsdp"), None, None),
            P(("dp", "fsdp"), None, None),
            P(),
            P(("dp", "fsdp")),
            P(("dp", "fsdp")),
            P(("dp", "fsdp")),
        ),
        check_vma=False,
    )
```

```python
import functools
import math

import jax
import jax.numpy as jnp
from jax import lax
from jax.experimental import pallas as pl
from jax.experimental.pallas import tpu as pltpu
from jax.sharding import PartitionSpec as P

D = 768
HEADS = 12
HD = 64
FF = 3072
CTX = 1024
STEP = 5


NORM_EPS = 1e-06
BETA_ONE = 0.9
BETA_TWO = 0.999
ADAM_EPS = 1e-08
RATE = 0.03
DECAY = 0.01
CLIP = 500.0


def layout_sizes():
    return [
        (D, 9 * D),
        (9 * D,),
        (D, 3 * D),
        (D, D),
        (D,),
        (D, D),
        (CTX, 2 * D),
        (D, D),
        (D,),
        (D, FF),
        (FF,),
        (FF, D),
        (D,),
    ]


def unpack(flat_vector):
    pieces = []
    offset = 0
    for layout_shape in layout_sizes():
        number = math.prod(layout_shape)
        pieces.append(flat_vector[offset : offset + number].reshape(layout_shape))
        offset += number
    return pieces


def embed(steps_in):
    half_width = D // 2
    frequency = jnp.exp(-math.log(10000.0) * jnp.arange(half_width, dtype=jnp.float32) / half_width)
    angles = steps_in.astype(jnp.float32)[:, None] * frequency[None, :]
    return jnp.concatenate([jnp.cos(angles), jnp.sin(angles)], axis=1)


def normalize(hidden):
    centred = hidden - jnp.mean(hidden, axis=-1, keepdims=True)
    inverse = lax.rsqrt(jnp.mean(centred * centred, axis=-1, keepdims=True) + NORM_EPS)
    return (centred * inverse, inverse)


def norm_back(normed, inverse, grad_normed):
    return inverse * (
        grad_normed
        - jnp.mean(grad_normed, axis=-1, keepdims=True)
        - normed * jnp.mean(grad_normed * normed, axis=-1, keepdims=True)
    )


F32 = jnp.float32
BF = jnp.bfloat16
VMEM_LIMIT = 60 << 20


def nn(left_side, right_side):
    return lax.dot_general(
        left_side, right_side, (((1,), (0,)), ((), ())), preferred_element_type=F32
    )


def nt(left_side, right_side):
    return lax.dot_general(
        left_side, right_side, (((1,), (1,)), ((), ())), preferred_element_type=F32
    )


def tn(left_side, right_side):
    return lax.dot_general(
        left_side, right_side, (((0,), (0,)), ((), ())), preferred_element_type=F32
    )


def call(body, grid, in_specs, out_specs, out_shape, name, scratch=()):
    return pl.pallas_call(
        body,
        grid=grid,
        in_specs=in_specs,
        out_specs=out_specs,
        out_shape=out_shape,
        scratch_shapes=list(scratch),
        compiler_params=pltpu.CompilerParams(vmem_limit_bytes=VMEM_LIMIT),
        name=name,
    )


def struct(shape, dtype):
    return jax.ShapeDtypeStruct(shape, dtype)


def rows_spec(rows, width):
    return pl.BlockSpec((1, rows, width), lambda i, j: (i, j, 0))


def clip_spec(count, width):
    return pl.BlockSpec((1, count, width), lambda i, j: (i, 0, 0))


def whole_spec(shape):
    return pl.BlockSpec(shape, lambda *_: (0,) * len(shape))


def row_block(frames):
    for parts in (2, 3, 4, 6):
        if frames % (16 * parts) == 0:
            return frames // parts
    return frames


def add_to(ref, first, value):
    @pl.when(first)
    def _():
        ref[...] = value

    @pl.when(jnp.logical_not(first))
    def _():
        ref[...] += value


def span_of(rows):
    start = (pl.program_id(0) * pl.num_programs(1) + pl.program_id(1)) * rows
    return pl.ds(pl.multiple_of(start, rows), rows)


def clear_at(first, *refs):
    @pl.when(first)
    def _():
        for ref in refs:
            ref[...] = jnp.zeros_like(ref)


def column_sum(value):
    return jnp.sum(value, axis=0, keepdims=True)


def qkv_kernel(x_ref, mod_ref, w_ref, out_ref):
    normed, _ = normalize(x_ref[0].astype(F32))
    first_in = (normed * (1.0 + mod_ref[0, 1:2]) + mod_ref[0, 0:1]).astype(BF)
    out_ref[0] = nn(first_in, w_ref[...]).astype(BF)


def qkv_forward(latents, mod, weight):
    clips, frames, width = latents.shape
    rows = row_block(frames)
    wide = weight.shape[1]
    return call(
        qkv_kernel,
        (clips, frames // rows),
        [rows_spec(rows, width), clip_spec(9, width), whole_spec(weight.shape)],
        rows_spec(rows, wide),
        struct((clips, frames, wide), BF),
        "qkv_forward",
    )(latents, mod, weight)


def head_lanes():
    lane = lax.broadcasted_iota(jnp.int32, (1, 2 * HD), 1)
    return lane, lane < HD


def usable_bias(length, count):
    row = lax.broadcasted_iota(jnp.int32, (count, 2 * HD), 0)
    return jnp.where(row < length, 0.0, -1e30).astype(BF)


def attend_kernel(*refs, masked):
    if masked:
        len_ref, q_ref, k_ref, v_ref, o_ref, l_ref = refs
    else:
        q_ref, k_ref, v_ref, o_ref, l_ref = refs
    lane, low = head_lanes()
    for pair in range(l_ref.shape[1]):
        columns = slice(pair * 2 * HD, (pair + 1) * 2 * HD)
        length = len_ref[pl.program_id(0)] if masked else None
        attend_pair(
            lane,
            low,
            length,
            q_ref[0, :, columns],
            k_ref[0, :, columns],
            v_ref[0, :, columns],
            o_ref.at[0, :, columns],
            l_ref.at[0, pair],
        )


def attend_pair(lane, low, length, q, k, v, o_ref, l_ref):
    masked = length is not None
    scaled = q * jnp.asarray(HD**-0.5, BF)
    one = jnp.ones((), BF)
    zero = jnp.zeros((), BF)
    values = [jnp.where(low, v, one), jnp.where(low, one, v)]
    if masked:
        bias = usable_bias(length, k.shape[0])
        tag = jnp.where(lane % HD == 0, one, zero)
        queries = [jnp.where(low, scaled, tag), jnp.where(low, tag, scaled)]
        keys = [jnp.where(low, k, bias), jnp.where(low, bias, k)]
    else:
        queries = [jnp.where(low, scaled, zero), jnp.where(low, zero, scaled)]
        keys = [k, k]
    tops, mixes = [], []
    for head in range(2):
        scores = nt(queries[head], keys[head])
        top = jnp.max(scores, axis=1, keepdims=True)
        mixes.append(nn(jnp.exp(scores - top).astype(BF), values[head]))
        tops.append(top)
    total = jnp.where(low, mixes[1], mixes[0])
    l_ref[...] = jnp.where(low, tops[1], tops[0]) + jnp.log(total)
    o_ref[...] = (jnp.where(low, mixes[0], mixes[1]) / pltpu.roll(total, HD, 1)).astype(BF)


def pair_spec(rows, offset, pairs):
    return pl.BlockSpec((1, rows, 2 * HD * pairs), lambda i, j: (i, 0, j + offset // pairs))


def lse_spec(rows, pairs):
    return pl.BlockSpec((1, pairs, rows, 2 * HD), lambda i, j: (i, j, 0, 0))


def attend_forward(queries, key_offset, keyvals, value_offset, lengths, name, pairs=1):
    clips, frames = queries.shape[:2]
    slots = keyvals.shape[1]
    groups = HEADS // 2
    masked = lengths is not None
    specs = [
        pair_spec(frames, 0, pairs),
        pair_spec(slots, key_offset, pairs),
        pair_spec(slots, value_offset, pairs),
    ]
    args = [queries, keyvals, keyvals]
    if masked:
        specs.insert(0, pl.BlockSpec(memory_space=pltpu.SMEM))
        args.insert(0, lengths)
    return call(
        functools.partial(attend_kernel, masked=masked),
        (clips, groups // pairs),
        specs,
        [pair_spec(frames, 0, pairs), lse_spec(frames, pairs)],
        [struct((clips, frames, D), BF), struct((clips, groups, frames, 2 * HD), F32)],
        name,
    )(*args)


def three_parts(value):
    high = value.astype(BF)
    rest = value - high.astype(F32)
    middle = rest.astype(BF)
    return high, middle, (rest - middle.astype(F32)).astype(BF)


def attend_back_kernel(*refs, masked):
    if masked:
        len_ref, q_ref, k_ref, v_ref, do_ref, o_ref, l_ref, dq_ref, dk_ref, dv_ref = refs
    else:
        q_ref, k_ref, v_ref, do_ref, o_ref, l_ref, dq_ref, dk_ref, dv_ref = refs
    length = len_ref[pl.program_id(0)] if masked else None
    attend_back_step(
        length, q_ref, k_ref, v_ref, do_ref, o_ref, l_ref, dq_ref, dk_ref, dv_ref
    )


def attend_back_step(length, q_ref, k_ref, v_ref, do_ref, o_ref, l_ref, dq_ref, dk_ref, dv_ref):
    lane, low = head_lanes()
    for pair in range(l_ref.shape[1]):
        columns = slice(pair * 2 * HD, (pair + 1) * 2 * HD)
        attend_back_pair(
            lane,
            low,
            length,
            q_ref[0, :, columns],
            k_ref[0, :, columns],
            v_ref[0, :, columns],
            do_ref[0, :, columns],
            o_ref[0, :, columns],
            l_ref[0, pair],
            dq_ref.at[0, :, columns],
            dk_ref.at[0, :, columns],
            dv_ref.at[0, :, columns],
        )


def attend_back_pair(lane, low, length, q, k, v, grad, mixed, lse, dq_ref, dk_ref, dv_ref):
    masked = length is not None
    scaled = q * jnp.asarray(HD**-0.5, BF)
    spot = lane % HD
    one = jnp.ones((), BF)
    zero = jnp.zeros((), BF)
    product = grad.astype(F32) * mixed.astype(F32)
    delta_low = jnp.sum(jnp.where(low, product, 0.0), axis=1, keepdims=True)
    delta_high = jnp.sum(jnp.where(low, 0.0, product), axis=1, keepdims=True)

    def negated(value, last):
        high, middle, rest = three_parts(-value)
        return jnp.where(
            spot == 0,
            high,
            jnp.where(spot == 1, middle, jnp.where(spot == 2, rest, last)),
        )

    tag = jnp.where(spot == 3, one, zero) if masked else zero
    lse_lanes = negated(lse, tag)
    delta_lanes = negated(jnp.where(low, delta_high, delta_low), zero)
    ones = jnp.broadcast_to(jnp.where(spot < 3, one, zero), k.shape)
    key_lanes = ones
    if masked:
        bias = usable_bias(length, k.shape[0])
        key_lanes = jnp.where(spot == 3, bias, ones)
    transposed = k.astype(F32).T.astype(BF)
    grad_queries, grad_keys, grad_values = [], [], []
    for head in range(2):

        def merge(own, other):
            return jnp.where(low, own, other) if head == 0 else jnp.where(low, other, own)

        probability = jnp.exp(nt(merge(k, key_lanes), merge(scaled, lse_lanes)))
        centred = nt(merge(v, ones), merge(grad, delta_lanes))
        grad_scores = (probability * centred).astype(BF)
        grad_values.append(nn(probability.astype(BF), grad))
        grad_keys.append(nn(grad_scores, scaled))
        grad_queries.append(nn(transposed[HD * head : HD * (head + 1)], grad_scores))
    dv_ref[...] = jnp.where(low, grad_values[0], grad_values[1]).astype(BF)
    dk_ref[...] = jnp.where(low, grad_keys[0], grad_keys[1]).astype(BF)
    dq_ref[...] = (jnp.concatenate(grad_queries, axis=0).T * HD**-0.5).astype(BF)


def attend_backward(
    queries, key_offset, keyvals, value_offset, lengths, grad, mixed, lse, name, pairs=1
):
    clips, frames = queries.shape[:2]
    slots = keyvals.shape[1]
    groups = HEADS // 2
    masked = lengths is not None
    specs = [
        pair_spec(frames, 0, pairs),
        pair_spec(slots, key_offset, pairs),
        pair_spec(slots, value_offset, pairs),
        pair_spec(frames, 0, pairs),
        pair_spec(frames, 0, pairs),
        lse_spec(frames, pairs),
    ]
    args = [queries, keyvals, keyvals, grad, mixed, lse]
    if masked:
        specs.insert(0, pl.BlockSpec(memory_space=pltpu.SMEM))
        args.insert(0, lengths)
    return call(
        functools.partial(attend_back_kernel, masked=masked),
        (clips, groups // pairs),
        specs,
        [pair_spec(frames, 0, pairs), pair_spec(slots, 0, pairs), pair_spec(slots, 0, pairs)],
        [
            struct((clips, frames, D), BF),
            struct((clips, slots, D), BF),
            struct((clips, slots, D), BF),
        ],
        name,
    )(*args)


def after_self_kernel(
    o_ref, x_ref, mod_ref, wo_ref, bo_ref, wq_ref, cap_ref, wkv_ref, z_ref, h_ref, q_ref, kv_ref
):
    @pl.when(pl.program_id(1) == 0)
    def _():
        kv_ref[0] = nn(cap_ref[0], wkv_ref[...]).astype(BF)

    branch = nn(o_ref[0], wo_ref[...]) + bo_ref[...]
    hidden = x_ref[0].astype(F32) + mod_ref[0, 2:3] * branch
    normed, _ = normalize(hidden)
    second_in = (normed * (1.0 + mod_ref[0, 4:5]) + mod_ref[0, 3:4]).astype(BF)
    z_ref[0] = branch.astype(BF)
    h_ref[0] = hidden
    q_ref[0] = nn(second_in, wq_ref[...]).astype(BF)


def after_self(mixed, latents, mod, weight, bias, query_weight, captions, keyval_weight):
    clips, frames, width = latents.shape
    slots, context = captions.shape[1:]
    wide = keyval_weight.shape[1]
    rows = frames
    spec = rows_spec(rows, width)
    square = whole_spec((width, width))
    return call(
        after_self_kernel,
        (clips, frames // rows),
        [
            spec,
            spec,
            clip_spec(9, width),
            square,
            whole_spec((1, width)),
            square,
            clip_spec(slots, context),
            whole_spec(keyval_weight.shape),
        ],
        [spec, spec, spec, clip_spec(slots, wide)],
        [
            struct(latents.shape, BF),
            struct(latents.shape, F32),
            struct(latents.shape, BF),
            struct((clips, slots, wide), BF),
        ],
        "after_self",
    )(mixed, latents, mod, weight, bias, query_weight, captions, keyval_weight)


def after_cross_kernel(o_ref, h_ref, mod_ref, wo_ref, bo_ref, z_ref, out_ref):
    branch = nn(o_ref[0], wo_ref[...]) + bo_ref[...]
    z_ref[0] = branch.astype(BF)
    out_ref[0] = h_ref[0] + mod_ref[0, 5:6] * branch


def after_cross(mixed, hidden, mod, weight, bias):
    clips, frames, width = hidden.shape
    rows = frames
    spec = rows_spec(rows, width)
    return call(
        after_cross_kernel,
        (clips, frames // rows),
        [
            spec,
            spec,
            clip_spec(9, width),
            whole_spec((width, width)),
            whole_spec((1, width)),
        ],
        [spec, spec],
        [struct(hidden.shape, BF), struct(hidden.shape, F32)],
        "after_cross",
    )(mixed, hidden, mod, weight, bias)


GELU_ROOT = math.sqrt(2.0 / math.pi)


def feed_kernel(
    h_ref,
    dy_ref,
    mod_ref,
    up_ref,
    upb_ref,
    down_ref,
    downb_ref,
    out_ref,
    dh_ref,
    dup_ref,
    ddown_ref,
    dupb_ref,
    ddownb_ref,
    sums_ref,
    in_s,
    int_s,
    dz_s,
    dzt_s,
    z_s,
    act_s,
    du_s,
    *,
    clips,
    frames,
    rows,
):
    step = pl.program_id(0)
    last = pl.num_programs(0) - 1
    spans = [
        (clip, start, clip * frames + start)
        for clip in range(clips)
        for start in range(0, frames, rows)
    ]

    @pl.when(step == 0)
    def _():
        bias_sum = jnp.zeros((1, h_ref.shape[2]), F32)
        for clip, start, at in spans:
            normed, _ = normalize(h_ref[clip, start : start + rows])
            third_in = normed * (1.0 + mod_ref[clip, 7:8]) + mod_ref[clip, 6:7]
            dz = (mod_ref[clip, 8:9] * dy_ref[clip, start : start + rows].astype(F32)).astype(BF)
            in_s[at : at + rows] = third_in.astype(BF)
            dz_s[at : at + rows] = dz
            bias_sum += column_sum(dz.astype(F32))
        ddownb_ref[...] = bias_sum
        int_s[...] = in_s[...].T
        dzt_s[...] = dz_s[...].T
        z_s[...] = jnp.zeros_like(z_s)
        dh_ref[...] = jnp.zeros_like(dh_ref)

    up, down = up_ref[...], down_ref[...]

    per = frames // rows

    def one(index):
        at = pl.multiple_of(index * rows, rows)
        here = pl.ds(at, rows)
        hidden = nn(in_s[here], up) + upb_ref[...]
        square = hidden * hidden
        tanh = jnp.tanh(hidden * (GELU_ROOT + (GELU_ROOT * 0.044715) * square))
        half = 0.5 + 0.5 * tanh
        lifted = hidden * half
        activated = lifted.astype(BF)
        slope = half + lifted * (1.0 - tanh) * (
            GELU_ROOT + (GELU_ROOT * 3 * 0.044715) * square
        )
        grad_hidden = (nt(dz_s[here], down) * slope).astype(BF)
        z_s[here] += nn(activated, down)
        spot = pl.ds(pl.multiple_of(index % per * rows, rows), rows)
        dh_ref[index // per, spot] += nt(grad_hidden, up)
        act_s[here] = activated
        du_s[here] = grad_hidden

    def one_clip(clip, _):
        for part in range(per):
            one(clip * per + part)
        return 0

    lax.fori_loop(0, clips, one_clip, 0)
    dup_ref[...] = nn(int_s[...], du_s[...]).astype(BF)
    ddown_ref[...] = nn(dzt_s[...], act_s[...]).T.astype(BF)
    dupb_ref[...] = column_sum(du_s[...].astype(F32))

    @pl.when(step == last)
    def _():
        for clip in range(clips):
            sums = None
            for start in range(0, frames, rows):
                at = clip * frames + start
                block = slice(start, start + rows)
                hidden = h_ref[clip, block]
                dy = dy_ref[clip, block].astype(F32)
                branch = z_s[at : at + rows] + downb_ref[...]
                out_ref[clip, block] = (hidden + mod_ref[clip, 8:9] * branch).astype(BF)
                normed, inverse = normalize(hidden)
                grad_in = dh_ref[clip, block]
                dh_ref[clip, block] = dy + norm_back(
                    normed, inverse, grad_in * (1.0 + mod_ref[clip, 7:8])
                )
                here = [
                    column_sum(grad_in),
                    column_sum(grad_in * normed),
                    column_sum(dy * branch),
                ]
                sums = here if sums is None else [a + b for a, b in zip(sums, here)]
            for index in range(3):
                sums_ref[clip, index : index + 1] = sums[index]


def feed(hidden, cotangent, mod, up, up_bias, down, down_bias, block=768):
    clips, frames, width = hidden.shape
    inner = up.shape[1]
    rows = row_block(frames)
    tokens = clips * frames

    def once(shape):
        return pl.BlockSpec(
            shape, lambda j: (0,) * len(shape), pipeline_mode=pl.Buffered(1)
        )

    def columns(count):
        return pl.BlockSpec((count, block), lambda j: (0, j))

    lines = pl.BlockSpec((block, width), lambda j: (j, 0))
    cube = once((clips, frames, width))
    return call(
        functools.partial(feed_kernel, clips=clips, frames=frames, rows=rows),
        (inner // block,),
        [
            cube,
            cube,
            once(mod.shape),
            columns(width),
            columns(1),
            lines,
            once((1, width)),
        ],
        [
            cube,
            cube,
            columns(width),
            lines,
            columns(1),
            once((1, width)),
            once((clips, 3, width)),
        ],
        [
            struct(hidden.shape, BF),
            struct(hidden.shape, F32),
            struct(up.shape, BF),
            struct(down.shape, BF),
            struct((1, inner), F32),
            struct((1, width), F32),
            struct((clips, 3, width), F32),
        ],
        "feed",
        [
            pltpu.VMEM((tokens, width), BF),
            pltpu.VMEM((width, tokens), BF),
            pltpu.VMEM((tokens, width), BF),
            pltpu.VMEM((width, tokens), BF),
            pltpu.VMEM((tokens, width), F32),
            pltpu.VMEM((tokens, block), BF),
            pltpu.VMEM((tokens, block), BF),
        ],
    )(hidden, cotangent, mod, up, up_bias, down, down_bias)


def ends():
    i, j = pl.program_id(0), pl.program_id(1)
    first = (i == 0) & (j == 0)
    last = (i == pl.num_programs(0) - 1) & (j == pl.num_programs(1) - 1)
    return j == 0, first, last


def before_cross_kernel(
    dh_ref, z_ref, o_ref, mod_ref, w_ref, do_ref, dw_ref, db_ref, sums_ref, ot_s, dz_s
):
    new_clip, first, last = ends()
    clear_at(new_clip, sums_ref)
    clear_at(first, db_ref)
    dh = dh_ref[0]
    here = span_of(dh.shape[0])
    dz = (mod_ref[0, 5:6] * dh).astype(BF)
    dz_s[here] = dz
    ot_s[here] = o_ref[0]
    sums_ref[0] += column_sum(dh * z_ref[0].astype(F32))
    db_ref[...] += column_sum(dz.astype(F32))
    do_ref[0] = nt(dz, w_ref[...]).astype(BF)

    @pl.when(last)
    def _():
        dw_ref[...] = tn(ot_s[...], dz_s[...]).astype(BF)


def before_cross(dh, branch, mixed, mod, weight):
    clips, frames, width = dh.shape
    rows = frames
    spec = rows_spec(rows, width)
    square = whole_spec((width, width))
    return call(
        before_cross_kernel,
        (clips, frames // rows),
        [spec, spec, spec, clip_spec(9, width), square],
        [spec, square, whole_spec((1, width)), clip_spec(1, width)],
        [
            struct(dh.shape, BF),
            struct((width, width), BF),
            struct((1, width), F32),
            struct((clips, 1, width), F32),
        ],
        "before_cross",
        [pltpu.VMEM((clips * frames, width), BF)] * 2,
    )(dh, branch, mixed, mod, weight)


def before_self_kernel(
    dq_ref,
    h_ref,
    dh_ref,
    z_ref,
    o_ref,
    mod_ref,
    wq_ref,
    wo_ref,
    cap_ref,
    dk_ref,
    dv_ref,
    out_ref,
    do_ref,
    dwq_ref,
    dwo_ref,
    db_ref,
    sums_ref,
    dkv_ref,
    in_s,
    dq_s,
    o_s,
    dz_s,
):
    new_clip, first, last = ends()
    clear_at(new_clip, sums_ref)
    clear_at(first, db_ref)
    here = span_of(dq_ref.shape[1])
    normed, inverse = normalize(h_ref[0])
    in_s[here] = (normed * (1.0 + mod_ref[0, 4:5]) + mod_ref[0, 3:4]).astype(BF)
    grad_query = dq_ref[0]
    dq_s[here] = grad_query
    o_s[here] = o_ref[0]
    grad_in = nt(grad_query, wq_ref[...])
    dh = dh_ref[0] + norm_back(normed, inverse, grad_in * (1.0 + mod_ref[0, 4:5]))
    out_ref[0] = dh
    dz = (mod_ref[0, 2:3] * dh).astype(BF)
    dz_s[here] = dz
    sums_ref[0] += jnp.concatenate(
        [
            column_sum(grad_in),
            column_sum(grad_in * normed),
            column_sum(dh * z_ref[0].astype(F32)),
        ],
        axis=0,
    )
    db_ref[...] += column_sum(dz.astype(F32))
    do_ref[0] = nt(dz, wo_ref[...]).astype(BF)

    @pl.when(last)
    def _():
        dwq_ref[...] = tn(in_s[...], dq_s[...]).astype(BF)
        dwo_ref[...] = tn(o_s[...], dz_s[...]).astype(BF)
        turned = cap_ref[...].T
        half = dk_ref.shape[1]
        dkv_ref[:, :half] = nn(turned, dk_ref[...]).astype(BF)
        dkv_ref[:, half:] = nn(turned, dv_ref[...]).astype(BF)


def before_self(
    grad_query, hidden, dh, branch, mixed, mod, query_weight, weight, captions, grad_k, grad_v
):
    clips, frames, width = dh.shape
    captions, grad_k, grad_v = [t.reshape(-1, t.shape[2]) for t in (captions, grad_k, grad_v)]
    keyval_shape = (captions.shape[1], 2 * width)
    rows = row_block(frames)
    spec = rows_spec(rows, width)
    square = whole_spec((width, width))
    return call(
        before_self_kernel,
        (clips, frames // rows),
        [spec, spec, spec, spec, spec, clip_spec(9, width), square, square]
        + [whole_spec(t.shape) for t in (captions, grad_k, grad_v)],
        [
            spec,
            spec,
            square,
            square,
            whole_spec((1, width)),
            clip_spec(3, width),
            whole_spec(keyval_shape),
        ],
        [
            struct(dh.shape, F32),
            struct(dh.shape, BF),
            struct((width, width), BF),
            struct((width, width), BF),
            struct((1, width), F32),
            struct((clips, 3, width), F32),
            struct(keyval_shape, BF),
        ],
        "before_self",
        [pltpu.VMEM((clips * frames, width), BF)] * 4,
    )(
        grad_query,
        hidden,
        dh,
        branch,
        mixed,
        mod,
        query_weight,
        weight,
        captions,
        grad_k,
        grad_v,
    )


def input_kernel(
    dq_ref, dk_ref, dv_ref, x_ref, dh_ref, mod_ref, w_ref, out_ref, dw_ref, sums_ref, in_s, g_s
):
    new_clip, _, last = ends()
    width = x_ref.shape[2]
    clear_at(new_clip, sums_ref)
    here = span_of(x_ref.shape[1])
    normed, inverse = normalize(x_ref[0].astype(F32))
    in_s[here] = (normed * (1.0 + mod_ref[0, 1:2]) + mod_ref[0, 0:1]).astype(BF)
    grad_in = None
    for index, ref in enumerate((dq_ref, dk_ref, dv_ref)):
        columns = slice(index * width, (index + 1) * width)
        grad = ref[0]
        g_s[here, columns] = grad
        part = nt(grad, w_ref[:, columns])
        grad_in = part if grad_in is None else grad_in + part
    out_ref[0] = (
        dh_ref[0] + norm_back(normed, inverse, grad_in * (1.0 + mod_ref[0, 1:2]))
    ).astype(BF)
    sums_ref[0] += jnp.concatenate(
        [column_sum(grad_in), column_sum(grad_in * normed)], axis=0
    )

    @pl.when(last)
    def _():
        turned = in_s[...].T
        for index in range(3):
            columns = slice(index * width, (index + 1) * width)
            dw_ref[:, columns] = nn(turned, g_s[:, columns]).astype(BF)


def input_back(grads, latents, dh, mod, weight):
    clips, frames, width = dh.shape
    rows = row_block(frames)
    spec = rows_spec(rows, width)
    return call(
        input_kernel,
        (clips, frames // rows),
        [spec] * 5 + [clip_spec(9, width), whole_spec(weight.shape)],
        [spec, whole_spec(weight.shape), clip_spec(2, width)],
        [
            struct(dh.shape, BF),
            struct(weight.shape, BF),
            struct((clips, 2, width), F32),
        ],
        "input_back",
        [
            pltpu.VMEM((clips * frames, width), BF),
            pltpu.VMEM((clips * frames, weight.shape[1]), BF),
        ],
    )(*grads, latents, dh, mod, weight)


def block_pass(latents, captions, lengths, cotangent, mod, triple_weight, front, back):
    triple, mixed_one, lse_one, weights = front(latents, mod, triple_weight)
    (
        output_weight,
        output_bias,
        cross_query,
        cross_keyval,
        cross_output,
        cross_bias,
        up_weight,
        up_bias,
        down_weight,
        down_bias,
    ) = weights
    groups = HEADS // 2
    branch_one, hidden_one, cross_queries, pairs = after_self(
        mixed_one, latents, mod, output_weight, output_bias, cross_query, captions, cross_keyval
    )
    mixed_two, lse_two = attend_forward(cross_queries, 0, pairs, groups, lengths, "cross_forward")
    branch_two, hidden_two = after_cross(mixed_two, hidden_one, mod, cross_output, cross_bias)
    output, dh_two, grad_up, grad_down, grad_up_bias, grad_down_bias, sums_three = feed(
        hidden_two, cotangent, mod, up_weight, up_bias, down_weight, down_bias
    )
    grad_mixed_two, grad_cross_output, grad_cross_bias, gate_two = before_cross(
        dh_two, branch_two, mixed_two, mod, cross_output
    )
    grad_cq, grad_ck, grad_cv = attend_backward(
        cross_queries,
        0,
        pairs,
        groups,
        lengths,
        grad_mixed_two,
        mixed_two,
        lse_two,
        "cross_back",
        2,
    )
    (
        dh_one,
        grad_mixed_one,
        grad_cross_query,
        grad_output,
        grad_output_bias,
        sums_two,
        grad_keyval,
    ) = before_self(
        grad_cq,
        hidden_one,
        dh_two,
        branch_one,
        mixed_one,
        mod,
        cross_query,
        output_weight,
        captions,
        grad_ck,
        grad_cv,
    )
    gradients = [
        grad_output,
        grad_output_bias,
        grad_cross_query,
        grad_keyval,
        grad_cross_output,
        grad_cross_bias,
        grad_up,
        grad_up_bias,
        grad_down,
        grad_down_bias,
    ]
    input_grad, grad_triple, sums_one, rest = back(
        triple, grad_mixed_one, mixed_one, lse_one, latents, dh_one, mod, triple_weight, gradients
    )
    grad_mod = jnp.concatenate(
        [sums_one, sums_two[:, 2:], sums_two[:, :2], gate_two, sums_three], axis=1
    ).astype(BF)
    return output, input_grad, grad_mod, grad_triple, gradients, rest


def plain_front(weights, latents, mod, triple_weight):
    groups = HEADS // 2
    triple = qkv_forward(latents, mod, triple_weight)
    mixed, lse = attend_forward(triple, groups, triple, 2 * groups, None, "self_forward", 2)
    return triple, mixed, lse, weights


def plain_back(triple, grad_mixed, mixed, lse, latents, dh, mod, triple_weight, gradients):
    groups = HEADS // 2
    grads = attend_backward(
        triple, groups, triple, 2 * groups, None, grad_mixed, mixed, lse, "self_back", 2
    )
    return *input_back(grads, latents, dh, mod, triple_weight), None


LANE = 128
TILE = 16


def linear_layout():
    spots = []
    offset = 0
    for shape in layout_sizes():
        number = math.prod(shape) // LANE
        spots.append((offset, number, shape))
        offset += number
    return spots


class Group:
    def __init__(self, devices, inner, share, first, last):
        self.devices, self.share, self.first, self.last = devices, share, first, last
        self.padded = -(-share // TILE) * TILE
        owners, total = {}, 0
        for owner in range(first // share, (last - 1) // share + 1):
            low = max(first - owner * share, 0) // TILE
            high = -(-min(last - owner * share, share) // TILE)
            owners[owner] = [low, high]
            total += high - low
        self.tiles = 2 * -(-total // (2 * devices))
        self.chunk = self.tiles * TILE
        self.half = self.chunk // 2
        small = self.tiles // 9 * TILE
        large = self.half - small
        self.parts = (
            (0, large),
            (large, large),
            (2 * large, small),
            (2 * large + small, small),
        )
        self.folds = next(
            n
            for n in range(1, 99)
            if self.half % (n * TILE) == 0 and self.half // n <= 512
        )
        room = [self.tiles] * devices
        self.pieces = []

        def give(owner, device):
            low, high = owners[owner]
            take = min(high - low, room[device])
            if take > 0:
                place = self.tiles - room[device]
                self.pieces.append((owner, device, low * TILE, place * TILE, take * TILE))
                room[device] -= take
                owners[owner][0] += take

        for flip in (0, 2 * inner, inner):
            for owner in owners:
                give(owner, owner ^ flip)
        for owner in owners:
            while owners[owner][0] < owners[owner][1]:
                give(owner, max(range(devices), key=lambda device: room[device]))

    def find(self, row):
        owner, at = divmod(row, self.share)
        for holder, device, start, place, count in self.pieces:
            if holder == owner and start <= at < start + count:
                return device, place + at - start, min(self.share, start + count) - at
        raise ValueError(row)

    def segments(self, start, count):
        found = []
        row = start
        while row < start + count:
            chunk, place, left = self.find(row)
            take = min(left, start + count - row)
            found.append((chunk, place, row, take))
            row += take
        return found

    def moves(self):
        return self.pieces


def unpack_kernel(*refs, plan, indices, step):
    n = len(indices)
    spots = linear_layout()
    g_ref, outs, rest = refs[0], refs[1 : 1 + n], refs[1 + n :]
    lin, in_sem, out_sem = rest[0], rest[1], rest[2]
    stages, results = rest[3 : 3 + n], rest[3 + n :]
    loads = []
    for which, index in enumerate(indices):
        offset, number, _ = spots[index]
        place = 0
        mine = []
        for slot, (chunk, row, at, take) in enumerate(plan.segments(offset, number)):
            low = row // TILE * TILE
            high = -(-(row + take) // TILE) * TILE
            copy = pltpu.make_async_copy(
                g_ref.at[chunk, pl.ds(low, high - low)],
                stages[which].at[pl.ds(place, high - low)],
                in_sem.at[which, slot],
            )
            copy.start()
            mine.append((copy, place, row - low, high - low, at - offset, take))
            place += high - low
        loads.append(mine)
    stores = []
    for which, index in enumerate(indices):
        offset, number, shape = spots[index]
        for copy, place, skip, size, at, take in loads[which]:
            copy.wait()
            first = stages[which][place : place + TILE].astype(F32)
            lin[at : at + TILE - skip] = first[skip:]
            blocks, tail = divmod(size - TILE, step)

            def body(i, _, place=place, at=at, skip=skip, which=which):
                source = pl.multiple_of(place + TILE + i * step, TILE)
                lin[pl.ds(at + TILE - skip + i * step, step)] = stages[which][
                    pl.ds(source, step)
                ].astype(F32)
                return 0

            lax.fori_loop(0, blocks, body, 0)
            if tail:
                source = place + TILE + blocks * step
                target = at + TILE - skip + blocks * step
                lin[target : target + tail] = stages[which][source : source + tail].astype(F32)
        if len(shape) == 1:
            for c in range(number):
                results[which][0:1, c * LANE : (c + 1) * LANE] = lin[c : c + 1]
        else:
            high, wide = shape
            count = wide // LANE
            rows = 64

            def turn(i, _, which=which, count=count):
                top = pl.multiple_of(i * rows, rows)
                for c in range(count):
                    results[which][pl.ds(top, rows), c * LANE : (c + 1) * LANE] = lin[
                        pl.ds(top * count + c, rows, stride=count)
                    ].astype(BF)
                return 0

            lax.fori_loop(0, high // rows, turn, 0)
        copy = pltpu.make_async_copy(results[which], outs[which], out_sem.at[which])
        copy.start()
        stores.append(copy)
    for copy in stores:
        copy.wait()


def unpack_weights(gathered, plan, indices, step=128):
    spots = linear_layout()
    stage_shapes, result_shapes, most, tallest = [], [], 0, 0
    for index in indices:
        offset, number, shape = spots[index]
        found = plan.segments(offset, number)
        size = sum(-(-(r + t) // TILE) * TILE - r // TILE * TILE for _, r, _, t in found)
        stage_shapes.append(pltpu.VMEM((size, LANE), BF))
        most = max(most, len(found))
        tallest = max(tallest, number)
        result_shapes.append((shape, BF) if len(shape) == 2 else ((1, shape[0]), F32))
    anywhere = pl.BlockSpec(memory_space=pl.ANY)
    return pl.pallas_call(
        functools.partial(unpack_kernel, plan=plan, indices=indices, step=step),
        in_specs=[anywhere],
        out_specs=[anywhere] * len(indices),
        out_shape=[jax.ShapeDtypeStruct(s, t) for s, t in result_shapes],
        scratch_shapes=[
            pltpu.VMEM((tallest + 2 * TILE, LANE), F32),
            pltpu.SemaphoreType.DMA((len(indices), most)),
            pltpu.SemaphoreType.DMA((len(indices),)),
        ]
        + stage_shapes
        + [pltpu.VMEM(s, t) for s, t in result_shapes],
        compiler_params=pltpu.CompilerParams(vmem_limit_bytes=VMEM_LIMIT),
        name="unpack",
    )(gathered)


def pack_kernel(*refs, plan, indices, step):
    n = len(indices)
    spots = linear_layout()
    ins, out_ref, rest = refs[:n], refs[n], refs[n + 1 :]
    lin, stage, in_sem, out_sem = rest[:4]
    held = rest[4:]
    copies = []
    for which in range(n):
        copy = pltpu.make_async_copy(ins[which], held[which], in_sem.at[which])
        copy.start()
        copies.append(copy)
    stores = []
    begin = spots[indices[0]][0]
    total = spots[indices[-1]][0] + spots[indices[-1]][1] - begin
    pieces = plan.segments(begin, total)
    place = 0
    done = -TILE
    lin[0:TILE] = jnp.zeros((TILE, LANE), F32)
    slot = 0
    for which, index in enumerate(indices):
        offset, number, shape = spots[index]
        copies[which].wait()
        if len(shape) == 1:
            for c in range(number):
                lin[TILE + c : TILE + c + 1] = held[which][0:1, c * LANE : (c + 1) * LANE]
        else:
            high, wide = shape
            count = wide // LANE
            rows = 64

            def turn(i, _, which=which, count=count):
                top = pl.multiple_of(i * rows, rows)
                for c in range(count):
                    lin[pl.ds(TILE + top * count + c, rows, stride=count)] = held[which][
                        pl.ds(top, rows), c * LANE : (c + 1) * LANE
                    ].astype(F32)
                return 0

            lax.fori_loop(0, high // rows, turn, 0)
        low, high_row = offset - begin, offset - begin + number
        last = which == n - 1
        while slot < len(pieces):
            chunk, row, at, take = pieces[slot]
            at -= begin
            head = row - row // TILE * TILE
            start, stop = at - head, at + take
            ceil = start + -(-(stop - start) // TILE) * TILE
            first = max(start, done)
            whole = stop <= high_row
            end = ceil if whole else start + (high_row - start) // TILE * TILE
            if end > first:
                base = row - head + first - start
                blocks, tail = divmod(end - first, step)
                shift = TILE + first - low

                def body(i, _, place=place, shift=shift):
                    target = pl.multiple_of(place + i * step, TILE)
                    stage[pl.ds(target, step)] = lin[pl.ds(shift + i * step, step)].astype(BF)
                    return 0

                lax.fori_loop(0, blocks, body, 0)
                if tail:
                    source = shift + blocks * step
                    target = place + blocks * step
                    stage[target : target + tail] = lin[source : source + tail].astype(BF)
                copy = pltpu.make_async_copy(
                    stage.at[pl.ds(place, end - first)],
                    out_ref.at[chunk, pl.ds(base, end - first)],
                    out_sem.at[len(stores)],
                )
                copy.start()
                stores.append(copy)
                place += end - first
                done = end
            if not whole:
                break
            done = stop if slot + 1 == len(pieces) else min(done, stop)
            slot += 1
        if not last:
            lin[0:TILE] = lin[number : number + TILE]
    for copy in stores:
        copy.wait()


def pack_grads(grads, plan, indices, step=128):
    spots = linear_layout()
    tallest = max(spots[i][1] for i in indices)
    begin = spots[indices[0]][0]
    total = spots[indices[-1]][0] + spots[indices[-1]][1] - begin
    count = len(plan.segments(begin, total))
    anywhere = pl.BlockSpec(memory_space=pl.ANY)
    return pl.pallas_call(
        functools.partial(pack_kernel, plan=plan, indices=indices, step=step),
        in_specs=[anywhere] * len(indices),
        out_specs=anywhere,
        out_shape=jax.ShapeDtypeStruct((plan.devices, plan.chunk, LANE), BF),
        scratch_shapes=[
            pltpu.VMEM((tallest + 2 * TILE, LANE), F32),
            pltpu.VMEM((total + 2 * TILE * (count + len(indices)), LANE), BF),
            pltpu.SemaphoreType.DMA((len(indices),)),
            pltpu.SemaphoreType.DMA((count + len(indices),)),
        ]
        + [pltpu.VMEM(g.shape, g.dtype) for g in grads],
        compiler_params=pltpu.CompilerParams(vmem_limit_bytes=VMEM_LIMIT),
        name="pack",
    )(*grads)


MESH = pl.DeviceIdType.MESH


def place_of():
    dp, fs = lax.axis_index("dp"), lax.axis_index("fsdp")
    return dp, fs, dp // 2, dp % 2, fs // 2, fs % 2


def meet_all(me, devices, inner):
    barrier = pltpu.get_barrier_semaphore()

    def greet(i, _):
        other = (me + i) % devices
        pl.semaphore_signal(
            barrier, inc=1, device_id=(other // inner, other % inner), device_id_type=MESH
        )
        return 0

    lax.fori_loop(1, devices, greet, 0)
    pl.semaphore_wait(barrier, devices - 1)


class Trade:
    def __init__(self, source, target, own_sem, send_sem, recv_sem, group, inner, senders, receivers):
        self.source, self.target, self.own_sem = source, target, own_sem
        self.send_sem, self.recv_sem = send_sem, recv_sem
        self.devices, self.inner = group.devices, inner
        self.senders, self.receivers = senders, receivers
        self.me = lax.axis_index("dp") * inner + lax.axis_index("fsdp")
        self.many = len(source.shape) == 3

    def piece(self, target):
        return self.source.at[target] if self.many else self.source

    def copy(self, source, target):
        return pltpu.make_async_remote_copy(
            src_ref=self.piece(target),
            dst_ref=self.target.at[source],
            send_sem=self.send_sem.at[target],
            recv_sem=self.recv_sem.at[source],
            device_id=(target // self.inner, target % self.inner),
            device_id_type=MESH,
        )

    def own(self):
        return pltpu.make_async_copy(
            self.piece(self.me), self.target.at[self.me], self.own_sem
        )

    def each(self, act):
        def body(i, _):
            act((self.me + i) % self.devices)
            return 0

        lax.fori_loop(1, self.devices, body, 0)

    def both(self):
        return (self.me < self.senders) & (self.me < self.receivers)

    def start(self):
        pl.when(self.both())(lambda: self.own().start())

        def act(other):
            ok = (self.me < self.senders) & (other < self.receivers)
            pl.when(ok)(lambda: self.copy(self.me, other).start())

        self.each(act)

    def wait(self):
        pl.when(self.both())(lambda: self.own().wait())

        def landed(other):
            ok = (other < self.senders) & (self.me < self.receivers)
            pl.when(ok)(lambda: self.copy(other, other).wait_recv())

        def gone(other):
            ok = (self.me < self.senders) & (other < self.receivers)
            pl.when(ok)(lambda: self.copy(self.me, other).wait_send())

        self.each(landed)
        self.each(gone)


def when_all(conditions):
    total = None
    for condition in conditions:
        if condition is not None:
            total = condition if total is None else total & condition
    return total


def guarded(condition, body):
    if condition is None:
        body()
    else:
        pl.when(condition)(body)


class Deal:
    def __init__(self, group, source, target, send_sem, recv_sem, inner, back):
        self.source, self.target, self.back = source, target, back
        self.send_sem, self.recv_sem, self.inner = send_sem, recv_sem, inner
        self.me = lax.axis_index("dp") * inner + lax.axis_index("fsdp")
        self.moves = []
        for owner, device, row, place, count in group.moves():
            if back:
                self.moves.append((device, owner, place, row, count))
            else:
                self.moves.append((owner, device, row, place, count))

    def copy(self, move):
        source, target, start, place, count = move
        out = [m for m in self.moves if m[0] == source].index(move)
        into = [m for m in self.moves if m[1] == target].index(move)
        from_ref = self.source.at[pl.ds(start, count)]
        to_ref = self.target.at[pl.ds(place, count)]
        if source == target:
            return pltpu.make_async_copy(from_ref, to_ref, self.recv_sem.at[into])
        return pltpu.make_async_remote_copy(
            src_ref=from_ref,
            dst_ref=to_ref,
            send_sem=self.send_sem.at[out],
            recv_sem=self.recv_sem.at[into],
            device_id=(target // self.inner, target % self.inner),
            device_id_type=MESH,
        )

    def each(self, key, act):
        for device in sorted({m[key] for m in self.moves}):
            mine = [m for m in self.moves if m[key] == device]

            @pl.when(self.me == device)
            def _(mine=mine):
                for move in mine:
                    act(move)

    def start(self):
        self.each(0, lambda move: self.copy(move).start())

    def landed(self):
        def act(move):
            if move[0] == move[1]:
                self.copy(move).wait()
            else:
                self.copy(move).wait_recv()

        self.each(1, act)

    def gone(self):
        def act(move):
            if move[0] != move[1]:
                self.copy(move).wait_send()

        self.each(0, act)

    @staticmethod
    def semaphores(group, back):
        sends = recvs = 0
        for device in range(group.devices):
            sends = max(sends, sum(1 for m in group.moves() if m[1 if back else 0] == device))
            recvs = max(recvs, sum(1 for m in group.moves() if m[0 if back else 1] == device))
        dma = pltpu.SemaphoreType.DMA
        return [dma((sends,)), dma((recvs,))]


def remote_call(body, in_specs, out_specs, out_shape, scratch, collective, name, grid=()):
    return pl.pallas_call(
        body,
        grid=grid,
        in_specs=in_specs,
        out_specs=out_specs,
        out_shape=out_shape,
        scratch_shapes=scratch,
        compiler_params=pltpu.CompilerParams(
            collective_id=collective, has_side_effects=True, vmem_limit_bytes=VMEM_LIMIT
        ),
        name=name,
    )


ANYWHERE = pl.BlockSpec(memory_space=pl.ANY)


def start_kernel(
    step_ref, slot_ref, all_ref, chunk_ref, own_sem, send_sem, recv_sem, deal_send, deal_recv,
    *, group, inner
):
    me = lax.axis_index("dp") * inner + lax.axis_index("fsdp")
    meet_all(me, group.devices, inner)
    deal = Deal(group, slot_ref, chunk_ref, deal_send, deal_recv, inner, False)
    trade = Trade(
        step_ref, all_ref, own_sem, send_sem, recv_sem, group, inner, group.devices, group.devices
    )
    trade.start()
    deal.start()
    trade.wait()
    deal.landed()
    deal.gone()


def start_chunks(steps, slot, group, inner, collective):
    dma = pltpu.SemaphoreType.DMA
    return remote_call(
        functools.partial(start_kernel, group=group, inner=inner),
        [ANYWHERE] * 2,
        [ANYWHERE] * 2,
        [
            jax.ShapeDtypeStruct((group.devices, *steps.shape), steps.dtype),
            jax.ShapeDtypeStruct((group.chunk, LANE), BF),
        ],
        [dma, dma((group.devices,)), dma((group.devices,))] + Deal.semaphores(group, False),
        collective,
        "start_chunks",
    )(steps, slot)


class Gather:
    def __init__(self, group, inner, chunk_ref, out_ref, own_sem, send_sem, recv_sem):
        self.group, self.inner = group, inner
        self.chunk_ref, self.out_ref = chunk_ref, out_ref
        self.send_sem, self.recv_sem = send_sem, recv_sem
        dp, fs, self.y, self.x, self.z, self.c = place_of()
        self.levels = inner // 2
        self.own = pltpu.make_async_copy(chunk_ref, out_ref.at[dp * inner + fs], own_sem)
        self.across = {
            "up": (dp, fs + 2),
            "down": (dp, fs - 2),
            "x": (dp + 1 - 2 * self.x, fs),
            "y": (dp + 2 - 4 * self.y, fs),
            "twin": (dp, fs + 1 - 2 * self.c),
        }
        self.kinds = tuple(self.across)
        self.closing = False

    @staticmethod
    def semaphores(group):
        dma = pltpu.SemaphoreType.DMA
        return [dma, dma((5, group.devices // 2, 4)), dma((group.devices, 4))]

    def copy(self, kind, yy, xx, zz, part, cc=None, mine=False):
        core = self.c if cc is None else cc
        column = yy * 2 + xx
        index = column * self.inner + zz * 2 + core
        rows = pl.ds(*self.group.parts[part])
        return pltpu.make_async_remote_copy(
            src_ref=self.chunk_ref.at[rows] if mine else self.out_ref.at[index, rows],
            dst_ref=self.out_ref.at[index, rows],
            send_sem=self.send_sem.at[
                self.kinds.index(kind), column * self.levels + zz, part
            ],
            recv_sem=self.recv_sem.at[index, part],
            device_id=self.across[kind],
            device_id_type=MESH,
        )

    def send(self, condition, kind, yy, xx, zz, part, mine=False):
        copy = functools.partial(self.copy, kind, yy, xx, zz, part, mine=mine)
        if self.closing:
            guarded(condition, lambda: copy().wait_send())
        else:
            guarded(condition, lambda: copy().start())

    def arrive(self, condition, yy, xx, zz, part):
        if self.closing:
            return
        guarded(condition, lambda: self.copy("x", yy, xx, zz, part).wait_recv())

    def spread(self, distance):
        for sign in (1, -1) if distance else (0,):
            zz = self.z + sign * distance
            inside = when_all(
                [zz < self.levels if sign > 0 else None, zz >= 0 if sign < 0 else None]
            )
            yield zz, sign, inside

    def relay(self, distance, sign, inside, yy, xx, zz):
        own = yy is self.y and xx is self.x
        for part in (2, 3):
            mine = own and distance == 0
            if not mine:
                self.arrive(inside, yy, xx, zz, part)
            if distance == 0:
                if own:
                    kinds = ("x", "y") if part == 2 else ("y", "x")
                elif part == 2 and yy is self.y:
                    kinds = ("y",)
                elif part == 3 and xx is self.x:
                    kinds = ("x",)
                else:
                    kinds = ()
                for kind in kinds:
                    self.send(inside, kind, yy, xx, zz, part, mine)
            if sign <= 0:
                on = when_all([inside, self.z < self.levels - 1])
                self.send(on, "up", yy, xx, zz, part, mine)
            if sign >= 0:
                self.send(when_all([inside, self.z > 0]), "down", yy, xx, zz, part, mine)
            self.send(inside, "twin", yy, xx, zz, part, mine)

    def turn(self, turn):
        y, x, z, levels = self.y, self.x, self.z, self.levels
        if turn == 0 and not self.closing:
            self.own.start()
        if turn < levels:
            for zz, sign, inside in self.spread(turn):
                mine = turn == 0
                for part in range(2):
                    if turn:
                        self.arrive(inside, y, x, zz, part)
                    if sign <= 0:
                        self.send(when_all([inside, z < levels - 1]), "up", y, x, zz, part, mine)
                    if sign >= 0:
                        self.send(when_all([inside, z > 0]), "down", y, x, zz, part, mine)
                    for kind in ("x", "y") if part else ("y", "x"):
                        self.send(inside, kind, y, x, zz, part, mine)
                    self.send(inside, "twin", y, x, zz, part, mine)
                self.relay(turn, sign, inside, y, x, zz)
        if 1 <= turn <= levels:
            for zz, sign, inside in self.spread(turn - 1):
                self.arrive(inside, y, 1 - x, zz, 0)
                self.send(inside, "y", y, 1 - x, zz, 0)
                self.send(inside, "twin", y, 1 - x, zz, 0)
                self.arrive(inside, 1 - y, x, zz, 1)
                self.send(inside, "x", 1 - y, x, zz, 1)
                self.send(inside, "twin", 1 - y, x, zz, 1)
                self.arrive(inside, 1 - y, x, zz, 0)
                self.send(inside, "twin", 1 - y, x, zz, 0)
                self.arrive(inside, y, 1 - x, zz, 1)
                self.send(inside, "twin", y, 1 - x, zz, 1)
                self.relay(turn - 1, sign, inside, y, 1 - x, zz)
                self.relay(turn - 1, sign, inside, 1 - y, x, zz)
        if turn >= 2:
            for zz, sign, inside in self.spread(turn - 2):
                for part in range(2):
                    self.arrive(inside, 1 - y, 1 - x, zz, part)
                    self.send(inside, "twin", 1 - y, 1 - x, zz, part)
                self.relay(turn - 2, sign, inside, 1 - y, 1 - x, zz)

    def finish(self):
        def twin_arrivals(i, _):
            column, zz = i // self.levels, i % self.levels
            for part in range(4):
                self.copy("twin", column // 2, column % 2, zz, part, 1 - self.c).wait_recv()
            return 0

        lax.fori_loop(0, 4 * self.levels, twin_arrivals, 0)
        self.closing = True
        for turn in range(self.levels + 2):
            self.turn(turn)
        self.own.wait()


class ShortGather:
    def __init__(self, group, inner, chunk_ref, out_ref, own_sem, send_sem, recv_sem):
        self.group, self.inner = group, inner
        self.chunk_ref, self.out_ref = chunk_ref, out_ref
        self.send_sem, self.recv_sem = send_sem, recv_sem
        dp, fs, self.y, self.x, self.z, self.c = place_of()
        self.levels = inner // 2
        self.own = pltpu.make_async_copy(chunk_ref, out_ref.at[dp * inner + fs], own_sem)
        self.across = {
            "z1": (dp, self.level(-1) * 2 + self.c),
            "z2": (dp, self.level(-2) * 2 + self.c),
            "z3": (dp, self.level(-3) * 2 + self.c),
            "x": (dp + 1 - 2 * self.x, fs),
            "y": (dp + 2 - 4 * self.y, fs),
            "twin": (dp, fs + 1 - 2 * self.c),
        }
        self.kinds = tuple(self.across)
        self.closing = False

    @staticmethod
    def semaphores(group):
        dma = pltpu.SemaphoreType.DMA
        return [dma, dma((6, group.devices // 2, 2)), dma((group.devices, 2))]

    def copy(self, kind, yy, xx, zz, part, cc=None, mine=False):
        core = self.c if cc is None else cc
        column = yy * 2 + xx
        index = column * self.inner + zz * 2 + core
        rows = pl.ds(part * self.group.half, self.group.half)
        return pltpu.make_async_remote_copy(
            src_ref=self.chunk_ref.at[rows] if mine else self.out_ref.at[index, rows],
            dst_ref=self.out_ref.at[index, rows],
            send_sem=self.send_sem.at[
                self.kinds.index(kind), column * self.levels + zz, part
            ],
            recv_sem=self.recv_sem.at[index, part],
            device_id=self.across[kind],
            device_id_type=MESH,
        )

    def level(self, back):
        return (self.z - back + self.levels) % self.levels

    def send(self, kind, yy, xx, zz, part, mine=False):
        copy = self.copy(kind, yy, xx, zz, part, mine=mine)
        if self.closing:
            copy.wait_send()
        else:
            copy.start()

    def arrive(self, yy, xx, zz, part):
        if not self.closing:
            self.copy("x", yy, xx, zz, part).wait_recv()

    def turn(self, turn):
        y, x, levels = self.y, self.x, self.levels
        if turn == 0 and not self.closing:
            self.own.start()
        if turn < levels:
            zz = self.level(turn)
            for part in range(2):
                if turn:
                    self.arrive(y, x, zz, part)
                for kind in ("x", "y") if part else ("y", "x"):
                    self.send(kind, y, x, zz, part, turn == 0)
                if turn == 0:
                    for kind in ("z1", "z2", "z3"):
                        self.send(kind, y, x, zz, part, True)
                self.send("twin", y, x, zz, part, turn == 0)
        if 1 <= turn <= levels:
            zz = self.level(turn - 1)
            self.arrive(y, 1 - x, zz, 0)
            self.send("y", y, 1 - x, zz, 0)
            self.send("twin", y, 1 - x, zz, 0)
            self.arrive(1 - y, x, zz, 1)
            self.send("x", 1 - y, x, zz, 1)
            self.send("twin", 1 - y, x, zz, 1)
            self.arrive(1 - y, x, zz, 0)
            self.send("twin", 1 - y, x, zz, 0)
            self.arrive(y, 1 - x, zz, 1)
            self.send("twin", y, 1 - x, zz, 1)
        if turn >= 2:
            zz = self.level(turn - 2)
            for part in range(2):
                self.arrive(1 - y, 1 - x, zz, part)
                self.send("twin", 1 - y, 1 - x, zz, part)

    def finish(self):
        def twin_arrivals(i, _):
            column, zz = i // self.levels, i % self.levels
            for part in range(2):
                self.copy("twin", column // 2, column % 2, zz, part, 1 - self.c).wait_recv()
            return 0

        lax.fori_loop(0, 4 * self.levels, twin_arrivals, 0)
        self.closing = True
        for turn in range(self.levels + 2):
            self.turn(turn)
        self.own.wait()


class PairTrade:
    def __init__(self, slab_ref, out_ref, mine, theirs, sems, inner, devices):
        self.slab_ref, self.out_ref, self.mine, self.theirs = slab_ref, out_ref, mine, theirs
        self.pair_sem, self.send_sem, self.recv_sem = sems
        self.inner, self.chips, self.senders = inner, devices // 2, out_ref.shape[0]
        dp, fs, _, _, _, self.core = place_of()
        self.twin = (dp, fs + 1 - 2 * self.core)
        self.chip = (dp * inner + fs) // 2

    def load(self):
        return pltpu.make_async_copy(self.slab_ref.at[self.core], self.mine, self.pair_sem.at[0])

    def pair(self):
        return pltpu.make_async_remote_copy(
            src_ref=self.slab_ref.at[1 - self.core],
            dst_ref=self.theirs,
            send_sem=self.pair_sem.at[1],
            recv_sem=self.pair_sem.at[2],
            device_id=self.twin,
            device_id_type=MESH,
        )

    def copy(self, source, target):
        device = 2 * target + self.core
        return pltpu.make_async_remote_copy(
            src_ref=self.mine.at[target],
            dst_ref=self.out_ref.at[source],
            send_sem=self.send_sem.at[target],
            recv_sem=self.recv_sem.at[source],
            device_id=(device // self.inner, device % self.inner),
            device_id_type=MESH,
        )

    def own(self):
        return pltpu.make_async_copy(
            self.mine.at[self.chip], self.out_ref.at[self.chip], self.pair_sem.at[3]
        )

    def each(self, act):
        def body(i, _):
            act((self.chip + i) % self.chips)
            return 0

        lax.fori_loop(1, self.chips, body, 0)

    def begin(self):
        @pl.when(self.chip < self.senders)
        def _():
            self.pair().start()
            self.load().start()

    def start(self):
        @pl.when(self.chip < self.senders)
        def _():
            self.load().wait()
            self.pair().wait_recv()

            def add(i, _):
                self.mine[i] = self.mine[i] + self.theirs[i]
                return 0

            lax.fori_loop(0, self.chips, add, 0)
            self.own().start()
            self.each(lambda other: self.copy(self.chip, other).start())

    def wait(self):
        def landed(other):
            pl.when(other < self.senders)(lambda: self.copy(other, other).wait_recv())

        self.each(landed)

        @pl.when(self.chip < self.senders)
        def _():
            self.own().wait()
            self.pair().wait_send()
            self.each(lambda other: self.copy(self.chip, other).wait_send())


def gather_kernel(
    chunk_ref, slab_ref, slot_ref, out_ref, parts_ref, next_ref, mine, theirs, *sems,
    group, later, inner
):
    me = lax.axis_index("dp") * inner + lax.axis_index("fsdp")
    meet_all(me, group.devices, inner)
    trade = PairTrade(slab_ref, parts_ref, mine, theirs, sems[:3], inner, group.devices)
    gather = ShortGather(group, inner, chunk_ref, out_ref, *sems[3:6])
    deal = Deal(later, slot_ref, next_ref, *sems[6:], inner, False)
    trade.begin()
    gather.turn(0)
    trade.start()
    gather.turn(1)
    deal.start()
    for turn in range(2, inner // 2 + 2):
        gather.turn(turn)
    gather.finish()
    trade.wait()
    deal.landed()
    deal.gone()


def gather_chunks(chunk, slabs, slot, group, later, inner, senders, collective):
    dma = pltpu.SemaphoreType.DMA
    return remote_call(
        functools.partial(gather_kernel, group=group, later=later, inner=inner),
        [ANYWHERE] * 3,
        [ANYWHERE] * 3,
        [
            jax.ShapeDtypeStruct((group.devices, group.chunk, LANE), BF),
            jax.ShapeDtypeStruct((senders // 2, *slabs.shape[2:]), slabs.dtype),
            jax.ShapeDtypeStruct((later.chunk, LANE), BF),
        ],
        [
            pltpu.VMEM(slabs.shape[1:], slabs.dtype),
            pltpu.VMEM(slabs.shape[1:], slabs.dtype),
            dma((4,)),
            dma((group.devices // 2,)),
            dma((group.devices // 2,)),
        ]
        + ShortGather.semaphores(group)
        + Deal.semaphores(later, False),
        collective,
        "gather_chunks",
    )(chunk, slabs, slot)


def scatter_stages(
    group,
    inner,
    g_ref,
    acc,
    twin,
    wide_y,
    wide_x,
    slim_x,
    slim_y,
    line,
    load_sem,
    twin_send,
    twin_recv,
    wide_send,
    wide_recv,
    slim_send,
    slim_recv,
    line_send,
    line_recv,
):
    dp, fs, y, x, z, c = place_of()
    me = dp * inner + fs
    lent = group.half
    levels = inner // 2
    x_mate = (dp + 1 - 2 * x, fs)
    y_mate = (dp + 2 - 4 * y, fs)

    def remote(source, target, send, receive, device):
        return pltpu.make_async_remote_copy(
            src_ref=source,
            dst_ref=target,
            send_sem=send,
            recv_sem=receive,
            device_id=device,
            device_id_type=MESH,
        )

    def slot_of(yy, xx, zz):
        return (yy * 2 + xx) * levels + zz

    def load(yy, xx, zz):
        slot = slot_of(yy, xx, zz)
        return pltpu.make_async_copy(
            g_ref.at[(yy * 2 + xx) * inner + zz * 2 + c], acc.at[slot], load_sem.at[slot]
        )

    def to_twin(yy, xx, zz):
        slot = slot_of(yy, xx, zz)
        return remote(
            g_ref.at[(yy * 2 + xx) * inner + zz * 2 + 1 - c],
            twin.at[slot],
            twin_send.at[slot],
            twin_recv.at[slot],
            (dp, fs + 1 - 2 * c),
        )

    def piece(slot, part):
        return acc.at[slot, pl.ds(part * lent, lent)]

    def wide(part, other, zz, yy=0, xx=0):
        buffer, device = (wide_x, x_mate) if part else (wide_y, y_mate)
        index = other * levels + zz
        return remote(
            piece(slot_of(yy, xx, zz), part),
            buffer.at[index],
            wide_send.at[part, index],
            wide_recv.at[part, index],
            device,
        )

    def slim(part, zz, yy=0, xx=0):
        buffer, device = (slim_y, y_mate) if part else (slim_x, x_mate)
        return remote(
            piece(slot_of(yy, xx, zz), part),
            buffer.at[zz],
            slim_send.at[part, zz],
            slim_recv.at[part, zz],
            device,
        )

    def along(upward, zz, part):
        way = 0 if upward else 1
        return remote(
            piece(slot_of(y, x, zz), part),
            line.at[way, zz, part],
            line_send.at[way, zz, part],
            line_recv.at[way, zz, part],
            (dp, fs + 2 if upward else fs - 2),
        )

    block = lent // group.folds

    def add(slot, first, count, source):
        def body(i, _):
            at = pl.multiple_of(i * block, TILE)
            to = pl.ds(pl.multiple_of(first + i * block, TILE), block)
            acc[slot, to] = acc[slot, to] + source[pl.ds(at, block)]
            return 0

        lax.fori_loop(0, count // block, body, 0)

    def add_part(slot, part, source):
        add(slot, part * lent, lent, source)

    def level(k):
        return jnp.where(z < levels // 2, z + levels - 1 - k, z + 1 + k) % levels

    columns = ((1 - y, 1 - x), (1 - y, x), (y, 1 - x), (y, x))

    def begin():
        for k in range(levels):
            for yy, xx in columns:
                to_twin(yy, xx, level(k)).start()
                load(yy, xx, level(k)).start()

    def settle(yy, xx, zz):
        slot = slot_of(yy, xx, zz)
        load(yy, xx, zz).wait()
        to_twin(yy, xx, zz).wait_recv()
        add(slot, 0, group.chunk, twin.at[slot])

    def diagonal(k):
        zz = level(k)
        settle(1 - y, 1 - x, zz)
        wide(0, 1 - x, zz, 1 - y, 1 - x).start()
        wide(1, 1 - y, zz, 1 - y, 1 - x).start()

    def sides(k):
        zz = level(k)
        settle(1 - y, x, zz)
        wide(0, x, zz, 1 - y, x).start()
        settle(y, 1 - x, zz)
        wide(1, y, zz, y, 1 - x).start()

    def middle(k):
        zz = level(k)
        wide(0, 1 - x, zz).wait_recv()
        add_part(slot_of(y, 1 - x, zz), 0, wide_y.at[(1 - x) * levels + zz])
        slim(0, zz, y, 1 - x).start()
        wide(1, 1 - y, zz).wait_recv()
        add_part(slot_of(1 - y, x, zz), 1, wide_x.at[(1 - y) * levels + zz])
        slim(1, zz, 1 - y, x).start()

    def home(k):
        zz = level(k)
        slot = slot_of(y, x, zz)
        settle(y, x, zz)
        wide(0, x, zz).wait_recv()
        add_part(slot, 0, wide_y.at[x * levels + zz])
        wide(1, y, zz).wait_recv()
        add_part(slot, 1, wide_x.at[y * levels + zz])
        slim(0, zz).wait_recv()
        add_part(slot, 0, slim_x.at[zz])
        slim(1, zz).wait_recv()
        add_part(slot, 1, slim_y.at[zz])

    def take(upward, zz, part):
        along(upward, zz, part).wait_recv()
        add_part(slot_of(y, x, zz), part, line.at[0 if upward else 1, zz, part])

    def ways(k, allowed):
        zz = level(k)
        for upward in (True, False):
            yield zz, upward, allowed() & (zz > z if upward else zz < z)

    def pass_on(k, allowed):
        more = {True: z > 0, False: z < levels - 1}
        for zz, upward, inside in ways(k, allowed):

            @pl.when(inside)
            def _(zz=zz, upward=upward):
                for part in range(2):

                    @pl.when(more[upward])
                    def _(part=part):
                        take(upward, zz, part)

                    along(upward, zz, part).start()

    def close_pass(k, allowed):
        for zz, upward, inside in ways(k, allowed):

            @pl.when(inside)
            def _(zz=zz, upward=upward):
                for part in range(2):
                    along(upward, zz, part).wait_send()

    def at_edge():
        return (z == 0) | (z == levels - 1)

    def off_edge():
        return (z > 0) & (z < levels - 1)

    def anywhere():
        return z >= 0

    def once(k):
        diagonal(k)
        sides(k)

    def final():
        for part in range(2):

            @pl.when(z > 0)
            def _(part=part):
                take(True, z, part)

            @pl.when(z < levels - 1)
            def _(part=part):
                take(False, z, part)

    stages = {
        "begin": begin,
        "once0": lambda: once(0),
        "once1": lambda: once(1),
        "middle0": lambda: middle(0),
        "once2": lambda: once(2),
        "middle1": lambda: middle(1),
        "home0": lambda: home(0),
        "pass0": lambda: pass_on(0, at_edge),
        "once3": lambda: once(3),
        "middle2": lambda: middle(2),
        "middle3": lambda: middle(3),
        "home1": lambda: home(1),
        "pass1": lambda: pass_on(1, anywhere),
        "home2": lambda: home(2),
        "pass2": lambda: pass_on(2, anywhere),
        "inner0": lambda: pass_on(0, off_edge),
        "home3": lambda: home(3),
        "final": final,
    }

    def finish():
        for k, allowed in ((0, at_edge), (1, anywhere), (2, anywhere), (0, off_edge)):
            close_pass(k, allowed)

        def close(k, _):
            zz = level(k)
            for yy, xx in columns:
                to_twin(yy, xx, zz).wait_send()
            wide(0, 1 - x, zz).wait_send()
            wide(0, x, zz).wait_send()
            wide(1, 1 - y, zz).wait_send()
            wide(1, y, zz).wait_send()
            slim(0, zz).wait_send()
            slim(1, zz).wait_send()
            return 0

        lax.fori_loop(0, levels, close, 0)

    return stages, finish, acc.at[slot_of(y, x, z)]


def scatter_scratch(group, inner):
    dma = pltpu.SemaphoreType.DMA
    half, levels = group.devices // 2, inner // 2
    part = (group.half, LANE)
    return [
        pltpu.VMEM((half, group.chunk, LANE), BF),
        pltpu.VMEM((half, group.chunk, LANE), BF),
        pltpu.VMEM((2 * levels, *part), BF),
        pltpu.VMEM((2 * levels, *part), BF),
        pltpu.VMEM((levels, *part), BF),
        pltpu.VMEM((levels, *part), BF),
        pltpu.VMEM((2, levels, 2, *part), BF),
        dma((half,)),
        dma((half,)),
        dma((half,)),
        dma((2, 2 * levels)),
        dma((2, 2 * levels)),
        dma((2, levels)),
        dma((2, levels)),
        dma((2, levels, 2)),
        dma((2, levels, 2)),
    ]


def scatter_kernel(
    g_ref, rows_ref, out_ref, all_ref, own_sem, row_send, row_recv, *rest, group, inner, receivers
):
    me = lax.axis_index("dp") * inner + lax.axis_index("fsdp")
    meet_all(me, group.devices, inner)
    stages, finish, total = scatter_stages(group, inner, g_ref, *rest[:-2])
    trade = Trade(
        rows_ref, all_ref, own_sem, row_send, row_recv, group, inner, group.devices, receivers
    )
    trade.start()
    for stage in stages.values():
        stage()
    deal = Deal(group, total, out_ref, *rest[-2:], inner, True)
    deal.start()
    finish()
    trade.wait()
    deal.landed()
    deal.gone()


def scatter_chunks(grads, rows, group, inner, receivers, collective):
    dma = pltpu.SemaphoreType.DMA
    return remote_call(
        functools.partial(scatter_kernel, group=group, inner=inner, receivers=receivers),
        [ANYWHERE] * 2,
        [ANYWHERE] * 2,
        [
            jax.ShapeDtypeStruct((group.padded, LANE), BF),
            jax.ShapeDtypeStruct((group.devices, *rows.shape), rows.dtype),
        ],
        [dma, dma((group.devices,)), dma((group.devices,))]
        + scatter_scratch(group, inner)
        + Deal.semaphores(group, True),
        collective,
        "scatter_chunks",
    )(grads, rows)


def front_kernel(
    x_ref, mod_ref, w_ref, chunk_ref, qkv_ref, o_ref, l_ref, out_ref, qkv_s, *sems,
    group, inner, leads, pairs
):
    step = pl.program_id(0)
    last = pl.num_programs(0) - 1
    clips, frames, _ = qkv_s.shape
    rows = x_ref.shape[1]
    gather = Gather(group, inner, chunk_ref, out_ref, *sems)
    me = lax.axis_index("dp") * inner + lax.axis_index("fsdp")

    @pl.when(step == 0)
    def _():
        meet_all(me, group.devices, inner)
        gather.turn(0)

    for turn, at in ((1, leads + 1), (2, leads + 3), (3, leads + 5)):

        @pl.when(step == at)
        def _(turn=turn):
            gather.turn(turn)

    @pl.when(step < leads)
    def _():
        normed, _ = normalize(x_ref[0].astype(F32))
        first_in = (normed * (1.0 + mod_ref[0, 1:2]) + mod_ref[0, 0:1]).astype(BF)
        block = nn(first_in, w_ref[...]).astype(BF)
        qkv_ref[0] = block
        start = pl.multiple_of(step * rows % frames, rows)
        qkv_s[step * rows // frames, pl.ds(start, rows)] = block

    @pl.when(step >= leads)
    def _():
        lane, low = head_lanes()
        count = HEADS // 2 // pairs
        clip, group_index = (step - leads) // count, (step - leads) % count
        for pair in range(pairs):

            def columns(part):
                at = (group_index * pairs + pair + part * HEADS // 2) * 2 * HD
                return qkv_s[clip, :, pl.ds(pl.multiple_of(at, 2 * HD), 2 * HD)]

            attend_pair(
                lane,
                low,
                None,
                columns(0),
                columns(1),
                columns(2),
                o_ref.at[0, :, pair * 2 * HD : (pair + 1) * 2 * HD],
                l_ref.at[0, pair],
            )

    @pl.when(step == last)
    def _():
        for turn in range(4, inner // 2 + 2):
            gather.turn(turn)
        gather.finish()


def front_and_gather(latents, mod, weight, chunk, group, inner, collective, pairs=2):
    clips, frames, width = latents.shape
    rows = row_block(frames)
    per = frames // rows
    leads = clips * per
    count = HEADS // 2 // pairs

    def lead(s):
        return jnp.minimum(s, leads - 1)

    def tail(s):
        return jnp.maximum(s - leads, 0)

    wide = weight.shape[1]
    return remote_call(
        functools.partial(front_kernel, group=group, inner=inner, leads=leads, pairs=pairs),
        [
            pl.BlockSpec((1, rows, width), lambda s: (lead(s) // per, lead(s) % per, 0)),
            pl.BlockSpec((1, 9, width), lambda s: (lead(s) // per, 0, 0)),
            whole_spec(weight.shape),
            ANYWHERE,
        ],
        [
            pl.BlockSpec((1, rows, wide), lambda s: (lead(s) // per, lead(s) % per, 0)),
            pl.BlockSpec(
                (1, frames, 2 * HD * pairs), lambda s: (tail(s) // count, 0, tail(s) % count)
            ),
            pl.BlockSpec(
                (1, pairs, frames, 2 * HD), lambda s: (tail(s) // count, tail(s) % count, 0, 0)
            ),
            ANYWHERE,
        ],
        [
            struct((clips, frames, wide), BF),
            struct((clips, frames, width), BF),
            struct((clips, HEADS // 2, frames, 2 * HD), F32),
            struct((group.devices, group.chunk, LANE), BF),
        ],
        [pltpu.VMEM((clips, frames, wide), BF)] + Gather.semaphores(group),
        collective,
        "front_and_gather",
        (leads + clips * count,),
    )(latents, mod, weight, chunk)


def back_kernel(
    q_ref, k_ref, v_ref, do_ref, o_ref, l_ref, x_ref, dh_ref, mod_ref, w_ref, g_ref,
    out_ref, dw_ref, sums_ref, rest_ref, grad_s, in_s, *scratch,
    group, inner, pairs, period
):
    step = pl.program_id(0)
    last = pl.num_programs(0) - 1
    clip, turn = step // period, step % period
    width = x_ref.shape[2]
    rows = x_ref.shape[1]
    stages, finish, total = scatter_stages(group, inner, g_ref, *scratch[:-2])
    deal = Deal(group, total, rest_ref, *scratch[-2:], inner, True)
    me = lax.axis_index("dp") * inner + lax.axis_index("fsdp")

    @pl.when(step == 0)
    def _():
        meet_all(me, group.devices, inner)

    plan = (
        (0, ("begin",)),
        (1, ("once0", "once1")),
        (3, ("middle0", "once2")),
        (5, ("middle1", "once3")),
        (7, ("home0", "pass0")),
        (8, ("middle2",)),
        (11, ("middle3",)),
        (12, ("home1", "pass1")),
        (14, ("home2", "pass2")),
        (16, ("inner0",)),
    )
    for at, names in plan:

        @pl.when(step == at)
        def _(names=names):
            for name in names:
                stages[name]()

    @pl.when(turn < pairs)
    def _():
        lane, low = head_lanes()

        def columns(part):
            at = pl.multiple_of(turn * 2 * HD, 2 * HD)
            return grad_s.at[:, pl.ds(part * width + at, 2 * HD)]

        attend_back_pair(
            lane,
            low,
            None,
            q_ref[0],
            k_ref[0],
            v_ref[0],
            do_ref[0],
            o_ref[0],
            l_ref[0, 0],
            columns(0),
            columns(1),
            columns(2),
        )

    clear_at(turn == pairs, sums_ref)

    @pl.when(turn >= pairs)
    def _():
        here = pl.ds(pl.multiple_of((turn - pairs) * rows, rows), rows)
        normed, inverse = normalize(x_ref[0].astype(F32))
        in_s[here] = (normed * (1.0 + mod_ref[0, 1:2]) + mod_ref[0, 0:1]).astype(BF)
        grad_in = None
        for index in range(3):
            part = slice(index * width, (index + 1) * width)
            product = nt(grad_s[here, part], w_ref[:, part])
            grad_in = product if grad_in is None else grad_in + product
        out_ref[0] = (
            dh_ref[0] + norm_back(normed, inverse, grad_in * (1.0 + mod_ref[0, 1:2]))
        ).astype(BF)
        sums_ref[0] += jnp.concatenate(
            [column_sum(grad_in), column_sum(grad_in * normed)], axis=0
        )

    @pl.when(turn == period - 1)
    def _():
        turned = in_s[...].T
        for index in range(3):
            part = slice(index * width, (index + 1) * width)
            product = nn(turned, grad_s[:, part])

            @pl.when(clip == 0)
            def _(product=product, part=part):
                dw_ref[:, part] = product.astype(BF)

            @pl.when(clip > 0)
            def _(product=product, part=part):
                dw_ref[:, part] = (dw_ref[:, part].astype(F32) + product).astype(BF)

    @pl.when(step == last)
    def _():
        for name in ("home3", "final"):
            stages[name]()
        deal.start()
        finish()
        deal.landed()
        deal.gone()


def back_and_scatter(
    queries, grad, mixed, lse, latents, dh, mod, weight, chunks, group, inner, collective
):
    clips, frames, wide = queries.shape
    width = wide // 3
    pairs = HEADS // 2
    rows = frames // 3
    period = pairs + frames // rows

    def pair_at(part):
        return pl.BlockSpec(
            (1, frames, 2 * HD),
            lambda s: (s // period, 0, jnp.minimum(s % period, pairs - 1) + part * pairs),
        )

    lse_at = pl.BlockSpec(
        (1, 1, frames, 2 * HD),
        lambda s: (s // period, jnp.minimum(s % period, pairs - 1), 0, 0),
    )
    rows_at = pl.BlockSpec(
        (1, rows, width), lambda s: (s // period, jnp.maximum(s % period - pairs, 0), 0)
    )

    def clip_at(count):
        return pl.BlockSpec((1, count, width), lambda s: (s // period, 0, 0))

    whole = pl.BlockSpec(weight.shape, lambda s: (0, 0), pipeline_mode=pl.Buffered(1))
    return remote_call(
        functools.partial(back_kernel, group=group, inner=inner, pairs=pairs, period=period),
        [
            pair_at(0),
            pair_at(1),
            pair_at(2),
            pair_at(0),
            pair_at(0),
            lse_at,
            rows_at,
            rows_at,
            clip_at(9),
            whole,
            ANYWHERE,
        ],
        [rows_at, whole, clip_at(2), ANYWHERE],
        [
            struct((clips, frames, width), BF),
            struct(weight.shape, BF),
            struct((clips, 2, width), F32),
            struct((group.padded, LANE), BF),
        ],
        [pltpu.VMEM((frames, wide), BF), pltpu.VMEM((frames, width), BF)]
        + scatter_scratch(group, inner)
        + Deal.semaphores(group, True),
        collective,
        "back_and_scatter",
        (clips * period,),
    )(queries, queries, queries, grad, mixed, lse, latents, dh, mod, weight, chunks)


def exchange_kernel(in_ref, out_ref, own_sem, send_sem, recv_sem, *, group, inner):
    me = lax.axis_index("dp") * inner + lax.axis_index("fsdp")
    meet_all(me, group.devices, inner)
    trade = Trade(
        in_ref, out_ref, own_sem, send_sem, recv_sem, group, inner, group.devices, group.devices
    )
    trade.start()
    trade.wait()


def exchange(value, group, inner, collective, name):
    dma = pltpu.SemaphoreType.DMA
    return remote_call(
        functools.partial(exchange_kernel, group=group, inner=inner),
        [ANYWHERE],
        ANYWHERE,
        jax.ShapeDtypeStruct((group.devices, *value.shape), value.dtype),
        [dma, dma((group.devices,)), dma((group.devices,))],
        collective,
        name,
    )(value)


HALF = 27
TALL = 72
SLAB = 112
CONDITION_ROWS = 832


def ada_spots(me, group):
    lines = group.share // HALF
    odd = me % 2
    limit = CONDITION_ROWS - TALL
    return [
        (odd, jnp.minimum((lines * me + odd) // 2, limit)),
        (1 - odd, jnp.minimum((lines * me - odd) // 2, limit)),
    ]


def ada_kernel(lin_ref, cond_ref, out_ref, *, group, inner):
    me = lax.axis_index("dp") * inner + lax.axis_index("fsdp")
    for half, (shift, top) in enumerate(ada_spots(me, group)):
        condition = cond_ref[pl.ds(top, TALL)].astype(BF)

        def body(c, _, half=half, shift=shift, condition=condition):
            rows = lin_ref[pl.ds(HALF * shift + c, TALL, stride=2 * HALF)].astype(BF)
            part = tn(condition, rows)
            count = group.devices
            for clip in range(2):
                out_ref[pl.ds((2 * clip + half) * HALF + c, count, stride=SLAB)] = part[
                    clip * count : (clip + 1) * count
                ]
            return 0

        lax.fori_loop(0, HALF, body, 0, unroll=True)


def ada_partial(lin, cond, group, inner):
    return pl.pallas_call(
        functools.partial(ada_kernel, group=group, inner=inner),
        out_shape=jax.ShapeDtypeStruct((group.devices * SLAB, LANE), F32),
        compiler_params=pltpu.CompilerParams(vmem_limit_bytes=VMEM_LIMIT),
        name="ada_partial",
    )(lin, cond)


def own_grad_kernel(
    cond_ref, given_ref, early_ref, late_ref, g_ref, sums_ref, lin, dmod_ref, *, group, inner
):
    me = lax.axis_index("dp") * inner + lax.axis_index("fsdp")
    count = group.devices // 2
    border = jnp.clip(group.first - group.share * me, 0, group.share)
    middle = jnp.clip(group.last - group.share * me, 0, group.share)

    @pl.when(border > 0)
    def _():
        dmod_ref[...] = given_ref[...].astype(F32)

    for half, (shift, top) in enumerate(ada_spots(me, group)):
        condition = cond_ref[pl.ds(top, TALL)].astype(BF)

        def body(c, _, half=half, shift=shift, condition=condition):
            grads = jnp.concatenate(
                [
                    dmod_ref[
                        pl.ds(core * SLAB + (2 * clip + half) * HALF + c, count, stride=2 * SLAB)
                    ]
                    for clip in range(2)
                    for core in range(2)
                ],
                axis=0,
            ).astype(BF)
            lin[pl.ds(HALF * shift + c, TALL, stride=2 * HALF)] = nn(condition, grads)
            return 0

        @pl.when(border > 0)
        def _(body=body):
            lax.fori_loop(0, HALF, body, 0, unroll=True)

    rows = 64

    def merge(i, total):
        at = pl.multiple_of(i * rows, rows)
        row = lax.broadcasted_iota(jnp.int32, (rows, LANE), 0) + at
        early = early_ref[pl.ds(at, rows)].astype(F32)
        late = jnp.where(row < group.share, late_ref[pl.ds(at, rows)].astype(F32), 0.0)
        value = jnp.where(
            row < border, lin[pl.ds(at, rows)], jnp.where(row < middle, early, late)
        )
        g_ref[pl.ds(at, rows)] = value
        square = value * value
        return total + sum(square[k : k + 8] for k in range(0, rows, 8))

    sums_ref[...] = lax.fori_loop(0, group.padded // rows, merge, jnp.zeros((8, LANE), F32))


def own_grad(cond, dmod, early, late, group, inner):
    return pl.pallas_call(
        functools.partial(own_grad_kernel, group=group, inner=inner),
        out_shape=[
            jax.ShapeDtypeStruct((group.padded, LANE), F32),
            jax.ShapeDtypeStruct((8, LANE), F32),
        ],
        scratch_shapes=[
            pltpu.VMEM((2 * HALF * TALL, LANE), F32),
            pltpu.VMEM(dmod.shape, F32),
        ],
        compiler_params=pltpu.CompilerParams(vmem_limit_bytes=VMEM_LIMIT),
        name="own_grad",
    )(cond, dmod, early, late)


def fits(devices, inner, share):
    return inner == 8 and devices == 32 and share % (LANE * HALF) == 0


def local_fast(latents, captions, lengths, timesteps, cotangent, master):
    clips, frames, width = latents.shape
    share = master.shape[0]
    inner = lax.axis_size("fsdp")
    devices = inner * lax.axis_size("dp")
    spots = linear_layout()
    end = spots[-1][0] + spots[-1][1]
    early = Group(devices, inner, share // LANE, spots[2][0], spots[3][0])
    late = Group(devices, inner, share // LANE, spots[3][0], end)
    holders = spots[2][0] // early.share + 1

    lin = lax.optimization_barrier(
        jnp.pad(
            master.reshape(early.share, LANE), ((0, 2 * HALF * TALL - early.share), (0, 0))
        )
    )
    slot = lin[: early.padded].astype(BF)
    steps, chunk = start_chunks(
        jnp.broadcast_to(
            jnp.pad(timesteps.astype(F32), (0, 8 - clips))[:, None], (8, LANE)
        ),
        slot,
        early,
        inner,
        1,
    )
    steps = steps[:, :clips, 0].reshape(devices // 2, 2, clips).T.reshape(devices * clips)
    columns = jax.nn.silu(embed(steps)).astype(BF).astype(F32).T
    columns = jnp.concatenate(
        [
            columns,
            jnp.ones((1, clips * devices), F32),
            jnp.zeros((CONDITION_ROWS - width - 1, clips * devices), F32),
        ],
        axis=0,
    )
    slabs = ada_partial(lin, columns, early, inner).reshape(2, devices // 2, SLAB, LANE)
    gathered, parts, later_chunk = gather_chunks(
        chunk, slabs, slot, early, late, inner, holders, 2
    )
    mod = jnp.sum(parts, axis=0)[: 54 * clips].reshape(clips, 9, width)
    (triple_weight,) = unpack_weights(gathered, early, (2,))

    def front(latents, mod, triple_weight):
        triple, mixed, lse, later = front_and_gather(
            latents, mod, triple_weight, later_chunk, late, inner, 3
        )
        return triple, mixed, lse, unpack_weights(later, late, tuple(range(3, 13)))

    def back(triple, grad_mixed, mixed, lse, latents, dh, mod, triple_weight, gradients):
        chunks = pack_grads(gradients, late, tuple(range(3, 13)))
        return back_and_scatter(
            triple,
            grad_mixed,
            mixed,
            lse,
            latents,
            dh,
            mod,
            triple_weight,
            chunks,
            late,
            inner,
            4,
        )

    output, input_grad, grad_mod, grad_triple, _, late_grads = block_pass(
        latents, captions, lengths, cotangent, mod, triple_weight, front, back
    )
    grad_rows = jnp.pad(
        grad_mod.reshape(54 * clips, LANE), ((0, SLAB - 54 * clips), (0, 0))
    )
    chunks = pack_grads([grad_triple], early, (2,))
    early_grads, dmod = scatter_chunks(chunks, grad_rows, early, inner, holders, 5)
    grads, squares = own_grad(
        columns,
        dmod.reshape(devices * SLAB, LANE),
        early_grads,
        late_grads,
        early,
        inner,
    )
    squares = exchange(squares, early, inner, 6, "squares")
    return (
        output,
        input_grad,
        grads[: early.share].reshape(share),
        jnp.sum(squares),
    )


def local_any(latents, captions, lengths, timesteps, cotangent, master):
    clips, frames, width = latents.shape
    share = master.shape[0]
    devices = lax.axis_size("dp") * lax.axis_size("fsdp")
    gathered = lax.all_gather(
        master.astype(BF).reshape(1, share), ("dp", "fsdp"), axis=0, tiled=True
    ).reshape(-1)
    weights = unpack(gathered)
    condition = jax.nn.silu(embed(timesteps)).astype(BF)
    mod = jnp.dot(condition, weights[0], preferred_element_type=F32) + weights[1].astype(F32)
    block_weights = [w.astype(F32).reshape(1, -1) if w.ndim == 1 else w for w in weights[2:]]
    output, input_grad, grad_mod, grad_triple, gradients, _ = block_pass(
        latents,
        captions,
        lengths,
        cotangent,
        mod.reshape(clips, 9, width),
        block_weights[0],
        functools.partial(plain_front, block_weights[1:]),
        plain_back,
    )
    grad_mod = grad_mod.reshape(clips, 9 * width)
    grad_ada = jnp.dot(condition.T, grad_mod, preferred_element_type=F32)
    grad_list = [grad_ada, jnp.sum(grad_mod.astype(F32), axis=0), grad_triple] + gradients
    flat = jnp.concatenate([piece.astype(F32).reshape(-1) for piece in grad_list])
    grad = lax.psum_scatter(
        flat.reshape(devices, share), ("dp", "fsdp"), scatter_dimension=0, tiled=True
    ).reshape(share)
    return output, input_grad, grad, lax.psum(jnp.sum(grad * grad), ("dp", "fsdp"))


def local(
    latents,
    captions,
    caption_lengths,
    timesteps,
    cotangent,
    master_weights,
    first_moment,
    second_moment,
):
    inner = lax.axis_size("fsdp")
    devices = inner * lax.axis_size("dp")
    run = local_fast if fits(devices, inner, master_weights.shape[0]) else local_any
    output, input_grad, grad_shard, squares = run(
        latents,
        captions,
        caption_lengths,
        timesteps,
        cotangent,
        master_weights,
    )
    grad_norm = jnp.sqrt(squares)
    clipped = grad_shard * (CLIP / jnp.maximum(grad_norm, CLIP))
    new_first = BETA_ONE * first_moment + (1.0 - BETA_ONE) * clipped
    new_second = BETA_TWO * second_moment + (1.0 - BETA_TWO) * clipped * clipped
    step_first = new_first / (1.0 - BETA_ONE**STEP)
    step_second = new_second / (1.0 - BETA_TWO**STEP)
    new_master = master_weights - RATE * (
        step_first / (jnp.sqrt(step_second) + ADAM_EPS) + DECAY * master_weights
    )
    return (output, input_grad, grad_norm, new_master, new_first, new_second)


def solution(mesh):
    placed = (
        P(("dp", "fsdp"), None, None),
        P(("dp", "fsdp"), None, None),
        P(("dp", "fsdp")),
        P(("dp", "fsdp")),
        P(("dp", "fsdp"), None, None),
        P(("dp", "fsdp")),
        P(("dp", "fsdp")),
        P(("dp", "fsdp")),
    )
    return jax.shard_map(
        local,
        mesh=mesh,
        in_specs=placed,
        out_specs=(
            P(("dp", "fsdp"), None, None),
            P(("dp", "fsdp"), None, None),
            P(),
            P(("dp", "fsdp")),
            P(("dp", "fsdp")),
            P(("dp", "fsdp")),
        ),
        check_vma=False,
    )
```
